32 devices in a mesh: dp: 8 (over z, y), seq: 4 (over x, core).
Axes of the slice: x: 2, y: 2, z: 4, core: 2. Of those that a mesh axis runs over, the one named last changes fastest.
Arguments:
- decoder_in: bfloat16 [32, 512, 768], P(('dp', 'seq')), may hold values from -6 to 6
- memory: bfloat16 [32, 8192, 768], P(None, ('dp', 'seq')), may hold values from -6 to 6
- memory_lengths: int32 [32], P(('dp', 'seq')), may hold values from 3072 to 8192, as said below
- cotangent: bfloat16 [32, 512, 768], P(('dp', 'seq')), may hold values from -6 to 6
- norm_self: float32 [768], replicated, may hold values from 0.5 to 1.5
- self_query: bfloat16 [768, 768], replicated, may hold values from -0.0546875 to 0.0546875
- self_key: bfloat16 [768, 768], replicated, may hold values from -0.21875 to 0.21875
- self_value: bfloat16 [768, 768], replicated, may hold values from -0.21875 to 0.21875
- self_out: bfloat16 [768, 768], replicated, may hold values from -0.625 to 0.625
- norm_cross: float32 [768], replicated, may hold values from 0.5 to 1.5
- cross_query: bfloat16 [768, 768], replicated, may hold values from -0.0546875 to 0.0546875
- cross_key: bfloat16 [768, 768], replicated, may hold values from -0.21875 to 0.21875
- cross_value: bfloat16 [768, 768], replicated, may hold values from -0.21875 to 0.21875
- cross_out: bfloat16 [768, 768], replicated, may hold values from -0.875 to 0.875
- norm_ffn: float32 [768], replicated, may hold values from 0.5 to 1.5
- ffn_gate: bfloat16 [768, 2048], replicated, may hold values from -0.21875 to 0.21875
- ffn_up: bfloat16 [768, 2048], replicated, may hold values from -0.21875 to 0.21875
- ffn_down: bfloat16 [2048, 768], replicated, may hold values from -0.125 to 0.125
Outputs:
- decoder_out: bfloat16 [32, 512, 768], P(('dp', 'seq'))
- decoder_in_grad: float32 [32, 512, 768], P(('dp', 'seq'))
- memory_grad: bfloat16 [32, 8192, 768], P(None, ('dp', 'seq'))
- norm_self_grad: float32 [768], P(('dp', 'seq'))
- self_query_grad: float32 [768, 768], P(('dp', 'seq'))
- self_key_grad: float32 [768, 768], P(('dp', 'seq'))
- self_value_grad: float32 [768, 768], P(('dp', 'seq'))
- self_out_grad: float32 [768, 768], P(('dp', 'seq'))
- norm_cross_grad: float32 [768], P(('dp', 'seq'))
- cross_query_grad: float32 [768, 768], P(('dp', 'seq'))
- cross_key_grad: float32 [768, 768], P(('dp', 'seq'))
- cross_value_grad: float32 [768, 768], P(('dp', 'seq'))
- cross_out_grad: float32 [768, 768], P(('dp', 'seq'))
- norm_ffn_grad: float32 [768], P(('dp', 'seq'))
- ffn_gate_grad: float32 [768, 2048], P(('dp', 'seq'))
- ffn_up_grad: float32 [768, 2048], P(('dp', 'seq'))
- ffn_down_grad: float32 [2048, 768], P(('dp', 'seq'))
The draws below stay inside these ranges and needn't reach their ends.
Inputs may be any that keep to these rules, and one draw needn't show every extreme that they name: `memory_lengths`: memory positions of each sequence that are valid; in every draw at least one sequence uses all 8192 positions.
All inputs are finite; a program needn't handle non-finite values.
Results may differ from the reference program's by a relative error of at most 0.025.
The reference program's roundings to bfloat16 on the way count: a program that leaves them out, or rounds other values in their place, can miss the bound.
Values may be sent and summed in bfloat16 or wider, within the bound.
A program may use at most 384 MiB of HBM per device.

```python
import jax
import jax.numpy as jnp
from jax import lax

D = 768
H = 12
HD = 64
FF = 2048
TGT = 512
MEMLEN = 8192
B_TOTAL = 32


def draw_memory_lengths(key, part):
    key = jax.random.fold_in(key, 11)
    first, second, third = jax.random.split(key, 3)
    base = jax.random.randint(first, (B_TOTAL,), 3 * MEMLEN // 8, 5 * MEMLEN // 8 + 1)
    longest = jax.random.randint(second, (B_TOTAL,), 0, 8) == 0
    chosen = jax.random.randint(third, (), 0, B_TOTAL)
    longest = longest | (jnp.arange(B_TOTAL) == chosen)
    return jnp.where(longest, MEMLEN, base).astype(jnp.int32)


def steps_of(rng, extent, shards, low, largest):
    def one(position, shards_of):
        steps = jax.random.uniform(jax.random.fold_in(jax.random.fold_in(rng, 6), position), (shards_of,), jnp.float32, low / len(shards), largest / len(shards))
        return jnp.repeat(jnp.exp(steps), extent[position] // shards_of).reshape((-1,) + (1,) * (len(extent) - position - 1))

    level = one(*shards[0])
    for cut in shards[1:]:
        level = level * one(*cut)
    return level


def centred(stream_key, extent, deviation, bound, cuts=(), dtype=jnp.bfloat16):
    values = jax.random.normal(stream_key, extent, jnp.float32) * deviation
    if len(cuts) > 0:
        values = steps_of(stream_key, extent, cuts, -0.22, 0.18) * values
    return jnp.clip(values, min=-bound, max=bound).astype(dtype)


def setup_inputs(seed: int = 0) -> dict:
    key_list = jax.random.split(jax.random.key(seed), 19)
    decoder_in = centred(key_list[0], (B_TOTAL, TGT, D), 1.0, 6.0, ((0, 32),))
    memory = centred(key_list[1], (B_TOTAL, MEMLEN, D), 1.0, 6.0, ((1, 32),))
    memory_lengths = draw_memory_lengths(jax.random.fold_in(key_list[18], 71), 0)
    cotangent = centred(key_list[3], (B_TOTAL, TGT, D), 1.0, 6.0, ((0, 32),))
    norm_self = jnp.clip(1.0 + 0.1 * jax.random.normal(key_list[4], (D,), jnp.float32), 0.5, 1.5)
    self_query = centred(key_list[5], (D, D), (16 * D) ** -0.5, 0.0546875)
    self_key = centred(key_list[6], (D, D), D ** -0.5, 0.21875)
    self_value = centred(key_list[7], (D, D), D ** -0.5, 0.21875)
    self_out = centred(key_list[8], (D, D), (D // 8) ** -0.5, 0.625)
    norm_cross = jnp.clip(1.0 + 0.1 * jax.random.normal(key_list[9], (D,), jnp.float32), 0.5, 1.5)
    cross_query = centred(key_list[10], (D, D), (16 * D) ** -0.5, 0.0546875)
    cross_key = centred(key_list[11], (D, D), D ** -0.5, 0.21875)
    cross_value = centred(key_list[12], (D, D), D ** -0.5, 0.21875)
    cross_out = centred(key_list[13], (D, D), (D // 16) ** -0.5, 0.875)
    norm_ffn = jnp.clip(1.0 + 0.1 * jax.random.normal(key_list[14], (D,), jnp.float32), 0.5, 1.5)
    ffn_gate = centred(key_list[15], (D, FF), D ** -0.5, 0.21875)
    ffn_up = centred(key_list[16], (D, FF), D ** -0.5, 0.21875)
    ffn_down = centred(key_list[17], (FF, D), FF ** -0.5, 0.125)
    return {"decoder_in": decoder_in, "memory": memory, "memory_lengths": memory_lengths, "cotangent": cotangent, "norm_self": norm_self, "self_query": self_query, "self_key": self_key, "self_value": self_value, "self_out": self_out, "norm_cross": norm_cross, "cross_query": cross_query, "cross_key": cross_key, "cross_value": cross_value, "cross_out": cross_out, "norm_ffn": norm_ffn, "ffn_gate": ffn_gate, "ffn_up": ffn_up, "ffn_down": ffn_down}


EPSILON = 1e-06
MASKED_SCORE = -1e+30

@jax.custom_vjp
def low(v):
    return lax.optimization_barrier(v.astype(jnp.bfloat16)).astype(jnp.float32)

@jax.custom_vjp
def low_back(v):
    return v

def low_keep(v):
    return (low(v), None)

def low_pass(kept, grad):
    return (grad,)

def back_keep(v):
    return (v, None)

def back_low(kept, grad):
    return (low(grad),)
low.defvjp(low_keep, low_pass)
low_back.defvjp(back_keep, back_low)

def highest(left, right):
    return jnp.dot(left, right, precision=lax.Precision.HIGHEST, preferred_element_type=jnp.float32)

def rounded(values):
    return low(low_back(values))

def rms_norm(values, gain):
    return values * lax.rsqrt(lax.optimization_barrier(jnp.mean(values * values, axis=-1, keepdims=True)) + EPSILON) * gain

def to_heads(matrix):
    return matrix.reshape(matrix.shape[0], H, HD).transpose(1, 0, 2)

def attention(queries, keyset, valset, allowed):

    def one_head(head_entry):
        queries_head, keys_head, values_head = head_entry
        scores = low_back(highest(queries_head, keys_head.T))
        scores = jnp.where(allowed, scores, MASKED_SCORE)
        row_max = lax.optimization_barrier(jnp.max(scores, axis=-1, keepdims=True))
        numerators = jnp.exp(scores - row_max)
        probs = low(numerators / lax.optimization_barrier(jnp.sum(numerators, axis=-1, keepdims=True)))
        return highest(probs, values_head)
    outputs = lax.map(jax.checkpoint(one_head), (to_heads(queries), to_heads(keyset), to_heads(valset)))
    return outputs.transpose(1, 0, 2).reshape(queries.shape[0], H * HD)

def layer(inputs, memory_rows, key_limit, params):
    norm_self, self_query, self_key, self_value, self_out, norm_cross, cross_query, cross_key, cross_value, cross_out, norm_ffn, ffn_gate, ffn_up, ffn_down = params
    row_index = lax.broadcasted_iota(jnp.int32, (TGT, TGT), 0)
    col_index = lax.broadcasted_iota(jnp.int32, (TGT, TGT), 1)
    causal = col_index <= row_index
    reach = lax.broadcasted_iota(jnp.int32, (TGT, MEMLEN), 1) < key_limit
    normed_one = low(rms_norm(inputs, norm_self))
    query_one = rounded(highest(normed_one, self_query))
    key_one = rounded(highest(normed_one, self_key))
    value_one = rounded(highest(normed_one, self_value))
    attn_one = rounded(attention(query_one, key_one, value_one, causal))
    hidden_one = inputs + low_back(highest(attn_one, self_out))
    normed_two = low(rms_norm(hidden_one, norm_cross))
    query_two = rounded(highest(normed_two, cross_query))
    key_two = rounded(highest(memory_rows, cross_key))
    value_two = rounded(highest(memory_rows, cross_value))
    attn_two = rounded(attention(query_two, key_two, value_two, reach))
    hidden_two = hidden_one + low_back(highest(attn_two, cross_out))
    normed_three = low(rms_norm(hidden_two, norm_ffn))
    gate_vals = low_back(highest(normed_three, ffn_gate))
    up_vals = low_back(highest(normed_three, ffn_up))
    inner = low(jax.nn.gelu(gate_vals, approximate=True) * up_vals)
    return hidden_two + low_back(highest(inner, ffn_down))

def reference(decoder_in, memory, memory_lengths, cotangent, norm_self, self_query, self_key, self_value, self_out, norm_cross, cross_query, cross_key, cross_value, cross_out, norm_ffn, ffn_gate, ffn_up, ffn_down):
    params = tuple((weight.astype(jnp.float32) for weight in (norm_self, self_query, self_key, self_value, self_out, norm_cross, cross_query, cross_key, cross_value, cross_out, norm_ffn, ffn_gate, ffn_up, ffn_down)))

    def per_sequence(totals, entry):
        inputs, memory_rows, key_limit, grad_rows = entry

        def forward(inputs_f, memory_f, weights):
            return layer(inputs_f, memory_f, key_limit, weights)
        result, pullback = jax.vjp(forward, inputs.astype(jnp.float32), memory_rows.astype(jnp.float32), params)
        grad_in, grad_mem, grad_weights = pullback(grad_rows.astype(jnp.float32))
        totals = jax.tree.map(lambda summed, added: summed + added, totals, grad_weights)
        return (totals, (result.astype(jnp.bfloat16), grad_in, grad_mem.astype(jnp.bfloat16)))
    zeros = jax.tree.map(jnp.zeros_like, params)
    totals, stacked = lax.scan(per_sequence, zeros, (decoder_in, memory, memory_lengths, cotangent))
    return (stacked[0], stacked[1], stacked[2], totals[0], totals[1], totals[2], totals[3], totals[4], totals[5], totals[6], totals[7], totals[8], totals[9], totals[10], totals[11], totals[12], totals[13])
```

```python
import functools

import jax
import jax.numpy as jnp
from jax import lax
from jax.experimental import pallas as pl
from jax.experimental.pallas import tpu as pltpu
from jax.sharding import Mesh
from jax.sharding import PartitionSpec as P

H = 12
HD = 64
PAIRS = 6
PLANES = 4
EPSILON = 1e-06
MASKED = -1e30
VMEM = 56 * 2**20
BF = jnp.bfloat16
F32 = jnp.float32
ALL = ("z", "y", "x", "c")
PLANE = ("y", "x", "c")


def dot(left, right, left_dim, right_dim):
    return lax.dot_general(
        left, right, (((left_dim,), (right_dim,)), ((), ())), preferred_element_type=F32
    )


def lane_masks():
    lane = lax.broadcasted_iota(jnp.int32, (1, 2 * HD), 1)
    low = jnp.where(lane < HD, 1.0, 0.0)
    first = jnp.where(lane == HD, 1.0, 0.0)
    second = jnp.where(lane == 0, 1.0, 0.0)
    low, high, first, second = (
        v.astype(BF) for v in (low, 1.0 - low, first, second)
    )
    return ((low, high, first), (high, low, second))


def causal_mask(scores):
    key = lax.broadcasted_iota(jnp.int32, scores.shape, 0)
    query = lax.broadcasted_iota(jnp.int32, scores.shape, 1)
    return jnp.where(key <= query, scores, MASKED)


def forward_kernel(*refs, causal):
    if causal:
        q_ref, kv_ref, o_ref, lse_ref = refs
    else:
        q_ref, kv_ref, bias_ref, o_ref, lse_ref = refs
        bias = bias_ref[...]
    masks = lane_masks()
    queries = q_ref[...]
    keys = kv_ref[:, 0:128]
    values = kv_ref[:, 128:256]
    all_scores = []
    for mine, other, one in masks:
        if causal:
            all_scores.append(causal_mask(dot(keys, queries * mine, 1, 1)))
        else:
            all_scores.append(dot(keys * mine + bias * one, queries * mine + one, 1, 1))
    parts = []
    for h in range(2):
        mine, other, _ = masks[h]
        scores = all_scores[h]
        row_max = jnp.max(scores, axis=0, keepdims=True)
        probs = jnp.exp(scores - row_max).astype(BF)
        both = dot(values * mine + other, probs, 0, 0)
        halves = (both[:HD], both[HD:])
        total = halves[1 - h]
        parts.append(halves[h] / total)
        lse_ref[0, h : h + 1, :] = row_max + jnp.log(total[0:1])
    o_ref[...] = jnp.concatenate(parts, axis=0).T.astype(BF)


def backward_kernel(*refs, causal):
    if causal:
        q_ref, da_ref, kv_ref, lse_ref, dkv_ref, dq_ref = refs
    else:
        q_ref, da_ref, kv_ref, bias_ref, lse_ref, delta_ref, dkv_ref, dq_ref = refs
        bias = bias_ref[...]
    queries = q_ref[...]
    grad = da_ref[...]
    keys = kv_ref[:, 0:128]
    values = kv_ref[:, 128:256]
    grad_k = None
    grad_v = None
    grad_q = []
    for h, (mine, other, one) in enumerate(lane_masks()):
        query_h = queries * mine
        grad_h = grad * mine
        if causal:
            scores = causal_mask(dot(keys, query_h, 1, 1))
        else:
            scores = dot(keys * mine + bias * one, query_h + one, 1, 1)
        probs = jnp.exp(scores - lse_ref[0, h : h + 1, :])
        grad_p = dot(values, grad_h, 1, 1)
        if causal:
            delta = jnp.sum(probs * grad_p, axis=0, keepdims=True)
        else:
            delta = delta_ref[0, h : h + 1, :]
        grad_s = (probs * (grad_p - delta)).astype(BF)
        term_v = dot(probs.astype(BF), grad_h, 1, 0)
        term_k = dot(grad_s, query_h, 1, 0)
        grad_v = term_v if grad_v is None else grad_v + term_v
        grad_k = term_k if grad_k is None else grad_k + term_k
        grad_q.append(dot(keys, grad_s, 0, 0)[h * HD : (h + 1) * HD])
    dkv_ref[:, 0:128] = grad_k.astype(BF)
    dkv_ref[:, 128:256] = grad_v.astype(BF)
    dq_ref[...] = jnp.concatenate(grad_q, axis=0).T.astype(BF)


def specs(tokens, keys):
    return (
        pl.BlockSpec((tokens, 128), lambda p: (0, p)),
        pl.BlockSpec((keys, 256), lambda p: (0, p)),
        pl.BlockSpec((keys, 128), lambda p: (0, 0)),
        pl.BlockSpec((1, 2, tokens), lambda p: (p, 0, 0)),
    )


def estimate(tokens, keys, count):
    work = tokens * keys * H
    return pl.CostEstimate(
        flops=2 * 4 * count * work * HD, bytes_accessed=keys * 6144, transcendentals=work
    )


def attend(queries, keyvals, bias=None):
    tokens, keys = queries.shape[0], keyvals.shape[0]
    col, pair, mask, row = specs(tokens, keys)
    causal = bias is None
    return pl.pallas_call(
        functools.partial(forward_kernel, causal=causal),
        grid=(PAIRS,),
        out_shape=[
            jax.ShapeDtypeStruct((tokens, H * HD), BF),
            jax.ShapeDtypeStruct((PAIRS, 2, tokens), F32),
        ],
        in_specs=[col, pair] + ([] if causal else [mask]),
        out_specs=[col, row],
        compiler_params=pltpu.CompilerParams(vmem_limit_bytes=VMEM),
        cost_estimate=estimate(tokens, keys, 2),
    )(queries, keyvals, *(() if causal else (bias,)))


def attend_back(queries, grad, keyvals, lse, bias=None, delta=None):
    tokens, keys = queries.shape[0], keyvals.shape[0]
    col, pair, mask, row = specs(tokens, keys)
    causal = bias is None
    if causal:
        in_specs, args = [col, col, pair, row], (queries, grad, keyvals, lse)
    else:
        in_specs = [col, col, pair, mask, row, row]
        args = (queries, grad, keyvals, bias, lse, delta)
    return pl.pallas_call(
        functools.partial(backward_kernel, causal=causal),
        grid=(PAIRS,),
        out_shape=[
            jax.ShapeDtypeStruct((keys, 2 * H * HD), BF),
            jax.ShapeDtypeStruct((tokens, H * HD), BF),
        ],
        in_specs=in_specs,
        out_specs=[pair, col],
        compiler_params=pltpu.CompilerParams(vmem_limit_bytes=VMEM),
        cost_estimate=estimate(tokens, keys, 4),
    )(*args)


def place_kernel(*refs, plane_size):
    *blocks, out_ref, sems = refs
    z = lax.axis_index("z")
    me = lax.axis_index(PLANE)
    copies = []
    for n, block in enumerate(blocks):
        r, k = divmod(n, plane_size)
        row = (z ^ r) * plane_size + (me ^ k)
        copies.append(pltpu.make_async_copy(block, out_ref.at[row], sems.at[n]))
    for copy in copies:
        copy.start()
    for copy in copies:
        copy.wait()


def place(blocks, plane_size):
    shape = blocks[0].shape
    hbm = pl.BlockSpec(memory_space=pl.ANY)
    return pl.pallas_call(
        functools.partial(place_kernel, plane_size=plane_size),
        out_shape=jax.ShapeDtypeStruct((len(blocks),) + shape, blocks[0].dtype),
        in_specs=[hbm] * len(blocks),
        out_specs=hbm,
        scratch_shapes=[pltpu.SemaphoreType.DMA((len(blocks),))],
    )(*blocks)


def interleave(keys, values):
    width = keys.shape[0]
    return jnp.stack(
        [keys.reshape(width, PAIRS, 128), values.reshape(width, PAIRS, 128)], axis=2
    ).reshape(width, 2 * H * HD)


def separate(both):
    rows = both.shape[0]
    parts = both.reshape(rows, PAIRS, 2, 128)
    return parts[:, :, 0].reshape(rows, H * HD), parts[:, :, 1].reshape(rows, H * HD)


def per_row(stat):
    tokens = stat.shape[-1]
    return jnp.repeat(stat.reshape(H, tokens).T, HD, axis=1)


def norm_apply(values, gain):
    return values * lax.rsqrt(jnp.mean(values * values, axis=-1, keepdims=True) + EPSILON) * gain


def norm_back(values, gain, grad):
    r = lax.rsqrt(jnp.mean(values * values, axis=-1, keepdims=True) + EPSILON)
    u = gain * grad
    dv = r * u - values * (r * r * r) * jnp.mean(u * values, axis=-1, keepdims=True)
    return dv, jnp.sum(grad * values * r, axis=0)


def glu_apply(gate_vals, up_vals):
    return jax.nn.gelu(gate_vals, approximate=True) * up_vals


def matmul(left, right):
    return dot(left, right, 1, 0)


def matmul_t(left, right):
    return dot(left, right, 1, 1)


def tmatmul(left, right):
    return dot(left, right, 0, 0)


def scatter_sum(arrays, devices):
    flat = [a.astype(BF).reshape(devices, -1) for a in arrays]
    sizes = [f.shape[1] for f in flat]
    extra = -sum(sizes) % 128
    if extra:
        flat.append(jnp.zeros((devices, extra), BF))
    joined = jnp.concatenate(flat, axis=1)
    mine = lax.psum_scatter(
        joined.reshape(devices, -1, 128), ALL, scatter_dimension=0, tiled=True
    ).reshape(-1).astype(F32)
    out = []
    at = 0
    for size, a in zip(sizes, arrays):
        out.append(mine[at : at + size].reshape((a.shape[0] // devices,) + a.shape[1:]))
        at += size
    return out


def on_device(
    plane_size,
    decoder_in,
    memory,
    memory_lengths,
    cotangent,
    norm_self,
    self_query,
    self_key,
    self_value,
    self_out,
    norm_cross,
    cross_query,
    cross_key,
    cross_value,
    cross_out,
    norm_ffn,
    ffn_gate,
    ffn_up,
    ffn_down,
):
    devices, positions, width = memory.shape
    z = lax.axis_index("z")
    me = lax.axis_index(PLANE)

    def along_z(value, r):
        if r == 0:
            return value
        return lax.ppermute(value, "z", [(i, i ^ r) for i in range(PLANES)])

    def in_plane(value, k):
        if k == 0:
            return value
        return lax.ppermute(value, PLANE, [(i, i ^ k) for i in range(plane_size)])

    by_plane = memory.reshape(PLANES, plane_size, positions, width)
    arrived = {}
    for r in (1, 2, 3, 0):
        group = lax.dynamic_index_in_dim(by_plane, z ^ r, 0, keepdims=False)
        blocks = []
        for k in range(plane_size):
            block = lax.dynamic_index_in_dim(group, me ^ k, 0, keepdims=False)
            blocks.append(in_plane(block, k))
        arrived[r] = blocks

    within = jnp.arange(positions, dtype=jnp.int32)
    places = jnp.concatenate([(z * plane_size + (me ^ k)) * positions + within for k in range(plane_size)])

    inputs = decoder_in[0].astype(F32)
    normed_one = norm_apply(inputs, norm_self).astype(BF)
    self_weights = jnp.concatenate([self_query, interleave(self_key, self_value)], axis=1)
    qkv_one = matmul(normed_one, self_weights).astype(BF)
    query_one, keyval_one = qkv_one[:, :width], qkv_one[:, width:]
    attn_one, lse_one = attend(query_one, keyval_one)
    hidden_one = inputs + matmul(attn_one, self_out)
    normed_two = norm_apply(hidden_one, norm_cross).astype(BF)
    query_two = matmul(normed_two, cross_query).astype(BF)

    cross_weights = interleave(cross_key, cross_value)
    queries, rows, keyvals, biases, partial = {}, {}, {}, {}, {}
    for r in (1, 2, 3, 0):
        queries[r] = along_z(query_two, r)
        limit = along_z(memory_lengths, r)
        bias = jnp.where(places < limit, 0.0, MASKED).astype(BF)
        biases[r] = jnp.broadcast_to(bias[:, None], (bias.shape[0], 128))
    for r in (1, 2, 3, 0):
        rows[r] = jnp.concatenate(arrived[r], axis=0)
        keyvals[r] = matmul(rows[r], cross_weights).astype(BF)
        out_r, lse_r = attend(queries[r], keyvals[r], biases[r])
        partial[r] = (along_z(out_r, r), along_z(lse_r, r))
    lses = jnp.stack([partial[r][1] for r in range(PLANES)])
    top = jnp.max(lses, axis=0)
    scale = jnp.exp(lses - top)
    total = jnp.sum(scale, axis=0)
    lse_two = top + jnp.log(total)
    share = scale / total
    attn_raw_two = sum(per_row(share[r]) * partial[r][0].astype(F32) for r in range(PLANES))
    attn_two = attn_raw_two.astype(BF)
    hidden_two = hidden_one + matmul(attn_two, cross_out)

    normed_three = norm_apply(hidden_two, norm_ffn).astype(BF)
    gate_vals = matmul(normed_three, ffn_gate)
    up_vals = matmul(normed_three, ffn_up)
    inner = glu_apply(gate_vals, up_vals).astype(BF)
    output = hidden_two + matmul(inner, ffn_down)
    decoder_out = output.astype(BF)[None]

    branch_three = cotangent[0]
    grad_out = branch_three.astype(F32)
    grad_inner = matmul_t(branch_three, ffn_down)
    _, glu_pull = jax.vjp(glu_apply, gate_vals, up_vals)
    grad_gate_raw, grad_up_raw = glu_pull(grad_inner)
    grad_gate_low = grad_gate_raw.astype(BF)
    grad_up_low = grad_up_raw.astype(BF)
    grad_normed_three = matmul_t(grad_gate_low, ffn_gate) + matmul_t(grad_up_low, ffn_up)
    back_two, grad_norm_ffn = norm_back(hidden_two, norm_ffn, grad_normed_three)
    grad_two = grad_out + back_two
    branch_two = grad_two.astype(BF)
    grad_attn_two = matmul_t(branch_two, cross_out).astype(BF)
    products = grad_attn_two.astype(F32) * attn_raw_two
    delta_two = jnp.sum(products.reshape(-1, H, HD), axis=-1).T.reshape(PAIRS, 2, -1)

    grad_down = tmatmul(inner, branch_three)
    grad_gate = tmatmul(normed_three, grad_gate_low)
    grad_up = tmatmul(normed_three, grad_up_low)
    grad_cross_out = tmatmul(attn_two, branch_two)
    ffn_sums = scatter_sum((grad_gate, grad_up, grad_down, grad_cross_out), devices)

    order = (0, 2, 3, 1)
    stats = jnp.stack([lse_two, delta_two])
    sent = {r: (along_z(grad_attn_two, r), along_z(stats, r)) for r in order}
    returned = {}
    grad_q = {}
    grad_weights = None
    for r in order:
        grad_r, stats_r = sent[r]
        grad_kv, grad_q_r = attend_back(
            queries[r], grad_r, keyvals[r], stats_r[0], biases[r], stats_r[1]
        )
        grad_q[r] = along_z(grad_q_r, r)
        grad_rows = matmul_t(grad_kv, cross_weights).astype(BF)
        returned[r] = [
            in_plane(grad_rows[k * positions : (k + 1) * positions], k) for k in range(plane_size)
        ]
        term = tmatmul(rows[r], grad_kv)
        grad_weights = term if grad_weights is None else grad_weights + term
    memory_grad = place(
        [block for r in range(PLANES) for block in returned[r]], plane_size
    )

    grad_q_two = sum(grad_q[r].astype(F32) for r in range(PLANES)).astype(BF)
    grad_cross_query = tmatmul(normed_two, grad_q_two)
    grad_normed_two = matmul_t(grad_q_two, cross_query)
    back_one, grad_norm_cross = norm_back(hidden_one, norm_cross, grad_normed_two)
    grad_one = grad_two + back_one
    branch_one = grad_one.astype(BF)
    cross_sums = scatter_sum((grad_weights, grad_cross_query), devices)
    grad_self_out = tmatmul(attn_one, branch_one)
    grad_attn_one = matmul_t(branch_one, self_out).astype(BF)
    grad_kv_one, grad_q_one = attend_back(query_one, grad_attn_one, keyval_one, lse_one)
    grad_qkv = jnp.concatenate([grad_q_one, grad_kv_one], axis=1)
    grad_self = tmatmul(normed_one, grad_qkv)
    grad_normed_one = matmul_t(grad_qkv, self_weights)
    back_in, grad_norm_self = norm_back(inputs, norm_self, grad_normed_one)
    decoder_in_grad = (grad_one + back_in)[None]
    self_sums = scatter_sum(
        (grad_self, grad_self_out, grad_norm_self, grad_norm_cross, grad_norm_ffn), devices
    )

    sum_cross_key, sum_cross_value = separate(cross_sums[0])
    sum_self_query = self_sums[0][:, :width]
    sum_self_key, sum_self_value = separate(self_sums[0][:, width:])
    return (
        decoder_out,
        decoder_in_grad,
        memory_grad,
        self_sums[2],
        sum_self_query,
        sum_self_key,
        sum_self_value,
        self_sums[1],
        self_sums[3],
        cross_sums[1],
        sum_cross_key,
        sum_cross_value,
        ffn_sums[3],
        self_sums[4],
        ffn_sums[0],
        ffn_sums[1],
        ffn_sums[2],
    )


def solution(mesh):
    dp, seq = mesh.devices.shape
    cores = 2
    lines = dp // PLANES
    split = Mesh(mesh.devices.reshape(PLANES, lines, seq // cores, cores), ALL)
    plane_size = lines * seq
    first = P(ALL)
    middle = P(None, ALL)
    whole = P()
    return jax.shard_map(
        functools.partial(on_device, plane_size),
        mesh=split,
        in_specs=(first, middle, first, first) + (whole,) * 14,
        out_specs=(first, first, middle) + (first,) * 14,
        check_vma=False,
    )
```

```python
import functools

import jax
import jax.numpy as jnp
from jax import lax
from jax.experimental import pallas as pl
from jax.experimental.pallas import tpu as pltpu
from jax.sharding import Mesh
from jax.sharding import PartitionSpec as P

H = 12
HD = 64
PAIRS = 6
PLANES = 4
EPSILON = 1e-06
MASKED = -1e30
VMEM = 56 * 2**20
BF = jnp.bfloat16
F32 = jnp.float32
ALL = ("z", "y", "x", "c")
PLANE = ("y", "x", "c")


def dot(left, right, left_dim, right_dim):
    return lax.dot_general(
        left, right, (((left_dim,), (right_dim,)), ((), ())), preferred_element_type=F32
    )


def lane_masks():
    lane = lax.broadcasted_iota(jnp.int32, (1, 2 * HD), 1)
    low = jnp.where(lane < HD, 1.0, 0.0)
    first = jnp.where(lane == HD, 1.0, 0.0)
    second = jnp.where(lane == 0, 1.0, 0.0)
    low, high, first, second = (
        v.astype(BF) for v in (low, 1.0 - low, first, second)
    )
    return ((low, high, first), (high, low, second))


def causal_mask(scores):
    key = lax.broadcasted_iota(jnp.int32, scores.shape, 0)
    query = lax.broadcasted_iota(jnp.int32, scores.shape, 1)
    return jnp.where(key <= query, scores, MASKED)


def rem(value, size):
    return lax.rem(value, size)


class Courier:
    def __init__(self, sizes, jobs):
        self.sizes = sizes
        self.jobs = jobs
        self.plane = sizes[1] * sizes[2] * sizes[3]
        self.in_plane = any(job[0] != "line" for job in jobs)
        self.lines = [job[1] for job in jobs if job[0] == "line"]

    def out_shape(self):
        shapes = []
        for kind, _, value in self.jobs:
            shape = value.shape
            if kind == "fetch":
                shape = (self.plane,) + shape[1:]
            shapes.append(jax.ShapeDtypeStruct(shape, value.dtype))
        return shapes

    def specs(self):
        return [pl.BlockSpec(memory_space=pl.ANY)] * len(self.jobs)

    def values(self):
        return [job[2] for job in self.jobs]

    def scratch(self):
        count = sum(1 if job[0] == "line" else self.plane - 1 for job in self.jobs)
        own = max(1, sum(job[0] != "line" for job in self.jobs))
        return [pltpu.SemaphoreType.DMA((n,)) for n in (count, count, own)]

    def params(self, ident):
        return pltpu.CompilerParams(
            vmem_limit_bytes=VMEM, collective_id=ident, has_side_effects=True
        )

    def me(self):
        _, _, x_size, c_size = self.sizes
        y, x, c = (lax.axis_index(name) for name in PLANE)
        return (y * x_size + x) * c_size + c

    def along(self, offset):
        return {"z": rem(lax.axis_index("z") + (offset + PLANES), PLANES)}

    def across(self, offset):
        _, _, x_size, c_size = self.sizes
        other = rem(self.me() + offset, self.plane)
        line = lax.div(other, c_size)
        return other, {"y": lax.div(line, x_size), "x": rem(line, x_size), "c": rem(other, c_size)}

    def greet(self):
        barrier = pltpu.get_barrier_semaphore()
        count = 0
        if self.in_plane:
            for k in range(1, self.plane):
                _, device = self.across(k)
                pl.semaphore_signal(
                    barrier, inc=1, device_id=device, device_id_type=pl.DeviceIdType.MESH
                )
                count += 1
        for offset in self.lines:
            pl.semaphore_signal(
                barrier,
                inc=1,
                device_id=self.along(-offset),
                device_id_type=pl.DeviceIdType.MESH,
            )
            count += 1
        pl.semaphore_wait(barrier, count)

    def copies(self, sources, targets, sems):
        send, receive, own = sems
        remote = []
        local = []

        def add(source, target, device):
            n = len(remote)
            remote.append(
                pltpu.make_async_remote_copy(
                    src_ref=source,
                    dst_ref=target,
                    send_sem=send.at[n],
                    recv_sem=receive.at[n],
                    device_id=device,
                    device_id_type=pl.DeviceIdType.MESH,
                )
            )

        me = self.me()
        for (kind, offset, _), source, target in zip(self.jobs, sources, targets):
            if kind == "line":
                add(source, target, self.along(offset))
                continue
            base = 0
            if kind == "fetch":
                base = rem(lax.axis_index("z") + offset, PLANES) * self.plane
            for k in range(1, self.plane):
                other, device = self.across(k)
                add(source.at[base + other], target.at[me], device)
            local.append(
                pltpu.make_async_copy(source.at[base + me], target.at[me], own.at[len(local)])
            )
        return local + remote

    def start(self, sources, targets, sems):
        self.greet()
        for copy in self.copies(sources, targets, sems):
            copy.start()

    def wait(self, sources, targets, sems):
        for copy in self.copies(sources, targets, sems):
            copy.wait()


def forward_pair(queries, keys, values, bias):
    masks = lane_masks()
    all_scores = []
    for mine, other, one in masks:
        if bias is None:
            all_scores.append(causal_mask(dot(keys, queries * mine, 1, 1)))
        else:
            all_scores.append(dot(keys * mine + bias * one, queries * mine + one, 1, 1))
    parts = []
    lse = []
    for h in range(2):
        mine, other, _ = masks[h]
        scores = all_scores[h]
        row_max = jnp.max(scores, axis=0, keepdims=True)
        probs = jnp.exp(scores - row_max).astype(BF)
        both = dot(values * mine + other, probs, 0, 0)
        halves = (both[:HD], both[HD:])
        total = halves[1 - h]
        parts.append(halves[h] / total)
        lse.append(row_max + jnp.log(total[0:1]))
    return jnp.concatenate(parts, axis=0).T.astype(BF), lse


def backward_pair(queries, grad, keys, values, bias, lse, delta):
    grad_k = None
    grad_v = None
    grad_q = []
    for h, (mine, other, one) in enumerate(lane_masks()):
        query_h = queries * mine
        grad_h = grad * mine
        if bias is None:
            scores = causal_mask(dot(keys, query_h, 1, 1))
        else:
            scores = dot(keys * mine + bias * one, query_h + one, 1, 1)
        probs = jnp.exp(scores - lse[h])
        grad_p = dot(values, grad_h, 1, 1)
        if delta is None:
            delta_h = jnp.sum(probs * grad_p, axis=0, keepdims=True)
        else:
            delta_h = delta[h]
        grad_s = (probs * (grad_p - delta_h)).astype(BF)
        term_v = dot(probs.astype(BF), grad_h, 1, 0)
        term_k = dot(grad_s, query_h, 1, 0)
        grad_v = term_v if grad_v is None else grad_v + term_v
        grad_k = term_k if grad_k is None else grad_k + term_k
        grad_q.append(dot(keys, grad_s, 0, 0)[h * HD : (h + 1) * HD])
    grad_kv = jnp.concatenate([grad_k, grad_v], axis=1).astype(BF)
    return grad_kv, jnp.concatenate(grad_q, axis=0).T.astype(BF)


def two_rows(ref):
    return [ref[0, h : h + 1, :] for h in range(2)]


def split_refs(refs, *counts):
    groups = []
    at = 0
    for count in counts:
        groups.append(refs[at : at + count])
        at += count
    return groups


def carried(courier, body):
    jobs = len(courier.jobs)

    def kernel(ins, outs, scratch, refs):
        own_in, sources, own_out, targets, own_scratch, sems = split_refs(
            refs, ins, jobs, outs, jobs, scratch, 3
        )

        @pl.when(pl.program_id(0) == 0)
        def _():
            courier.start(sources, targets, sems)

        body(own_in, own_out, own_scratch)

        @pl.when(pl.program_id(0) == PAIRS - 1)
        def _():
            courier.wait(sources, targets, sems)

    return kernel


def call(courier, ident, body, args, in_specs, out_shape, out_specs, scratch, flops):
    kernel = carried(courier, body)
    counts = (len(args), len(out_shape), len(scratch))
    outs = pl.pallas_call(
        lambda *refs: kernel(*counts, refs),
        grid=(PAIRS,),
        out_shape=out_shape + courier.out_shape(),
        in_specs=in_specs + courier.specs(),
        out_specs=out_specs + courier.specs(),
        scratch_shapes=scratch + courier.scratch(),
        compiler_params=courier.params(ident),
        cost_estimate=pl.CostEstimate(flops=flops, bytes_accessed=2**24, transcendentals=2**20),
    )(*args, *courier.values())
    return outs[: len(out_shape)], outs[len(out_shape) :]


def block_specs(tokens, keys):
    return dict(
        col=pl.BlockSpec((tokens, 128), lambda p: (0, p)),
        pair=pl.BlockSpec((keys, 256), lambda p: (0, p)),
        bias=pl.BlockSpec((keys, 128), lambda p: (0, 0)),
        rows=pl.BlockSpec((keys, H * HD), lambda p: (0, 0)),
        weight=pl.BlockSpec((H * HD, 128), lambda p: (0, p)),
        stat=pl.BlockSpec((1, 2, tokens), lambda p: (p, 0, 0)),
    )


def self_forward(courier, ident, queries, keyvals):
    tokens = queries.shape[0]
    spec = block_specs(tokens, tokens)

    def body(ins, outs, _):
        q_ref, kv_ref = ins
        o_ref, lse_ref = outs
        out, lse = forward_pair(q_ref[...], kv_ref[:, :128], kv_ref[:, 128:], None)
        o_ref[...] = out
        for h in range(2):
            lse_ref[0, h : h + 1, :] = lse[h]

    return call(
        courier,
        ident,
        body,
        [queries, keyvals],
        [spec["col"], spec["pair"]],
        [
            jax.ShapeDtypeStruct((tokens, H * HD), BF),
            jax.ShapeDtypeStruct((PAIRS, 2, tokens), F32),
        ],
        [spec["col"], spec["stat"]],
        [],
        2**32,
    )


def cross_forward(courier, ident, queries, rows, bias, key_weight, value_weight):
    tokens, keys = queries.shape[0], rows.shape[0]
    spec = block_specs(tokens, keys)

    def body(ins, outs, _):
        q_ref, rows_ref, bias_ref, wk_ref, wv_ref = ins
        o_ref, lse_ref, kv_ref = outs
        weights = jnp.concatenate([wk_ref[...], wv_ref[...]], axis=1)
        kv_ref[...] = dot(rows_ref[...], weights, 1, 0).astype(BF)
        out, lse = forward_pair(q_ref[...], kv_ref[:, :128], kv_ref[:, 128:], bias_ref[...])
        o_ref[...] = out
        for h in range(2):
            lse_ref[0, h : h + 1, :] = lse[h]

    return call(
        courier,
        ident,
        body,
        [queries, rows, bias, key_weight, value_weight],
        [spec["col"], spec["rows"], spec["bias"], spec["weight"], spec["weight"]],
        [
            jax.ShapeDtypeStruct((tokens, H * HD), BF),
            jax.ShapeDtypeStruct((PAIRS, 2, tokens), F32),
            jax.ShapeDtypeStruct((keys, 2 * H * HD), BF),
        ],
        [spec["col"], spec["stat"], spec["pair"]],
        [],
        2**34,
    )


def cross_backward(courier, ident, queries, grad, keyvals, bias, lse, delta, key_weight, value_weight):
    tokens, keys = queries.shape[0], keyvals.shape[0]
    width = H * HD
    spec = block_specs(tokens, keys)

    def body(ins, outs, scratch):
        q_ref, da_ref, kv_ref, bias_ref, lse_ref, delta_ref, wk_ref, wv_ref = ins
        dkv_ref, dq_ref, dm_ref = outs
        (total_ref,) = scratch
        step = pl.program_id(0)

        @pl.when(step == 0)
        def _():
            total_ref[...] = jnp.zeros_like(total_ref)

        weights = jnp.concatenate([wk_ref[...], wv_ref[...]], axis=1)
        grad_kv, grad_q = backward_pair(
            q_ref[...],
            da_ref[...],
            kv_ref[:, :128],
            kv_ref[:, 128:],
            bias_ref[...],
            two_rows(lse_ref),
            two_rows(delta_ref),
        )
        dkv_ref[...] = grad_kv
        dq_ref[...] = grad_q
        total_ref[...] += dot(grad_kv, weights, 1, 1)

        @pl.when(step == PAIRS - 1)
        def _():
            dm_ref[...] = total_ref[...].astype(BF)

    return call(
        courier,
        ident,
        body,
        [queries, grad, keyvals, bias, lse, delta, key_weight, value_weight],
        [spec[n] for n in ("col", "col", "pair", "bias", "stat", "stat", "weight", "weight")],
        [
            jax.ShapeDtypeStruct((keys, 2 * width), BF),
            jax.ShapeDtypeStruct((tokens, width), BF),
            jax.ShapeDtypeStruct((keys, width), BF),
        ],
        [spec["pair"], spec["col"], spec["rows"]],
        [pltpu.VMEM((keys, width), F32)],
        2**35,
    )


def weight_terms(courier, ident, rows, grads):
    keys, width = rows[0].shape
    spec = block_specs(keys, keys)
    count = len(rows)

    def body(ins, outs, _):
        total = None
        for rows_ref, grad_ref in zip(ins[:count], ins[count:]):
            term = dot(rows_ref[...], grad_ref[...], 0, 0)
            total = term if total is None else total + term
        outs[0][...] = total.astype(BF)

    return call(
        courier,
        ident,
        body,
        list(rows) + list(grads),
        [spec["rows"]] * count + [spec["pair"]] * count,
        [jax.ShapeDtypeStruct((width, 2 * width), BF)],
        [pl.BlockSpec((width, 256), lambda p: (0, p))],
        [],
        2**34,
    )


def self_backward_kernel(q_ref, da_ref, kv_ref, lse_ref, dkv_ref, dq_ref):
    dkv_ref[...], dq_ref[...] = backward_pair(
        q_ref[...], da_ref[...], kv_ref[:, :128], kv_ref[:, 128:], None, two_rows(lse_ref), None
    )


def self_backward(queries, grad, keyvals, lse):
    tokens = queries.shape[0]
    spec = block_specs(tokens, tokens)
    return pl.pallas_call(
        self_backward_kernel,
        grid=(PAIRS,),
        out_shape=[
            jax.ShapeDtypeStruct((tokens, 2 * H * HD), BF),
            jax.ShapeDtypeStruct((tokens, H * HD), BF),
        ],
        in_specs=[spec["col"], spec["col"], spec["pair"], spec["stat"]],
        out_specs=[spec["pair"], spec["col"]],
        compiler_params=pltpu.CompilerParams(vmem_limit_bytes=VMEM),
        cost_estimate=pl.CostEstimate(flops=2**33, bytes_accessed=2**23, transcendentals=2**20),
    )(queries, grad, keyvals, lse)


def place_kernel(*refs):
    *blocks, out_ref, held, arrive, leave = refs
    z = lax.axis_index("z")
    size = held.shape[1]
    inward = []
    outward = []
    for r, block in enumerate(blocks):
        at = rem(z + r, PLANES) * size
        inward.append(pltpu.make_async_copy(block, held.at[r], arrive.at[r]))
        outward.append(
            pltpu.make_async_copy(held.at[r], out_ref.at[pl.ds(at, size)], leave.at[r])
        )
        inward[r].start()
    for r in range(len(blocks)):
        inward[r].wait()
        outward[r].start()
    for copy in outward:
        copy.wait()


def place(blocks):
    shape = blocks[0].shape
    count = len(blocks)
    hbm = pl.BlockSpec(memory_space=pl.ANY)
    return pl.pallas_call(
        place_kernel,
        out_shape=jax.ShapeDtypeStruct((count * shape[0],) + shape[1:], blocks[0].dtype),
        in_specs=[hbm] * count,
        out_specs=hbm,
        scratch_shapes=[
            pltpu.VMEM((count,) + shape, blocks[0].dtype),
            pltpu.SemaphoreType.DMA((count,)),
            pltpu.SemaphoreType.DMA((count,)),
        ],
        compiler_params=pltpu.CompilerParams(vmem_limit_bytes=VMEM),
    )(*blocks)


def interleave(keys, values):
    width = keys.shape[0]
    return jnp.stack(
        [keys.reshape(width, PAIRS, 128), values.reshape(width, PAIRS, 128)], axis=2
    ).reshape(width, 2 * H * HD)


def separate(both):
    rows = both.shape[0]
    parts = both.reshape(rows, PAIRS, 2, 128)
    return parts[:, :, 0].reshape(rows, H * HD), parts[:, :, 1].reshape(rows, H * HD)


def per_row(stat):
    tokens = stat.shape[-1]
    return jnp.repeat(stat.reshape(H, tokens).T, HD, axis=1)


def norm_apply(values, gain):
    return values * lax.rsqrt(jnp.mean(values * values, axis=-1, keepdims=True) + EPSILON) * gain


def norm_back(values, gain, grad):
    r = lax.rsqrt(jnp.mean(values * values, axis=-1, keepdims=True) + EPSILON)
    u = gain * grad
    dv = r * u - values * (r * r * r) * jnp.mean(u * values, axis=-1, keepdims=True)
    return dv, jnp.sum(grad * values * r, axis=0)


def glu_apply(gate_vals, up_vals):
    return jax.nn.gelu(gate_vals, approximate=True) * up_vals


def matmul(left, right):
    return dot(left, right, 1, 0)


def matmul_t(left, right):
    return dot(left, right, 1, 1)


def tmatmul(left, right):
    return dot(left, right, 0, 0)


def scatter_sum(arrays, devices):
    flat = [a.astype(BF).reshape(devices, -1) for a in arrays]
    sizes = [f.shape[1] for f in flat]
    extra = -sum(sizes) % 128
    if extra:
        flat.append(jnp.zeros((devices, extra), BF))
    joined = jnp.concatenate(flat, axis=1)
    mine = lax.psum_scatter(
        joined.reshape(devices, -1, 128), ALL, scatter_dimension=0, tiled=True
    ).reshape(-1).astype(F32)
    out = []
    at = 0
    for size, a in zip(sizes, arrays):
        out.append(mine[at : at + size].reshape((a.shape[0] // devices,) + a.shape[1:]))
        at += size
    return out


def on_device(
    sizes,
    decoder_in,
    memory,
    memory_lengths,
    cotangent,
    norm_self,
    self_query,
    self_key,
    self_value,
    self_out,
    norm_cross,
    cross_query,
    cross_key,
    cross_value,
    cross_out,
    norm_ffn,
    ffn_gate,
    ffn_up,
    ffn_down,
):
    devices, positions, width = memory.shape
    plane_size = sizes[1] * sizes[2] * sizes[3]
    z = lax.axis_index("z")

    def along_z(value, r):
        return lax.ppermute(value, "z", [(i, (i + r) % PLANES) for i in range(PLANES)])

    def flat(blocks):
        return blocks.reshape(plane_size * positions, width)

    def cut(rows):
        return rows.reshape(plane_size, positions, width)

    span = plane_size * positions
    places = z * span + jnp.arange(span, dtype=jnp.int32)

    inputs = decoder_in[0].astype(F32)
    normed_one = norm_apply(inputs, norm_self).astype(BF)
    self_weights = jnp.concatenate([self_query, interleave(self_key, self_value)], axis=1)
    qkv_one = matmul(normed_one, self_weights).astype(BF)
    query_one, keyval_one = qkv_one[:, :width], qkv_one[:, width:]
    (attn_one, lse_one), (fetched,) = self_forward(
        Courier(sizes, [("fetch", 1, memory)]), 0, query_one, keyval_one
    )
    hidden_one = inputs + matmul(attn_one, self_out)
    normed_two = norm_apply(hidden_one, norm_cross).astype(BF)
    query_two = matmul(normed_two, cross_query).astype(BF)

    queries, rows, keyvals, biases, partial, stats_out = {}, {}, {}, {}, {}, {}
    for r in range(PLANES):
        limit = memory_lengths if r == 0 else along_z(memory_lengths, -r)
        bias = jnp.where(places < limit, 0.0, MASKED).astype(BF)
        biases[r] = jnp.broadcast_to(bias[:, None], (bias.shape[0], 128))
    queries[0] = query_two
    queries[1] = along_z(query_two, -1)
    order = (1, 2, 3, 0)
    for at, r in enumerate(order):
        rows[r] = flat(fetched)
        jobs = []
        if at + 1 < PLANES:
            jobs.append(("fetch", order[at + 1], memory))
        if at + 2 < PLANES:
            jobs.append(("line", -order[at + 1], query_two))
        if at >= 1:
            before = order[at - 1]
            jobs.append(("line", before, partial[before]))
            jobs.append(("line", before, stats_out[before]))
        (partial[r], stats_out[r], keyvals[r]), moved = cross_forward(
            Courier(sizes, jobs), 1 + at, queries[r], rows[r], biases[r], cross_key, cross_value
        )
        moved = list(moved)
        if at + 1 < PLANES:
            fetched = moved.pop(0)
        if at + 2 < PLANES:
            queries[order[at + 1]] = moved.pop(0)
        if at >= 1:
            partial[before], stats_out[before] = moved
    lses = jnp.stack([stats_out[r] for r in range(PLANES)])
    top = jnp.max(lses, axis=0)
    scale = jnp.exp(lses - top)
    total = jnp.sum(scale, axis=0)
    lse_two = top + jnp.log(total)
    share = scale / total
    attn_raw_two = sum(per_row(share[r]) * partial[r].astype(F32) for r in range(PLANES))
    attn_two = attn_raw_two.astype(BF)
    hidden_two = hidden_one + matmul(attn_two, cross_out)

    normed_three = norm_apply(hidden_two, norm_ffn).astype(BF)
    gate_vals = matmul(normed_three, ffn_gate)
    up_vals = matmul(normed_three, ffn_up)
    inner = glu_apply(gate_vals, up_vals).astype(BF)
    output = hidden_two + matmul(inner, ffn_down)
    decoder_out = output.astype(BF)[None]

    branch_three = cotangent[0]
    grad_out = branch_three.astype(F32)
    grad_inner = matmul_t(branch_three, ffn_down)
    _, glu_pull = jax.vjp(glu_apply, gate_vals, up_vals)
    grad_gate_raw, grad_up_raw = glu_pull(grad_inner)
    grad_gate_low = grad_gate_raw.astype(BF)
    grad_up_low = grad_up_raw.astype(BF)
    grad_normed_three = matmul_t(grad_gate_low, ffn_gate) + matmul_t(grad_up_low, ffn_up)
    back_two, grad_norm_ffn = norm_back(hidden_two, norm_ffn, grad_normed_three)
    grad_two = grad_out + back_two
    branch_two = grad_two.astype(BF)
    grad_attn_two = matmul_t(branch_two, cross_out).astype(BF)
    products = grad_attn_two.astype(F32) * attn_raw_two
    delta_two = jnp.sum(products.reshape(-1, H, HD), axis=-1).T.reshape(PAIRS, 2, -1)

    grad_down = tmatmul(inner, branch_three)
    grad_gate = tmatmul(normed_three, grad_gate_low)
    grad_up = tmatmul(normed_three, grad_up_low)
    grad_cross_out = tmatmul(attn_two, branch_two)
    ffn_sums = scatter_sum((grad_gate, grad_up, grad_down, grad_cross_out), devices)

    stats = jnp.stack([lse_two, delta_two])
    grads = {0: grad_attn_two}
    both = {0: stats}
    grad_kv, grad_q, grad_rows, returned = {}, {}, {}, {}
    for r in range(PLANES):
        jobs = []
        if r + 1 < PLANES:
            jobs.append(("line", -(r + 1), grad_attn_two))
            jobs.append(("line", -(r + 1), stats))
        if r >= 1:
            jobs.append(("return", 0, cut(grad_rows[r - 1])))
        if r >= 2:
            jobs.append(("line", r - 1, grad_q[r - 1]))
        (grad_kv[r], grad_q[r], grad_rows[r]), moved = cross_backward(
            Courier(sizes, jobs),
            5 + r,
            queries[r],
            grads[r],
            keyvals[r],
            biases[r],
            both[r][0],
            both[r][1],
            cross_key,
            cross_value,
        )
        moved = list(moved)
        if r + 1 < PLANES:
            grads[r + 1], both[r + 1] = moved.pop(0), moved.pop(0)
        if r >= 1:
            returned[r - 1] = moved.pop(0)
        if r >= 2:
            grad_q[r - 1] = moved.pop(0)
    last = PLANES - 1
    (grad_weights,), (grad_q[last], returned[last]) = weight_terms(
        Courier(sizes, [("line", last, grad_q[last]), ("return", 0, cut(grad_rows[last]))]),
        9,
        [rows[r] for r in range(PLANES)],
        [grad_kv[r] for r in range(PLANES)],
    )
    memory_grad = place([returned[r] for r in range(PLANES)])

    grad_q_two = sum(grad_q[r].astype(F32) for r in range(PLANES)).astype(BF)
    grad_cross_query = tmatmul(normed_two, grad_q_two)
    grad_normed_two = matmul_t(grad_q_two, cross_query)
    back_one, grad_norm_cross = norm_back(hidden_one, norm_cross, grad_normed_two)
    grad_one = grad_two + back_one
    branch_one = grad_one.astype(BF)
    cross_sums = scatter_sum((grad_weights, grad_cross_query), devices)
    grad_self_out = tmatmul(attn_one, branch_one)
    grad_attn_one = matmul_t(branch_one, self_out).astype(BF)
    grad_kv_one, grad_q_one = self_backward(query_one, grad_attn_one, keyval_one, lse_one)
    grad_qkv = jnp.concatenate([grad_q_one, grad_kv_one], axis=1)
    grad_self = tmatmul(normed_one, grad_qkv)
    grad_normed_one = matmul_t(grad_qkv, self_weights)
    back_in, grad_norm_self = norm_back(inputs, norm_self, grad_normed_one)
    decoder_in_grad = (grad_one + back_in)[None]
    self_sums = scatter_sum(
        (grad_self, grad_self_out, grad_norm_self, grad_norm_cross, grad_norm_ffn), devices
    )

    sum_cross_key, sum_cross_value = separate(cross_sums[0])
    sum_self_query = self_sums[0][:, :width]
    sum_self_key, sum_self_value = separate(self_sums[0][:, width:])
    return (
        decoder_out,
        decoder_in_grad,
        memory_grad,
        self_sums[2],
        sum_self_query,
        sum_self_key,
        sum_self_value,
        self_sums[1],
        self_sums[3],
        cross_sums[1],
        sum_cross_key,
        sum_cross_value,
        ffn_sums[3],
        self_sums[4],
        ffn_sums[0],
        ffn_sums[1],
        ffn_sums[2],
    )


def solution(mesh):
    dp, seq = mesh.devices.shape
    cores = 2
    lines = dp // PLANES
    split = Mesh(mesh.devices.reshape(PLANES, lines, seq // cores, cores), ALL)
    sizes = split.devices.shape
    first = P(ALL)
    middle = P(None, ALL)
    whole = P()
    return jax.shard_map(
        functools.partial(on_device, sizes),
        mesh=split,
        in_specs=(first, middle, first, first) + (whole,) * 14,
        out_specs=(first, first, middle) + (first,) * 14,
        check_vma=False,
    )
```

```python
import functools

import jax
import jax.numpy as jnp
from jax import lax
from jax.experimental import pallas as pl
from jax.experimental.pallas import tpu as pltpu
from jax.sharding import Mesh
from jax.sharding import PartitionSpec as P

H = 12
HD = 64
PAIRS = 6
PLANES = 4
EPSILON = 1e-06
MASKED = -1e30
VMEM = 56 * 2**20
BF = jnp.bfloat16
F32 = jnp.float32
ALL = ("z", "y", "x", "c")
PLANE = ("y", "x", "c")


def dot(left, right, left_dim, right_dim):
    return lax.dot_general(
        left, right, (((left_dim,), (right_dim,)), ((), ())), preferred_element_type=F32
    )


def lane_masks():
    lane = lax.broadcasted_iota(jnp.int32, (1, 2 * HD), 1)
    low = jnp.where(lane < HD, 1.0, 0.0)
    first = jnp.where(lane == HD, 1.0, 0.0)
    second = jnp.where(lane == 0, 1.0, 0.0)
    low, high, first, second = (
        v.astype(BF) for v in (low, 1.0 - low, first, second)
    )
    return ((low, high, first), (high, low, second))


def causal_mask(scores):
    key = lax.broadcasted_iota(jnp.int32, scores.shape, 0)
    query = lax.broadcasted_iota(jnp.int32, scores.shape, 1)
    return jnp.where(key <= query, scores, MASKED)


def rem(value, size):
    return lax.rem(value, size)


class Courier:
    def __init__(self, sizes, jobs):
        self.sizes = sizes
        self.jobs = jobs
        self.plane = sizes[1] * sizes[2] * sizes[3]
        self.in_plane = any(job[0] in ("fetch", "return") for job in jobs)
        self.lines = [job[1] for job in jobs if job[0] == "line"]
        for job in jobs:
            if job[0] == "scatter":
                self.lines += list(range(1, PLANES))

    def out_shape(self):
        shapes = []
        for kind, _, value in self.jobs:
            shape = value.shape
            if kind == "fetch":
                shape = (self.plane,) + shape[1:]
            elif kind == "scatter":
                shape = (PLANES - 1,) + shape[1:]
            shapes.append(jax.ShapeDtypeStruct(shape, value.dtype))
        return shapes

    def specs(self):
        return [pl.BlockSpec(memory_space=pl.ANY)] * len(self.jobs)

    def values(self):
        return [job[2] for job in self.jobs]

    def scratch(self):
        each = {"line": 1, "scatter": PLANES - 1}
        count = max(1, sum(each.get(job[0], self.plane - 1) for job in self.jobs))
        own = max(1, sum(job[0] in ("fetch", "return") for job in self.jobs))
        return [pltpu.SemaphoreType.DMA((n,)) for n in (count, count, own)]

    def params(self, ident):
        return pltpu.CompilerParams(
            vmem_limit_bytes=VMEM, collective_id=ident, has_side_effects=True
        )

    def me(self):
        _, _, x_size, c_size = self.sizes
        y, x, c = (lax.axis_index(name) for name in PLANE)
        return (y * x_size + x) * c_size + c

    def along(self, offset):
        return {"z": rem(lax.axis_index("z") + (offset + PLANES), PLANES)}

    def across(self, offset):
        _, _, x_size, c_size = self.sizes
        other = rem(self.me() + offset, self.plane)
        line = lax.div(other, c_size)
        return other, {"y": lax.div(line, x_size), "x": rem(line, x_size), "c": rem(other, c_size)}

    def greet(self):
        barrier = pltpu.get_barrier_semaphore()
        count = 0
        if self.in_plane:
            for k in range(1, self.plane):
                _, device = self.across(k)
                pl.semaphore_signal(
                    barrier, inc=1, device_id=device, device_id_type=pl.DeviceIdType.MESH
                )
                count += 1
        for offset in self.lines:
            pl.semaphore_signal(
                barrier,
                inc=1,
                device_id=self.along(-offset),
                device_id_type=pl.DeviceIdType.MESH,
            )
            count += 1
        pl.semaphore_wait(barrier, count)

    def copies(self, sources, targets, sems):
        send, receive, own = sems
        remote = []
        local = []

        def add(source, target, device):
            n = len(remote)
            remote.append(
                pltpu.make_async_remote_copy(
                    src_ref=source,
                    dst_ref=target,
                    send_sem=send.at[n],
                    recv_sem=receive.at[n],
                    device_id=device,
                    device_id_type=pl.DeviceIdType.MESH,
                )
            )

        me = self.me()
        for (kind, offset, _), source, target in zip(self.jobs, sources, targets):
            if kind == "line":
                add(source, target, self.along(offset))
                continue
            if kind == "scatter":
                for k in range(1, PLANES):
                    there = rem(lax.axis_index("z") + k, PLANES)
                    add(source.at[there], target.at[k - 1], self.along(k))
                continue
            base = 0
            if kind == "fetch":
                base = rem(lax.axis_index("z") + offset, PLANES) * self.plane
            for k in range(1, self.plane):
                other, device = self.across(k)
                add(source.at[base + other], target.at[me], device)
            local.append(
                pltpu.make_async_copy(source.at[base + me], target.at[me], own.at[len(local)])
            )
        return local + remote

    def start(self, sources, targets, sems):
        self.greet()
        for copy in self.copies(sources, targets, sems):
            copy.start()

    def wait(self, sources, targets, sems):
        for copy in self.copies(sources, targets, sems):
            copy.wait()


class Reducer:
    def __init__(self, sizes, shape):
        self.sizes = sizes
        self.rows, self.lanes = shape[-2:]
        self.half = self.lanes // 2

    def scratch(self):
        z, y, x, _ = self.sizes
        r, w, h = self.rows, self.lanes, self.half
        crossing = x + y - 2
        return [
            pltpu.VMEM((z, y, x, r, w), BF),
            pltpu.VMEM((z, y, x, r, w), BF),
            pltpu.VMEM((x - 1, z, y, r, h), BF),
            pltpu.VMEM((y - 1, z, x, r, h), BF),
            pltpu.VMEM((y - 1, z, r, h), BF),
            pltpu.VMEM((x - 1, z, r, h), BF),
            pltpu.SemaphoreType.DMA((1,)),
            pltpu.SemaphoreType.DMA((1 + 2 * crossing,)),
            pltpu.SemaphoreType.DMA((1 + 2 * crossing,)),
        ]

    def bind(self, source, refs):
        self.source = source
        self.own, self.got0, self.got1x, self.got1y, self.got2y, self.got2x = refs[:6]
        self.local, self.send, self.receive = refs[6:]
        self.z, self.y, self.x, self.c = (lax.axis_index(name) for name in ALL)
        return self

    def remote(self, n, source, target, device):
        return pltpu.make_async_remote_copy(
            src_ref=source,
            dst_ref=target,
            send_sem=self.send.at[n],
            recv_sem=self.receive.at[n],
            device_id=device,
            device_id_type=pl.DeviceIdType.MESH,
        )

    def first(self):
        other = 1 - self.c
        return [
            pltpu.make_async_copy(self.source.at[:, :, :, self.c], self.own, self.local.at[0]),
            self.remote(0, self.source.at[:, :, :, other], self.got0, {"c": other}),
        ]

    def second(self):
        _, y_size, x_size, _ = self.sizes
        left, right = pl.ds(0, self.half), pl.ds(self.half, self.half)
        copies = []
        for k in range(1, x_size):
            there = rem(self.x + k, x_size)
            copies.append((self.own.at[:, :, there, :, left], self.got1x.at[k - 1], {"x": there}))
        for k in range(1, y_size):
            there = rem(self.y + k, y_size)
            copies.append((self.own.at[:, there, :, :, right], self.got1y.at[k - 1], {"y": there}))
        return [self.remote(1 + n, *copy) for n, copy in enumerate(copies)]

    def third(self):
        _, y_size, x_size, _ = self.sizes
        left, right = pl.ds(0, self.half), pl.ds(self.half, self.half)
        at = 1 + x_size + y_size - 2
        copies = []
        for k in range(1, y_size):
            there = rem(self.y + k, y_size)
            copies.append(
                (self.own.at[:, there, self.x, :, left], self.got2y.at[k - 1], {"y": there})
            )
        for k in range(1, x_size):
            there = rem(self.x + k, x_size)
            copies.append(
                (self.own.at[:, self.y, there, :, right], self.got2x.at[k - 1], {"x": there})
            )
        return [self.remote(at + n, *copy) for n, copy in enumerate(copies)]

    def begin(self):
        for copy in self.first():
            copy.start()

    def after_first(self):
        for copy in self.first():
            copy.wait()

        @pl.loop(0, self.sizes[0])
        def _(z):
            self.own[z] = (self.own[z].astype(F32) + self.got0[z].astype(F32)).astype(BF)

        for copy in self.second():
            copy.start()

    def after_second(self):
        _, y_size, x_size, _ = self.sizes
        for copy in self.second():
            copy.wait()
        h = self.half

        @pl.loop(0, self.sizes[0])
        def _(z):
            for y in range(y_size):
                total = self.own[z, y, self.x, :, :h].astype(F32)
                for k in range(x_size - 1):
                    total += self.got1x[k, z, y].astype(F32)
                self.own[z, y, self.x, :, :h] = total.astype(BF)
            for x in range(x_size):
                total = self.own[z, self.y, x, :, h:].astype(F32)
                for k in range(y_size - 1):
                    total += self.got1y[k, z, x].astype(F32)
                self.own[z, self.y, x, :, h:] = total.astype(BF)

        for copy in self.third():
            copy.start()

    def after_third(self, out_ref):
        _, y_size, x_size, _ = self.sizes
        for copy in self.third():
            copy.wait()
        h = self.half

        @pl.loop(0, self.sizes[0])
        def _(z):
            total = self.own[z, self.y, self.x, :, :h].astype(F32)
            for k in range(y_size - 1):
                total += self.got2y[k, z].astype(F32)
            out_ref[z, :, :h] = total.astype(BF)
            total = self.own[z, self.y, self.x, :, h:].astype(F32)
            for k in range(x_size - 1):
                total += self.got2x[k, z].astype(F32)
            out_ref[z, :, h:] = total.astype(BF)


def forward_pair(queries, keys, values, bias):
    masks = lane_masks()
    all_scores = []
    for mine, other, one in masks:
        if bias is None:
            all_scores.append(causal_mask(dot(keys, queries * mine, 1, 1)))
        else:
            all_scores.append(dot(keys * mine + bias * one, queries * mine + one, 1, 1))
    parts = []
    lse = []
    for h in range(2):
        mine, other, _ = masks[h]
        scores = all_scores[h]
        row_max = jnp.max(scores, axis=0, keepdims=True)
        probs = jnp.exp(scores - row_max).astype(BF)
        both = dot(values * mine + other, probs, 0, 0)
        halves = (both[:HD], both[HD:])
        total = halves[1 - h]
        parts.append(halves[h] / total)
        lse.append(row_max + jnp.log(total[0:1]))
    return jnp.concatenate(parts, axis=0).T.astype(BF), lse


def backward_pair(queries, grad, keys, values, bias, lse, delta):
    grad_k = None
    grad_v = None
    grad_q = []
    for h, (mine, other, one) in enumerate(lane_masks()):
        query_h = queries * mine
        grad_h = grad * mine
        if bias is None:
            scores = causal_mask(dot(keys, query_h, 1, 1))
        else:
            scores = dot(keys * mine + bias * one, query_h + one, 1, 1)
        probs = jnp.exp(scores - lse[h])
        grad_p = dot(values, grad_h, 1, 1)
        if delta is None:
            delta_h = jnp.sum(probs * grad_p, axis=0, keepdims=True)
        else:
            delta_h = delta[h]
        grad_s = (probs * (grad_p - delta_h)).astype(BF)
        term_v = dot(probs.astype(BF), grad_h, 1, 0)
        term_k = dot(grad_s, query_h, 1, 0)
        grad_v = term_v if grad_v is None else grad_v + term_v
        grad_k = term_k if grad_k is None else grad_k + term_k
        grad_q.append(dot(keys, grad_s, 0, 0)[h * HD : (h + 1) * HD])
    grad_kv = jnp.concatenate([grad_k, grad_v], axis=1).astype(BF)
    return grad_kv, jnp.concatenate(grad_q, axis=0).T.astype(BF)


def two_rows(ref):
    return [ref[0, h : h + 1, :] for h in range(2)]


def split_refs(refs, *counts):
    groups = []
    at = 0
    for count in counts:
        groups.append(refs[at : at + count])
        at += count
    return groups


def carried(courier, reducer, body):
    jobs = len(courier.jobs)
    sums = 0 if reducer is None else 1

    def kernel(ins, outs, scratch, refs):
        own_in, sources, summands, own_out, targets, results, own_scratch, sems, rest = split_refs(
            refs, ins, jobs, sums, outs, jobs, sums, scratch, 3, 9 * sums
        )
        step = pl.program_id(0)

        @pl.when(step == 0)
        def _():
            courier.start(sources, targets, sems)
            if sums:
                reducer.bind(summands[0], rest).begin()

        body(own_in, own_out, own_scratch)

        if sums:

            @pl.when(step == 1)
            def _():
                reducer.bind(summands[0], rest).after_first()

            @pl.when(step == 3)
            def _():
                reducer.bind(summands[0], rest).after_second()

        @pl.when(step == PAIRS - 1)
        def _():
            if sums:
                reducer.bind(summands[0], rest).after_third(results[0])
            courier.wait(sources, targets, sems)

    return kernel


def call(courier, ident, body, args, in_specs, out_shape, out_specs, scratch, flops, summand=None):
    reducer = None
    extra_in, extra_out, extra_out_specs, extra_scratch = [], [], [], []
    if summand is not None:
        courier.in_plane = True
        reducer = Reducer(courier.sizes, summand.shape)
        shape = (PLANES,) + summand.shape[-2:]
        extra_in = [summand]
        extra_out = [jax.ShapeDtypeStruct(shape, BF)]
        extra_out_specs = [pl.BlockSpec(shape, lambda p: (0, 0, 0))]
        extra_scratch = reducer.scratch()
    kernel = carried(courier, reducer, body)
    counts = (len(args), len(out_shape), len(scratch))
    outs = pl.pallas_call(
        lambda *refs: kernel(*counts, refs),
        grid=(PAIRS,),
        out_shape=out_shape + courier.out_shape() + extra_out,
        in_specs=in_specs + courier.specs() + [pl.BlockSpec(memory_space=pl.ANY)] * len(extra_in),
        out_specs=out_specs + courier.specs() + extra_out_specs,
        scratch_shapes=scratch + courier.scratch() + extra_scratch,
        compiler_params=courier.params(ident),
        cost_estimate=pl.CostEstimate(flops=flops, bytes_accessed=2**24, transcendentals=2**20),
    )(*args, *courier.values(), *extra_in)
    return outs[: len(out_shape)], outs[len(out_shape) :]


def reduce_all(sizes, ident, summands, scattered):
    courier = Courier(sizes, [("scatter", 0, value) for value in scattered])
    courier.in_plane = True
    courier.lines += list(range(1, PLANES))
    jobs = len(scattered)
    count = len(summands)
    reducers = [Reducer(sizes, value.shape) for value in summands]
    shapes = [value.shape[-2:] for value in summands]

    def kernel(*refs):
        sources, arrays, targets, results, sems, rest = split_refs(
            refs, jobs, count, jobs, count, 3, len(refs) - 2 * jobs - 2 * count - 3
        )
        courier.start(sources, targets, sems)
        bound = []
        last = []
        for n in range(count):
            refs_n = rest[13 * n : 13 * n + 13]
            bound.append(reducers[n].bind(arrays[n], refs_n[:9]))
            last.append(refs_n[9:])

        def leave(n):
            left, got, send, receive = last[n]
            copies = []
            for k in range(1, PLANES):
                copies.append(
                    pltpu.make_async_remote_copy(
                        src_ref=left.at[rem(lax.axis_index("z") + k, PLANES)],
                        dst_ref=got.at[k - 1],
                        send_sem=send.at[k - 1],
                        recv_sem=receive.at[k - 1],
                        device_id=courier.along(k),
                        device_id_type=pl.DeviceIdType.MESH,
                    )
                )
            return copies

        for one in bound:
            one.begin()
        for one in bound:
            one.after_first()
        for one in bound:
            one.after_second()
        for n, one in enumerate(bound):
            one.after_third(last[n][0])
            for copy in leave(n):
                copy.start()
        for n in range(count):
            for copy in leave(n):
                copy.wait()
            left, got = last[n][:2]
            total = left[lax.axis_index("z")].astype(F32)
            for k in range(PLANES - 1):
                total += got[k].astype(F32)
            results[n][...] = total
        courier.wait(sources, targets, sems)

    scratch = []
    for n in range(count):
        scratch += reducers[n].scratch() + [
            pltpu.VMEM((PLANES,) + shapes[n], BF),
            pltpu.VMEM((PLANES - 1,) + shapes[n], BF),
            pltpu.SemaphoreType.DMA((PLANES - 1,)),
            pltpu.SemaphoreType.DMA((PLANES - 1,)),
        ]
    outs = pl.pallas_call(
        kernel,
        out_shape=courier.out_shape() + [jax.ShapeDtypeStruct(shape, F32) for shape in shapes],
        in_specs=courier.specs() + [pl.BlockSpec(memory_space=pl.ANY)] * count,
        out_specs=courier.specs() + [pl.BlockSpec(memory_space=pltpu.VMEM)] * count,
        scratch_shapes=courier.scratch() + scratch,
        compiler_params=courier.params(ident),
    )(*courier.values(), *summands)
    return outs[:jobs], outs[jobs:]


def summand_of(sizes, arrays):
    devices = sizes[0] * sizes[1] * sizes[2] * sizes[3]
    parts = [a.reshape(devices, a.shape[0] // devices, a.shape[1]) for a in arrays]
    joined = parts[0] if len(parts) == 1 else jnp.concatenate(parts, axis=1)
    return joined.astype(BF).reshape(tuple(sizes) + joined.shape[1:])


def over_z(left, got):
    own = lax.dynamic_index_in_dim(left, lax.axis_index("z"), 0, keepdims=False)
    return own.astype(F32) + jnp.sum(got.astype(F32), axis=0)


def block_specs(tokens, keys):
    return dict(
        col=pl.BlockSpec((tokens, 128), lambda p: (0, p)),
        pair=pl.BlockSpec((keys, 256), lambda p: (0, p)),
        bias=pl.BlockSpec((keys, 128), lambda p: (0, 0)),
        rows=pl.BlockSpec((keys, H * HD), lambda p: (0, 0)),
        weight=pl.BlockSpec((H * HD, 128), lambda p: (0, p)),
        stat=pl.BlockSpec((1, 2, tokens), lambda p: (p, 0, 0)),
    )


def self_forward(courier, ident, queries, keyvals):
    tokens = queries.shape[0]
    spec = block_specs(tokens, tokens)

    def body(ins, outs, _):
        q_ref, kv_ref = ins
        o_ref, lse_ref = outs
        out, lse = forward_pair(q_ref[...], kv_ref[:, :128], kv_ref[:, 128:], None)
        o_ref[...] = out
        for h in range(2):
            lse_ref[0, h : h + 1, :] = lse[h]

    return call(
        courier,
        ident,
        body,
        [queries, keyvals],
        [spec["col"], spec["pair"]],
        [
            jax.ShapeDtypeStruct((tokens, H * HD), BF),
            jax.ShapeDtypeStruct((PAIRS, 2, tokens), F32),
        ],
        [spec["col"], spec["stat"]],
        [],
        2**32,
    )


def cross_forward(courier, ident, queries, rows, bias, key_weight, value_weight):
    tokens, keys = queries.shape[0], rows.shape[0]
    spec = block_specs(tokens, keys)

    def body(ins, outs, _):
        q_ref, rows_ref, bias_ref, wk_ref, wv_ref = ins
        o_ref, lse_ref, kv_ref = outs
        weights = jnp.concatenate([wk_ref[...], wv_ref[...]], axis=1)
        kv_ref[...] = dot(rows_ref[...], weights, 1, 0).astype(BF)
        out, lse = forward_pair(q_ref[...], kv_ref[:, :128], kv_ref[:, 128:], bias_ref[...])
        o_ref[...] = out
        for h in range(2):
            lse_ref[0, h : h + 1, :] = lse[h]

    return call(
        courier,
        ident,
        body,
        [queries, rows, bias, key_weight, value_weight],
        [spec["col"], spec["rows"], spec["bias"], spec["weight"], spec["weight"]],
        [
            jax.ShapeDtypeStruct((tokens, H * HD), BF),
            jax.ShapeDtypeStruct((PAIRS, 2, tokens), F32),
            jax.ShapeDtypeStruct((keys, 2 * H * HD), BF),
        ],
        [spec["col"], spec["stat"], spec["pair"]],
        [],
        2**34,
    )


def cross_backward(
    courier, ident, queries, grad, keyvals, bias, lse, delta, key_weight, value_weight, summand=None
):
    tokens, keys = queries.shape[0], keyvals.shape[0]
    width = H * HD
    spec = block_specs(tokens, keys)

    def body(ins, outs, scratch):
        q_ref, da_ref, kv_ref, bias_ref, lse_ref, delta_ref, wk_ref, wv_ref = ins
        dkv_ref, dq_ref, dm_ref = outs
        (total_ref,) = scratch
        step = pl.program_id(0)

        @pl.when(step == 0)
        def _():
            total_ref[...] = jnp.zeros_like(total_ref)

        weights = jnp.concatenate([wk_ref[...], wv_ref[...]], axis=1)
        grad_kv, grad_q = backward_pair(
            q_ref[...],
            da_ref[...],
            kv_ref[:, :128],
            kv_ref[:, 128:],
            bias_ref[...],
            two_rows(lse_ref),
            two_rows(delta_ref),
        )
        dkv_ref[...] = grad_kv
        dq_ref[...] = grad_q
        total_ref[...] += dot(grad_kv, weights, 1, 1)

        @pl.when(step == PAIRS - 1)
        def _():
            dm_ref[...] = total_ref[...].astype(BF)

    return call(
        courier,
        ident,
        body,
        [queries, grad, keyvals, bias, lse, delta, key_weight, value_weight],
        [spec[n] for n in ("col", "col", "pair", "bias", "stat", "stat", "weight", "weight")],
        [
            jax.ShapeDtypeStruct((keys, 2 * width), BF),
            jax.ShapeDtypeStruct((tokens, width), BF),
            jax.ShapeDtypeStruct((keys, width), BF),
        ],
        [spec["pair"], spec["col"], spec["rows"]],
        [pltpu.VMEM((keys, width), F32)],
        2**35,
        summand,
    )


def weight_terms(courier, ident, rows, grads):
    keys, width = rows[0].shape
    spec = block_specs(keys, keys)
    count = len(rows)

    def body(ins, outs, _):
        total = None
        for rows_ref, grad_ref in zip(ins[:count], ins[count:]):
            term = dot(rows_ref[...], grad_ref[...], 0, 0)
            total = term if total is None else total + term
        outs[0][...] = total[:, :128]
        outs[1][...] = total[:, 128:]

    return call(
        courier,
        ident,
        body,
        list(rows) + list(grads),
        [spec["rows"]] * count + [spec["pair"]] * count,
        [jax.ShapeDtypeStruct((width, width), F32)] * 2,
        [spec["weight"]] * 2,
        [],
        2**34,
    )


def self_backward(courier, ident, queries, grad, keyvals, lse, summand):
    tokens, width = queries.shape
    spec = block_specs(tokens, tokens)

    def body(ins, outs, _):
        q_ref, da_ref, kv_ref, lse_ref = ins
        dq_ref, dk_ref, dv_ref = outs
        grad_kv, dq_ref[...] = backward_pair(
            q_ref[...], da_ref[...], kv_ref[:, :128], kv_ref[:, 128:], None, two_rows(lse_ref), None
        )
        dk_ref[...] = grad_kv[:, :128]
        dv_ref[...] = grad_kv[:, 128:]

    return call(
        courier,
        ident,
        body,
        [queries, grad, keyvals, lse],
        [spec["col"], spec["col"], spec["pair"], spec["stat"]],
        [jax.ShapeDtypeStruct((tokens, width), BF)] * 3,
        [spec["col"]] * 3,
        [],
        2**33,
        summand,
    )


def place_kernel(*refs):
    *blocks, out_ref, held, arrive, leave = refs
    z = lax.axis_index("z")
    size = held.shape[1]
    inward = []
    outward = []
    for r, block in enumerate(blocks):
        at = rem(z + r, PLANES) * size
        inward.append(pltpu.make_async_copy(block, held.at[r], arrive.at[r]))
        outward.append(
            pltpu.make_async_copy(held.at[r], out_ref.at[pl.ds(at, size)], leave.at[r])
        )
        inward[r].start()
    for r in range(len(blocks)):
        inward[r].wait()
        outward[r].start()
    for copy in outward:
        copy.wait()


def place(blocks):
    shape = blocks[0].shape
    count = len(blocks)
    hbm = pl.BlockSpec(memory_space=pl.ANY)
    return pl.pallas_call(
        place_kernel,
        out_shape=jax.ShapeDtypeStruct((count * shape[0],) + shape[1:], blocks[0].dtype),
        in_specs=[hbm] * count,
        out_specs=hbm,
        scratch_shapes=[
            pltpu.VMEM((count,) + shape, blocks[0].dtype),
            pltpu.SemaphoreType.DMA((count,)),
            pltpu.SemaphoreType.DMA((count,)),
        ],
        compiler_params=pltpu.CompilerParams(vmem_limit_bytes=VMEM),
    )(*blocks)


def interleave(keys, values):
    width = keys.shape[0]
    return jnp.stack(
        [keys.reshape(width, PAIRS, 128), values.reshape(width, PAIRS, 128)], axis=2
    ).reshape(width, 2 * H * HD)


def separate(both):
    rows = both.shape[0]
    parts = both.reshape(rows, PAIRS, 2, 128)
    return parts[:, :, 0].reshape(rows, H * HD), parts[:, :, 1].reshape(rows, H * HD)


def per_row(stat):
    tokens = stat.shape[-1]
    return jnp.repeat(stat.reshape(H, tokens).T, HD, axis=1)


def norm_apply(values, gain):
    return values * lax.rsqrt(jnp.mean(values * values, axis=-1, keepdims=True) + EPSILON) * gain


def norm_back(values, gain, grad):
    r = lax.rsqrt(jnp.mean(values * values, axis=-1, keepdims=True) + EPSILON)
    u = gain * grad
    dv = r * u - values * (r * r * r) * jnp.mean(u * values, axis=-1, keepdims=True)
    return dv, jnp.sum(grad * values * r, axis=0)


def glu_apply(gate_vals, up_vals):
    return jax.nn.gelu(gate_vals, approximate=True) * up_vals


def matmul(left, right):
    return dot(left, right, 1, 0)


def matmul_t(left, right):
    return dot(left, right, 1, 1)


def tmatmul(left, right):
    return dot(left, right, 0, 0)


def on_device(
    sizes,
    decoder_in,
    memory,
    memory_lengths,
    cotangent,
    norm_self,
    self_query,
    self_key,
    self_value,
    self_out,
    norm_cross,
    cross_query,
    cross_key,
    cross_value,
    cross_out,
    norm_ffn,
    ffn_gate,
    ffn_up,
    ffn_down,
):
    devices, positions, width = memory.shape
    plane_size = sizes[1] * sizes[2] * sizes[3]
    z = lax.axis_index("z")

    def along_z(value, r):
        return lax.ppermute(value, "z", [(i, (i + r) % PLANES) for i in range(PLANES)])

    def flat(blocks):
        return blocks.reshape(plane_size * positions, width)

    def cut(rows):
        return rows.reshape(plane_size, positions, width)

    span = plane_size * positions
    places = z * span + jnp.arange(span, dtype=jnp.int32)

    inputs = decoder_in[0].astype(F32)
    normed_one = norm_apply(inputs, norm_self).astype(BF)
    self_weights = jnp.concatenate([self_query, interleave(self_key, self_value)], axis=1)
    qkv_one = matmul(normed_one, self_weights).astype(BF)
    query_one, keyval_one = qkv_one[:, :width], qkv_one[:, width:]
    (attn_one, lse_one), (fetched,) = self_forward(
        Courier(sizes, [("fetch", 1, memory)]), 0, query_one, keyval_one
    )
    hidden_one = inputs + matmul(attn_one, self_out)
    normed_two = norm_apply(hidden_one, norm_cross).astype(BF)
    query_two = matmul(normed_two, cross_query).astype(BF)

    queries, rows, keyvals, biases, partial, stats_out = {}, {}, {}, {}, {}, {}
    for r in range(PLANES):
        limit = memory_lengths if r == 0 else along_z(memory_lengths, -r)
        bias = jnp.where(places < limit, 0.0, MASKED).astype(BF)
        biases[r] = jnp.broadcast_to(bias[:, None], (bias.shape[0], 128))
    queries[0] = query_two
    queries[1] = along_z(query_two, -1)
    order = (1, 2, 3, 0)
    for at, r in enumerate(order):
        rows[r] = flat(fetched)
        jobs = []
        if at + 1 < PLANES:
            jobs.append(("fetch", order[at + 1], memory))
        if at + 2 < PLANES:
            jobs.append(("line", -order[at + 1], query_two))
        if at >= 1:
            before = order[at - 1]
            jobs.append(("line", before, partial[before]))
            jobs.append(("line", before, stats_out[before]))
        (partial[r], stats_out[r], keyvals[r]), moved = cross_forward(
            Courier(sizes, jobs), 1 + at, queries[r], rows[r], biases[r], cross_key, cross_value
        )
        moved = list(moved)
        if at + 1 < PLANES:
            fetched = moved.pop(0)
        if at + 2 < PLANES:
            queries[order[at + 1]] = moved.pop(0)
        if at >= 1:
            partial[before], stats_out[before] = moved
    lses = jnp.stack([stats_out[r] for r in range(PLANES)])
    top = jnp.max(lses, axis=0)
    scale = jnp.exp(lses - top)
    total = jnp.sum(scale, axis=0)
    lse_two = top + jnp.log(total)
    share = scale / total
    attn_raw_two = sum(per_row(share[r]) * partial[r].astype(F32) for r in range(PLANES))
    attn_two = attn_raw_two.astype(BF)
    hidden_two = hidden_one + matmul(attn_two, cross_out)

    normed_three = norm_apply(hidden_two, norm_ffn).astype(BF)
    gate_vals = matmul(normed_three, ffn_gate)
    up_vals = matmul(normed_three, ffn_up)
    inner = glu_apply(gate_vals, up_vals).astype(BF)
    output = hidden_two + matmul(inner, ffn_down)
    decoder_out = output.astype(BF)[None]

    branch_three = cotangent[0]
    grad_out = branch_three.astype(F32)
    grad_inner = matmul_t(branch_three, ffn_down)
    _, glu_pull = jax.vjp(glu_apply, gate_vals, up_vals)
    grad_gate_raw, grad_up_raw = glu_pull(grad_inner)
    grad_gate_low = grad_gate_raw.astype(BF)
    grad_up_low = grad_up_raw.astype(BF)
    grad_normed_three = matmul_t(grad_gate_low, ffn_gate) + matmul_t(grad_up_low, ffn_up)
    back_two, grad_norm_ffn = norm_back(hidden_two, norm_ffn, grad_normed_three)
    grad_two = grad_out + back_two
    branch_two = grad_two.astype(BF)
    grad_attn_two = matmul_t(branch_two, cross_out).astype(BF)
    products = grad_attn_two.astype(F32) * attn_raw_two
    delta_two = jnp.sum(products.reshape(-1, H, HD), axis=-1).T.reshape(PAIRS, 2, -1)

    grad_down = tmatmul(inner, branch_three)
    grad_gate = tmatmul(normed_three, grad_gate_low)
    grad_up = tmatmul(normed_three, grad_up_low)
    grad_cross_out = tmatmul(attn_two, branch_two)
    summands = {0: summand_of(sizes, (grad_gate, grad_up)), 1: summand_of(sizes, (grad_down,))}
    left, got = {}, {}

    stats = jnp.stack([lse_two, delta_two])
    grads = {0: grad_attn_two}
    both = {0: stats}
    grad_kv, grad_q, grad_rows, returned = {}, {}, {}, {}
    for r in range(PLANES):
        jobs = []
        if r + 1 < PLANES:
            jobs.append(("line", -(r + 1), grad_attn_two))
            jobs.append(("line", -(r + 1), stats))
        if r >= 1:
            jobs.append(("return", 0, cut(grad_rows[r - 1])))
        if r >= 2:
            jobs.append(("line", r - 1, grad_q[r - 1]))
        if r - 1 in left:
            jobs.append(("scatter", 0, left[r - 1]))
        (grad_kv[r], grad_q[r], grad_rows[r]), moved = cross_backward(
            Courier(sizes, jobs),
            5 + r,
            queries[r],
            grads[r],
            keyvals[r],
            biases[r],
            both[r][0],
            both[r][1],
            cross_key,
            cross_value,
            summands.get(r),
        )
        moved = list(moved)
        if r in summands:
            left[r] = moved.pop()
        if r + 1 < PLANES:
            grads[r + 1], both[r + 1] = moved.pop(0), moved.pop(0)
        if r >= 1:
            returned[r - 1] = moved.pop(0)
        if r >= 2:
            grad_q[r - 1] = moved.pop(0)
        if r - 1 in left:
            got[r - 1] = moved.pop(0)
    last = PLANES - 1
    (grad_cross_key, grad_cross_value), (grad_q[last], returned[last]) = weight_terms(
        Courier(sizes, [("line", last, grad_q[last]), ("return", 0, cut(grad_rows[last]))]),
        9,
        [rows[r] for r in range(PLANES)],
        [grad_kv[r] for r in range(PLANES)],
    )
    memory_grad = place([returned[r] for r in range(PLANES)])

    grad_q_two = sum(grad_q[r].astype(F32) for r in range(PLANES)).astype(BF)
    grad_cross_query = tmatmul(normed_two, grad_q_two)
    grad_normed_two = matmul_t(grad_q_two, cross_query)
    back_one, grad_norm_cross = norm_back(hidden_one, norm_cross, grad_normed_two)
    grad_one = grad_two + back_one
    branch_one = grad_one.astype(BF)
    grad_self_out = tmatmul(attn_one, branch_one)
    grad_attn_one = matmul_t(branch_one, self_out).astype(BF)
    (grad_q_one, grad_k_one, grad_v_one), (cross_left,) = self_backward(
        Courier(sizes, []),
        10,
        query_one,
        grad_attn_one,
        keyval_one,
        lse_one,
        summand_of(sizes, (grad_cross_key, grad_cross_value)),
    )
    grad_normed_one = (
        matmul_t(grad_q_one, self_query)
        + matmul_t(grad_k_one, self_key)
        + matmul_t(grad_v_one, self_value)
    )
    back_in, grad_norm_self = norm_back(inputs, norm_self, grad_normed_one)
    decoder_in_grad = (grad_one + back_in)[None]
    share_of_norms = width // devices
    norms = jnp.stack(
        [g.reshape(devices, share_of_norms) for g in (grad_norm_self, grad_norm_cross, grad_norm_ffn)],
        axis=1,
    ).reshape(devices, 1, 3 * share_of_norms)
    norms = jnp.pad(norms, ((0, 0), (0, 15), (0, 256 - 3 * share_of_norms)))
    (cross_got,), sums = reduce_all(
        sizes,
        11,
        [
            norms.astype(BF).reshape(tuple(sizes) + norms.shape[1:]),
            summand_of(sizes, (grad_cross_query, grad_cross_out)),
            summand_of(sizes, (tmatmul(normed_one, grad_q_one), tmatmul(normed_one, grad_k_one))),
            summand_of(sizes, (tmatmul(normed_one, grad_v_one), grad_self_out)),
        ],
        [cross_left],
    )
    norm_sums = sums[0][0, : 3 * share_of_norms].reshape(3, share_of_norms)
    gate_up = over_z(left[0], got[0])
    cross_kv = over_z(cross_left, cross_got)
    part = share_of_norms
    return (
        decoder_out,
        decoder_in_grad,
        memory_grad,
        norm_sums[0],
        sums[2][:part],
        sums[2][part:],
        sums[3][:part],
        sums[3][part:],
        norm_sums[1],
        sums[1][:part],
        cross_kv[:part],
        cross_kv[part:],
        sums[1][part:],
        norm_sums[2],
        gate_up[:part],
        gate_up[part:],
        over_z(left[1], got[1]),
    )


def solution(mesh):
    dp, seq = mesh.devices.shape
    cores = 2
    lines = dp // PLANES
    split = Mesh(mesh.devices.reshape(PLANES, lines, seq // cores, cores), ALL)
    sizes = split.devices.shape
    first = P(ALL)
    middle = P(None, ALL)
    whole = P()
    return jax.shard_map(
        functools.partial(on_device, sizes),
        mesh=split,
        in_specs=(first, middle, first, first) + (whole,) * 14,
        out_specs=(first, first, middle) + (first,) * 14,
        check_vma=False,
    )
```

```python
import functools

import jax
import jax.numpy as jnp
from jax import lax
from jax.experimental import pallas as pl
from jax.experimental.pallas import tpu as pltpu
from jax.sharding import Mesh
from jax.sharding import PartitionSpec as P

H = 12
HD = 64
PAIRS = 6
PLANES = 4
EPSILON = 1e-06
MASKED = -1e30
VMEM = 56 * 2**20
BF = jnp.bfloat16
F32 = jnp.float32
ALL = ("z", "y", "x", "c")
PLANE = ("y", "x", "c")


def dot(left, right, left_dim, right_dim):
    return lax.dot_general(
        left, right, (((left_dim,), (right_dim,)), ((), ())), preferred_element_type=F32
    )


def lane_masks():
    lane = lax.broadcasted_iota(jnp.int32, (1, 2 * HD), 1)
    low = jnp.where(lane < HD, 1.0, 0.0)
    first = jnp.where(lane == HD, 1.0, 0.0)
    second = jnp.where(lane == 0, 1.0, 0.0)
    low, high, first, second = (
        v.astype(BF) for v in (low, 1.0 - low, first, second)
    )
    return ((low, high, first), (high, low, second))


def causal_mask(scores):
    key = lax.broadcasted_iota(jnp.int32, scores.shape, 0)
    query = lax.broadcasted_iota(jnp.int32, scores.shape, 1)
    return jnp.where(key <= query, scores, MASKED)


def rem(value, size):
    return lax.rem(value, size)


class Courier:
    def __init__(self, sizes, jobs):
        self.sizes = sizes
        self.jobs = jobs
        self.plane = sizes[1] * sizes[2] * sizes[3]
        self.in_plane = any(job[0] in ("fetch", "return") for job in jobs)
        self.lines = [job[1] for job in jobs if job[0] == "line"]
        for job in jobs:
            if job[0] == "scatter":
                self.lines += list(range(1, PLANES))

    def out_shape(self):
        shapes = []
        for kind, _, value in self.jobs:
            shape = value.shape
            if kind == "fetch":
                shape = (self.plane,) + shape[1:]
            elif kind == "scatter":
                shape = (PLANES - 1,) + shape[1:]
            shapes.append(jax.ShapeDtypeStruct(shape, value.dtype))
        return shapes

    def specs(self):
        return [pl.BlockSpec(memory_space=pl.ANY)] * len(self.jobs)

    def values(self):
        return [job[2] for job in self.jobs]

    def scratch(self):
        each = {"line": 1, "scatter": PLANES - 1}
        count = max(1, sum(each.get(job[0], self.plane - 1) for job in self.jobs))
        own = max(1, sum(job[0] in ("fetch", "return") for job in self.jobs))
        return [pltpu.SemaphoreType.DMA((n,)) for n in (count, count, own)]

    def params(self, ident):
        return pltpu.CompilerParams(
            vmem_limit_bytes=VMEM, collective_id=ident, has_side_effects=True
        )

    def me(self):
        _, _, x_size, c_size = self.sizes
        y, x, c = (lax.axis_index(name) for name in PLANE)
        return (y * x_size + x) * c_size + c

    def along(self, offset):
        return {"z": rem(lax.axis_index("z") + (offset + PLANES), PLANES)}

    def across(self, offset):
        _, _, x_size, c_size = self.sizes
        other = rem(self.me() + offset, self.plane)
        line = lax.div(other, c_size)
        return other, {"y": lax.div(line, x_size), "x": rem(line, x_size), "c": rem(other, c_size)}

    def greet(self):
        barrier = pltpu.get_barrier_semaphore()
        count = 0
        if self.in_plane:
            for k in range(1, self.plane):
                _, device = self.across(k)
                pl.semaphore_signal(
                    barrier, inc=1, device_id=device, device_id_type=pl.DeviceIdType.MESH
                )
                count += 1
        for offset in self.lines:
            pl.semaphore_signal(
                barrier,
                inc=1,
                device_id=self.along(-offset),
                device_id_type=pl.DeviceIdType.MESH,
            )
            count += 1
        pl.semaphore_wait(barrier, count)

    def copies(self, sources, targets, sems):
        send, receive, own = sems
        remote = []
        local = []

        def add(source, target, device):
            n = len(remote)
            remote.append(
                pltpu.make_async_remote_copy(
                    src_ref=source,
                    dst_ref=target,
                    send_sem=send.at[n],
                    recv_sem=receive.at[n],
                    device_id=device,
                    device_id_type=pl.DeviceIdType.MESH,
                )
            )

        me = self.me()
        for (kind, offset, _), source, target in zip(self.jobs, sources, targets):
            if kind == "line":
                add(source, target, self.along(offset))
                continue
            if kind == "scatter":
                for k in range(1, PLANES):
                    there = rem(lax.axis_index("z") + k, PLANES)
                    add(source.at[there], target.at[k - 1], self.along(k))
                continue
            base = 0
            if kind == "fetch":
                base = rem(lax.axis_index("z") + offset, PLANES) * self.plane
            for k in range(1, self.plane):
                other, device = self.across(k)
                add(source.at[base + other], target.at[me], device)
            local.append(
                pltpu.make_async_copy(source.at[base + me], target.at[me], own.at[len(local)])
            )
        return local + remote

    def start(self, sources, targets, sems):
        self.greet()
        for copy in self.copies(sources, targets, sems):
            copy.start()

    def wait(self, sources, targets, sems):
        for copy in self.copies(sources, targets, sems):
            copy.wait()


class Reducer:
    def __init__(self, sizes, shape):
        self.sizes = sizes
        self.rows, self.lanes = shape[-2:]
        self.half = self.lanes // 2

    def scratch(self):
        z, y, x, _ = self.sizes
        r, w, h = self.rows, self.lanes, self.half
        crossing = x + y - 2
        return [
            pltpu.VMEM((z, y, x, r, w), BF),
            pltpu.VMEM((z, y, x, r, w), BF),
            pltpu.VMEM((x - 1, z, y, r, h), BF),
            pltpu.VMEM((y - 1, z, x, r, h), BF),
            pltpu.VMEM((y - 1, z, r, h), BF),
            pltpu.VMEM((x - 1, z, r, h), BF),
            pltpu.SemaphoreType.DMA((1,)),
            pltpu.SemaphoreType.DMA((1 + 2 * crossing,)),
            pltpu.SemaphoreType.DMA((1 + 2 * crossing,)),
        ]

    def bind(self, source, refs):
        self.source = source
        self.own, self.got0, self.got1x, self.got1y, self.got2y, self.got2x = refs[:6]
        self.local, self.send, self.receive = refs[6:]
        self.z, self.y, self.x, self.c = (lax.axis_index(name) for name in ALL)
        return self

    def remote(self, n, source, target, device):
        return pltpu.make_async_remote_copy(
            src_ref=source,
            dst_ref=target,
            send_sem=self.send.at[n],
            recv_sem=self.receive.at[n],
            device_id=device,
            device_id_type=pl.DeviceIdType.MESH,
        )

    def first(self):
        other = 1 - self.c
        return [
            pltpu.make_async_copy(self.source.at[:, :, :, self.c], self.own, self.local.at[0]),
            self.remote(0, self.source.at[:, :, :, other], self.got0, {"c": other}),
        ]

    def second(self):
        _, y_size, x_size, _ = self.sizes
        left, right = pl.ds(0, self.half), pl.ds(self.half, self.half)
        copies = []
        for k in range(1, x_size):
            there = rem(self.x + k, x_size)
            copies.append((self.own.at[:, :, there, :, left], self.got1x.at[k - 1], {"x": there}))
        for k in range(1, y_size):
            there = rem(self.y + k, y_size)
            copies.append((self.own.at[:, there, :, :, right], self.got1y.at[k - 1], {"y": there}))
        return [self.remote(1 + n, *copy) for n, copy in enumerate(copies)]

    def third(self):
        _, y_size, x_size, _ = self.sizes
        left, right = pl.ds(0, self.half), pl.ds(self.half, self.half)
        at = 1 + x_size + y_size - 2
        copies = []
        for k in range(1, y_size):
            there = rem(self.y + k, y_size)
            copies.append(
                (self.own.at[:, there, self.x, :, left], self.got2y.at[k - 1], {"y": there})
            )
        for k in range(1, x_size):
            there = rem(self.x + k, x_size)
            copies.append(
                (self.own.at[:, self.y, there, :, right], self.got2x.at[k - 1], {"x": there})
            )
        return [self.remote(at + n, *copy) for n, copy in enumerate(copies)]

    def begin(self):
        for copy in self.first():
            copy.start()

    def after_first(self):
        for copy in self.first():
            copy.wait()

        @pl.loop(0, self.sizes[0])
        def _(z):
            self.own[z] = (self.own[z].astype(F32) + self.got0[z].astype(F32)).astype(BF)

        for copy in self.second():
            copy.start()

    def after_second(self):
        _, y_size, x_size, _ = self.sizes
        for copy in self.second():
            copy.wait()
        h = self.half

        @pl.loop(0, self.sizes[0])
        def _(z):
            for y in range(y_size):
                total = self.own[z, y, self.x, :, :h].astype(F32)
                for k in range(x_size - 1):
                    total += self.got1x[k, z, y].astype(F32)
                self.own[z, y, self.x, :, :h] = total.astype(BF)
            for x in range(x_size):
                total = self.own[z, self.y, x, :, h:].astype(F32)
                for k in range(y_size - 1):
                    total += self.got1y[k, z, x].astype(F32)
                self.own[z, self.y, x, :, h:] = total.astype(BF)

        for copy in self.third():
            copy.start()

    def after_third(self, out_ref):
        _, y_size, x_size, _ = self.sizes
        for copy in self.third():
            copy.wait()
        h = self.half

        @pl.loop(0, self.sizes[0])
        def _(z):
            total = self.own[z, self.y, self.x, :, :h].astype(F32)
            for k in range(y_size - 1):
                total += self.got2y[k, z].astype(F32)
            out_ref[z, :, :h] = total.astype(BF)
            total = self.own[z, self.y, self.x, :, h:].astype(F32)
            for k in range(x_size - 1):
                total += self.got2x[k, z].astype(F32)
            out_ref[z, :, h:] = total.astype(BF)


def forward_pair(queries, keys, values, bias):
    masks = lane_masks()
    all_scores = []
    for mine, other, one in masks:
        if bias is None:
            all_scores.append(causal_mask(dot(keys, queries * mine, 1, 1)))
        else:
            all_scores.append(dot(keys * mine + bias * one, queries * mine + one, 1, 1))
    parts = []
    lse = []
    for h in range(2):
        mine, other, _ = masks[h]
        scores = all_scores[h]
        row_max = jnp.max(scores, axis=0, keepdims=True)
        probs = jnp.exp(scores - row_max).astype(BF)
        both = dot(values * mine + other, probs, 0, 0)
        halves = (both[:HD], both[HD:])
        total = halves[1 - h]
        parts.append(halves[h] / total)
        lse.append(row_max + jnp.log(total[0:1]))
    return jnp.concatenate(parts, axis=0).T.astype(BF), lse


def backward_pair(queries, grad, keys, values, bias, lse, delta):
    grad_k = None
    grad_v = None
    grad_q = []
    for h, (mine, other, one) in enumerate(lane_masks()):
        query_h = queries * mine
        grad_h = grad * mine
        if bias is None:
            scores = causal_mask(dot(keys, query_h, 1, 1))
        else:
            scores = dot(keys * mine + bias * one, query_h + one, 1, 1)
        probs = jnp.exp(scores - lse[h])
        grad_p = dot(values, grad_h, 1, 1)
        if delta is None:
            delta_h = jnp.sum(probs * grad_p, axis=0, keepdims=True)
        else:
            delta_h = delta[h]
        grad_s = (probs * (grad_p - delta_h)).astype(BF)
        term_v = dot(probs.astype(BF), grad_h, 1, 0)
        term_k = dot(grad_s, query_h, 1, 0)
        grad_v = term_v if grad_v is None else grad_v + term_v
        grad_k = term_k if grad_k is None else grad_k + term_k
        grad_q.append(dot(keys, grad_s, 0, 0)[h * HD : (h + 1) * HD])
    grad_kv = jnp.concatenate([grad_k, grad_v], axis=1).astype(BF)
    return grad_kv, jnp.concatenate(grad_q, axis=0).T.astype(BF)


def key_bias(keys, lens_ref):
    row = lax.broadcasted_iota(jnp.int32, (keys, 128), 0) + lax.axis_index("z") * keys
    return jnp.where(row < lens_ref[0:1, :], 0.0, MASKED).astype(BF)


def two_rows(ref):
    return [ref[0, h : h + 1, :] for h in range(2)]


def split_refs(refs, *counts):
    groups = []
    at = 0
    for count in counts:
        groups.append(refs[at : at + count])
        at += count
    return groups


def carried(courier, reducer, body):
    jobs = len(courier.jobs)
    sums = 0 if reducer is None else 1

    def kernel(ins, outs, scratch, refs):
        own_in, sources, summands, own_out, targets, results, own_scratch, sems, rest = split_refs(
            refs, ins, jobs, sums, outs, jobs, sums, scratch, 3, 9 * sums
        )
        step = pl.program_id(0)

        @pl.when(step == 0)
        def _():
            courier.start(sources, targets, sems)
            if sums:
                reducer.bind(summands[0], rest).begin()

        body(own_in, own_out, own_scratch)

        if sums:

            @pl.when(step == 1)
            def _():
                reducer.bind(summands[0], rest).after_first()

            @pl.when(step == 3)
            def _():
                reducer.bind(summands[0], rest).after_second()

        @pl.when(step == PAIRS - 1)
        def _():
            if sums:
                reducer.bind(summands[0], rest).after_third(results[0])
            courier.wait(sources, targets, sems)

    return kernel


def call(courier, ident, body, args, in_specs, out_shape, out_specs, scratch, flops, summand=None):
    reducer = None
    extra_in, extra_out, extra_out_specs, extra_scratch = [], [], [], []
    if summand is not None:
        courier.in_plane = True
        reducer = Reducer(courier.sizes, summand.shape)
        shape = (PLANES,) + summand.shape[-2:]
        extra_in = [summand]
        extra_out = [jax.ShapeDtypeStruct(shape, BF)]
        extra_out_specs = [pl.BlockSpec(shape, lambda p: (0, 0, 0))]
        extra_scratch = reducer.scratch()
    kernel = carried(courier, reducer, body)
    counts = (len(args), len(out_shape), len(scratch))
    outs = pl.pallas_call(
        lambda *refs: kernel(*counts, refs),
        grid=(PAIRS,),
        out_shape=out_shape + courier.out_shape() + extra_out,
        in_specs=in_specs + courier.specs() + [pl.BlockSpec(memory_space=pl.ANY)] * len(extra_in),
        out_specs=out_specs + courier.specs() + extra_out_specs,
        scratch_shapes=scratch + courier.scratch() + extra_scratch,
        compiler_params=courier.params(ident),
        cost_estimate=pl.CostEstimate(flops=flops, bytes_accessed=2**24, transcendentals=2**20),
    )(*args, *courier.values(), *extra_in)
    return outs[: len(out_shape)], outs[len(out_shape) :]


def reduce_all(sizes, ident, summands, scattered):
    courier = Courier(sizes, [("scatter", 0, value) for value in scattered])
    courier.in_plane = True
    courier.lines += list(range(1, PLANES))
    jobs = len(scattered)
    count = len(summands)
    reducers = [Reducer(sizes, value.shape) for value in summands]
    shapes = [value.shape[-2:] for value in summands]

    def kernel(*refs):
        sources, arrays, targets, results, sems, rest = split_refs(
            refs, jobs, count, jobs, count, 3, len(refs) - 2 * jobs - 2 * count - 3
        )
        courier.start(sources, targets, sems)
        bound = []
        last = []
        for n in range(count):
            refs_n = rest[13 * n : 13 * n + 13]
            bound.append(reducers[n].bind(arrays[n], refs_n[:9]))
            last.append(refs_n[9:])

        def leave(n):
            left, got, send, receive = last[n]
            copies = []
            for k in range(1, PLANES):
                copies.append(
                    pltpu.make_async_remote_copy(
                        src_ref=left.at[rem(lax.axis_index("z") + k, PLANES)],
                        dst_ref=got.at[k - 1],
                        send_sem=send.at[k - 1],
                        recv_sem=receive.at[k - 1],
                        device_id=courier.along(k),
                        device_id_type=pl.DeviceIdType.MESH,
                    )
                )
            return copies

        for one in bound:
            one.begin()
        for one in bound:
            one.after_first()
        for one in bound:
            one.after_second()
        for n, one in enumerate(bound):
            one.after_third(last[n][0])
            for copy in leave(n):
                copy.start()
        for n in range(count):
            for copy in leave(n):
                copy.wait()
            left, got = last[n][:2]
            total = left[lax.axis_index("z")].astype(F32)
            for k in range(PLANES - 1):
                total += got[k].astype(F32)
            results[n][...] = total
        courier.wait(sources, targets, sems)

    scratch = []
    for n in range(count):
        scratch += reducers[n].scratch() + [
            pltpu.VMEM((PLANES,) + shapes[n], BF),
            pltpu.VMEM((PLANES - 1,) + shapes[n], BF),
            pltpu.SemaphoreType.DMA((PLANES - 1,)),
            pltpu.SemaphoreType.DMA((PLANES - 1,)),
        ]
    outs = pl.pallas_call(
        kernel,
        out_shape=courier.out_shape() + [jax.ShapeDtypeStruct(shape, F32) for shape in shapes],
        in_specs=courier.specs() + [pl.BlockSpec(memory_space=pl.ANY)] * count,
        out_specs=courier.specs() + [pl.BlockSpec(memory_space=pltpu.VMEM)] * count,
        scratch_shapes=courier.scratch() + scratch,
        compiler_params=courier.params(ident),
    )(*courier.values(), *summands)
    return outs[:jobs], outs[jobs:]


def summand_of(sizes, arrays):
    devices = sizes[0] * sizes[1] * sizes[2] * sizes[3]
    parts = [a.reshape(devices, a.shape[0] // devices, a.shape[1]) for a in arrays]
    joined = parts[0] if len(parts) == 1 else jnp.concatenate(parts, axis=1)
    return joined.astype(BF).reshape(tuple(sizes) + joined.shape[1:])


def over_z(left, got):
    own = lax.dynamic_index_in_dim(left, lax.axis_index("z"), 0, keepdims=False)
    return own.astype(F32) + jnp.sum(got.astype(F32), axis=0)


def block_specs(tokens, keys):
    return dict(
        col=pl.BlockSpec((tokens, 128), lambda p: (0, p)),
        pair=pl.BlockSpec((keys, 256), lambda p: (0, p)),
        lens=pl.BlockSpec((8, 128), lambda p: (0, 0)),
        rows=pl.BlockSpec((keys, H * HD), lambda p: (0, 0)),
        weight=pl.BlockSpec((H * HD, 128), lambda p: (0, p)),
        stat=pl.BlockSpec((1, 2, tokens), lambda p: (p, 0, 0)),
    )


def rms(values, gain):
    r = lax.rsqrt(jnp.mean(values * values, axis=-1, keepdims=True) + EPSILON)
    return values * r * gain


def self_part(courier, ident, inputs, gains, weights):
    tokens, width = inputs.shape
    jobs = len(courier.jobs)

    def kernel(*refs):
        ins, sources, outs, targets, sems = split_refs(refs, 8, jobs - 1, 7, jobs, 3)
        x_ref, self_gain, cross_gain, wq_ref, wk_ref, wv_ref, wo_ref, wc_ref = ins
        q_ref, k_ref, v_ref, lse_ref, attn_ref, hidden_ref, query_ref = outs
        copies = courier.copies(list(sources) + [query_ref], targets, sems)
        courier.greet()
        for copy in copies[:-1]:
            copy.start()
        values = x_ref[...].astype(F32)
        normed = rms(values, self_gain[...]).astype(BF)
        q_ref[...] = dot(normed, wq_ref[...], 1, 0).astype(BF)
        k_ref[...] = dot(normed, wk_ref[...], 1, 0).astype(BF)
        v_ref[...] = dot(normed, wv_ref[...], 1, 0).astype(BF)

        for p in range(PAIRS):
            cols = pl.ds(p * 128, 128)
            out, lse = forward_pair(q_ref[:, cols], k_ref[:, cols], v_ref[:, cols], None)
            attn_ref[:, cols] = out
            for h in range(2):
                lse_ref[p, h : h + 1, :] = lse[h]

        hidden = values + dot(attn_ref[...], wo_ref[...], 1, 0)
        hidden_ref[...] = hidden
        query_ref[...] = dot(rms(hidden, cross_gain[...]).astype(BF), wc_ref[...], 1, 0).astype(BF)
        copies[-1].start()
        for copy in copies:
            copy.wait()

    rows = jax.ShapeDtypeStruct((tokens, width), BF)
    vmem = pl.BlockSpec(memory_space=pltpu.VMEM)
    stat = jax.ShapeDtypeStruct((PAIRS, 2, tokens), F32)
    wide = jax.ShapeDtypeStruct((tokens, width), F32)
    outs = pl.pallas_call(
        kernel,
        out_shape=[rows, rows, rows, stat, rows, wide, rows] + courier.out_shape(),
        in_specs=[vmem] * 8 + courier.specs()[1:],
        out_specs=[vmem] * 7 + courier.specs(),
        scratch_shapes=courier.scratch(),
        compiler_params=courier.params(ident),
    )(inputs, *gains, *weights, *courier.values()[:-1])
    return outs[:7], outs[7:]


def glu_parts(gate_vals):
    inner = 0.7978845608028654 * (gate_vals + 0.044715 * gate_vals * gate_vals * gate_vals)
    t = jnp.tanh(inner)
    gelu = 0.5 * gate_vals * (1.0 + t)
    slope = 0.5 * (1.0 + t) + 0.5 * gate_vals * (1.0 - t * t) * 0.7978845608028654 * (
        1.0 + 0.134145 * gate_vals * gate_vals
    )
    return gelu, slope


def spread(rows):
    both = [jnp.broadcast_to(rows[h : h + 1], (HD, rows.shape[1])) for h in range(2)]
    return jnp.concatenate(both, axis=0).T


def middle_kernel(*refs, devices, packed):
    (
        part0,
        part1,
        part2,
        part3,
        lse0,
        lse1,
        lse2,
        lse3,
        h1_ref,
        wo_ref,
        gain_ref,
        cot_ref,
        gate_ref,
        up_ref,
        down_ref,
        out_ref,
        attn_ref,
        two_ref,
        da_ref,
        stats_ref,
        gnorm_ref,
        gwo_ref,
        *grad_refs,
        gdown_ref,
        raw_ref,
        h2_ref,
        n3_ref,
        total_ref,
        dn3_ref,
    ) = refs
    step = pl.program_id(0)
    parts = (part0, part1, part2, part3)
    lses = (lse0, lse1, lse2, lse3)

    @pl.when(step == 0)
    def _():
        for p in range(PAIRS):
            cols = pl.ds(p * 128, 128)
            values = [ref[p] for ref in lses]
            top = functools.reduce(jnp.maximum, values)
            scales = [jnp.exp(v - top) for v in values]
            total = functools.reduce(jnp.add, scales)
            stats_ref[0, p] = top + jnp.log(total)
            raw = None
            for ref, scale in zip(parts, scales):
                term = spread(scale / total) * ref[:, cols].astype(F32)
                raw = term if raw is None else raw + term
            raw_ref[:, cols] = raw
            attn_ref[:, cols] = raw.astype(BF)
        hidden = h1_ref[...] + dot(attn_ref[...], wo_ref[...], 1, 0)
        h2_ref[...] = hidden
        n3_ref[...] = rms(hidden, gain_ref[...]).astype(BF)
        total_ref[...] = hidden
        dn3_ref[...] = jnp.zeros_like(dn3_ref)

    normed = n3_ref[...]
    branch = cot_ref[...]
    gate_vals = dot(normed, gate_ref[...], 1, 0)
    up_vals = dot(normed, up_ref[...], 1, 0)
    grad_inner = dot(branch, down_ref[...], 1, 1)
    gelu, slope = glu_parts(gate_vals)
    inner = (gelu * up_vals).astype(BF)
    grad_gate = (grad_inner * up_vals * slope).astype(BF)
    grad_up = (grad_inner * gelu).astype(BF)
    total_ref[...] += dot(inner, down_ref[...], 1, 0)
    dn3_ref[...] += dot(grad_gate, gate_ref[...], 1, 1) + dot(grad_up, up_ref[...], 1, 1)
    terms = [dot(normed, grad_gate, 0, 0), dot(normed, grad_up, 0, 0)]
    if packed:
        shape = (devices, terms[0].shape[0] // devices, terms[0].shape[1])
        grad_refs[0][...] = jnp.concatenate([t.reshape(shape) for t in terms], axis=1).astype(BF)
    else:
        for ref, term in zip(grad_refs, terms):
            ref[...] = term
    gdown_ref[...] = dot(inner, branch, 0, 0).astype(BF).reshape(gdown_ref.shape)

    @pl.when(step == pl.num_programs(0) - 1)
    def _():
        out_ref[...] = total_ref[...].astype(BF)
        hidden = h2_ref[...]
        grad = dn3_ref[...]
        r = lax.rsqrt(jnp.mean(hidden * hidden, axis=-1, keepdims=True) + EPSILON)
        u = gain_ref[...] * grad
        back = r * u - hidden * (r * r * r) * jnp.mean(u * hidden, axis=-1, keepdims=True)
        gnorm_ref[...] = jnp.sum(grad * hidden * r, axis=0, keepdims=True)
        two = cot_ref[...].astype(F32) + back
        two_ref[...] = two
        low = two.astype(BF)
        da_ref[...] = dot(low, wo_ref[...], 1, 1).astype(BF)
        gwo_ref[...] = dot(attn_ref[...], low, 0, 0)
        for p in range(PAIRS):
            cols = pl.ds(p * 128, 128)
            product = (da_ref[:, cols].astype(F32) * raw_ref[:, cols]).T
            for h in range(2):
                stats_ref[1, p, h : h + 1] = jnp.sum(
                    product[h * HD : (h + 1) * HD], axis=0, keepdims=True
                )


def middle(devices, parts, lses, hidden, out_weight, gain, cotangent, gate, up, down):
    tokens, width = hidden.shape
    inner = gate.shape[1]
    chunk = 512
    share = width // devices
    packed = share % 8 == 0
    down_share = inner // devices
    fixed = lambda *shape: pl.BlockSpec(shape, lambda p: (0,) * len(shape))
    whole = fixed(tokens, width)
    square = fixed(width, width)
    stat = fixed(PAIRS, 2, tokens)
    column = pl.BlockSpec((width, chunk), lambda p: (0, p))
    if packed:
        grad_shapes = [jax.ShapeDtypeStruct((devices, 2 * share, inner), BF)]
        grad_specs = [pl.BlockSpec((devices, 2 * share, chunk), lambda p: (0, 0, p))]
    else:
        grad_shapes = [jax.ShapeDtypeStruct((width, inner), F32)] * 2
        grad_specs = [column] * 2
    rows = jax.ShapeDtypeStruct((tokens, width), BF)
    wide = jax.ShapeDtypeStruct((tokens, width), F32)
    return pl.pallas_call(
        functools.partial(middle_kernel, devices=devices, packed=packed),
        grid=(inner // chunk,),
        out_shape=[
            rows,
            rows,
            wide,
            rows,
            jax.ShapeDtypeStruct((2, PAIRS, 2, tokens), F32),
            jax.ShapeDtypeStruct((1, width), F32),
            jax.ShapeDtypeStruct((width, width), F32),
        ]
        + grad_shapes
        + [jax.ShapeDtypeStruct((devices, down_share, width), BF)],
        in_specs=[whole] * 4
        + [stat] * 4
        + [whole, square, fixed(1, width), whole]
        + [column, column, pl.BlockSpec((chunk, width), lambda p: (p, 0))],
        out_specs=[whole] * 4
        + [fixed(2, PAIRS, 2, tokens), fixed(1, width), square]
        + grad_specs
        + [pl.BlockSpec((chunk // down_share, down_share, width), lambda p: (p, 0, 0))],
        scratch_shapes=[
            pltpu.VMEM((tokens, width), F32),
            pltpu.VMEM((tokens, width), F32),
            pltpu.VMEM((tokens, width), BF),
            pltpu.VMEM((tokens, width), F32),
            pltpu.VMEM((tokens, width), F32),
        ],
        compiler_params=pltpu.CompilerParams(vmem_limit_bytes=VMEM),
    )(*parts, *lses, hidden, out_weight, gain, cotangent, gate, up, down)


def cross_forward(courier, ident, queries, rows, lens, key_weight, value_weight):
    tokens, keys = queries.shape[0], rows.shape[0]
    spec = block_specs(tokens, keys)

    def body(ins, outs, _):
        q_ref, rows_ref, lens_ref, wk_ref, wv_ref = ins
        o_ref, lse_ref, kv_ref = outs
        weights = jnp.concatenate([wk_ref[...], wv_ref[...]], axis=1)
        kv_ref[...] = dot(rows_ref[...], weights, 1, 0).astype(BF)
        bias = key_bias(keys, lens_ref)
        out, lse = forward_pair(q_ref[...], kv_ref[:, :128], kv_ref[:, 128:], bias)
        o_ref[...] = out
        for h in range(2):
            lse_ref[0, h : h + 1, :] = lse[h]

    return call(
        courier,
        ident,
        body,
        [queries, rows, lens, key_weight, value_weight],
        [spec["col"], spec["rows"], spec["lens"], spec["weight"], spec["weight"]],
        [
            jax.ShapeDtypeStruct((tokens, H * HD), BF),
            jax.ShapeDtypeStruct((PAIRS, 2, tokens), F32),
            jax.ShapeDtypeStruct((keys, 2 * H * HD), BF),
        ],
        [spec["col"], spec["stat"], spec["pair"]],
        [],
        2**34,
    )


def cross_backward(
    courier, ident, queries, grad, keyvals, lens, lse, delta, key_weight, value_weight, summand=None
):
    tokens, keys = queries.shape[0], keyvals.shape[0]
    width = H * HD
    spec = block_specs(tokens, keys)

    def body(ins, outs, scratch):
        q_ref, da_ref, kv_ref, lens_ref, lse_ref, delta_ref, wk_ref, wv_ref = ins
        dkv_ref, dq_ref, dm_ref = outs
        (total_ref,) = scratch
        step = pl.program_id(0)

        @pl.when(step == 0)
        def _():
            total_ref[...] = jnp.zeros_like(total_ref)

        weights = jnp.concatenate([wk_ref[...], wv_ref[...]], axis=1)
        grad_kv, grad_q = backward_pair(
            q_ref[...],
            da_ref[...],
            kv_ref[:, :128],
            kv_ref[:, 128:],
            key_bias(keys, lens_ref),
            two_rows(lse_ref),
            two_rows(delta_ref),
        )
        dkv_ref[...] = grad_kv
        dq_ref[...] = grad_q
        total_ref[...] += dot(grad_kv, weights, 1, 1)

        @pl.when(step == PAIRS - 1)
        def _():
            dm_ref[...] = total_ref[...].astype(BF)

    return call(
        courier,
        ident,
        body,
        [queries, grad, keyvals, lens, lse, delta, key_weight, value_weight],
        [spec[n] for n in ("col", "col", "pair", "lens", "stat", "stat", "weight", "weight")],
        [
            jax.ShapeDtypeStruct((keys, 2 * width), BF),
            jax.ShapeDtypeStruct((tokens, width), BF),
            jax.ShapeDtypeStruct((keys, width), BF),
        ],
        [spec["pair"], spec["col"], spec["rows"]],
        [pltpu.VMEM((keys, width), F32)],
        2**35,
        summand,
    )


def weight_terms(courier, ident, rows, grads):
    keys, width = rows[0].shape
    spec = block_specs(keys, keys)
    count = len(rows)

    def body(ins, outs, _):
        total = None
        for rows_ref, grad_ref in zip(ins[:count], ins[count:]):
            term = dot(rows_ref[...], grad_ref[...], 0, 0)
            total = term if total is None else total + term
        outs[0][...] = total[:, :128]
        outs[1][...] = total[:, 128:]

    return call(
        courier,
        ident,
        body,
        list(rows) + list(grads),
        [spec["rows"]] * count + [spec["pair"]] * count,
        [jax.ShapeDtypeStruct((width, width), F32)] * 2,
        [spec["weight"]] * 2,
        [],
        2**34,
    )


def self_backward(courier, ident, queries, grad, keys, values, lse, summand):
    tokens, width = queries.shape
    spec = block_specs(tokens, tokens)

    def body(ins, outs, _):
        q_ref, da_ref, k_ref, v_ref, lse_ref = ins
        dq_ref, dk_ref, dv_ref = outs
        grad_kv, dq_ref[...] = backward_pair(
            q_ref[...], da_ref[...], k_ref[...], v_ref[...], None, two_rows(lse_ref), None
        )
        dk_ref[...] = grad_kv[:, :128]
        dv_ref[...] = grad_kv[:, 128:]

    return call(
        courier,
        ident,
        body,
        [queries, grad, keys, values, lse],
        [spec["col"]] * 4 + [spec["stat"]],
        [jax.ShapeDtypeStruct((tokens, width), BF)] * 3,
        [spec["col"]] * 3,
        [],
        2**33,
        summand,
    )


def place_kernel(*refs):
    *blocks, out_ref, held, arrive, leave = refs
    z = lax.axis_index("z")
    size = held.shape[1]
    inward = []
    outward = []
    for r, block in enumerate(blocks):
        at = rem(z + r, PLANES) * size
        inward.append(pltpu.make_async_copy(block, held.at[r], arrive.at[r]))
        outward.append(
            pltpu.make_async_copy(held.at[r], out_ref.at[pl.ds(at, size)], leave.at[r])
        )
        inward[r].start()
    for r in range(len(blocks)):
        inward[r].wait()
        outward[r].start()
    for copy in outward:
        copy.wait()


def place(blocks):
    shape = blocks[0].shape
    count = len(blocks)
    hbm = pl.BlockSpec(memory_space=pl.ANY)
    return pl.pallas_call(
        place_kernel,
        out_shape=jax.ShapeDtypeStruct((count * shape[0],) + shape[1:], blocks[0].dtype),
        in_specs=[hbm] * count,
        out_specs=hbm,
        scratch_shapes=[
            pltpu.VMEM((count,) + shape, blocks[0].dtype),
            pltpu.SemaphoreType.DMA((count,)),
            pltpu.SemaphoreType.DMA((count,)),
        ],
        compiler_params=pltpu.CompilerParams(vmem_limit_bytes=VMEM),
    )(*blocks)


def norm_apply(values, gain):
    return values * lax.rsqrt(jnp.mean(values * values, axis=-1, keepdims=True) + EPSILON) * gain


def norm_back(values, gain, grad):
    r = lax.rsqrt(jnp.mean(values * values, axis=-1, keepdims=True) + EPSILON)
    u = gain * grad
    dv = r * u - values * (r * r * r) * jnp.mean(u * values, axis=-1, keepdims=True)
    return dv, jnp.sum(grad * values * r, axis=0)


def matmul(left, right):
    return dot(left, right, 1, 0)


def matmul_t(left, right):
    return dot(left, right, 1, 1)


def tmatmul(left, right):
    return dot(left, right, 0, 0)


def on_device(
    sizes,
    decoder_in,
    memory,
    memory_lengths,
    cotangent,
    norm_self,
    self_query,
    self_key,
    self_value,
    self_out,
    norm_cross,
    cross_query,
    cross_key,
    cross_value,
    cross_out,
    norm_ffn,
    ffn_gate,
    ffn_up,
    ffn_down,
):
    devices, positions, width = memory.shape
    plane_size = sizes[1] * sizes[2] * sizes[3]
    z = lax.axis_index("z")

    def flat(blocks):
        return blocks.reshape(plane_size * positions, width)

    def cut(rows):
        return rows.reshape(plane_size, positions, width)

    inputs = decoder_in[0].astype(F32)
    lens = {0: jnp.broadcast_to(memory_lengths[None, :], (8, 128))}
    jobs = [("fetch", 1, memory)]
    jobs += [("line", -r, lens[0]) for r in range(1, PLANES)]
    jobs += [("line", -1, jax.ShapeDtypeStruct(decoder_in.shape[1:], BF))]
    (query_one, key_one, value_one, lse_one, attn_one, hidden_one, query_two), moved = self_part(
        Courier(sizes, jobs),
        0,
        decoder_in[0],
        (norm_self[None], norm_cross[None]),
        (self_query, self_key, self_value, self_out, cross_query),
    )
    fetched, lens[1], lens[2], lens[3], query_near = moved
    normed_one = norm_apply(inputs, norm_self).astype(BF)
    normed_two = norm_apply(hidden_one, norm_cross).astype(BF)
    queries, rows, keyvals, partial, stats_out = {0: query_two, 1: query_near}, {}, {}, {}, {}
    order = (1, 2, 3, 0)
    for at, r in enumerate(order):
        rows[r] = flat(fetched)
        jobs = []
        if at + 1 < PLANES:
            jobs.append(("fetch", order[at + 1], memory))
        if at + 2 < PLANES:
            jobs.append(("line", -order[at + 1], query_two))
        if at >= 1:
            before = order[at - 1]
            jobs.append(("line", before, partial[before]))
            jobs.append(("line", before, stats_out[before]))
        (partial[r], stats_out[r], keyvals[r]), moved = cross_forward(
            Courier(sizes, jobs), 1 + at, queries[r], rows[r], lens[r], cross_key, cross_value
        )
        moved = list(moved)
        if at + 1 < PLANES:
            fetched = moved.pop(0)
        if at + 2 < PLANES:
            queries[order[at + 1]] = moved.pop(0)
        if at >= 1:
            partial[before], stats_out[before] = moved
    (
        output,
        attn_two,
        grad_two,
        grad_attn_two,
        stats,
        grad_norm_ffn,
        grad_cross_out,
        *grads_in,
        grad_down,
    ) = middle(
        devices,
        [partial[r] for r in range(PLANES)],
        [stats_out[r] for r in range(PLANES)],
        hidden_one,
        cross_out,
        norm_ffn[None],
        cotangent[0],
        ffn_gate,
        ffn_up,
        ffn_down,
    )
    decoder_out = output[None]
    if len(grads_in) == 2:
        summand = summand_of(sizes, grads_in)
    else:
        summand = grads_in[0].reshape(tuple(sizes) + grads_in[0].shape[1:])
    summands = {0: summand, 1: grad_down.reshape(tuple(sizes) + grad_down.shape[1:])}
    left, got = {}, {}

    grads = {0: grad_attn_two}
    both = {0: stats}
    grad_kv, grad_q, grad_rows, returned = {}, {}, {}, {}
    for r in range(PLANES):
        jobs = []
        if r + 1 < PLANES:
            jobs.append(("line", -(r + 1), grad_attn_two))
            jobs.append(("line", -(r + 1), stats))
        if r >= 1:
            jobs.append(("return", 0, cut(grad_rows[r - 1])))
        if r >= 2:
            jobs.append(("line", r - 1, grad_q[r - 1]))
        (grad_kv[r], grad_q[r], grad_rows[r]), moved = cross_backward(
            Courier(sizes, jobs),
            5 + r,
            queries[r],
            grads[r],
            keyvals[r],
            lens[r],
            both[r][0],
            both[r][1],
            cross_key,
            cross_value,
            summands.get(r),
        )
        moved = list(moved)
        if r in summands:
            left[r] = moved.pop()
        if r + 1 < PLANES:
            grads[r + 1], both[r + 1] = moved.pop(0), moved.pop(0)
        if r >= 1:
            returned[r - 1] = moved.pop(0)
        if r >= 2:
            grad_q[r - 1] = moved.pop(0)
    last = PLANES - 1
    jobs = [
        ("line", last, grad_q[last]),
        ("return", 0, cut(grad_rows[last])),
        ("scatter", 0, left[0]),
        ("scatter", 0, left[1]),
    ]
    (grad_cross_key, grad_cross_value), (grad_q[last], returned[last], got[0], got[1]) = weight_terms(
        Courier(sizes, jobs),
        9,
        [rows[r] for r in range(PLANES)],
        [grad_kv[r] for r in range(PLANES)],
    )
    memory_grad = place([returned[r] for r in range(PLANES)])

    grad_q_two = sum(grad_q[r].astype(F32) for r in range(PLANES)).astype(BF)
    grad_cross_query = tmatmul(normed_two, grad_q_two)
    grad_normed_two = matmul_t(grad_q_two, cross_query)
    back_one, grad_norm_cross = norm_back(hidden_one, norm_cross, grad_normed_two)
    grad_one = grad_two + back_one
    branch_one = grad_one.astype(BF)
    grad_self_out = tmatmul(attn_one, branch_one)
    grad_attn_one = matmul_t(branch_one, self_out).astype(BF)
    (grad_q_one, grad_k_one, grad_v_one), (cross_left,) = self_backward(
        Courier(sizes, []),
        10,
        query_one,
        grad_attn_one,
        key_one,
        value_one,
        lse_one,
        summand_of(sizes, (grad_cross_key, grad_cross_value)),
    )
    grad_normed_one = (
        matmul_t(grad_q_one, self_query)
        + matmul_t(grad_k_one, self_key)
        + matmul_t(grad_v_one, self_value)
    )
    back_in, grad_norm_self = norm_back(inputs, norm_self, grad_normed_one)
    decoder_in_grad = (grad_one + back_in)[None]
    share_of_norms = width // devices
    norms = jnp.stack(
        [g.reshape(devices, share_of_norms) for g in (grad_norm_self, grad_norm_cross, grad_norm_ffn[0])],
        axis=1,
    ).reshape(devices, 1, 3 * share_of_norms)
    norms = jnp.pad(norms, ((0, 0), (0, 15), (0, 256 - 3 * share_of_norms)))
    (cross_got,), sums = reduce_all(
        sizes,
        11,
        [
            norms.astype(BF).reshape(tuple(sizes) + norms.shape[1:]),
            summand_of(sizes, (grad_cross_query, grad_cross_out)),
            summand_of(sizes, (tmatmul(normed_one, grad_q_one), tmatmul(normed_one, grad_k_one))),
            summand_of(sizes, (tmatmul(normed_one, grad_v_one), grad_self_out)),
        ],
        [cross_left],
    )
    norm_sums = sums[0][0, : 3 * share_of_norms].reshape(3, share_of_norms)
    gate_up = over_z(left[0], got[0])
    cross_kv = over_z(cross_left, cross_got)
    part = share_of_norms
    return (
        decoder_out,
        decoder_in_grad,
        memory_grad,
        norm_sums[0],
        sums[2][:part],
        sums[2][part:],
        sums[3][:part],
        sums[3][part:],
        norm_sums[1],
        sums[1][:part],
        cross_kv[:part],
        cross_kv[part:],
        sums[1][part:],
        norm_sums[2],
        gate_up[:part],
        gate_up[part:],
        over_z(left[1], got[1]),
    )


def solution(mesh):
    dp, seq = mesh.devices.shape
    cores = 2
    lines = dp // PLANES
    split = Mesh(mesh.devices.reshape(PLANES, lines, seq // cores, cores), ALL)
    sizes = split.devices.shape
    first = P(ALL)
    middle = P(None, ALL)
    whole = P()
    return jax.shard_map(
        functools.partial(on_device, sizes),
        mesh=split,
        in_specs=(first, middle, first, first) + (whole,) * 14,
        out_specs=(first, first, middle) + (first,) * 14,
        check_vma=False,
    )
```

```python
import functools

import jax
import jax.numpy as jnp
from jax import lax
from jax.experimental import pallas as pl
from jax.experimental.pallas import tpu as pltpu
from jax.sharding import Mesh
from jax.sharding import PartitionSpec as P

H = 12
HD = 64
PAIRS = 6
PLANES = 4
EPSILON = 1e-06
MASKED = -1e30
VMEM = 56 * 2**20
BF = jnp.bfloat16
F32 = jnp.float32
ALL = ("z", "y", "x", "c")
PLANE = ("y", "x", "c")
EVERY = slice(None)


def dot(left, right, left_dim, right_dim):
    return lax.dot_general(
        left, right, (((left_dim,), (right_dim,)), ((), ())), preferred_element_type=F32
    )


def lane_masks():
    lane = lax.broadcasted_iota(jnp.int32, (1, 2 * HD), 1)
    low = jnp.where(lane < HD, 1.0, 0.0)
    first = jnp.where(lane == HD, 1.0, 0.0)
    second = jnp.where(lane == 0, 1.0, 0.0)
    low, high, first, second = (
        v.astype(BF) for v in (low, 1.0 - low, first, second)
    )
    return ((low, high, first), (high, low, second))


def causal_mask(scores):
    key = lax.broadcasted_iota(jnp.int32, scores.shape, 0)
    query = lax.broadcasted_iota(jnp.int32, scores.shape, 1)
    return jnp.where(key <= query, scores, MASKED)


def rem(value, size):
    return lax.rem(value, size)


class Courier:
    def __init__(self, sizes, jobs):
        self.sizes = sizes
        self.jobs = jobs
        self.plane = sizes[1] * sizes[2] * sizes[3]
        self.in_plane = any(job[0] in ("fetch", "return") for job in jobs)
        self.lines = [job[1] for job in jobs if job[0] == "line"]
        for job in jobs:
            if job[0] == "scatter":
                self.lines += list(range(1, PLANES))

    def out_shape(self):
        shapes = []
        for kind, _, value in self.jobs:
            shape = value.shape
            if kind == "fetch":
                shape = (self.plane,) + shape[1:]
            elif kind == "scatter":
                shape = (PLANES - 1,) + shape[1:]
            shapes.append(jax.ShapeDtypeStruct(shape, value.dtype))
        return shapes

    def specs(self):
        return [pl.BlockSpec(memory_space=pl.ANY)] * len(self.jobs)

    def values(self):
        return [job[2] for job in self.jobs]

    def scratch(self):
        each = {"line": 1, "scatter": PLANES - 1}
        count = max(1, sum(each.get(job[0], self.plane - 1) for job in self.jobs))
        own = max(1, sum(job[0] in ("fetch", "return") for job in self.jobs))
        return [pltpu.SemaphoreType.DMA((n,)) for n in (count, count, own)]

    def params(self, ident):
        return pltpu.CompilerParams(
            vmem_limit_bytes=VMEM, collective_id=ident, has_side_effects=True
        )

    def me(self):
        _, _, x_size, c_size = self.sizes
        y, x, c = (lax.axis_index(name) for name in PLANE)
        return (y * x_size + x) * c_size + c

    def along(self, offset):
        return {"z": rem(lax.axis_index("z") + (offset + PLANES), PLANES)}

    def across(self, offset):
        _, _, x_size, c_size = self.sizes
        other = rem(self.me() + offset, self.plane)
        line = lax.div(other, c_size)
        return other, {"y": lax.div(line, x_size), "x": rem(line, x_size), "c": rem(other, c_size)}

    def greet(self):
        barrier = pltpu.get_barrier_semaphore()
        count = 0
        if self.in_plane:
            for k in range(1, self.plane):
                _, device = self.across(k)
                pl.semaphore_signal(
                    barrier, inc=1, device_id=device, device_id_type=pl.DeviceIdType.MESH
                )
                count += 1
        for offset in self.lines:
            pl.semaphore_signal(
                barrier,
                inc=1,
                device_id=self.along(-offset),
                device_id_type=pl.DeviceIdType.MESH,
            )
            count += 1
        pl.semaphore_wait(barrier, count)

    def copies(self, sources, targets, sems):
        send, receive, own = sems
        remote = []
        local = []

        def add(source, target, device):
            n = len(remote)
            remote.append(
                pltpu.make_async_remote_copy(
                    src_ref=source,
                    dst_ref=target,
                    send_sem=send.at[n],
                    recv_sem=receive.at[n],
                    device_id=device,
                    device_id_type=pl.DeviceIdType.MESH,
                )
            )

        me = self.me()
        for (kind, offset, _), source, target in zip(self.jobs, sources, targets):
            if kind == "line":
                add(source, target, self.along(offset))
                continue
            if kind == "scatter":
                for k in range(1, PLANES):
                    there = rem(lax.axis_index("z") + k, PLANES)
                    add(source.at[there], target.at[k - 1], self.along(k))
                continue
            base = 0
            if kind == "fetch":
                base = rem(lax.axis_index("z") + offset, PLANES) * self.plane
            for k in range(1, self.plane):
                other, device = self.across(k)
                add(source.at[base + other], target.at[me], device)
            local.append(
                pltpu.make_async_copy(source.at[base + me], target.at[me], own.at[len(local)])
            )
        return local + remote

    def start(self, sources, targets, sems):
        self.greet()
        for copy in self.copies(sources, targets, sems):
            copy.start()

    def wait(self, sources, targets, sems):
        for copy in self.copies(sources, targets, sems):
            copy.wait()


class Reducer:
    def __init__(self, sizes, shape):
        self.sizes = sizes
        self.rows, self.lanes = shape[-2:]
        self.half = self.lanes // 2

    def scratch(self):
        z, y, x, _ = self.sizes
        r, w, h = self.rows, self.lanes, self.half
        crossing = x + y - 2
        return [
            pltpu.VMEM((z, y, x, r, w), BF),
            pltpu.VMEM((z, y, x, r, w), BF),
            pltpu.VMEM((x - 1, z, y, r, h), BF),
            pltpu.VMEM((y - 1, z, x, r, h), BF),
            pltpu.VMEM((y - 1, z, r, h), BF),
            pltpu.VMEM((x - 1, z, r, h), BF),
            pltpu.SemaphoreType.DMA((1,)),
            pltpu.SemaphoreType.DMA((1 + 2 * crossing,)),
            pltpu.SemaphoreType.DMA((1 + 2 * crossing,)),
        ]

    def bind(self, source, refs):
        self.source = source
        self.held, self.got0, self.got1x, self.got1y, self.got2y, self.got2x = refs[:6]
        self.local, self.send, self.receive = refs[6:]
        self.z, self.y, self.x, self.c = (lax.axis_index(name) for name in ALL)
        return self

    def index(self, z, y, x, lanes):
        return (z, y, x, EVERY, lanes)

    def slab(self, z, y, x, lanes):
        return self.held.at[self.index(z, y, x, lanes)]

    def remote(self, n, source, target, device):
        return pltpu.make_async_remote_copy(
            src_ref=source,
            dst_ref=target,
            send_sem=self.send.at[n],
            recv_sem=self.receive.at[n],
            device_id=device,
            device_id_type=pl.DeviceIdType.MESH,
        )

    def first(self):
        other = 1 - self.c
        return [
            pltpu.make_async_copy(self.source.at[:, :, :, self.c], self.held, self.local.at[0]),
            self.remote(0, self.source.at[:, :, :, other], self.got0, {"c": other}),
        ]

    def second(self):
        _, y_size, x_size, _ = self.sizes
        left, right = pl.ds(0, self.half), pl.ds(self.half, self.half)
        copies = []
        for k in range(1, x_size):
            there = rem(self.x + k, x_size)
            copies.append((self.slab(EVERY, EVERY, there, left), self.got1x.at[k - 1], {"x": there}))
        for k in range(1, y_size):
            there = rem(self.y + k, y_size)
            copies.append((self.slab(EVERY, there, EVERY, right), self.got1y.at[k - 1], {"y": there}))
        return [self.remote(1 + n, *copy) for n, copy in enumerate(copies)]

    def third(self):
        _, y_size, x_size, _ = self.sizes
        left, right = pl.ds(0, self.half), pl.ds(self.half, self.half)
        at = 1 + x_size + y_size - 2
        copies = []
        for k in range(1, y_size):
            there = rem(self.y + k, y_size)
            copies.append(
                (self.slab(EVERY, there, self.x, left), self.got2y.at[k - 1], {"y": there})
            )
        for k in range(1, x_size):
            there = rem(self.x + k, x_size)
            copies.append(
                (self.slab(EVERY, self.y, there, right), self.got2x.at[k - 1], {"x": there})
            )
        return [self.remote(at + n, *copy) for n, copy in enumerate(copies)]

    def begin(self):
        for copy in self.first():
            copy.start()

    def after_first(self):
        for copy in self.first():
            copy.wait()

        @pl.loop(0, self.sizes[0])
        def _(z):
            at = self.index(z, EVERY, EVERY, EVERY)
            self.held[at] = (self.held[at].astype(F32) + self.got0[z].astype(F32)).astype(BF)

        for copy in self.second():
            copy.start()

    def after_second(self):
        _, y_size, x_size, _ = self.sizes
        for copy in self.second():
            copy.wait()
        h = self.half

        @pl.loop(0, self.sizes[0])
        def _(z):
            for y in range(y_size):
                at = self.index(z, y, self.x, pl.ds(0, h))
                total = self.held[at].astype(F32)
                for k in range(x_size - 1):
                    total += self.got1x[k, z, y].astype(F32)
                self.held[at] = total.astype(BF)
            for x in range(x_size):
                at = self.index(z, self.y, x, pl.ds(h, h))
                total = self.held[at].astype(F32)
                for k in range(y_size - 1):
                    total += self.got1y[k, z, x].astype(F32)
                self.held[at] = total.astype(BF)

        for copy in self.third():
            copy.start()

    def after_third(self, out_ref):
        _, y_size, x_size, _ = self.sizes
        for copy in self.third():
            copy.wait()
        h = self.half

        @pl.loop(0, self.sizes[0])
        def _(z):
            total = self.held[self.index(z, self.y, self.x, pl.ds(0, h))].astype(F32)
            for k in range(y_size - 1):
                total += self.got2y[k, z].astype(F32)
            out_ref[z, :, :h] = total.astype(BF)
            total = self.held[self.index(z, self.y, self.x, pl.ds(h, h))].astype(F32)
            for k in range(x_size - 1):
                total += self.got2x[k, z].astype(F32)
            out_ref[z, :, h:] = total.astype(BF)


class Resident(Reducer):
    def scratch(self):
        z, y, x, c = self.sizes
        r, w, h = self.rows, self.lanes, self.half
        count = 1 + 2 * (x + y - 2) + z - 1
        return [
            pltpu.VMEM((z, y, x, c, r, w), BF),
            pltpu.VMEM((z, y, x, r, w), BF),
            pltpu.VMEM((x - 1, z, y, r, h), BF),
            pltpu.VMEM((y - 1, z, x, r, h), BF),
            pltpu.VMEM((y - 1, z, r, h), BF),
            pltpu.VMEM((x - 1, z, r, h), BF),
            pltpu.VMEM((z, r, w), BF),
            pltpu.VMEM((z - 1, r, w), BF),
            pltpu.SemaphoreType.DMA((count,)),
            pltpu.SemaphoreType.DMA((count,)),
        ]

    def bind(self, refs):
        self.held, self.got0, self.got1x, self.got1y, self.got2y, self.got2x = refs[:6]
        self.left, self.got3, self.send, self.receive = refs[6:]
        self.z, self.y, self.x, self.c = (lax.axis_index(name) for name in ALL)
        return self

    def index(self, z, y, x, lanes):
        return (z, y, x, self.c, EVERY, lanes)

    def first(self):
        other = 1 - self.c
        return [self.remote(0, self.held.at[:, :, :, other], self.got0, {"c": other})]

    def fourth(self):
        _, y_size, x_size, _ = self.sizes
        at = 1 + 2 * (x_size + y_size - 2)
        copies = []
        for k in range(1, PLANES):
            there = rem(self.z + k, PLANES)
            copies.append(
                self.remote(at + k - 1, self.left.at[there], self.got3.at[k - 1], {"z": there})
            )
        return copies

    def after_third_start(self):
        self.after_third(self.left)
        for copy in self.fourth():
            copy.start()

    def finish(self, out_ref):
        for copy in self.fourth():
            copy.wait()
        total = self.left[self.z].astype(F32)
        for k in range(PLANES - 1):
            total += self.got3[k].astype(F32)
        out_ref[...] = total


class SmallSum:
    def __init__(self, sizes, shape):
        self.shape = shape
        self.steps = list(zip(("c", "x", "y", "z"), (sizes[3], sizes[2], sizes[1], sizes[0])))

    def scratch(self):
        count = sum(n - 1 for _, n in self.steps)
        return (
            [pltpu.VMEM(self.shape, F32) for _ in range(4)]
            + [pltpu.VMEM((n - 1,) + self.shape, F32) for _, n in self.steps]
            + [pltpu.SemaphoreType.DMA((count,))] * 2
        )

    def bind(self, refs):
        self.held, self.got = refs[:4], refs[4:8]
        self.send, self.receive = refs[8:]
        return self

    def copies(self, step):
        axis, n = self.steps[step]
        at = sum(m - 1 for _, m in self.steps[:step])
        me = lax.axis_index(axis)
        return [
            pltpu.make_async_remote_copy(
                src_ref=self.held[step],
                dst_ref=self.got[step].at[k - 1],
                send_sem=self.send.at[at + k - 1],
                recv_sem=self.receive.at[at + k - 1],
                device_id={axis: rem(me + k, n)},
                device_id_type=pl.DeviceIdType.MESH,
            )
            for k in range(1, n)
        ]

    def start(self, step):
        for copy in self.copies(step):
            copy.start()

    def advance(self, step, out_ref=None):
        for copy in self.copies(step):
            copy.wait()
        total = self.held[step][...]
        for k in range(self.steps[step][1] - 1):
            total += self.got[step][k]
        if step < 3:
            self.held[step + 1][...] = total
            self.start(step + 1)
        else:
            out_ref[...] = total


def forward_pair(queries, keys, values, bias):
    masks = lane_masks()
    all_scores = []
    for mine, other, one in masks:
        if bias is None:
            all_scores.append(causal_mask(dot(keys, queries * mine, 1, 1)))
        else:
            all_scores.append(dot(keys * mine + bias * one, queries * mine + one, 1, 1))
    parts = []
    lse = []
    for h in range(2):
        mine, other, _ = masks[h]
        scores = all_scores[h]
        row_max = jnp.max(scores, axis=0, keepdims=True)
        probs = jnp.exp(scores - row_max).astype(BF)
        both = dot(values * mine + other, probs, 0, 0)
        halves = (both[:HD], both[HD:])
        total = halves[1 - h]
        parts.append(halves[h] / total)
        lse.append(row_max + jnp.log(total[0:1]))
    return jnp.concatenate(parts, axis=0).T.astype(BF), lse


def backward_pair(queries, grad, keys, values, bias, lse, delta):
    grad_k = None
    grad_v = None
    grad_q = []
    for h, (mine, other, one) in enumerate(lane_masks()):
        query_h = queries * mine
        grad_h = grad * mine
        if bias is None:
            scores = causal_mask(dot(keys, query_h, 1, 1))
        else:
            scores = dot(keys * mine + bias * one, query_h + one, 1, 1)
        probs = jnp.exp(scores - lse[h])
        grad_p = dot(values, grad_h, 1, 1)
        if delta is None:
            delta_h = jnp.sum(probs * grad_p, axis=0, keepdims=True)
        else:
            delta_h = delta[h]
        grad_s = (probs * (grad_p - delta_h)).astype(BF)
        term_v = dot(probs.astype(BF), grad_h, 1, 0)
        term_k = dot(grad_s, query_h, 1, 0)
        grad_v = term_v if grad_v is None else grad_v + term_v
        grad_k = term_k if grad_k is None else grad_k + term_k
        grad_q.append(dot(keys, grad_s, 0, 0)[h * HD : (h + 1) * HD])
    grad_kv = jnp.concatenate([grad_k, grad_v], axis=1).astype(BF)
    return grad_kv, jnp.concatenate(grad_q, axis=0).T.astype(BF)


def key_bias(keys, lens_ref):
    row = lax.broadcasted_iota(jnp.int32, (keys, 128), 0) + lax.axis_index("z") * keys
    return jnp.where(row < lens_ref[0:1, :], 0.0, MASKED).astype(BF)


def two_rows(ref):
    return [ref[0, h : h + 1, :] for h in range(2)]


def split_refs(refs, *counts):
    groups = []
    at = 0
    for count in counts:
        groups.append(refs[at : at + count])
        at += count
    return groups


def carried(courier, reducer, body):
    jobs = len(courier.jobs)
    sums = 0 if reducer is None else 1

    def kernel(ins, outs, scratch, refs):
        own_in, sources, summands, own_out, targets, results, own_scratch, sems, rest = split_refs(
            refs, ins, jobs, sums, outs, jobs, sums, scratch, 3, 9 * sums
        )
        step = pl.program_id(0)

        @pl.when(step == 0)
        def _():
            courier.start(sources, targets, sems)
            if sums:
                reducer.bind(summands[0], rest).begin()

        body(own_in, own_out, own_scratch)

        if sums:

            @pl.when(step == 1)
            def _():
                reducer.bind(summands[0], rest).after_first()

            @pl.when(step == 3)
            def _():
                reducer.bind(summands[0], rest).after_second()

        @pl.when(step == PAIRS - 1)
        def _():
            if sums:
                reducer.bind(summands[0], rest).after_third(results[0])
            courier.wait(sources, targets, sems)

    return kernel


def call(courier, ident, body, args, in_specs, out_shape, out_specs, scratch, flops, summand=None):
    reducer = None
    extra_in, extra_out, extra_out_specs, extra_scratch = [], [], [], []
    if summand is not None:
        courier.in_plane = True
        reducer = Reducer(courier.sizes, summand.shape)
        shape = (PLANES,) + summand.shape[-2:]
        extra_in = [summand]
        extra_out = [jax.ShapeDtypeStruct(shape, BF)]
        extra_out_specs = [pl.BlockSpec(shape, lambda p: (0, 0, 0))]
        extra_scratch = reducer.scratch()
    kernel = carried(courier, reducer, body)
    counts = (len(args), len(out_shape), len(scratch))
    outs = pl.pallas_call(
        lambda *refs: kernel(*counts, refs),
        grid=(PAIRS,),
        out_shape=out_shape + courier.out_shape() + extra_out,
        in_specs=in_specs + courier.specs() + [pl.BlockSpec(memory_space=pl.ANY)] * len(extra_in),
        out_specs=out_specs + courier.specs() + extra_out_specs,
        scratch_shapes=scratch + courier.scratch() + extra_scratch,
        compiler_params=courier.params(ident),
        cost_estimate=pl.CostEstimate(flops=flops, bytes_accessed=2**24, transcendentals=2**20),
    )(*args, *courier.values(), *extra_in)
    return outs[: len(out_shape)], outs[len(out_shape) :]


def reduce_all(sizes, ident, summands, scattered):
    courier = Courier(sizes, [("scatter", 0, value) for value in scattered])
    courier.in_plane = True
    courier.lines += list(range(1, PLANES))
    jobs = len(scattered)
    count = len(summands)
    reducers = [Reducer(sizes, value.shape) for value in summands]
    shapes = [value.shape[-2:] for value in summands]

    def kernel(*refs):
        sources, arrays, targets, results, sems, rest = split_refs(
            refs, jobs, count, jobs, count, 3, len(refs) - 2 * jobs - 2 * count - 3
        )
        courier.start(sources, targets, sems)
        bound = []
        last = []
        for n in range(count):
            refs_n = rest[13 * n : 13 * n + 13]
            bound.append(reducers[n].bind(arrays[n], refs_n[:9]))
            last.append(refs_n[9:])

        def leave(n):
            left, got, send, receive = last[n]
            copies = []
            for k in range(1, PLANES):
                copies.append(
                    pltpu.make_async_remote_copy(
                        src_ref=left.at[rem(lax.axis_index("z") + k, PLANES)],
                        dst_ref=got.at[k - 1],
                        send_sem=send.at[k - 1],
                        recv_sem=receive.at[k - 1],
                        device_id=courier.along(k),
                        device_id_type=pl.DeviceIdType.MESH,
                    )
                )
            return copies

        for one in bound:
            one.begin()
        for one in bound:
            one.after_first()
        for one in bound:
            one.after_second()
        for n, one in enumerate(bound):
            one.after_third(last[n][0])
            for copy in leave(n):
                copy.start()
        for n in range(count):
            for copy in leave(n):
                copy.wait()
            left, got = last[n][:2]
            total = left[lax.axis_index("z")].astype(F32)
            for k in range(PLANES - 1):
                total += got[k].astype(F32)
            results[n][...] = total
        courier.wait(sources, targets, sems)

    scratch = []
    for n in range(count):
        scratch += reducers[n].scratch() + [
            pltpu.VMEM((PLANES,) + shapes[n], BF),
            pltpu.VMEM((PLANES - 1,) + shapes[n], BF),
            pltpu.SemaphoreType.DMA((PLANES - 1,)),
            pltpu.SemaphoreType.DMA((PLANES - 1,)),
        ]
    outs = pl.pallas_call(
        kernel,
        out_shape=courier.out_shape() + [jax.ShapeDtypeStruct(shape, F32) for shape in shapes],
        in_specs=courier.specs() + [pl.BlockSpec(memory_space=pl.ANY)] * count,
        out_specs=courier.specs() + [pl.BlockSpec(memory_space=pltpu.VMEM)] * count,
        scratch_shapes=courier.scratch() + scratch,
        compiler_params=courier.params(ident),
    )(*courier.values(), *summands)
    return outs[:jobs], outs[jobs:]


def summand_of(sizes, arrays):
    devices = sizes[0] * sizes[1] * sizes[2] * sizes[3]
    parts = [a.reshape(devices, a.shape[0] // devices, a.shape[1]) for a in arrays]
    joined = parts[0] if len(parts) == 1 else jnp.concatenate(parts, axis=1)
    return joined.astype(BF).reshape(tuple(sizes) + joined.shape[1:])


def over_z(left, got):
    own = lax.dynamic_index_in_dim(left, lax.axis_index("z"), 0, keepdims=False)
    return own.astype(F32) + jnp.sum(got.astype(F32), axis=0)


def block_specs(tokens, keys):
    return dict(
        col=pl.BlockSpec((tokens, 128), lambda p: (0, p)),
        pair=pl.BlockSpec((keys, 256), lambda p: (0, p)),
        lens=pl.BlockSpec((8, 128), lambda p: (0, 0)),
        rows=pl.BlockSpec((keys, H * HD), lambda p: (0, 0)),
        weight=pl.BlockSpec((H * HD, 128), lambda p: (0, p)),
        stat=pl.BlockSpec((1, 2, tokens), lambda p: (p, 0, 0)),
    )


def rms(values, gain):
    r = lax.rsqrt(jnp.mean(values * values, axis=-1, keepdims=True) + EPSILON)
    return values * r * gain


def self_part(courier, ident, inputs, gains, weights):
    tokens, width = inputs.shape
    jobs = len(courier.jobs)

    def kernel(*refs):
        ins, sources, outs, targets, sems = split_refs(refs, 8, jobs - 1, 7, jobs, 3)
        x_ref, self_gain, cross_gain, wq_ref, wk_ref, wv_ref, wo_ref, wc_ref = ins
        q_ref, k_ref, v_ref, lse_ref, attn_ref, hidden_ref, query_ref = outs
        copies = courier.copies(list(sources) + [query_ref], targets, sems)
        courier.greet()
        for copy in copies[:-1]:
            copy.start()
        values = x_ref[...].astype(F32)
        normed = rms(values, self_gain[...]).astype(BF)
        q_ref[...] = dot(normed, wq_ref[...], 1, 0).astype(BF)
        k_ref[...] = dot(normed, wk_ref[...], 1, 0).astype(BF)
        v_ref[...] = dot(normed, wv_ref[...], 1, 0).astype(BF)

        for p in range(PAIRS):
            cols = pl.ds(p * 128, 128)
            out, lse = forward_pair(q_ref[:, cols], k_ref[:, cols], v_ref[:, cols], None)
            attn_ref[:, cols] = out
            for h in range(2):
                lse_ref[p, h : h + 1, :] = lse[h]

        hidden = values + dot(attn_ref[...], wo_ref[...], 1, 0)
        hidden_ref[...] = hidden
        query_ref[...] = dot(rms(hidden, cross_gain[...]).astype(BF), wc_ref[...], 1, 0).astype(BF)
        copies[-1].start()
        for copy in copies:
            copy.wait()

    rows = jax.ShapeDtypeStruct((tokens, width), BF)
    vmem = pl.BlockSpec(memory_space=pltpu.VMEM)
    stat = jax.ShapeDtypeStruct((PAIRS, 2, tokens), F32)
    wide = jax.ShapeDtypeStruct((tokens, width), F32)
    outs = pl.pallas_call(
        kernel,
        out_shape=[rows, rows, rows, stat, rows, wide, rows] + courier.out_shape(),
        in_specs=[vmem] * 8 + courier.specs()[1:],
        out_specs=[vmem] * 7 + courier.specs(),
        scratch_shapes=courier.scratch(),
        compiler_params=courier.params(ident),
    )(inputs, *gains, *weights, *courier.values()[:-1])
    return outs[:7], outs[7:]


def glu_parts(gate_vals):
    inner = 0.7978845608028654 * (gate_vals + 0.044715 * gate_vals * gate_vals * gate_vals)
    t = jnp.tanh(inner)
    gelu = 0.5 * gate_vals * (1.0 + t)
    slope = 0.5 * (1.0 + t) + 0.5 * gate_vals * (1.0 - t * t) * 0.7978845608028654 * (
        1.0 + 0.134145 * gate_vals * gate_vals
    )
    return gelu, slope


def spread(rows):
    both = [jnp.broadcast_to(rows[h : h + 1], (HD, rows.shape[1])) for h in range(2)]
    return jnp.concatenate(both, axis=0).T


def middle_kernel(*refs, devices, packed):
    (
        part0,
        part1,
        part2,
        part3,
        lse0,
        lse1,
        lse2,
        lse3,
        h1_ref,
        wo_ref,
        gain_ref,
        cot_ref,
        gate_ref,
        up_ref,
        down_ref,
        out_ref,
        attn_ref,
        two_ref,
        da_ref,
        stats_ref,
        gnorm_ref,
        gwo_ref,
        *grad_refs,
        gdown_ref,
        raw_ref,
        h2_ref,
        n3_ref,
        total_ref,
        dn3_ref,
    ) = refs
    step = pl.program_id(0)
    parts = (part0, part1, part2, part3)
    lses = (lse0, lse1, lse2, lse3)

    @pl.when(step == 0)
    def _():
        for p in range(PAIRS):
            cols = pl.ds(p * 128, 128)
            values = [ref[p] for ref in lses]
            top = functools.reduce(jnp.maximum, values)
            scales = [jnp.exp(v - top) for v in values]
            total = functools.reduce(jnp.add, scales)
            stats_ref[0, p] = top + jnp.log(total)
            raw = None
            for ref, scale in zip(parts, scales):
                term = spread(scale / total) * ref[:, cols].astype(F32)
                raw = term if raw is None else raw + term
            raw_ref[:, cols] = raw
            attn_ref[:, cols] = raw.astype(BF)
        hidden = h1_ref[...] + dot(attn_ref[...], wo_ref[...], 1, 0)
        h2_ref[...] = hidden
        n3_ref[...] = rms(hidden, gain_ref[...]).astype(BF)
        total_ref[...] = hidden
        dn3_ref[...] = jnp.zeros_like(dn3_ref)

    normed = n3_ref[...]
    branch = cot_ref[...]
    gate_vals = dot(normed, gate_ref[...], 1, 0)
    up_vals = dot(normed, up_ref[...], 1, 0)
    grad_inner = dot(branch, down_ref[...], 1, 1)
    gelu, slope = glu_parts(gate_vals)
    inner = (gelu * up_vals).astype(BF)
    grad_gate = (grad_inner * up_vals * slope).astype(BF)
    grad_up = (grad_inner * gelu).astype(BF)
    total_ref[...] += dot(inner, down_ref[...], 1, 0)
    dn3_ref[...] += dot(grad_gate, gate_ref[...], 1, 1) + dot(grad_up, up_ref[...], 1, 1)
    terms = [dot(normed, grad_gate, 0, 0), dot(normed, grad_up, 0, 0)]
    if packed:
        shape = (devices, terms[0].shape[0] // devices, terms[0].shape[1])
        grad_refs[0][...] = jnp.concatenate([t.reshape(shape) for t in terms], axis=1).astype(BF)
    else:
        for ref, term in zip(grad_refs, terms):
            ref[...] = term
    gdown_ref[...] = dot(inner, branch, 0, 0).astype(BF).reshape(gdown_ref.shape)

    @pl.when(step == pl.num_programs(0) - 1)
    def _():
        out_ref[...] = total_ref[...].astype(BF)
        hidden = h2_ref[...]
        grad = dn3_ref[...]
        r = lax.rsqrt(jnp.mean(hidden * hidden, axis=-1, keepdims=True) + EPSILON)
        u = gain_ref[...] * grad
        back = r * u - hidden * (r * r * r) * jnp.mean(u * hidden, axis=-1, keepdims=True)
        gnorm_ref[...] = jnp.sum(grad * hidden * r, axis=0, keepdims=True)
        two = cot_ref[...].astype(F32) + back
        two_ref[...] = two
        low = two.astype(BF)
        da_ref[...] = dot(low, wo_ref[...], 1, 1).astype(BF)
        gwo_ref[...] = dot(attn_ref[...], low, 0, 0).astype(BF)
        for p in range(PAIRS):
            cols = pl.ds(p * 128, 128)
            product = (da_ref[:, cols].astype(F32) * raw_ref[:, cols]).T
            for h in range(2):
                stats_ref[1, p, h : h + 1] = jnp.sum(
                    product[h * HD : (h + 1) * HD], axis=0, keepdims=True
                )


def middle(devices, parts, lses, hidden, out_weight, gain, cotangent, gate, up, down):
    tokens, width = hidden.shape
    inner = gate.shape[1]
    chunk = 512
    share = width // devices
    packed = share % 8 == 0
    down_share = inner // devices
    fixed = lambda *shape: pl.BlockSpec(shape, lambda p: (0,) * len(shape))
    whole = fixed(tokens, width)
    square = fixed(width, width)
    stat = fixed(PAIRS, 2, tokens)
    column = pl.BlockSpec((width, chunk), lambda p: (0, p))
    if packed:
        grad_shapes = [jax.ShapeDtypeStruct((devices, 2 * share, inner), BF)]
        grad_specs = [pl.BlockSpec((devices, 2 * share, chunk), lambda p: (0, 0, p))]
    else:
        grad_shapes = [jax.ShapeDtypeStruct((width, inner), F32)] * 2
        grad_specs = [column] * 2
    rows = jax.ShapeDtypeStruct((tokens, width), BF)
    wide = jax.ShapeDtypeStruct((tokens, width), F32)
    return pl.pallas_call(
        functools.partial(middle_kernel, devices=devices, packed=packed),
        grid=(inner // chunk,),
        out_shape=[
            rows,
            rows,
            wide,
            rows,
            jax.ShapeDtypeStruct((2, PAIRS, 2, tokens), F32),
            jax.ShapeDtypeStruct((1, width), F32),
            jax.ShapeDtypeStruct((width, width), BF),
        ]
        + grad_shapes
        + [jax.ShapeDtypeStruct((devices, down_share, width), BF)],
        in_specs=[whole] * 4
        + [stat] * 4
        + [whole, square, fixed(1, width), whole]
        + [column, column, pl.BlockSpec((chunk, width), lambda p: (p, 0))],
        out_specs=[whole] * 4
        + [fixed(2, PAIRS, 2, tokens), fixed(1, width), square]
        + grad_specs
        + [pl.BlockSpec((chunk // down_share, down_share, width), lambda p: (p, 0, 0))],
        scratch_shapes=[
            pltpu.VMEM((tokens, width), F32),
            pltpu.VMEM((tokens, width), F32),
            pltpu.VMEM((tokens, width), BF),
            pltpu.VMEM((tokens, width), F32),
            pltpu.VMEM((tokens, width), F32),
        ],
        compiler_params=pltpu.CompilerParams(vmem_limit_bytes=VMEM),
    )(*parts, *lses, hidden, out_weight, gain, cotangent, gate, up, down)


def cross_forward(courier, ident, queries, rows, lens, key_weight, value_weight):
    tokens, keys = queries.shape[0], rows.shape[0]
    spec = block_specs(tokens, keys)

    def body(ins, outs, _):
        q_ref, rows_ref, lens_ref, wk_ref, wv_ref = ins
        o_ref, lse_ref, kv_ref = outs
        weights = jnp.concatenate([wk_ref[...], wv_ref[...]], axis=1)
        kv_ref[...] = dot(rows_ref[...], weights, 1, 0).astype(BF)
        bias = key_bias(keys, lens_ref)
        out, lse = forward_pair(q_ref[...], kv_ref[:, :128], kv_ref[:, 128:], bias)
        o_ref[...] = out
        for h in range(2):
            lse_ref[0, h : h + 1, :] = lse[h]

    return call(
        courier,
        ident,
        body,
        [queries, rows, lens, key_weight, value_weight],
        [spec["col"], spec["rows"], spec["lens"], spec["weight"], spec["weight"]],
        [
            jax.ShapeDtypeStruct((tokens, H * HD), BF),
            jax.ShapeDtypeStruct((PAIRS, 2, tokens), F32),
            jax.ShapeDtypeStruct((keys, 2 * H * HD), BF),
        ],
        [spec["col"], spec["stat"], spec["pair"]],
        [],
        2**34,
    )


def cross_backward(
    courier, ident, queries, grad, keyvals, lens, lse, delta, key_weight, value_weight, summand=None
):
    tokens, keys = queries.shape[0], keyvals.shape[0]
    width = H * HD
    spec = block_specs(tokens, keys)

    def body(ins, outs, scratch):
        q_ref, da_ref, kv_ref, lens_ref, lse_ref, delta_ref, wk_ref, wv_ref = ins
        dkv_ref, dq_ref, dm_ref = outs
        (total_ref,) = scratch
        step = pl.program_id(0)

        @pl.when(step == 0)
        def _():
            total_ref[...] = jnp.zeros_like(total_ref)

        weights = jnp.concatenate([wk_ref[...], wv_ref[...]], axis=1)
        grad_kv, grad_q = backward_pair(
            q_ref[...],
            da_ref[...],
            kv_ref[:, :128],
            kv_ref[:, 128:],
            key_bias(keys, lens_ref),
            two_rows(lse_ref),
            two_rows(delta_ref),
        )
        dkv_ref[...] = grad_kv
        dq_ref[...] = grad_q
        total_ref[...] += dot(grad_kv, weights, 1, 1)

        @pl.when(step == PAIRS - 1)
        def _():
            dm_ref[...] = total_ref[...].astype(BF)

    return call(
        courier,
        ident,
        body,
        [queries, grad, keyvals, lens, lse, delta, key_weight, value_weight],
        [spec[n] for n in ("col", "col", "pair", "lens", "stat", "stat", "weight", "weight")],
        [
            jax.ShapeDtypeStruct((keys, 2 * width), BF),
            jax.ShapeDtypeStruct((tokens, width), BF),
            jax.ShapeDtypeStruct((keys, width), BF),
        ],
        [spec["pair"], spec["col"], spec["rows"]],
        [pltpu.VMEM((keys, width), F32)],
        2**35,
        summand,
    )


def weight_terms(courier, ident, rows, grads):
    keys, width = rows[0].shape
    spec = block_specs(keys, keys)
    count = len(rows)

    def body(ins, outs, _):
        total = None
        for rows_ref, grad_ref in zip(ins[:count], ins[count:]):
            term = dot(rows_ref[...], grad_ref[...], 0, 0)
            total = term if total is None else total + term
        outs[0][...] = total[:, :128]
        outs[1][...] = total[:, 128:]

    return call(
        courier,
        ident,
        body,
        list(rows) + list(grads),
        [spec["rows"]] * count + [spec["pair"]] * count,
        [jax.ShapeDtypeStruct((width, width), F32)] * 2,
        [spec["weight"]] * 2,
        [],
        2**34,
    )


def self_backward(courier, ident, queries, grad, keys, values, lse, summand):
    tokens, width = queries.shape
    spec = block_specs(tokens, tokens)

    def body(ins, outs, _):
        q_ref, da_ref, k_ref, v_ref, lse_ref = ins
        dq_ref, dk_ref, dv_ref = outs
        grad_kv, dq_ref[...] = backward_pair(
            q_ref[...], da_ref[...], k_ref[...], v_ref[...], None, two_rows(lse_ref), None
        )
        dk_ref[...] = grad_kv[:, :128]
        dv_ref[...] = grad_kv[:, 128:]

    return call(
        courier,
        ident,
        body,
        [queries, grad, keys, values, lse],
        [spec["col"]] * 4 + [spec["stat"]],
        [jax.ShapeDtypeStruct((tokens, width), BF)] * 3,
        [spec["col"]] * 3,
        [],
        2**33,
        summand,
    )


def rms_back(values, gain, grad):
    r = lax.rsqrt(jnp.mean(values * values, axis=-1, keepdims=True) + EPSILON)
    u = gain * grad
    back = r * u - values * (r * r * r) * jnp.mean(u * values, axis=-1, keepdims=True)
    return back, jnp.sum(grad * values * r, axis=0, keepdims=True)


def ending(sizes, ident, rows, grads, grad_q, grad_rows, left, two, held, lse, small_in):
    courier = Courier(
        sizes,
        [("line", PLANES - 1, grad_q[-1]), ("return", 0, grad_rows)]
        + [("scatter", 0, value) for value in left],
    )
    courier.lines = list(range(1, PLANES))
    jobs = len(courier.jobs)
    devices = sizes[0] * sizes[1] * sizes[2] * sizes[3]
    keys, width = rows[0].shape
    tokens = two.shape[0]
    share = width // devices
    chunk = 512
    cuts = keys // chunk
    groups = [Resident(sizes, (2 * share, width)) for _ in range(4)]
    small = SmallSum(sizes, (8, width))
    early = [two] + list(held) + list(grad_q[:-1])
    far = list(rows) + list(grads) + early
    counts = (len(far), len(small_in) + 1, jobs, 6, jobs - 1, 4, len(early) - 1, 8, 3, 40, 10)

    def pack(ref, first, second, cols=EVERY):
        lanes = first.shape[1]
        parts = [v.astype(F32).reshape(devices, share, lanes) for v in (first, second)]
        both = jnp.concatenate(parts, axis=1).astype(BF)
        ref[:, :, :, :, :, cols] = both.reshape(tuple(sizes) + both.shape[1:])

    def kernel(*refs):
        far_refs, near, sources, outs, targets, stage, loaded, work, sems, group_refs, rest = (
            split_refs(refs, *counts)
        )
        self_gain, cross_gain, ffn_term, lse_ref = near
        grad_in, *sums, norm_sums = outs
        row_buf, grad_buf, total, load_sems = stage
        dq_got, da_ref, dq1, dk1, dv1, *_ = work
        chunk_sems, early_sems = load_sems, work[5]
        copies = courier.copies(sources, [dq_got] + list(targets), sems)
        courier.greet()
        for copy in copies:
            copy.start()

        def chunk_loads(r, i):
            slot = rem(i, 2)
            where = pl.ds(pl.multiple_of(rem(i, cuts) * chunk, chunk), chunk)
            return [
                pltpu.make_async_copy(
                    far_refs[r].at[where], row_buf.at[slot], chunk_sems.at[slot, 0]
                ),
                pltpu.make_async_copy(
                    far_refs[PLANES + r].at[where], grad_buf.at[slot], chunk_sems.at[slot, 1]
                ),
            ]

        def start_chunk(i):
            for r in range(PLANES):

                @pl.when(lax.div(jnp.int32(i), cuts) == r)
                def _(r=r):
                    for copy in chunk_loads(r, i):
                        copy.start()

        total[...] = jnp.zeros_like(total)
        early_refs = far_refs[2 * PLANES :]
        early_loads = [
            pltpu.make_async_copy(source, target, early_sems.at[n])
            for n, (source, target) in enumerate(zip(early_refs, [grad_in] + list(loaded)))
        ]
        start_chunk(0)
        for copy in early_loads:
            copy.start()

        @pl.loop(0, PLANES * cuts)
        def _(i):
            @pl.when(i + 1 < PLANES * cuts)
            def _():
                start_chunk(i + 1)

            for copy in chunk_loads(0, i):
                copy.wait()
            slot = rem(i, 2)
            total[...] += dot(row_buf[slot], grad_buf[slot], 0, 0)

        bound = [
            one.bind(group_refs[10 * n : 10 * n + 10]) for n, one in enumerate(groups)
        ]
        bits = small.bind(rest)

        @pl.loop(0, PAIRS)
        def _(p):
            at = pl.multiple_of(p * 256, 256)
            pack(
                bound[0].held,
                total[:, pl.ds(at, 128)],
                total[:, pl.ds(at + 128, 128)],
                pl.ds(pl.multiple_of(p * 128, 128), 128),
            )

        bound[0].begin()
        for copy in early_loads:
            copy.wait()
        copies[1].wait()
        x_ref, h1_ref, gco_ref, q_ref, k_ref, v_ref, attn_ref = loaded[:7]
        wq_ref, wk_ref, wv_ref, wo_ref, wc_ref, *dq_refs = loaded[7:]
        grad = dq_got[...].astype(F32)
        for ref in dq_refs:
            grad += ref[...].astype(F32)
        dq_got[...] = grad.astype(BF)
        hidden = h1_ref[...]
        back, cross_norm = rms_back(hidden, cross_gain[...], dot(dq_got[...], wc_ref[...], 1, 1))
        grad_in[...] += back
        dv1[...] = rms(hidden, cross_gain[...]).astype(BF)
        bound[0].after_first()

        @pl.loop(0, 3)
        def _(i):
            cols = pl.ds(pl.multiple_of(i * 256, 256), 256)
            pack(bound[1].held, dot(dv1[...], dq_got[:, cols], 0, 0), gco_ref[:, cols], cols)

        bound[1].begin()
        low_ref = dq_got
        low_ref[...] = grad_in[...].astype(BF)
        da_ref[...] = dot(low_ref[...], wo_ref[...], 1, 1).astype(BF)

        @pl.loop(0, PAIRS)
        def _(p):
            cols = pl.ds(pl.multiple_of(p * 128, 128), 128)
            grad_kv, grad_q_p = backward_pair(
                q_ref[:, cols],
                da_ref[:, cols],
                k_ref[:, cols],
                v_ref[:, cols],
                None,
                [lse_ref[p, h : h + 1, :] for h in range(2)],
                None,
            )
            dq1[:, cols] = grad_q_p
            dk1[:, cols] = grad_kv[:, :128]
            dv1[:, cols] = grad_kv[:, 128:]

            @pl.when(p == 1)
            def _():
                bound[0].after_second()
                bound[1].after_first()

            @pl.when(p == 3)
            def _():
                bound[0].after_third_start()
                bound[1].after_second()

            @pl.when(p == 5)
            def _():
                bound[1].after_third_start()

        values = x_ref[...].astype(F32)
        normed_ref = da_ref
        normed_ref[...] = rms(values, self_gain[...]).astype(BF)

        @pl.loop(0, 3)
        def _(i):
            cols = pl.ds(pl.multiple_of(i * 256, 256), 256)
            pack(
                bound[2].held,
                dot(normed_ref[...], dv1[:, cols], 0, 0),
                dot(attn_ref[...], low_ref[:, cols], 0, 0),
                cols,
            )

        bound[2].begin()

        @pl.loop(0, 3)
        def _(i):
            cols = pl.ds(pl.multiple_of(i * 256, 256), 256)
            pack(
                bound[3].held,
                dot(normed_ref[...], dq1[:, cols], 0, 0),
                dot(normed_ref[...], dk1[:, cols], 0, 0),
                cols,
            )

        bound[3].begin()
        grad_normed = (
            dot(dq1[...], wq_ref[...], 1, 1)
            + dot(dk1[...], wk_ref[...], 1, 1)
            + dot(dv1[...], wv_ref[...], 1, 1)
        )
        back, self_norm = rms_back(values, self_gain[...], grad_normed)
        grad_in[...] += back
        bits.held[0][...] = jnp.concatenate(
            [self_norm, cross_norm, ffn_term[...], jnp.zeros((5, width), F32)], axis=0
        )
        bits.start(0)
        bound[2].after_first()
        bound[3].after_first()
        bits.advance(0)
        bound[2].after_second()
        bound[3].after_second()
        bits.advance(1)
        bound[2].after_third_start()
        bound[3].after_third_start()
        bits.advance(2)
        for n in range(4):
            bound[n].finish(sums[n])
        bits.advance(3, norm_sums)
        for n, copy in enumerate(copies):
            if n != 1:
                copy.wait()

    any_spec = pl.BlockSpec(memory_space=pl.ANY)
    vmem = pl.BlockSpec(memory_space=pltpu.VMEM)
    row = pltpu.VMEM((tokens, width), BF)
    scratch = [
        pltpu.VMEM((2, chunk, width), BF),
        pltpu.VMEM((2, chunk, 2 * width), BF),
        pltpu.VMEM((width, 2 * width), F32),
        pltpu.SemaphoreType.DMA((2, 2)),
    ]
    scratch += [pltpu.VMEM(v.shape, v.dtype) for v in early[1:]]
    scratch += [row] * 5 + [pltpu.SemaphoreType.DMA((len(early),))]
    scratch += [pltpu.SemaphoreType.DMA((1,))] * 2 + courier.scratch()
    for one in groups:
        scratch += one.scratch()
    scratch += small.scratch()
    outs = pl.pallas_call(
        kernel,
        out_shape=[jax.ShapeDtypeStruct((tokens, width), F32)]
        + [jax.ShapeDtypeStruct((2 * share, width), F32)] * 4
        + [jax.ShapeDtypeStruct((8, width), F32)]
        + courier.out_shape()[1:],
        in_specs=[any_spec] * len(far) + [vmem] * (len(small_in) + 1) + courier.specs(),
        out_specs=[vmem] * 6 + courier.specs()[1:],
        scratch_shapes=scratch,
        compiler_params=pltpu.CompilerParams(
            vmem_limit_bytes=62 * 2**20, collective_id=ident, has_side_effects=True
        ),
    )(*far, *small_in, lse, *courier.values())
    return outs[0], outs[1:5], outs[5], outs[6:]


def place_kernel(*refs):
    *blocks, out_ref, held, arrive, leave = refs
    z = lax.axis_index("z")
    size = held.shape[1]
    inward = []
    outward = []
    for r, block in enumerate(blocks):
        at = rem(z + r, PLANES) * size
        inward.append(pltpu.make_async_copy(block, held.at[r], arrive.at[r]))
        outward.append(
            pltpu.make_async_copy(held.at[r], out_ref.at[pl.ds(at, size)], leave.at[r])
        )
        inward[r].start()
    for r in range(len(blocks)):
        inward[r].wait()
        outward[r].start()
    for copy in outward:
        copy.wait()


def place(blocks):
    shape = blocks[0].shape
    count = len(blocks)
    hbm = pl.BlockSpec(memory_space=pl.ANY)
    return pl.pallas_call(
        place_kernel,
        out_shape=jax.ShapeDtypeStruct((count * shape[0],) + shape[1:], blocks[0].dtype),
        in_specs=[hbm] * count,
        out_specs=hbm,
        scratch_shapes=[
            pltpu.VMEM((count,) + shape, blocks[0].dtype),
            pltpu.SemaphoreType.DMA((count,)),
            pltpu.SemaphoreType.DMA((count,)),
        ],
        compiler_params=pltpu.CompilerParams(vmem_limit_bytes=VMEM),
    )(*blocks)


def norm_apply(values, gain):
    return values * lax.rsqrt(jnp.mean(values * values, axis=-1, keepdims=True) + EPSILON) * gain


def norm_back(values, gain, grad):
    r = lax.rsqrt(jnp.mean(values * values, axis=-1, keepdims=True) + EPSILON)
    u = gain * grad
    dv = r * u - values * (r * r * r) * jnp.mean(u * values, axis=-1, keepdims=True)
    return dv, jnp.sum(grad * values * r, axis=0)


def matmul(left, right):
    return dot(left, right, 1, 0)


def matmul_t(left, right):
    return dot(left, right, 1, 1)


def tmatmul(left, right):
    return dot(left, right, 0, 0)


def on_device(
    sizes,
    decoder_in,
    memory,
    memory_lengths,
    cotangent,
    norm_self,
    self_query,
    self_key,
    self_value,
    self_out,
    norm_cross,
    cross_query,
    cross_key,
    cross_value,
    cross_out,
    norm_ffn,
    ffn_gate,
    ffn_up,
    ffn_down,
):
    devices, positions, width = memory.shape
    plane_size = sizes[1] * sizes[2] * sizes[3]
    z = lax.axis_index("z")

    def flat(blocks):
        return blocks.reshape(plane_size * positions, width)

    def cut(rows):
        return rows.reshape(plane_size, positions, width)

    lens = {0: jnp.broadcast_to(memory_lengths[None, :], (8, 128))}
    jobs = [("fetch", 1, memory)]
    jobs += [("line", -r, lens[0]) for r in range(1, PLANES)]
    jobs += [("line", -1, jax.ShapeDtypeStruct(decoder_in.shape[1:], BF))]
    (query_one, key_one, value_one, lse_one, attn_one, hidden_one, query_two), moved = self_part(
        Courier(sizes, jobs),
        0,
        decoder_in[0],
        (norm_self[None], norm_cross[None]),
        (self_query, self_key, self_value, self_out, cross_query),
    )
    fetched, lens[1], lens[2], lens[3], query_near = moved
    queries, rows, keyvals, partial, stats_out = {0: query_two, 1: query_near}, {}, {}, {}, {}
    order = (1, 2, 3, 0)
    for at, r in enumerate(order):
        rows[r] = flat(fetched)
        jobs = []
        if at + 1 < PLANES:
            jobs.append(("fetch", order[at + 1], memory))
        if at + 2 < PLANES:
            jobs.append(("line", -order[at + 1], query_two))
        if at >= 1:
            before = order[at - 1]
            jobs.append(("line", before, partial[before]))
            jobs.append(("line", before, stats_out[before]))
        (partial[r], stats_out[r], keyvals[r]), moved = cross_forward(
            Courier(sizes, jobs), 1 + at, queries[r], rows[r], lens[r], cross_key, cross_value
        )
        moved = list(moved)
        if at + 1 < PLANES:
            fetched = moved.pop(0)
        if at + 2 < PLANES:
            queries[order[at + 1]] = moved.pop(0)
        if at >= 1:
            partial[before], stats_out[before] = moved
    (
        output,
        attn_two,
        grad_two,
        grad_attn_two,
        stats,
        grad_norm_ffn,
        grad_cross_out,
        *grads_in,
        grad_down,
    ) = middle(
        devices,
        [partial[r] for r in range(PLANES)],
        [stats_out[r] for r in range(PLANES)],
        hidden_one,
        cross_out,
        norm_ffn[None],
        cotangent[0],
        ffn_gate,
        ffn_up,
        ffn_down,
    )
    decoder_out = output[None]
    if len(grads_in) == 2:
        summand = summand_of(sizes, grads_in)
    else:
        summand = grads_in[0].reshape(tuple(sizes) + grads_in[0].shape[1:])
    summands = {0: summand, 1: grad_down.reshape(tuple(sizes) + grad_down.shape[1:])}
    left, got = {}, {}

    grads = {0: grad_attn_two}
    both = {0: stats}
    grad_kv, grad_q, grad_rows, returned = {}, {}, {}, {}
    for r in range(PLANES):
        jobs = []
        if r + 1 < PLANES:
            jobs.append(("line", -(r + 1), grad_attn_two))
            jobs.append(("line", -(r + 1), stats))
        if r >= 1:
            jobs.append(("return", 0, cut(grad_rows[r - 1])))
        if r >= 2:
            jobs.append(("line", r - 1, grad_q[r - 1]))
        (grad_kv[r], grad_q[r], grad_rows[r]), moved = cross_backward(
            Courier(sizes, jobs),
            5 + r,
            queries[r],
            grads[r],
            keyvals[r],
            lens[r],
            both[r][0],
            both[r][1],
            cross_key,
            cross_value,
            summands.get(r),
        )
        moved = list(moved)
        if r in summands:
            left[r] = moved.pop()
        if r + 1 < PLANES:
            grads[r + 1], both[r + 1] = moved.pop(0), moved.pop(0)
        if r >= 1:
            returned[r - 1] = moved.pop(0)
        if r >= 2:
            grad_q[r - 1] = moved.pop(0)
    last = PLANES - 1
    part = width // devices
    if part % 8 == 0:
        decoder_in_grad, sums, norm_sums, moved = ending(
            sizes,
            9,
            [rows[r] for r in range(PLANES)],
            [grad_kv[r] for r in range(PLANES)],
            [grad_q[r] for r in range(PLANES)],
            cut(grad_rows[last]),
            [left[0], left[1]],
            grad_two,
            (decoder_in[0], hidden_one, grad_cross_out, query_one, key_one, value_one, attn_one)
            + (self_query, self_key, self_value, self_out, cross_query),
            lse_one,
            (norm_self[None], norm_cross[None], grad_norm_ffn),
        )
        returned[last], got[0], got[1] = moved
        memory_grad = place([returned[r] for r in range(PLANES)])
        gate_up = over_z(left[0], got[0])
        here = lax.axis_index(ALL) * part
        norm_self_sum, norm_cross_sum, norm_ffn_sum = (
            lax.dynamic_slice_in_dim(norm_sums[n], here, part) for n in range(3)
        )
        return (
            decoder_out,
            decoder_in_grad[None],
            memory_grad,
            norm_self_sum,
            sums[3][:part],
            sums[3][part:],
            sums[2][:part],
            sums[2][part:],
            norm_cross_sum,
            sums[1][:part],
            sums[0][:part],
            sums[0][part:],
            sums[1][part:],
            norm_ffn_sum,
            gate_up[:part],
            gate_up[part:],
            over_z(left[1], got[1]),
        )

    jobs = [
        ("line", last, grad_q[last]),
        ("return", 0, cut(grad_rows[last])),
        ("scatter", 0, left[0]),
        ("scatter", 0, left[1]),
    ]
    (grad_cross_key, grad_cross_value), (grad_q[last], returned[last], got[0], got[1]) = weight_terms(
        Courier(sizes, jobs),
        9,
        [rows[r] for r in range(PLANES)],
        [grad_kv[r] for r in range(PLANES)],
    )
    memory_grad = place([returned[r] for r in range(PLANES)])

    inputs = decoder_in[0].astype(F32)
    normed_one = norm_apply(inputs, norm_self).astype(BF)
    normed_two = norm_apply(hidden_one, norm_cross).astype(BF)
    grad_q_two = sum(grad_q[r].astype(F32) for r in range(PLANES)).astype(BF)
    grad_cross_query = tmatmul(normed_two, grad_q_two)
    grad_normed_two = matmul_t(grad_q_two, cross_query)
    back_one, grad_norm_cross = norm_back(hidden_one, norm_cross, grad_normed_two)
    grad_one = grad_two + back_one
    branch_one = grad_one.astype(BF)
    grad_self_out = tmatmul(attn_one, branch_one)
    grad_attn_one = matmul_t(branch_one, self_out).astype(BF)
    (grad_q_one, grad_k_one, grad_v_one), (cross_left,) = self_backward(
        Courier(sizes, []),
        10,
        query_one,
        grad_attn_one,
        key_one,
        value_one,
        lse_one,
        summand_of(sizes, (grad_cross_key, grad_cross_value)),
    )
    grad_normed_one = (
        matmul_t(grad_q_one, self_query)
        + matmul_t(grad_k_one, self_key)
        + matmul_t(grad_v_one, self_value)
    )
    back_in, grad_norm_self = norm_back(inputs, norm_self, grad_normed_one)
    decoder_in_grad = (grad_one + back_in)[None]
    share_of_norms = width // devices
    norms = jnp.stack(
        [g.reshape(devices, share_of_norms) for g in (grad_norm_self, grad_norm_cross, grad_norm_ffn[0])],
        axis=1,
    ).reshape(devices, 1, 3 * share_of_norms)
    norms = jnp.pad(norms, ((0, 0), (0, 15), (0, 256 - 3 * share_of_norms)))
    (cross_got,), sums = reduce_all(
        sizes,
        11,
        [
            norms.astype(BF).reshape(tuple(sizes) + norms.shape[1:]),
            summand_of(sizes, (grad_cross_query, grad_cross_out.astype(F32))),
            summand_of(sizes, (tmatmul(normed_one, grad_q_one), tmatmul(normed_one, grad_k_one))),
            summand_of(sizes, (tmatmul(normed_one, grad_v_one), grad_self_out)),
        ],
        [cross_left],
    )
    norm_sums = sums[0][0, : 3 * share_of_norms].reshape(3, share_of_norms)
    gate_up = over_z(left[0], got[0])
    cross_kv = over_z(cross_left, cross_got)
    part = share_of_norms
    return (
        decoder_out,
        decoder_in_grad,
        memory_grad,
        norm_sums[0],
        sums[2][:part],
        sums[2][part:],
        sums[3][:part],
        sums[3][part:],
        norm_sums[1],
        sums[1][:part],
        cross_kv[:part],
        cross_kv[part:],
        sums[1][part:],
        norm_sums[2],
        gate_up[:part],
        gate_up[part:],
        over_z(left[1], got[1]),
    )


def solution(mesh):
    dp, seq = mesh.devices.shape
    cores = 2
    lines = dp // PLANES
    split = Mesh(mesh.devices.reshape(PLANES, lines, seq // cores, cores), ALL)
    sizes = split.devices.shape
    first = P(ALL)
    middle = P(None, ALL)
    whole = P()
    return jax.shard_map(
        functools.partial(on_device, sizes),
        mesh=split,
        in_specs=(first, middle, first, first) + (whole,) * 14,
        out_specs=(first, first, middle) + (first,) * 14,
        check_vma=False,
    )
```

```python
import functools

import jax
import jax.numpy as jnp
from jax import lax
from jax.experimental import pallas as pl
from jax.experimental.pallas import tpu as pltpu
from jax.sharding import Mesh
from jax.sharding import PartitionSpec as P

H = 12
HD = 64
PAIRS = 6
PLANES = 4
EPSILON = 1e-06
MASKED = -1e30
VMEM = 56 * 2**20
BF = jnp.bfloat16
F32 = jnp.float32
ALL = ("z", "y", "x", "c")
PLANE = ("y", "x", "c")
EVERY = slice(None)


def dot(left, right, left_dim, right_dim):
    return lax.dot_general(
        left, right, (((left_dim,), (right_dim,)), ((), ())), preferred_element_type=F32
    )


def lane_masks():
    lane = lax.broadcasted_iota(jnp.int32, (1, 2 * HD), 1)
    low = jnp.where(lane < HD, 1.0, 0.0)
    first = jnp.where(lane == HD, 1.0, 0.0)
    second = jnp.where(lane == 0, 1.0, 0.0)
    low, high, first, second = (
        v.astype(BF) for v in (low, 1.0 - low, first, second)
    )
    return ((low, high, first), (high, low, second))


def causal_mask(scores):
    key = lax.broadcasted_iota(jnp.int32, scores.shape, 0)
    query = lax.broadcasted_iota(jnp.int32, scores.shape, 1)
    return jnp.where(key <= query, scores, MASKED)


def rem(value, size):
    return lax.rem(value, size)


class Courier:
    def __init__(self, sizes, jobs):
        self.sizes = sizes
        self.jobs = jobs
        self.plane = sizes[1] * sizes[2] * sizes[3]
        self.in_plane = any(job[0] in ("fetch", "return") for job in jobs)
        self.lines = [job[1] for job in jobs if job[0] == "line"]
        for job in jobs:
            if job[0] == "scatter":
                self.lines += list(range(1, PLANES))

    def out_shape(self):
        shapes = []
        for kind, _, value in self.jobs:
            shape = value.shape
            if kind == "fetch":
                shape = (self.plane,) + shape[1:]
            elif kind == "scatter":
                shape = (PLANES - 1,) + shape[1:]
            shapes.append(jax.ShapeDtypeStruct(shape, value.dtype))
        return shapes

    def specs(self):
        return [pl.BlockSpec(memory_space=pl.ANY)] * len(self.jobs)

    def values(self):
        return [job[2] for job in self.jobs]

    def scratch(self):
        each = {"line": 1, "scatter": PLANES - 1}
        count = max(1, sum(each.get(job[0], self.plane - 1) for job in self.jobs))
        own = max(1, sum(job[0] in ("fetch", "return") for job in self.jobs))
        return [pltpu.SemaphoreType.DMA((n,)) for n in (count, count, own)]

    def params(self, ident):
        return pltpu.CompilerParams(
            vmem_limit_bytes=VMEM, collective_id=ident, has_side_effects=True
        )

    def me(self):
        _, _, x_size, c_size = self.sizes
        y, x, c = (lax.axis_index(name) for name in PLANE)
        return (y * x_size + x) * c_size + c

    def along(self, offset):
        return {"z": rem(lax.axis_index("z") + (offset + PLANES), PLANES)}

    def across(self, offset):
        _, _, x_size, c_size = self.sizes
        other = rem(self.me() + offset, self.plane)
        line = lax.div(other, c_size)
        return other, {"y": lax.div(line, x_size), "x": rem(line, x_size), "c": rem(other, c_size)}

    def greet(self):
        barrier = pltpu.get_barrier_semaphore()
        count = 0
        if self.in_plane:
            for k in range(1, self.plane):
                _, device = self.across(k)
                pl.semaphore_signal(
                    barrier, inc=1, device_id=device, device_id_type=pl.DeviceIdType.MESH
                )
                count += 1
        for offset in self.lines:
            pl.semaphore_signal(
                barrier,
                inc=1,
                device_id=self.along(-offset),
                device_id_type=pl.DeviceIdType.MESH,
            )
            count += 1
        pl.semaphore_wait(barrier, count)

    def copies(self, sources, targets, sems):
        send, receive, own = sems
        remote = []
        local = []

        def add(source, target, device):
            n = len(remote)
            remote.append(
                pltpu.make_async_remote_copy(
                    src_ref=source,
                    dst_ref=target,
                    send_sem=send.at[n],
                    recv_sem=receive.at[n],
                    device_id=device,
                    device_id_type=pl.DeviceIdType.MESH,
                )
            )

        me = self.me()
        for (kind, offset, _), source, target in zip(self.jobs, sources, targets):
            if kind == "line":
                add(source, target, self.along(offset))
                continue
            if kind == "scatter":
                for k in range(1, PLANES):
                    there = rem(lax.axis_index("z") + k, PLANES)
                    add(source.at[there], target.at[k - 1], self.along(k))
                continue
            base = 0
            if kind == "fetch":
                base = rem(lax.axis_index("z") + offset, PLANES) * self.plane
            for k in range(1, self.plane):
                other, device = self.across(k)
                add(source.at[base + other], target.at[me], device)
            local.append(
                pltpu.make_async_copy(source.at[base + me], target.at[me], own.at[len(local)])
            )
        return local + remote

    def start(self, sources, targets, sems):
        self.greet()
        for copy in self.copies(sources, targets, sems):
            copy.start()

    def wait(self, sources, targets, sems):
        for copy in self.copies(sources, targets, sems):
            copy.wait()


class Reducer:
    def __init__(self, sizes, shape):
        self.sizes = sizes
        self.rows, self.lanes = shape[-2:]
        self.half = self.lanes // 2

    def scratch(self):
        z, y, x, _ = self.sizes
        r, w, h = self.rows, self.lanes, self.half
        crossing = x + y - 2
        return [
            pltpu.VMEM((z, y, x, r, w), BF),
            pltpu.VMEM((z, y, x, r, w), BF),
            pltpu.VMEM((x - 1, z, y, r, h), BF),
            pltpu.VMEM((y - 1, z, x, r, h), BF),
            pltpu.VMEM((y - 1, z, r, h), BF),
            pltpu.VMEM((x - 1, z, r, h), BF),
            pltpu.SemaphoreType.DMA((1,)),
            pltpu.SemaphoreType.DMA((1 + 2 * crossing,)),
            pltpu.SemaphoreType.DMA((1 + 2 * crossing,)),
        ]

    def bind(self, source, refs):
        self.source = source
        self.held, self.got0, self.got1x, self.got1y, self.got2y, self.got2x = refs[:6]
        self.local, self.send, self.receive = refs[6:]
        self.z, self.y, self.x, self.c = (lax.axis_index(name) for name in ALL)
        return self

    def index(self, z, y, x, lanes):
        return (z, y, x, EVERY, lanes)

    def slab(self, z, y, x, lanes):
        return self.held.at[self.index(z, y, x, lanes)]

    given = slab

    def remote(self, n, source, target, device):
        return pltpu.make_async_remote_copy(
            src_ref=source,
            dst_ref=target,
            send_sem=self.send.at[n],
            recv_sem=self.receive.at[n],
            device_id=device,
            device_id_type=pl.DeviceIdType.MESH,
        )

    def first(self):
        other = 1 - self.c
        return [
            pltpu.make_async_copy(self.source.at[:, :, :, self.c], self.held, self.local.at[0]),
            self.remote(0, self.source.at[:, :, :, other], self.got0, {"c": other}),
        ]

    def second(self):
        _, y_size, x_size, _ = self.sizes
        left, right = pl.ds(0, self.half), pl.ds(self.half, self.half)
        copies = []
        for k in range(1, x_size):
            there = rem(self.x + k, x_size)
            copies.append((self.given(EVERY, EVERY, there, left), self.got1x.at[k - 1], {"x": there}))
        for k in range(1, y_size):
            there = rem(self.y + k, y_size)
            copies.append((self.given(EVERY, there, EVERY, right), self.got1y.at[k - 1], {"y": there}))
        return [self.remote(1 + n, *copy) for n, copy in enumerate(copies)]

    def third(self):
        _, y_size, x_size, _ = self.sizes
        left, right = pl.ds(0, self.half), pl.ds(self.half, self.half)
        at = 1 + x_size + y_size - 2
        copies = []
        for k in range(1, y_size):
            there = rem(self.y + k, y_size)
            copies.append(
                (self.slab(EVERY, there, self.x, left), self.got2y.at[k - 1], {"y": there})
            )
        for k in range(1, x_size):
            there = rem(self.x + k, x_size)
            copies.append(
                (self.slab(EVERY, self.y, there, right), self.got2x.at[k - 1], {"x": there})
            )
        return [self.remote(at + n, *copy) for n, copy in enumerate(copies)]

    def begin(self):
        for copy in self.first():
            copy.start()

    def after_first(self):
        for copy in self.first():
            copy.wait()

        @pl.loop(0, self.sizes[0])
        def _(z):
            at = self.index(z, EVERY, EVERY, EVERY)
            self.held[at] = (self.held[at].astype(F32) + self.got0[z].astype(F32)).astype(BF)

        for copy in self.second():
            copy.start()

    def after_second(self):
        _, y_size, x_size, _ = self.sizes
        for copy in self.second():
            copy.wait()
        h = self.half

        @pl.loop(0, self.sizes[0])
        def _(z):
            for y in range(y_size):
                at = self.index(z, y, self.x, pl.ds(0, h))
                total = self.held[at].astype(F32)
                for k in range(x_size - 1):
                    total += self.got1x[k, z, y].astype(F32)
                self.held[at] = total.astype(BF)
            for x in range(x_size):
                at = self.index(z, self.y, x, pl.ds(h, h))
                total = self.held[at].astype(F32)
                for k in range(y_size - 1):
                    total += self.got1y[k, z, x].astype(F32)
                self.held[at] = total.astype(BF)

        for copy in self.third():
            copy.start()

    def after_third(self, out_ref):
        _, y_size, x_size, _ = self.sizes
        for copy in self.third():
            copy.wait()
        h = self.half

        @pl.loop(0, self.sizes[0])
        def _(z):
            total = self.held[self.index(z, self.y, self.x, pl.ds(0, h))].astype(F32)
            for k in range(y_size - 1):
                total += self.got2y[k, z].astype(F32)
            out_ref[z, :, :h] = total.astype(BF)
            total = self.held[self.index(z, self.y, self.x, pl.ds(h, h))].astype(F32)
            for k in range(x_size - 1):
                total += self.got2x[k, z].astype(F32)
            out_ref[z, :, h:] = total.astype(BF)


class Halved(Reducer):
    def scratch(self):
        z, y, x, _ = self.sizes
        r, w, h = self.rows, self.lanes, self.half
        crossing = x + y - 2
        return [
            pltpu.VMEM((z, y, x, r, w), BF),
            pltpu.VMEM((x - 1, z, y, r, h), BF),
            pltpu.VMEM((y - 1, z, x, r, h), BF),
            pltpu.VMEM((y - 1, z, r, h), BF),
            pltpu.VMEM((x - 1, z, r, h), BF),
            pltpu.SemaphoreType.DMA((1,)),
            pltpu.SemaphoreType.DMA((1 + 2 * crossing,)),
            pltpu.SemaphoreType.DMA((1 + 2 * crossing,)),
        ]

    def bind(self, source, refs):
        self.source = source
        self.held, self.got1x, self.got1y, self.got2y, self.got2x = refs[:5]
        self.local, self.send, self.receive = refs[5:]
        self.z, self.y, self.x, self.c = (lax.axis_index(name) for name in ALL)
        return self

    def given(self, z, y, x, lanes):
        return self.source.at[self.index(z, y, x, lanes)]

    def first(self):
        return [pltpu.make_async_copy(self.source, self.held, self.local.at[0])]

    def begin(self):
        for copy in self.first() + self.second():
            copy.start()

    def after_first(self):
        pass

    def after_second(self):
        for copy in self.first():
            copy.wait()
        super().after_second()


class Resident(Reducer):
    def scratch(self):
        z, y, x, c = self.sizes
        r, w, h = self.rows, self.lanes, self.half
        count = 1 + 2 * (x + y - 2) + z - 1
        return [
            pltpu.VMEM((z, y, x, c, r, w), BF),
            pltpu.VMEM((z, y, x, r, w), BF),
            pltpu.VMEM((x - 1, z, y, r, h), BF),
            pltpu.VMEM((y - 1, z, x, r, h), BF),
            pltpu.VMEM((y - 1, z, r, h), BF),
            pltpu.VMEM((x - 1, z, r, h), BF),
            pltpu.VMEM((z, r, w), BF),
            pltpu.VMEM((z - 1, r, w), BF),
            pltpu.SemaphoreType.DMA((count,)),
            pltpu.SemaphoreType.DMA((count,)),
        ]

    def bind(self, refs):
        self.held, self.got0, self.got1x, self.got1y, self.got2y, self.got2x = refs[:6]
        self.left, self.got3, self.send, self.receive = refs[6:]
        self.z, self.y, self.x, self.c = (lax.axis_index(name) for name in ALL)
        return self

    def index(self, z, y, x, lanes):
        return (z, y, x, self.c, EVERY, lanes)

    def first(self):
        other = 1 - self.c
        return [self.remote(0, self.held.at[:, :, :, other], self.got0, {"c": other})]

    def fourth(self):
        _, y_size, x_size, _ = self.sizes
        at = 1 + 2 * (x_size + y_size - 2)
        copies = []
        for k in range(1, PLANES):
            there = rem(self.z + k, PLANES)
            copies.append(
                self.remote(at + k - 1, self.left.at[there], self.got3.at[k - 1], {"z": there})
            )
        return copies

    def after_third_start(self):
        self.after_third(self.left)
        for copy in self.fourth():
            copy.start()

    def finish(self, out_ref):
        for copy in self.fourth():
            copy.wait()
        total = self.left[self.z].astype(F32)
        for k in range(PLANES - 1):
            total += self.got3[k].astype(F32)
        out_ref[...] = total


class SmallSum:
    def __init__(self, sizes, shape):
        self.shape = shape
        self.steps = list(zip(("c", "x", "y", "z"), (sizes[3], sizes[2], sizes[1], sizes[0])))

    def scratch(self):
        count = sum(n - 1 for _, n in self.steps)
        return (
            [pltpu.VMEM(self.shape, F32) for _ in range(4)]
            + [pltpu.VMEM((n - 1,) + self.shape, F32) for _, n in self.steps]
            + [pltpu.SemaphoreType.DMA((count,))] * 2
        )

    def bind(self, refs):
        self.held, self.got = refs[:4], refs[4:8]
        self.send, self.receive = refs[8:]
        return self

    def copies(self, step):
        axis, n = self.steps[step]
        at = sum(m - 1 for _, m in self.steps[:step])
        me = lax.axis_index(axis)
        return [
            pltpu.make_async_remote_copy(
                src_ref=self.held[step],
                dst_ref=self.got[step].at[k - 1],
                send_sem=self.send.at[at + k - 1],
                recv_sem=self.receive.at[at + k - 1],
                device_id={axis: rem(me + k, n)},
                device_id_type=pl.DeviceIdType.MESH,
            )
            for k in range(1, n)
        ]

    def start(self, step):
        for copy in self.copies(step):
            copy.start()

    def advance(self, step, out_ref=None):
        for copy in self.copies(step):
            copy.wait()
        total = self.held[step][...]
        for k in range(self.steps[step][1] - 1):
            total += self.got[step][k]
        if step < 3:
            self.held[step + 1][...] = total
            self.start(step + 1)
        else:
            out_ref[...] = total


def forward_pair(queries, keys, values, bias):
    masks = lane_masks()
    all_scores = []
    for mine, other, one in masks:
        if bias is None:
            all_scores.append(causal_mask(dot(keys, queries * mine, 1, 1)))
        else:
            all_scores.append(dot(keys * mine + bias * one, queries * mine + one, 1, 1))
    parts = []
    lse = []
    for h in range(2):
        mine, other, _ = masks[h]
        scores = all_scores[h]
        row_max = jnp.max(scores, axis=0, keepdims=True)
        probs = jnp.exp(scores - row_max).astype(BF)
        both = dot(values * mine + other, probs, 0, 0)
        halves = (both[:HD], both[HD:])
        total = halves[1 - h]
        parts.append(halves[h] / total)
        lse.append(row_max + jnp.log(total[0:1]))
    return jnp.concatenate(parts, axis=0).T.astype(BF), lse


def backward_pair(queries, grad, keys, values, bias, lse, delta):
    grad_k = None
    grad_v = None
    grad_q = []
    for h, (mine, other, one) in enumerate(lane_masks()):
        query_h = queries * mine
        grad_h = grad * mine
        if bias is None:
            scores = causal_mask(dot(keys, query_h, 1, 1))
        else:
            scores = dot(keys * mine + bias * one, query_h + one, 1, 1)
        probs = jnp.exp(scores - lse[h])
        grad_p = dot(values, grad_h, 1, 1)
        if delta is None:
            delta_h = jnp.sum(probs * grad_p, axis=0, keepdims=True)
        else:
            delta_h = delta[h]
        grad_s = (probs * (grad_p - delta_h)).astype(BF)
        term_v = dot(probs.astype(BF), grad_h, 1, 0)
        term_k = dot(grad_s, query_h, 1, 0)
        grad_v = term_v if grad_v is None else grad_v + term_v
        grad_k = term_k if grad_k is None else grad_k + term_k
        grad_q.append(dot(keys, grad_s, 0, 0)[h * HD : (h + 1) * HD])
    grad_kv = jnp.concatenate([grad_k, grad_v], axis=1).astype(BF)
    return grad_kv, jnp.concatenate(grad_q, axis=0).T.astype(BF)


def key_bias(keys, lens_ref):
    row = lax.broadcasted_iota(jnp.int32, (keys, 128), 0) + lax.axis_index("z") * keys
    return jnp.where(row < lens_ref[0:1, :], 0.0, MASKED).astype(BF)


def two_rows(ref):
    return [ref[0, h : h + 1, :] for h in range(2)]


def split_refs(refs, *counts):
    groups = []
    at = 0
    for count in counts:
        groups.append(refs[at : at + count])
        at += count
    return groups


def carried(courier, reducers, body):
    jobs = len(courier.jobs)
    sums = len(reducers)
    parts = [len(one.scratch()) for one in reducers]

    def kernel(ins, outs, scratch, refs):
        own_in, sources, summands, own_out, targets, results, own_scratch, sems, rest = split_refs(
            refs, ins, jobs, sums, outs, jobs, sums, scratch, 3, sum(parts)
        )
        step = pl.program_id(0)
        work = split_refs(rest, *parts)

        def bound():
            return [one.bind(value, refs) for one, value, refs in zip(reducers, summands, work)]

        @pl.when(step == 0)
        def _():
            courier.start(sources, targets, sems)
            for one in bound():
                one.begin()

        body(own_in, own_out, own_scratch)

        if sums:

            @pl.when(step == 1)
            def _():
                for one in bound():
                    one.after_first()

            @pl.when(step == 3)
            def _():
                for one in bound():
                    one.after_second()

        @pl.when(step == PAIRS - 1)
        def _():
            for one, result in zip(bound(), results):
                one.after_third(result)
            courier.wait(sources, targets, sems)

    return kernel


def call(courier, ident, body, args, in_specs, out_shape, out_specs, scratch, flops, summands=()):
    if summands:
        courier.in_plane = True
    reducers = [
        (Halved if value.ndim == 5 else Reducer)(courier.sizes, value.shape) for value in summands
    ]
    shapes = [(PLANES,) + value.shape[-2:] for value in summands]
    kernel = carried(courier, reducers, body)
    counts = (len(args), len(out_shape), len(scratch))
    outs = pl.pallas_call(
        lambda *refs: kernel(*counts, refs),
        grid=(PAIRS,),
        out_shape=out_shape
        + courier.out_shape()
        + [jax.ShapeDtypeStruct(shape, BF) for shape in shapes],
        in_specs=in_specs + courier.specs() + [pl.BlockSpec(memory_space=pl.ANY)] * len(shapes),
        out_specs=out_specs
        + courier.specs()
        + [pl.BlockSpec(shape, lambda p: (0, 0, 0)) for shape in shapes],
        scratch_shapes=scratch
        + courier.scratch()
        + [ref for one in reducers for ref in one.scratch()],
        compiler_params=courier.params(ident),
        cost_estimate=pl.CostEstimate(flops=flops, bytes_accessed=2**24, transcendentals=2**20),
    )(*args, *courier.values(), *summands)
    return outs[: len(out_shape)], outs[len(out_shape) :]


def reduce_all(sizes, ident, summands, scattered):
    courier = Courier(sizes, [("scatter", 0, value) for value in scattered])
    courier.in_plane = True
    courier.lines += list(range(1, PLANES))
    jobs = len(scattered)
    count = len(summands)
    reducers = [Reducer(sizes, value.shape) for value in summands]
    shapes = [value.shape[-2:] for value in summands]

    def kernel(*refs):
        sources, arrays, targets, results, sems, rest = split_refs(
            refs, jobs, count, jobs, count, 3, len(refs) - 2 * jobs - 2 * count - 3
        )
        courier.start(sources, targets, sems)
        bound = []
        last = []
        for n in range(count):
            refs_n = rest[13 * n : 13 * n + 13]
            bound.append(reducers[n].bind(arrays[n], refs_n[:9]))
            last.append(refs_n[9:])

        def leave(n):
            left, got, send, receive = last[n]
            copies = []
            for k in range(1, PLANES):
                copies.append(
                    pltpu.make_async_remote_copy(
                        src_ref=left.at[rem(lax.axis_index("z") + k, PLANES)],
                        dst_ref=got.at[k - 1],
                        send_sem=send.at[k - 1],
                        recv_sem=receive.at[k - 1],
                        device_id=courier.along(k),
                        device_id_type=pl.DeviceIdType.MESH,
                    )
                )
            return copies

        for one in bound:
            one.begin()
        for one in bound:
            one.after_first()
        for one in bound:
            one.after_second()
        for n, one in enumerate(bound):
            one.after_third(last[n][0])
            for copy in leave(n):
                copy.start()
        for n in range(count):
            for copy in leave(n):
                copy.wait()
            left, got = last[n][:2]
            total = left[lax.axis_index("z")].astype(F32)
            for k in range(PLANES - 1):
                total += got[k].astype(F32)
            results[n][...] = total
        courier.wait(sources, targets, sems)

    scratch = []
    for n in range(count):
        scratch += reducers[n].scratch() + [
            pltpu.VMEM((PLANES,) + shapes[n], BF),
            pltpu.VMEM((PLANES - 1,) + shapes[n], BF),
            pltpu.SemaphoreType.DMA((PLANES - 1,)),
            pltpu.SemaphoreType.DMA((PLANES - 1,)),
        ]
    outs = pl.pallas_call(
        kernel,
        out_shape=courier.out_shape() + [jax.ShapeDtypeStruct(shape, F32) for shape in shapes],
        in_specs=courier.specs() + [pl.BlockSpec(memory_space=pl.ANY)] * count,
        out_specs=courier.specs() + [pl.BlockSpec(memory_space=pltpu.VMEM)] * count,
        scratch_shapes=courier.scratch() + scratch,
        compiler_params=courier.params(ident),
    )(*courier.values(), *summands)
    return outs[:jobs], outs[jobs:]


def summand_of(sizes, arrays):
    devices = sizes[0] * sizes[1] * sizes[2] * sizes[3]
    parts = [a.reshape(devices, a.shape[0] // devices, a.shape[1]) for a in arrays]
    joined = parts[0] if len(parts) == 1 else jnp.concatenate(parts, axis=1)
    return joined.astype(BF).reshape(tuple(sizes) + joined.shape[1:])


def over_z(left, got):
    own = lax.dynamic_index_in_dim(left, lax.axis_index("z"), 0, keepdims=False)
    return own.astype(F32) + jnp.sum(got.astype(F32), axis=0)


def block_specs(tokens, keys):
    return dict(
        col=pl.BlockSpec((tokens, 128), lambda p: (0, p)),
        pair=pl.BlockSpec((keys, 256), lambda p: (0, p)),
        lens=pl.BlockSpec((8, 128), lambda p: (0, 0)),
        rows=pl.BlockSpec((keys, H * HD), lambda p: (0, 0)),
        weight=pl.BlockSpec((H * HD, 128), lambda p: (0, p)),
        stat=pl.BlockSpec((1, 2, tokens), lambda p: (p, 0, 0)),
    )


def rms(values, gain):
    r = lax.rsqrt(jnp.mean(values * values, axis=-1, keepdims=True) + EPSILON)
    return values * r * gain


def self_part(courier, ident, inputs, gains, weights):
    tokens, width = inputs.shape
    jobs = len(courier.jobs)

    def kernel(*refs):
        ins, sources, outs, targets, sems = split_refs(refs, 8, jobs - 1, 7, jobs, 3)
        x_ref, self_gain, cross_gain, wq_ref, wk_ref, wv_ref, wo_ref, wc_ref = ins
        q_ref, k_ref, v_ref, lse_ref, attn_ref, hidden_ref, query_ref = outs
        copies = courier.copies(list(sources) + [query_ref], targets, sems)
        courier.greet()
        for copy in copies[:-1]:
            copy.start()
        values = x_ref[...].astype(F32)
        normed = rms(values, self_gain[...]).astype(BF)
        q_ref[...] = dot(normed, wq_ref[...], 1, 0).astype(BF)
        k_ref[...] = dot(normed, wk_ref[...], 1, 0).astype(BF)
        v_ref[...] = dot(normed, wv_ref[...], 1, 0).astype(BF)

        for p in range(PAIRS):
            cols = pl.ds(p * 128, 128)
            out, lse = forward_pair(q_ref[:, cols], k_ref[:, cols], v_ref[:, cols], None)
            attn_ref[:, cols] = out
            for h in range(2):
                lse_ref[p, h : h + 1, :] = lse[h]

        hidden = values + dot(attn_ref[...], wo_ref[...], 1, 0)
        hidden_ref[...] = hidden
        query_ref[...] = dot(rms(hidden, cross_gain[...]).astype(BF), wc_ref[...], 1, 0).astype(BF)
        copies[-1].start()
        for copy in copies:
            copy.wait()

    rows = jax.ShapeDtypeStruct((tokens, width), BF)
    vmem = pl.BlockSpec(memory_space=pltpu.VMEM)
    stat = jax.ShapeDtypeStruct((PAIRS, 2, tokens), F32)
    wide = jax.ShapeDtypeStruct((tokens, width), F32)
    outs = pl.pallas_call(
        kernel,
        out_shape=[rows, rows, rows, stat, rows, wide, rows] + courier.out_shape(),
        in_specs=[vmem] * 8 + courier.specs()[1:],
        out_specs=[vmem] * 7 + courier.specs(),
        scratch_shapes=courier.scratch(),
        compiler_params=courier.params(ident),
    )(inputs, *gains, *weights, *courier.values()[:-1])
    return outs[:7], outs[7:]


def glu_parts(gate_vals):
    inner = 0.7978845608028654 * (gate_vals + 0.044715 * gate_vals * gate_vals * gate_vals)
    t = jnp.tanh(inner)
    gelu = 0.5 * gate_vals * (1.0 + t)
    slope = 0.5 * (1.0 + t) + 0.5 * gate_vals * (1.0 - t * t) * 0.7978845608028654 * (
        1.0 + 0.134145 * gate_vals * gate_vals
    )
    return gelu, slope


def spread(rows):
    both = [jnp.broadcast_to(rows[h : h + 1], (HD, rows.shape[1])) for h in range(2)]
    return jnp.concatenate(both, axis=0).T


def middle_kernel(*refs, sizes, packed):
    (
        part0,
        part1,
        part2,
        part3,
        lse0,
        lse1,
        lse2,
        lse3,
        h1_ref,
        wo_ref,
        gain_ref,
        cot_ref,
        gate_ref,
        up_ref,
        down_ref,
        out_ref,
        attn_ref,
        two_ref,
        da_ref,
        stats_ref,
        gnorm_ref,
        gwo_ref,
        *grad_refs,
        gdown_ref,
        raw_ref,
        h2_ref,
        n3_ref,
        total_ref,
        dn3_ref,
    ) = refs[: 29 + (not packed)]
    step = pl.program_id(0)
    last = pl.num_programs(0) - 1
    devices = sizes[0] * sizes[1] * sizes[2] * sizes[3]
    if packed:
        wide_ref, wide_got, tall_ref, tall_got, send, receive = refs[29:]
        core = lax.axis_index("c")

    def exchange(n):
        slot = rem(n, 2)
        return [
            pltpu.make_async_remote_copy(
                src_ref=source,
                dst_ref=target,
                send_sem=send.at[n, at],
                recv_sem=receive.at[n, at],
                device_id={"c": 1 - core},
                device_id_type=pl.DeviceIdType.MESH,
            )
            for at, (source, target) in enumerate(
                (
                    (wide_ref.at[slot, :, :, :, 1 - core], wide_got.at[n]),
                    (tall_ref.at[slot, :, :, 1 - core], tall_got.at[n]),
                )
            )
        ]
    parts = (part0, part1, part2, part3)
    lses = (lse0, lse1, lse2, lse3)

    @pl.when(step == 0)
    def _():
        for p in range(PAIRS):
            cols = pl.ds(p * 128, 128)
            values = [ref[p] for ref in lses]
            top = functools.reduce(jnp.maximum, values)
            scales = [jnp.exp(v - top) for v in values]
            total = functools.reduce(jnp.add, scales)
            stats_ref[0, p] = top + jnp.log(total)
            raw = None
            for ref, scale in zip(parts, scales):
                term = spread(scale / total) * ref[:, cols].astype(F32)
                raw = term if raw is None else raw + term
            raw_ref[:, cols] = raw
            attn_ref[:, cols] = raw.astype(BF)
        hidden = h1_ref[...] + dot(attn_ref[...], wo_ref[...], 1, 0)
        h2_ref[...] = hidden
        n3_ref[...] = rms(hidden, gain_ref[...]).astype(BF)
        total_ref[...] = hidden
        dn3_ref[...] = jnp.zeros_like(dn3_ref)
        if packed:
            barrier = pltpu.get_barrier_semaphore()
            pl.semaphore_signal(
                barrier,
                inc=1,
                device_id={"c": 1 - core},
                device_id_type=pl.DeviceIdType.MESH,
            )
            pl.semaphore_wait(barrier, 1)

    def one_chunk():
        normed = n3_ref[...]
        branch = cot_ref[...]
        gate_vals = dot(normed, gate_ref[...], 1, 0)
        up_vals = dot(normed, up_ref[...], 1, 0)
        grad_inner = dot(branch, down_ref[...], 1, 1)
        gelu, slope = glu_parts(gate_vals)
        inner = (gelu * up_vals).astype(BF)
        grad_gate = (grad_inner * up_vals * slope).astype(BF)
        grad_up = (grad_inner * gelu).astype(BF)
        total_ref[...] += dot(inner, down_ref[...], 1, 0)
        dn3_ref[...] += dot(grad_gate, gate_ref[...], 1, 1) + dot(grad_up, up_ref[...], 1, 1)
        terms = [dot(normed, grad_gate, 0, 0), dot(normed, grad_up, 0, 0)]
        if packed:
            shape = (devices, terms[0].shape[0] // devices, terms[0].shape[1])
            both = jnp.concatenate([t.reshape(shape) for t in terms], axis=1).astype(BF)
            slot = rem(step, 2)
            wide_ref[slot] = both.reshape(wide_ref.shape[1:])
            tall_ref[slot] = dot(inner, branch, 0, 0).astype(BF).reshape(tall_ref.shape[1:])
            for copy in exchange(step):
                copy.start()
        else:
            for ref, term in zip(grad_refs, terms):
                ref[...] = term
            gdown_ref[...] = dot(inner, branch, 0, 0).astype(BF).reshape(gdown_ref.shape)

    if packed:

        @pl.when(step < last)
        def _():
            one_chunk()

    else:
        one_chunk()

    @pl.when(step == last)
    def _():
        out_ref[...] = total_ref[...].astype(BF)
        hidden = h2_ref[...]
        grad = dn3_ref[...]
        r = lax.rsqrt(jnp.mean(hidden * hidden, axis=-1, keepdims=True) + EPSILON)
        u = gain_ref[...] * grad
        back = r * u - hidden * (r * r * r) * jnp.mean(u * hidden, axis=-1, keepdims=True)
        gnorm_ref[...] = jnp.sum(grad * hidden * r, axis=0, keepdims=True)
        two = cot_ref[...].astype(F32) + back
        two_ref[...] = two
        low = two.astype(BF)
        da_ref[...] = dot(low, wo_ref[...], 1, 1).astype(BF)
        gwo_ref[...] = dot(attn_ref[...], low, 0, 0).astype(BF)
        for p in range(PAIRS):
            cols = pl.ds(p * 128, 128)
            product = (da_ref[:, cols].astype(F32) * raw_ref[:, cols]).T
            for h in range(2):
                stats_ref[1, p, h : h + 1] = jnp.sum(
                    product[h * HD : (h + 1) * HD], axis=0, keepdims=True
                )

    if packed:

        @pl.when(step > 0)
        def _():
            before = step - 1
            slot = rem(before, 2)
            for copy in exchange(before):
                copy.wait()
            mine = wide_ref[slot, :, :, :, core].astype(F32)
            grad_refs[0][...] = (mine + wide_got[before].astype(F32)).astype(BF)
            mine = tall_ref[slot, :, :, core].astype(F32)
            gdown_ref[0] = (mine + tall_got[before].astype(F32)).astype(BF)


def middle(sizes, parts, lses, hidden, out_weight, gain, cotangent, gate, up, down):
    tokens, width = hidden.shape
    inner = gate.shape[1]
    chunk = 512
    count = inner // chunk
    devices = sizes[0] * sizes[1] * sizes[2] * sizes[3]
    share = width // devices
    down_share = inner // devices
    packed = share % 8 == 0 and chunk * PLANES == inner
    first = lambda p: jnp.minimum(p, count - 1)
    fixed = lambda *shape: pl.BlockSpec(shape, lambda p: (0,) * len(shape))
    whole = fixed(tokens, width)
    square = fixed(width, width)
    stat = fixed(PAIRS, 2, tokens)
    column = pl.BlockSpec((width, chunk), lambda p: (0, first(p)))
    scratch = [
        pltpu.VMEM((tokens, width), F32),
        pltpu.VMEM((tokens, width), F32),
        pltpu.VMEM((tokens, width), BF),
        pltpu.VMEM((tokens, width), F32),
        pltpu.VMEM((tokens, width), F32),
    ]
    params = dict(vmem_limit_bytes=VMEM)
    if packed:
        z, y, x, c = sizes
        wide_shape = (z, y, x, 2 * share)
        tall_shape = (y, x, down_share, width)
        grad_shapes = [
            jax.ShapeDtypeStruct(wide_shape + (inner,), BF),
            jax.ShapeDtypeStruct((z,) + tall_shape, BF),
        ]
        before = lambda p: jnp.maximum(p - 1, 0)
        grad_specs = [
            pl.BlockSpec(wide_shape + (chunk,), lambda p: (0, 0, 0, 0, before(p))),
            pl.BlockSpec((1,) + tall_shape, lambda p: (before(p), 0, 0, 0, 0)),
        ]
        scratch += [
            pltpu.VMEM((2, z, y, x, c, 2 * share, chunk), BF),
            pltpu.VMEM((count,) + wide_shape + (chunk,), BF),
            pltpu.VMEM((2, y, x, c, down_share, width), BF),
            pltpu.VMEM((count,) + tall_shape, BF),
            pltpu.SemaphoreType.DMA((count, 2)),
            pltpu.SemaphoreType.DMA((count, 2)),
        ]
        params.update(collective_id=12, has_side_effects=True)
    else:
        grad_shapes = [jax.ShapeDtypeStruct((width, inner), F32)] * 2
        grad_shapes.append(jax.ShapeDtypeStruct((devices, down_share, width), BF))
        grad_specs = [column] * 2
        grad_specs.append(
            pl.BlockSpec((chunk // down_share, down_share, width), lambda p: (p, 0, 0))
        )
    rows = jax.ShapeDtypeStruct((tokens, width), BF)
    wide = jax.ShapeDtypeStruct((tokens, width), F32)
    return pl.pallas_call(
        functools.partial(middle_kernel, sizes=sizes, packed=packed),
        grid=(count + packed,),
        out_shape=[
            rows,
            rows,
            wide,
            rows,
            jax.ShapeDtypeStruct((2, PAIRS, 2, tokens), F32),
            jax.ShapeDtypeStruct((1, width), F32),
            jax.ShapeDtypeStruct((width, width), BF),
        ]
        + grad_shapes,
        in_specs=[whole] * 4
        + [stat] * 4
        + [whole, square, fixed(1, width), whole]
        + [column, column, pl.BlockSpec((chunk, width), lambda p: (first(p), 0))],
        out_specs=[whole] * 4
        + [fixed(2, PAIRS, 2, tokens), fixed(1, width), square]
        + grad_specs,
        scratch_shapes=scratch,
        compiler_params=pltpu.CompilerParams(**params),
    )(*parts, *lses, hidden, out_weight, gain, cotangent, gate, up, down)


def cross_forward(courier, ident, queries, rows, lens, key_weight, value_weight):
    tokens, keys = queries.shape[0], rows.shape[0]
    spec = block_specs(tokens, keys)

    def body(ins, outs, _):
        q_ref, rows_ref, lens_ref, wk_ref, wv_ref = ins
        o_ref, lse_ref, kv_ref = outs
        weights = jnp.concatenate([wk_ref[...], wv_ref[...]], axis=1)
        kv_ref[...] = dot(rows_ref[...], weights, 1, 0).astype(BF)
        bias = key_bias(keys, lens_ref)
        out, lse = forward_pair(q_ref[...], kv_ref[:, :128], kv_ref[:, 128:], bias)
        o_ref[...] = out
        for h in range(2):
            lse_ref[0, h : h + 1, :] = lse[h]

    return call(
        courier,
        ident,
        body,
        [queries, rows, lens, key_weight, value_weight],
        [spec["col"], spec["rows"], spec["lens"], spec["weight"], spec["weight"]],
        [
            jax.ShapeDtypeStruct((tokens, H * HD), BF),
            jax.ShapeDtypeStruct((PAIRS, 2, tokens), F32),
            jax.ShapeDtypeStruct((keys, 2 * H * HD), BF),
        ],
        [spec["col"], spec["stat"], spec["pair"]],
        [],
        2**34,
    )


def cross_backward(
    courier, ident, queries, grad, keyvals, lens, lse, delta, key_weight, value_weight, summands=()
):
    tokens, keys = queries.shape[0], keyvals.shape[0]
    width = H * HD
    spec = block_specs(tokens, keys)

    def body(ins, outs, scratch):
        q_ref, da_ref, kv_ref, lens_ref, lse_ref, delta_ref, wk_ref, wv_ref = ins
        dkv_ref, dq_ref, dm_ref = outs
        (total_ref,) = scratch
        step = pl.program_id(0)

        @pl.when(step == 0)
        def _():
            total_ref[...] = jnp.zeros_like(total_ref)

        weights = jnp.concatenate([wk_ref[...], wv_ref[...]], axis=1)
        grad_kv, grad_q = backward_pair(
            q_ref[...],
            da_ref[...],
            kv_ref[:, :128],
            kv_ref[:, 128:],
            key_bias(keys, lens_ref),
            two_rows(lse_ref),
            two_rows(delta_ref),
        )
        dkv_ref[...] = grad_kv
        dq_ref[...] = grad_q
        total_ref[...] += dot(grad_kv, weights, 1, 1)

        @pl.when(step == PAIRS - 1)
        def _():
            dm_ref[...] = total_ref[...].astype(BF)

    return call(
        courier,
        ident,
        body,
        [queries, grad, keyvals, lens, lse, delta, key_weight, value_weight],
        [spec[n] for n in ("col", "col", "pair", "lens", "stat", "stat", "weight", "weight")],
        [
            jax.ShapeDtypeStruct((keys, 2 * width), BF),
            jax.ShapeDtypeStruct((tokens, width), BF),
            jax.ShapeDtypeStruct((keys, width), BF),
        ],
        [spec["pair"], spec["col"], spec["rows"]],
        [pltpu.VMEM((keys, width), F32)],
        2**35,
        summands,
    )


def weight_terms(courier, ident, rows, grads):
    keys, width = rows[0].shape
    spec = block_specs(keys, keys)
    count = len(rows)

    def body(ins, outs, _):
        total = None
        for rows_ref, grad_ref in zip(ins[:count], ins[count:]):
            term = dot(rows_ref[...], grad_ref[...], 0, 0)
            total = term if total is None else total + term
        outs[0][...] = total[:, :128]
        outs[1][...] = total[:, 128:]

    return call(
        courier,
        ident,
        body,
        list(rows) + list(grads),
        [spec["rows"]] * count + [spec["pair"]] * count,
        [jax.ShapeDtypeStruct((width, width), F32)] * 2,
        [spec["weight"]] * 2,
        [],
        2**34,
    )


def self_backward(courier, ident, queries, grad, keys, values, lse, summand):
    tokens, width = queries.shape
    spec = block_specs(tokens, tokens)

    def body(ins, outs, _):
        q_ref, da_ref, k_ref, v_ref, lse_ref = ins
        dq_ref, dk_ref, dv_ref = outs
        grad_kv, dq_ref[...] = backward_pair(
            q_ref[...], da_ref[...], k_ref[...], v_ref[...], None, two_rows(lse_ref), None
        )
        dk_ref[...] = grad_kv[:, :128]
        dv_ref[...] = grad_kv[:, 128:]

    return call(
        courier,
        ident,
        body,
        [queries, grad, keys, values, lse],
        [spec["col"]] * 4 + [spec["stat"]],
        [jax.ShapeDtypeStruct((tokens, width), BF)] * 3,
        [spec["col"]] * 3,
        [],
        2**33,
        [summand],
    )


def rms_back(values, gain, grad):
    r = lax.rsqrt(jnp.mean(values * values, axis=-1, keepdims=True) + EPSILON)
    u = gain * grad
    back = r * u - values * (r * r * r) * jnp.mean(u * values, axis=-1, keepdims=True)
    return back, jnp.sum(grad * values * r, axis=0, keepdims=True)


def ending(sizes, ident, rows, grads, grad_q, grad_rows, left, two, held, lse, small_in):
    courier = Courier(
        sizes,
        [("line", PLANES - 1, grad_q[-1]), ("return", 0, grad_rows)]
        + [("scatter", 0, value) for value in left],
    )
    courier.lines = list(range(1, PLANES))
    jobs = len(courier.jobs)
    devices = sizes[0] * sizes[1] * sizes[2] * sizes[3]
    keys, width = rows[0].shape
    tokens = two.shape[0]
    share = width // devices
    chunk = 512
    cuts = keys // chunk
    groups = [Resident(sizes, (2 * share, width)) for _ in range(2)]
    groups += [Resident(sizes, (2 * share, 256)) for _ in range(6)]
    small = SmallSum(sizes, (8, width))
    early = [two] + list(held) + list(grad_q[:-1])
    far = list(rows) + list(grads) + early
    counts = (len(far), len(small_in) + 1, jobs, 6, jobs - 1, 4, len(early) - 1, 8, 3, 80, 10)

    def pack(ref, first, second, cols=EVERY):
        lanes = first.shape[1]
        parts = [v.astype(F32).reshape(devices, share, lanes) for v in (first, second)]
        both = jnp.concatenate(parts, axis=1).astype(BF)
        ref[:, :, :, :, :, cols] = both.reshape(tuple(sizes) + both.shape[1:])

    def kernel(*refs):
        far_refs, near, sources, outs, targets, stage, loaded, work, sems, group_refs, rest = (
            split_refs(refs, *counts)
        )
        self_gain, cross_gain, ffn_term, lse_ref = near
        grad_in, *sums, norm_sums = outs
        row_buf, grad_buf, total, load_sems = stage
        dq_got, da_ref, dq1, dk1, dv1, normed_ref, *_ = work
        chunk_sems, early_sems = load_sems, work[6]
        copies = courier.copies(sources, [dq_got] + list(targets), sems)
        courier.greet()
        for copy in copies:
            copy.start()

        def chunk_loads(r, i):
            slot = rem(i, 2)
            where = pl.ds(pl.multiple_of(rem(i, cuts) * chunk, chunk), chunk)
            return [
                pltpu.make_async_copy(
                    far_refs[r].at[where], row_buf.at[slot], chunk_sems.at[slot, 0]
                ),
                pltpu.make_async_copy(
                    far_refs[PLANES + r].at[where], grad_buf.at[slot], chunk_sems.at[slot, 1]
                ),
            ]

        def start_chunk(i):
            for r in range(PLANES):

                @pl.when(lax.div(jnp.int32(i), cuts) == r)
                def _(r=r):
                    for copy in chunk_loads(r, i):
                        copy.start()

        total[...] = jnp.zeros_like(total)
        early_refs = far_refs[2 * PLANES :]
        early_loads = [
            pltpu.make_async_copy(source, target, early_sems.at[n])
            for n, (source, target) in enumerate(zip(early_refs, [grad_in] + list(loaded)))
        ]
        start_chunk(0)
        for copy in early_loads:
            copy.start()

        @pl.loop(0, PLANES * cuts)
        def _(i):
            @pl.when(i + 1 < PLANES * cuts)
            def _():
                start_chunk(i + 1)

            for copy in chunk_loads(0, i):
                copy.wait()
            slot = rem(i, 2)
            total[...] += dot(row_buf[slot], grad_buf[slot], 0, 0)

        bound = [
            one.bind(group_refs[10 * n : 10 * n + 10]) for n, one in enumerate(groups)
        ]
        bits = small.bind(rest)

        @pl.loop(0, PAIRS)
        def _(p):
            at = pl.multiple_of(p * 256, 256)
            pack(
                bound[0].held,
                total[:, pl.ds(at, 128)],
                total[:, pl.ds(at + 128, 128)],
                pl.ds(pl.multiple_of(p * 128, 128), 128),
            )

        bound[0].begin()
        for copy in early_loads:
            copy.wait()
        copies[1].wait()
        x_ref, h1_ref, gco_ref, q_ref, k_ref, v_ref, attn_ref = loaded[:7]
        wq_ref, wk_ref, wv_ref, wo_ref, wc_ref, *dq_refs = loaded[7:]
        grad = dq_got[...].astype(F32)
        for ref in dq_refs:
            grad += ref[...].astype(F32)
        dq_got[...] = grad.astype(BF)
        hidden = h1_ref[...]
        back, cross_norm = rms_back(hidden, cross_gain[...], dot(dq_got[...], wc_ref[...], 1, 1))
        grad_in[...] += back
        dv1[...] = rms(hidden, cross_gain[...]).astype(BF)
        bound[0].after_first()

        @pl.loop(0, 3)
        def _(i):
            cols = pl.ds(pl.multiple_of(i * 256, 256), 256)
            pack(bound[1].held, dot(dv1[...], dq_got[:, cols], 0, 0), gco_ref[:, cols], cols)

        bound[1].begin()
        low_ref = dq_got
        low_ref[...] = grad_in[...].astype(BF)
        da_ref[...] = dot(low_ref[...], wo_ref[...], 1, 1).astype(BF)
        values = x_ref[...].astype(F32)
        normed_ref[...] = rms(values, self_gain[...]).astype(BF)

        for third in range(3):

            @pl.loop(2 * third, 2 * third + 2)
            def _(p):
                cols = pl.ds(pl.multiple_of(p * 128, 128), 128)
                grad_kv, grad_q_p = backward_pair(
                    q_ref[:, cols],
                    da_ref[:, cols],
                    k_ref[:, cols],
                    v_ref[:, cols],
                    None,
                    [lse_ref[p, h : h + 1, :] for h in range(2)],
                    None,
                )
                dq1[:, cols] = grad_q_p
                dk1[:, cols] = grad_kv[:, :128]
                dv1[:, cols] = grad_kv[:, 128:]

            cols = pl.ds(third * 256, 256)
            near_sum, far_sum = bound[2 + 2 * third], bound[3 + 2 * third]
            normed = normed_ref[...]
            pack(near_sum.held, dot(normed, dq1[:, cols], 0, 0), dot(normed, dk1[:, cols], 0, 0))
            near_sum.begin()
            pack(
                far_sum.held,
                dot(normed, dv1[:, cols], 0, 0),
                dot(attn_ref[...], low_ref[:, cols], 0, 0),
            )
            far_sum.begin()
            if third == 0:
                bound[0].after_second()
                bound[1].after_first()
            if third == 1:
                bound[0].after_third_start()
                bound[1].after_second()
                bound[2].after_first()
                bound[3].after_first()
            if third == 2:
                bound[1].after_third_start()
                bound[2].after_second()
                bound[3].after_second()
                bound[4].after_first()
                bound[5].after_first()
        grad_normed = (
            dot(dq1[...], wq_ref[...], 1, 1)
            + dot(dk1[...], wk_ref[...], 1, 1)
            + dot(dv1[...], wv_ref[...], 1, 1)
        )
        back, self_norm = rms_back(values, self_gain[...], grad_normed)
        grad_in[...] += back
        bits.held[0][...] = jnp.concatenate(
            [self_norm, cross_norm, ffn_term[...], jnp.zeros((5, width), F32)], axis=0
        )
        bits.start(0)
        bound[2].after_third_start()
        bound[3].after_third_start()
        bound[4].after_second()
        bound[5].after_second()
        bound[6].after_first()
        bound[7].after_first()
        bits.advance(0)
        bound[4].after_third_start()
        bound[5].after_third_start()
        bound[6].after_second()
        bound[7].after_second()
        bits.advance(1)
        bound[6].after_third_start()
        bound[7].after_third_start()
        bits.advance(2)
        bound[0].finish(sums[0])
        bound[1].finish(sums[1])
        for n in range(2, 8):
            third, kind = divmod(n - 2, 2)
            bound[n].finish(sums[2 + kind].at[:, pl.ds(third * 256, 256)])
        bits.advance(3, norm_sums)
        for n, copy in enumerate(copies):
            if n != 1:
                copy.wait()

    any_spec = pl.BlockSpec(memory_space=pl.ANY)
    vmem = pl.BlockSpec(memory_space=pltpu.VMEM)
    row = pltpu.VMEM((tokens, width), BF)
    scratch = [
        pltpu.VMEM((2, chunk, width), BF),
        pltpu.VMEM((2, chunk, 2 * width), BF),
        pltpu.VMEM((width, 2 * width), F32),
        pltpu.SemaphoreType.DMA((2, 2)),
    ]
    scratch += [pltpu.VMEM(v.shape, v.dtype) for v in early[1:]]
    scratch += [row] * 6 + [pltpu.SemaphoreType.DMA((len(early),))]
    scratch += [pltpu.SemaphoreType.DMA((1,))] + courier.scratch()
    for one in groups:
        scratch += one.scratch()
    scratch += small.scratch()
    outs = pl.pallas_call(
        kernel,
        out_shape=[jax.ShapeDtypeStruct((tokens, width), F32)]
        + [jax.ShapeDtypeStruct((2 * share, width), F32)] * 4
        + [jax.ShapeDtypeStruct((8, width), F32)]
        + courier.out_shape()[1:],
        in_specs=[any_spec] * len(far) + [vmem] * (len(small_in) + 1) + courier.specs(),
        out_specs=[vmem] * 6 + courier.specs()[1:],
        scratch_shapes=scratch,
        compiler_params=pltpu.CompilerParams(
            vmem_limit_bytes=62 * 2**20, collective_id=ident, has_side_effects=True
        ),
    )(*far, *small_in, lse, *courier.values())
    return outs[0], outs[1:5], outs[5], outs[6:]


def place_kernel(*refs):
    *blocks, out_ref, held, arrive, leave = refs
    z = lax.axis_index("z")
    size = held.shape[1]
    inward = []
    outward = []
    for r, block in enumerate(blocks):
        at = rem(z + r, PLANES) * size
        inward.append(pltpu.make_async_copy(block, held.at[r], arrive.at[r]))
        outward.append(
            pltpu.make_async_copy(held.at[r], out_ref.at[pl.ds(at, size)], leave.at[r])
        )
        inward[r].start()
    for r in range(len(blocks)):
        inward[r].wait()
        outward[r].start()
    for copy in outward:
        copy.wait()


def place(blocks):
    shape = blocks[0].shape
    count = len(blocks)
    hbm = pl.BlockSpec(memory_space=pl.ANY)
    return pl.pallas_call(
        place_kernel,
        out_shape=jax.ShapeDtypeStruct((count * shape[0],) + shape[1:], blocks[0].dtype),
        in_specs=[hbm] * count,
        out_specs=hbm,
        scratch_shapes=[
            pltpu.VMEM((count,) + shape, blocks[0].dtype),
            pltpu.SemaphoreType.DMA((count,)),
            pltpu.SemaphoreType.DMA((count,)),
        ],
        compiler_params=pltpu.CompilerParams(vmem_limit_bytes=VMEM),
    )(*blocks)


def norm_apply(values, gain):
    return values * lax.rsqrt(jnp.mean(values * values, axis=-1, keepdims=True) + EPSILON) * gain


def norm_back(values, gain, grad):
    r = lax.rsqrt(jnp.mean(values * values, axis=-1, keepdims=True) + EPSILON)
    u = gain * grad
    dv = r * u - values * (r * r * r) * jnp.mean(u * values, axis=-1, keepdims=True)
    return dv, jnp.sum(grad * values * r, axis=0)


def matmul(left, right):
    return dot(left, right, 1, 0)


def matmul_t(left, right):
    return dot(left, right, 1, 1)


def tmatmul(left, right):
    return dot(left, right, 0, 0)


def on_device(
    sizes,
    decoder_in,
    memory,
    memory_lengths,
    cotangent,
    norm_self,
    self_query,
    self_key,
    self_value,
    self_out,
    norm_cross,
    cross_query,
    cross_key,
    cross_value,
    cross_out,
    norm_ffn,
    ffn_gate,
    ffn_up,
    ffn_down,
):
    devices, positions, width = memory.shape
    plane_size = sizes[1] * sizes[2] * sizes[3]
    z = lax.axis_index("z")

    def flat(blocks):
        return blocks.reshape(plane_size * positions, width)

    def cut(rows):
        return rows.reshape(plane_size, positions, width)

    lens = {0: jnp.broadcast_to(memory_lengths[None, :], (8, 128))}
    jobs = [("fetch", 1, memory)]
    jobs += [("line", -r, lens[0]) for r in range(1, PLANES)]
    jobs += [("line", -1, jax.ShapeDtypeStruct(decoder_in.shape[1:], BF))]
    (query_one, key_one, value_one, lse_one, attn_one, hidden_one, query_two), moved = self_part(
        Courier(sizes, jobs),
        0,
        decoder_in[0],
        (norm_self[None], norm_cross[None]),
        (self_query, self_key, self_value, self_out, cross_query),
    )
    fetched, lens[1], lens[2], lens[3], query_near = moved
    queries, rows, keyvals, partial, stats_out = {0: query_two, 1: query_near}, {}, {}, {}, {}
    order = (1, 2, 3, 0)
    for at, r in enumerate(order):
        rows[r] = flat(fetched)
        jobs = []
        if at + 1 < PLANES:
            jobs.append(("fetch", order[at + 1], memory))
        if at + 2 < PLANES:
            jobs.append(("line", -order[at + 1], query_two))
        if at >= 1:
            before = order[at - 1]
            jobs.append(("line", before, partial[before]))
            jobs.append(("line", before, stats_out[before]))
        (partial[r], stats_out[r], keyvals[r]), moved = cross_forward(
            Courier(sizes, jobs), 1 + at, queries[r], rows[r], lens[r], cross_key, cross_value
        )
        moved = list(moved)
        if at + 1 < PLANES:
            fetched = moved.pop(0)
        if at + 2 < PLANES:
            queries[order[at + 1]] = moved.pop(0)
        if at >= 1:
            partial[before], stats_out[before] = moved
    (
        output,
        attn_two,
        grad_two,
        grad_attn_two,
        stats,
        grad_norm_ffn,
        grad_cross_out,
        *grads_in,
        grad_down,
    ) = middle(
        sizes,
        [partial[r] for r in range(PLANES)],
        [stats_out[r] for r in range(PLANES)],
        hidden_one,
        cross_out,
        norm_ffn[None],
        cotangent[0],
        ffn_gate,
        ffn_up,
        ffn_down,
    )
    decoder_out = output[None]
    if len(grads_in) == 2:
        summands = {
            0: [summand_of(sizes, grads_in)],
            1: [grad_down.reshape(tuple(sizes) + grad_down.shape[1:])],
        }
    else:
        summands = {0: [grads_in[0], grad_down]}
    left, got = {}, {}

    grads = {0: grad_attn_two}
    both = {0: stats}
    grad_kv, grad_q, grad_rows, returned = {}, {}, {}, {}
    for r in range(PLANES):
        jobs = []
        if r + 1 < PLANES:
            jobs.append(("line", -(r + 1), grad_attn_two))
            jobs.append(("line", -(r + 1), stats))
        if r >= 1:
            jobs.append(("return", 0, cut(grad_rows[r - 1])))
        if r >= 2:
            jobs.append(("line", r - 1, grad_q[r - 1]))
        (grad_kv[r], grad_q[r], grad_rows[r]), moved = cross_backward(
            Courier(sizes, jobs),
            5 + r,
            queries[r],
            grads[r],
            keyvals[r],
            lens[r],
            both[r][0],
            both[r][1],
            cross_key,
            cross_value,
            summands.get(r, []),
        )
        moved = list(moved)
        if r in summands:
            for value in moved[len(moved) - len(summands[r]) :]:
                left[len(left)] = value
        if r + 1 < PLANES:
            grads[r + 1], both[r + 1] = moved.pop(0), moved.pop(0)
        if r >= 1:
            returned[r - 1] = moved.pop(0)
        if r >= 2:
            grad_q[r - 1] = moved.pop(0)
    last = PLANES - 1
    part = width // devices
    if part % 8 == 0:
        decoder_in_grad, sums, norm_sums, moved = ending(
            sizes,
            9,
            [rows[r] for r in range(PLANES)],
            [grad_kv[r] for r in range(PLANES)],
            [grad_q[r] for r in range(PLANES)],
            cut(grad_rows[last]),
            [left[0], left[1]],
            grad_two,
            (decoder_in[0], hidden_one, grad_cross_out, query_one, key_one, value_one, attn_one)
            + (self_query, self_key, self_value, self_out, cross_query),
            lse_one,
            (norm_self[None], norm_cross[None], grad_norm_ffn),
        )
        returned[last], got[0], got[1] = moved
        memory_grad = place([returned[r] for r in range(PLANES)])
        gate_up = over_z(left[0], got[0])
        here = lax.axis_index(ALL) * part
        norm_self_sum, norm_cross_sum, norm_ffn_sum = (
            lax.dynamic_slice_in_dim(norm_sums[n], here, part) for n in range(3)
        )
        return (
            decoder_out,
            decoder_in_grad[None],
            memory_grad,
            norm_self_sum,
            sums[2][:part],
            sums[2][part:],
            sums[3][:part],
            sums[3][part:],
            norm_cross_sum,
            sums[1][:part],
            sums[0][:part],
            sums[0][part:],
            sums[1][part:],
            norm_ffn_sum,
            gate_up[:part],
            gate_up[part:],
            over_z(left[1], got[1]),
        )

    jobs = [
        ("line", last, grad_q[last]),
        ("return", 0, cut(grad_rows[last])),
        ("scatter", 0, left[0]),
        ("scatter", 0, left[1]),
    ]
    (grad_cross_key, grad_cross_value), (grad_q[last], returned[last], got[0], got[1]) = weight_terms(
        Courier(sizes, jobs),
        9,
        [rows[r] for r in range(PLANES)],
        [grad_kv[r] for r in range(PLANES)],
    )
    memory_grad = place([returned[r] for r in range(PLANES)])

    inputs = decoder_in[0].astype(F32)
    normed_one = norm_apply(inputs, norm_self).astype(BF)
    normed_two = norm_apply(hidden_one, norm_cross).astype(BF)
    grad_q_two = sum(grad_q[r].astype(F32) for r in range(PLANES)).astype(BF)
    grad_cross_query = tmatmul(normed_two, grad_q_two)
    grad_normed_two = matmul_t(grad_q_two, cross_query)
    back_one, grad_norm_cross = norm_back(hidden_one, norm_cross, grad_normed_two)
    grad_one = grad_two + back_one
    branch_one = grad_one.astype(BF)
    grad_self_out = tmatmul(attn_one, branch_one)
    grad_attn_one = matmul_t(branch_one, self_out).astype(BF)
    (grad_q_one, grad_k_one, grad_v_one), (cross_left,) = self_backward(
        Courier(sizes, []),
        10,
        query_one,
        grad_attn_one,
        key_one,
        value_one,
        lse_one,
        summand_of(sizes, (grad_cross_key, grad_cross_value)),
    )
    grad_normed_one = (
        matmul_t(grad_q_one, self_query)
        + matmul_t(grad_k_one, self_key)
        + matmul_t(grad_v_one, self_value)
    )
    back_in, grad_norm_self = norm_back(inputs, norm_self, grad_normed_one)
    decoder_in_grad = (grad_one + back_in)[None]
    share_of_norms = width // devices
    norms = jnp.stack(
        [g.reshape(devices, share_of_norms) for g in (grad_norm_self, grad_norm_cross, grad_norm_ffn[0])],
        axis=1,
    ).reshape(devices, 1, 3 * share_of_norms)
    norms = jnp.pad(norms, ((0, 0), (0, 15), (0, 256 - 3 * share_of_norms)))
    (cross_got,), sums = reduce_all(
        sizes,
        11,
        [
            norms.astype(BF).reshape(tuple(sizes) + norms.shape[1:]),
            summand_of(sizes, (grad_cross_query, grad_cross_out.astype(F32))),
            summand_of(sizes, (tmatmul(normed_one, grad_q_one), tmatmul(normed_one, grad_k_one))),
            summand_of(sizes, (tmatmul(normed_one, grad_v_one), grad_self_out)),
        ],
        [cross_left],
    )
    norm_sums = sums[0][0, : 3 * share_of_norms].reshape(3, share_of_norms)
    gate_up = over_z(left[0], got[0])
    cross_kv = over_z(cross_left, cross_got)
    part = share_of_norms
    return (
        decoder_out,
        decoder_in_grad,
        memory_grad,
        norm_sums[0],
        sums[2][:part],
        sums[2][part:],
        sums[3][:part],
        sums[3][part:],
        norm_sums[1],
        sums[1][:part],
        cross_kv[:part],
        cross_kv[part:],
        sums[1][part:],
        norm_sums[2],
        gate_up[:part],
        gate_up[part:],
        over_z(left[1], got[1]),
    )


def solution(mesh):
    dp, seq = mesh.devices.shape
    cores = 2
    lines = dp // PLANES
    split = Mesh(mesh.devices.reshape(PLANES, lines, seq // cores, cores), ALL)
    sizes = split.devices.shape
    first = P(ALL)
    middle = P(None, ALL)
    whole = P()
    return jax.shard_map(
        functools.partial(on_device, sizes),
        mesh=split,
        in_specs=(first, middle, first, first) + (whole,) * 14,
        out_specs=(first, first, middle) + (first,) * 14,
        check_vma=False,
    )
```

```python
import functools

import jax
import jax.numpy as jnp
from jax import lax
from jax.experimental import pallas as pl
from jax.experimental.pallas import tpu as pltpu
from jax.sharding import Mesh
from jax.sharding import PartitionSpec as P

H = 12
HD = 64
PAIRS = 6
PLANES = 4
EPSILON = 1e-06
MASKED = -1e30
VMEM = 56 * 2**20
BF = jnp.bfloat16
F32 = jnp.float32
ALL = ("z", "y", "x", "c")
PLANE = ("y", "x", "c")
EVERY = slice(None)


def dot(left, right, left_dim, right_dim):
    return lax.dot_general(
        left, right, (((left_dim,), (right_dim,)), ((), ())), preferred_element_type=F32
    )


def lane_masks():
    lane = lax.broadcasted_iota(jnp.int32, (1, 2 * HD), 1)
    low = jnp.where(lane < HD, 1.0, 0.0)
    first = jnp.where(lane == HD, 1.0, 0.0)
    second = jnp.where(lane == 0, 1.0, 0.0)
    low, high, first, second = (
        v.astype(BF) for v in (low, 1.0 - low, first, second)
    )
    return ((low, high, first), (high, low, second))


def causal_mask(scores):
    key = lax.broadcasted_iota(jnp.int32, scores.shape, 0)
    query = lax.broadcasted_iota(jnp.int32, scores.shape, 1)
    return jnp.where(key <= query, scores, MASKED)


def rem(value, size):
    return lax.rem(value, size)


class Courier:
    def __init__(self, sizes, jobs):
        self.sizes = sizes
        self.jobs = jobs
        self.plane = sizes[1] * sizes[2] * sizes[3]
        self.in_plane = any(job[0] in ("fetch", "return") for job in jobs)
        self.lines = [job[1] for job in jobs if job[0] == "line"]
        for job in jobs:
            if job[0] == "scatter":
                self.lines += list(range(1, PLANES))

    def out_shape(self):
        shapes = []
        for kind, _, value in self.jobs:
            shape = value.shape
            if kind == "fetch":
                shape = (self.plane,) + shape[1:]
            elif kind == "scatter":
                shape = (PLANES - 1,) + shape[1:]
            shapes.append(jax.ShapeDtypeStruct(shape, value.dtype))
        return shapes

    def specs(self):
        return [pl.BlockSpec(memory_space=pl.ANY)] * len(self.jobs)

    def values(self):
        return [job[2] for job in self.jobs]

    def scratch(self):
        each = {"line": 1, "scatter": PLANES - 1}
        count = max(1, sum(each.get(job[0], self.plane - 1) for job in self.jobs))
        own = max(1, sum(job[0] in ("fetch", "return") for job in self.jobs))
        return [pltpu.SemaphoreType.DMA((n,)) for n in (count, count, own)]

    def params(self, ident):
        return pltpu.CompilerParams(
            vmem_limit_bytes=VMEM, collective_id=ident, has_side_effects=True
        )

    def me(self):
        _, _, x_size, c_size = self.sizes
        y, x, c = (lax.axis_index(name) for name in PLANE)
        return (y * x_size + x) * c_size + c

    def along(self, offset):
        return {"z": rem(lax.axis_index("z") + (offset + PLANES), PLANES)}

    def across(self, offset):
        _, _, x_size, c_size = self.sizes
        other = rem(self.me() + offset, self.plane)
        line = lax.div(other, c_size)
        return other, {"y": lax.div(line, x_size), "x": rem(line, x_size), "c": rem(other, c_size)}

    def greet(self):
        barrier = pltpu.get_barrier_semaphore()
        count = 0
        if self.in_plane:
            for k in range(1, self.plane):
                _, device = self.across(k)
                pl.semaphore_signal(
                    barrier, inc=1, device_id=device, device_id_type=pl.DeviceIdType.MESH
                )
                count += 1
        for offset in self.lines:
            pl.semaphore_signal(
                barrier,
                inc=1,
                device_id=self.along(-offset),
                device_id_type=pl.DeviceIdType.MESH,
            )
            count += 1
        pl.semaphore_wait(barrier, count)

    def copies(self, sources, targets, sems):
        send, receive, own = sems
        remote = []
        local = []

        def add(source, target, device):
            n = len(remote)
            remote.append(
                pltpu.make_async_remote_copy(
                    src_ref=source,
                    dst_ref=target,
                    send_sem=send.at[n],
                    recv_sem=receive.at[n],
                    device_id=device,
                    device_id_type=pl.DeviceIdType.MESH,
                )
            )

        me = self.me()
        for (kind, offset, _), source, target in zip(self.jobs, sources, targets):
            if kind == "line":
                add(source, target, self.along(offset))
                continue
            if kind == "scatter":
                for k in range(1, PLANES):
                    there = rem(lax.axis_index("z") + k, PLANES)
                    add(source.at[there], target.at[k - 1], self.along(k))
                continue
            base = 0
            if kind == "fetch":
                base = rem(lax.axis_index("z") + offset, PLANES) * self.plane
            for k in range(1, self.plane):
                other, device = self.across(k)
                add(source.at[base + other], target.at[me], device)
            local.append(
                pltpu.make_async_copy(source.at[base + me], target.at[me], own.at[len(local)])
            )
        return local + remote

    def start(self, sources, targets, sems):
        self.greet()
        for copy in self.copies(sources, targets, sems):
            copy.start()

    def wait(self, sources, targets, sems):
        for copy in self.copies(sources, targets, sems):
            copy.wait()


class Reducer:
    def __init__(self, sizes, shape):
        self.sizes = sizes
        self.rows, self.lanes = shape[-2:]
        self.half = self.lanes // 2

    def scratch(self):
        z, y, x, _ = self.sizes
        r, w, h = self.rows, self.lanes, self.half
        crossing = x + y - 2
        return [
            pltpu.VMEM((z, y, x, r, w), BF),
            pltpu.VMEM((z, y, x, r, w), BF),
            pltpu.VMEM((x - 1, z, y, r, h), BF),
            pltpu.VMEM((y - 1, z, x, r, h), BF),
            pltpu.VMEM((y - 1, z, r, h), BF),
            pltpu.VMEM((x - 1, z, r, h), BF),
            pltpu.SemaphoreType.DMA((1,)),
            pltpu.SemaphoreType.DMA((1 + 2 * crossing,)),
            pltpu.SemaphoreType.DMA((1 + 2 * crossing,)),
        ]

    def bind(self, source, refs):
        self.source = source
        self.held, self.got0, self.got1x, self.got1y, self.got2y, self.got2x = refs[:6]
        self.local, self.send, self.receive = refs[6:]
        self.z, self.y, self.x, self.c = (lax.axis_index(name) for name in ALL)
        return self

    def index(self, z, y, x, lanes):
        return (z, y, x, EVERY, lanes)

    def slab(self, z, y, x, lanes):
        return self.held.at[self.index(z, y, x, lanes)]

    given = slab

    def remote(self, n, source, target, device):
        return pltpu.make_async_remote_copy(
            src_ref=source,
            dst_ref=target,
            send_sem=self.send.at[n],
            recv_sem=self.receive.at[n],
            device_id=device,
            device_id_type=pl.DeviceIdType.MESH,
        )

    def first(self):
        other = 1 - self.c
        return [
            pltpu.make_async_copy(self.source.at[:, :, :, self.c], self.held, self.local.at[0]),
            self.remote(0, self.source.at[:, :, :, other], self.got0, {"c": other}),
        ]

    def second(self):
        _, y_size, x_size, _ = self.sizes
        left, right = pl.ds(0, self.half), pl.ds(self.half, self.half)
        copies = []
        for k in range(1, x_size):
            there = rem(self.x + k, x_size)
            copies.append((self.given(EVERY, EVERY, there, left), self.got1x.at[k - 1], {"x": there}))
        for k in range(1, y_size):
            there = rem(self.y + k, y_size)
            copies.append((self.given(EVERY, there, EVERY, right), self.got1y.at[k - 1], {"y": there}))
        return [self.remote(1 + n, *copy) for n, copy in enumerate(copies)]

    def third(self):
        _, y_size, x_size, _ = self.sizes
        left, right = pl.ds(0, self.half), pl.ds(self.half, self.half)
        at = 1 + x_size + y_size - 2
        copies = []
        for k in range(1, y_size):
            there = rem(self.y + k, y_size)
            copies.append(
                (self.slab(EVERY, there, self.x, left), self.got2y.at[k - 1], {"y": there})
            )
        for k in range(1, x_size):
            there = rem(self.x + k, x_size)
            copies.append(
                (self.slab(EVERY, self.y, there, right), self.got2x.at[k - 1], {"x": there})
            )
        return [self.remote(at + n, *copy) for n, copy in enumerate(copies)]

    def begin(self):
        for copy in self.first():
            copy.start()

    def after_first(self):
        for copy in self.first():
            copy.wait()

        @pl.loop(0, self.sizes[0])
        def _(z):
            at = self.index(z, EVERY, EVERY, EVERY)
            self.held[at] = (self.held[at].astype(F32) + self.got0[z].astype(F32)).astype(BF)

        for copy in self.second():
            copy.start()

    def after_second(self):
        _, y_size, x_size, _ = self.sizes
        for copy in self.second():
            copy.wait()
        h = self.half

        @pl.loop(0, self.sizes[0])
        def _(z):
            for y in range(y_size):
                at = self.index(z, y, self.x, pl.ds(0, h))
                total = self.held[at].astype(F32)
                for k in range(x_size - 1):
                    total += self.got1x[k, z, y].astype(F32)
                self.held[at] = total.astype(BF)
            for x in range(x_size):
                at = self.index(z, self.y, x, pl.ds(h, h))
                total = self.held[at].astype(F32)
                for k in range(y_size - 1):
                    total += self.got1y[k, z, x].astype(F32)
                self.held[at] = total.astype(BF)

        for copy in self.third():
            copy.start()

    def after_third(self, out_ref):
        _, y_size, x_size, _ = self.sizes
        for copy in self.third():
            copy.wait()
        h = self.half

        @pl.loop(0, self.sizes[0])
        def _(z):
            total = self.held[self.index(z, self.y, self.x, pl.ds(0, h))].astype(F32)
            for k in range(y_size - 1):
                total += self.got2y[k, z].astype(F32)
            out_ref[z, :, :h] = total.astype(BF)
            total = self.held[self.index(z, self.y, self.x, pl.ds(h, h))].astype(F32)
            for k in range(x_size - 1):
                total += self.got2x[k, z].astype(F32)
            out_ref[z, :, h:] = total.astype(BF)


class Halved(Reducer):
    def scratch(self):
        z, y, x, _ = self.sizes
        r, w, h = self.rows, self.lanes, self.half
        crossing = x + y - 2
        return [
            pltpu.VMEM((z, y, x, r, w), BF),
            pltpu.VMEM((x - 1, z, y, r, h), BF),
            pltpu.VMEM((y - 1, z, x, r, h), BF),
            pltpu.VMEM((y - 1, z, r, h), BF),
            pltpu.VMEM((x - 1, z, r, h), BF),
            pltpu.SemaphoreType.DMA((1,)),
            pltpu.SemaphoreType.DMA((1 + 2 * crossing,)),
            pltpu.SemaphoreType.DMA((1 + 2 * crossing,)),
        ]

    def bind(self, source, refs):
        self.source = source
        self.held, self.got1x, self.got1y, self.got2y, self.got2x = refs[:5]
        self.local, self.send, self.receive = refs[5:]
        self.z, self.y, self.x, self.c = (lax.axis_index(name) for name in ALL)
        return self

    def given(self, z, y, x, lanes):
        return self.source.at[self.index(z, y, x, lanes)]

    def first(self):
        return [pltpu.make_async_copy(self.source, self.held, self.local.at[0])]

    def begin(self):
        for copy in self.first() + self.second():
            copy.start()

    def after_first(self):
        pass

    def after_second(self):
        for copy in self.first():
            copy.wait()
        super().after_second()


class Resident(Reducer):
    def scratch(self):
        z, y, x, c = self.sizes
        r, w, h = self.rows, self.lanes, self.half
        count = 1 + 2 * (x + y - 2) + z - 1
        return [
            pltpu.VMEM((z, y, x, c, r, w), BF),
            pltpu.VMEM((z, y, x, r, w), BF),
            pltpu.VMEM((x - 1, z, y, r, h), BF),
            pltpu.VMEM((y - 1, z, x, r, h), BF),
            pltpu.VMEM((y - 1, z, r, h), BF),
            pltpu.VMEM((x - 1, z, r, h), BF),
            pltpu.VMEM((z, r, w), BF),
            pltpu.VMEM((z - 1, r, w), BF),
            pltpu.SemaphoreType.DMA((count,)),
            pltpu.SemaphoreType.DMA((count,)),
        ]

    def bind(self, refs):
        self.held, self.got0, self.got1x, self.got1y, self.got2y, self.got2x = refs[:6]
        self.left, self.got3, self.send, self.receive = refs[6:]
        self.z, self.y, self.x, self.c = (lax.axis_index(name) for name in ALL)
        return self

    def index(self, z, y, x, lanes):
        return (z, y, x, self.c, EVERY, lanes)

    def first(self):
        other = 1 - self.c
        return [self.remote(0, self.held.at[:, :, :, other], self.got0, {"c": other})]

    def fourth(self):
        _, y_size, x_size, _ = self.sizes
        at = 1 + 2 * (x_size + y_size - 2)
        copies = []
        for k in range(1, PLANES):
            there = rem(self.z + k, PLANES)
            copies.append(
                self.remote(at + k - 1, self.left.at[there], self.got3.at[k - 1], {"z": there})
            )
        return copies

    def after_third_start(self):
        self.after_third(self.left)
        for copy in self.fourth():
            copy.start()

    def finish(self, out_ref):
        for copy in self.fourth():
            copy.wait()
        total = self.left[self.z].astype(F32)
        for k in range(PLANES - 1):
            total += self.got3[k].astype(F32)
        out_ref[...] = total


class SmallSum:
    def __init__(self, sizes, shape):
        self.shape = shape
        self.steps = list(zip(("c", "x", "y", "z"), (sizes[3], sizes[2], sizes[1], sizes[0])))

    def scratch(self):
        count = sum(n - 1 for _, n in self.steps)
        return (
            [pltpu.VMEM(self.shape, F32) for _ in range(4)]
            + [pltpu.VMEM((n - 1,) + self.shape, F32) for _, n in self.steps]
            + [pltpu.SemaphoreType.DMA((count,))] * 2
        )

    def bind(self, refs):
        self.held, self.got = refs[:4], refs[4:8]
        self.send, self.receive = refs[8:]
        return self

    def copies(self, step):
        axis, n = self.steps[step]
        at = sum(m - 1 for _, m in self.steps[:step])
        me = lax.axis_index(axis)
        return [
            pltpu.make_async_remote_copy(
                src_ref=self.held[step],
                dst_ref=self.got[step].at[k - 1],
                send_sem=self.send.at[at + k - 1],
                recv_sem=self.receive.at[at + k - 1],
                device_id={axis: rem(me + k, n)},
                device_id_type=pl.DeviceIdType.MESH,
            )
            for k in range(1, n)
        ]

    def start(self, step):
        for copy in self.copies(step):
            copy.start()

    def advance(self, step, out_ref=None):
        for copy in self.copies(step):
            copy.wait()
        total = self.held[step][...]
        for k in range(self.steps[step][1] - 1):
            total += self.got[step][k]
        if step < 3:
            self.held[step + 1][...] = total
            self.start(step + 1)
        else:
            out_ref[...] = total


def forward_pair(queries, keys, values, bias):
    masks = lane_masks()
    all_scores = []
    for mine, other, one in masks:
        if bias is None:
            all_scores.append(causal_mask(dot(keys, queries * mine, 1, 1)))
        else:
            all_scores.append(dot(keys * mine + bias * one, queries * mine + one, 1, 1))
    parts = []
    stats = []
    held = []
    for h in range(2):
        mine, other, _ = masks[h]
        scores = all_scores[h]
        row_max = jnp.max(scores, axis=0, keepdims=True)
        probs = jnp.exp(scores - row_max).astype(BF)
        both = dot(values * mine + other, probs, 0, 0)
        halves = (both[:HD], both[HD:])
        total = halves[1 - h]
        parts.append(halves[h] / total)
        stats.append((row_max + jnp.log(total[0:1]), row_max))
        held.append(probs)
    return jnp.concatenate(parts, axis=0).T.astype(BF), stats, held


def backward_pair(queries, grad, keys, values, probs_of, delta):
    grad_k = None
    grad_v = None
    grad_q = []
    for h, (mine, other, one) in enumerate(lane_masks()):
        query_h = queries * mine
        grad_h = grad * mine
        probs = probs_of(h, keys, query_h)
        grad_p = dot(values, grad_h, 1, 1)
        if delta is None:
            delta_h = jnp.sum(probs * grad_p, axis=0, keepdims=True)
        else:
            delta_h = delta[h]
        grad_s = (probs * (grad_p - delta_h)).astype(BF)
        term_v = dot(probs.astype(BF), grad_h, 1, 0)
        term_k = dot(grad_s, query_h, 1, 0)
        grad_v = term_v if grad_v is None else grad_v + term_v
        grad_k = term_k if grad_k is None else grad_k + term_k
        grad_q.append(dot(keys, grad_s, 0, 0)[h * HD : (h + 1) * HD])
    grad_kv = jnp.concatenate([grad_k, grad_v], axis=1).astype(BF)
    return grad_kv, jnp.concatenate(grad_q, axis=0).T.astype(BF)


def causal_probs(lse):
    return lambda h, keys, query: jnp.exp(causal_mask(dot(keys, query, 1, 1)) - lse[h])


def key_bias(keys, lens):
    row = lax.broadcasted_iota(jnp.int32, (keys, 128), 0) + lax.axis_index("z") * keys
    return jnp.where(row < lens[0:1, :], 0.0, MASKED).astype(BF)


def split_refs(refs, *counts):
    groups = []
    at = 0
    for count in counts:
        groups.append(refs[at : at + count])
        at += count
    return groups


def carried(courier, reducers, body):
    jobs = len(courier.jobs)
    sums = len(reducers)
    parts = [len(one.scratch()) for one in reducers]

    def kernel(ins, outs, scratch, refs):
        own_in, sources, summands, own_out, targets, results, own_scratch, sems, rest = split_refs(
            refs, ins, jobs, sums, outs, jobs, sums, scratch, 3, sum(parts)
        )
        step = pl.program_id(0)
        work = split_refs(rest, *parts)

        def bound():
            return [one.bind(value, refs) for one, value, refs in zip(reducers, summands, work)]

        @pl.when(step == 0)
        def _():
            courier.start(sources, targets, sems)
            for one in bound():
                one.begin()

        body(own_in, own_out, own_scratch)

        if sums:

            @pl.when(step == 1)
            def _():
                for one in bound():
                    one.after_first()

            @pl.when(step == 3)
            def _():
                for one in bound():
                    one.after_second()

        @pl.when(step == PAIRS - 1)
        def _():
            for one, result in zip(bound(), results):
                one.after_third(result)
            courier.wait(sources, targets, sems)

    return kernel


def call(courier, ident, body, args, in_specs, out_shape, out_specs, scratch, flops, summands=()):
    if summands:
        courier.in_plane = True
    reducers = [
        (Halved if value.ndim == 5 else Reducer)(courier.sizes, value.shape) for value in summands
    ]
    shapes = [(PLANES,) + value.shape[-2:] for value in summands]
    kernel = carried(courier, reducers, body)
    counts = (len(args), len(out_shape), len(scratch))
    outs = pl.pallas_call(
        lambda *refs: kernel(*counts, refs),
        grid=(PAIRS,),
        out_shape=out_shape
        + courier.out_shape()
        + [jax.ShapeDtypeStruct(shape, BF) for shape in shapes],
        in_specs=in_specs + courier.specs() + [pl.BlockSpec(memory_space=pl.ANY)] * len(shapes),
        out_specs=out_specs
        + courier.specs()
        + [pl.BlockSpec(shape, lambda p: (0, 0, 0)) for shape in shapes],
        scratch_shapes=scratch
        + courier.scratch()
        + [ref for one in reducers for ref in one.scratch()],
        compiler_params=courier.params(ident),
        cost_estimate=pl.CostEstimate(flops=flops, bytes_accessed=2**24, transcendentals=2**20),
    )(*args, *courier.values(), *summands)
    return outs[: len(out_shape)], outs[len(out_shape) :]


def reduce_all(sizes, ident, summands, scattered):
    courier = Courier(sizes, [("scatter", 0, value) for value in scattered])
    courier.in_plane = True
    courier.lines += list(range(1, PLANES))
    jobs = len(scattered)
    count = len(summands)
    reducers = [Reducer(sizes, value.shape) for value in summands]
    shapes = [value.shape[-2:] for value in summands]

    def kernel(*refs):
        sources, arrays, targets, results, sems, rest = split_refs(
            refs, jobs, count, jobs, count, 3, len(refs) - 2 * jobs - 2 * count - 3
        )
        courier.start(sources, targets, sems)
        bound = []
        last = []
        for n in range(count):
            refs_n = rest[13 * n : 13 * n + 13]
            bound.append(reducers[n].bind(arrays[n], refs_n[:9]))
            last.append(refs_n[9:])

        def leave(n):
            left, got, send, receive = last[n]
            copies = []
            for k in range(1, PLANES):
                copies.append(
                    pltpu.make_async_remote_copy(
                        src_ref=left.at[rem(lax.axis_index("z") + k, PLANES)],
                        dst_ref=got.at[k - 1],
                        send_sem=send.at[k - 1],
                        recv_sem=receive.at[k - 1],
                        device_id=courier.along(k),
                        device_id_type=pl.DeviceIdType.MESH,
                    )
                )
            return copies

        for one in bound:
            one.begin()
        for one in bound:
            one.after_first()
        for one in bound:
            one.after_second()
        for n, one in enumerate(bound):
            one.after_third(last[n][0])
            for copy in leave(n):
                copy.start()
        for n in range(count):
            for copy in leave(n):
                copy.wait()
            left, got = last[n][:2]
            total = left[lax.axis_index("z")].astype(F32)
            for k in range(PLANES - 1):
                total += got[k].astype(F32)
            results[n][...] = total
        courier.wait(sources, targets, sems)

    scratch = []
    for n in range(count):
        scratch += reducers[n].scratch() + [
            pltpu.VMEM((PLANES,) + shapes[n], BF),
            pltpu.VMEM((PLANES - 1,) + shapes[n], BF),
            pltpu.SemaphoreType.DMA((PLANES - 1,)),
            pltpu.SemaphoreType.DMA((PLANES - 1,)),
        ]
    outs = pl.pallas_call(
        kernel,
        out_shape=courier.out_shape() + [jax.ShapeDtypeStruct(shape, F32) for shape in shapes],
        in_specs=courier.specs() + [pl.BlockSpec(memory_space=pl.ANY)] * count,
        out_specs=courier.specs() + [pl.BlockSpec(memory_space=pltpu.VMEM)] * count,
        scratch_shapes=courier.scratch() + scratch,
        compiler_params=courier.params(ident),
    )(*courier.values(), *summands)
    return outs[:jobs], outs[jobs:]


def summand_of(sizes, arrays):
    devices = sizes[0] * sizes[1] * sizes[2] * sizes[3]
    parts = [a.reshape(devices, a.shape[0] // devices, a.shape[1]) for a in arrays]
    joined = parts[0] if len(parts) == 1 else jnp.concatenate(parts, axis=1)
    return joined.astype(BF).reshape(tuple(sizes) + joined.shape[1:])


def over_z(left, got):
    own = lax.dynamic_index_in_dim(left, lax.axis_index("z"), 0, keepdims=False)
    return own.astype(F32) + jnp.sum(got.astype(F32), axis=0)


def block_specs(tokens, keys):
    return dict(
        col=pl.BlockSpec((tokens, 128), lambda p: (0, p)),
        pair=pl.BlockSpec((keys, 256), lambda p: (0, p)),
        rows=pl.BlockSpec((keys, H * HD), lambda p: (0, 0)),
        weight=pl.BlockSpec((H * HD, 128), lambda p: (0, p)),
        stat=pl.BlockSpec((1, 2, tokens), lambda p: (p, 0, 0)),
    )


def rms(values, gain):
    r = lax.rsqrt(jnp.mean(values * values, axis=-1, keepdims=True) + EPSILON)
    return values * r * gain


ORDER = (1, 2, 3, 0)


def forward_part(sizes, ident, memory, lens, inputs, gains, weights, key_weight, value_weight):
    tokens, width = inputs.shape
    positions = memory.shape[1]
    plane = sizes[1] * sizes[2] * sizes[3]
    keys = plane * positions
    rows = jax.ShapeDtypeStruct((tokens, width), BF)
    wide = jax.ShapeDtypeStruct((tokens, width), F32)
    stat = jax.ShapeDtypeStruct((PAIRS, 2, tokens), F32)
    near = range(1, PLANES)
    jobs = [("fetch", r, memory) for r in ORDER]
    jobs += [("line", -r, lens) for r in near] + [("line", -r, rows) for r in near]
    jobs += [("line", r, rows) for r in near] + [("line", r, stat) for r in near]
    courier = Courier(sizes, jobs)
    courier.lines = list(near)
    count = PLANES * PAIRS

    def kernel(*refs):
        ins, sources, outs, parts, targets, work, sems = split_refs(refs, 11, 1, 8, 4, 13, 7, 3)
        x_ref, self_gain, cross_gain, wq_ref, wk_ref, wv_ref, wo_ref, wc_ref = ins[:8]
        lens_ref, key_ref, value_ref = ins[8:]
        (memory_ref,) = sources
        q_ref, k_ref, v_ref, lse_ref, attn_ref, hidden_ref, query_ref, top_ref = outs
        part_ref, part_lse_ref, kv_ref, probs_ref = parts
        row_buf, query_buf, out_buf, lse_buf, lens_buf, near_lens, load_sems = work
        copies = courier.copies(
            [memory_ref] * PLANES
            + [lens_ref] * 3
            + [query_ref] * 3
            + [out_buf.at[n] for n in range(3)]
            + [lse_buf.at[n] for n in range(3)],
            list(targets[:4])
            + [near_lens.at[n] for n in range(3)]
            + list(targets[4:]),
            sems,
        )
        own, remote = copies[:PLANES], copies[PLANES:]
        far = plane - 1
        lines = remote[PLANES * far :]
        lens_lines, query_lines, out_lines, lse_lines = split_refs(lines, 3, 3, 3, 3)
        step = pl.program_id(0)
        me = courier.me()

        def start_fetch(n):
            for copy in [own[n]] + remote[n * far : n * far + far]:
                copy.start()

        @pl.when(step == 0)
        def _():
            courier.greet()
            start_fetch(0)
            for copy in lens_lines:
                copy.start()
            values = x_ref[...].astype(F32)
            normed = rms(values, self_gain[...]).astype(BF)
            q_ref[...] = dot(normed, wq_ref[...], 1, 0).astype(BF)
            k_ref[...] = dot(normed, wk_ref[...], 1, 0).astype(BF)
            v_ref[...] = dot(normed, wv_ref[...], 1, 0).astype(BF)

            @pl.loop(0, PAIRS)
            def _(p):
                cols = pl.ds(pl.multiple_of(p * 128, 128), 128)
                out, stats, _ = forward_pair(q_ref[:, cols], k_ref[:, cols], v_ref[:, cols], None)
                attn_ref[:, cols] = out
                for h in range(2):
                    lse_ref[p, h : h + 1, :] = stats[h][0]

            hidden = values + dot(attn_ref[...], wo_ref[...], 1, 0)
            hidden_ref[...] = hidden
            normed = rms(hidden, cross_gain[...]).astype(BF)
            query_ref[...] = dot(normed, wc_ref[...], 1, 0).astype(BF)
            query_lines[0].start()

        for n, r in enumerate(ORDER):

            @pl.when(step == n * PAIRS)
            def _(n=n, r=r):
                loads = []

                def load(block):
                    at = pl.ds(pl.multiple_of(block * positions, positions), positions)
                    copy = pltpu.make_async_copy(
                        targets[n].at[block], row_buf.at[at], load_sems.at[len(loads)]
                    )
                    copy.start()
                    loads.append(copy)

                own[n].wait()
                load(me)
                for k in range(1, plane):
                    remote[n * far + k - 1].wait()
                    load(rem(me + (plane - k), plane))
                if n + 1 < PLANES:
                    start_fetch(n + 1)
                if r > 0:
                    query_lines[r - 1].wait()
                    copy = pltpu.make_async_copy(
                        targets[3 + r], query_buf, load_sems.at[plane]
                    )
                    copy.start()
                    if r + 1 < PLANES:
                        query_lines[r].start()
                    lens_lines[r - 1].wait()
                    lens_buf[...] = near_lens[r - 1]
                    copy.wait()
                else:
                    query_buf[...] = query_ref[...]
                    lens_buf[...] = lens_ref[...]
                for copy in loads:
                    copy.wait()

        phase = lax.div(step, PAIRS)
        p = rem(step, PAIRS)
        cols = pl.ds(pl.multiple_of(p * 128, 128), 128)
        both = jnp.concatenate([key_ref[...], value_ref[...]], axis=1)
        kv_ref[...] = dot(row_buf[...], both, 1, 0).astype(BF)
        bias = key_bias(keys, lens_buf[...])
        out, stats, held = forward_pair(query_buf[:, cols], kv_ref[:, :128], kv_ref[:, 128:], bias)
        out_buf[phase, :, cols] = out
        for h in range(2):
            probs_ref[h] = held[h]
            lse_buf[phase, p, h : h + 1, :] = stats[h][0]
            top_ref[phase, p, h : h + 1, :] = stats[h][1]

        for n, r in enumerate(ORDER[:-1]):

            @pl.when(step == n * PAIRS + PAIRS - 1)
            def _(r=r):
                out_lines[r - 1].start()
                lse_lines[r - 1].start()

        @pl.when(step == count - 1)
        def _():
            part_ref[...] = out_buf[PLANES - 1]
            part_lse_ref[...] = lse_buf[PLANES - 1]
            for copy in out_lines + lse_lines:
                copy.wait()

    once = pl.Buffered(1)

    def fixed(*shape):
        return pl.BlockSpec(shape, lambda t: (0,) * len(shape), pipeline_mode=once)

    def out_fixed(*shape):
        return pl.BlockSpec(shape, lambda t: (0,) * len(shape))

    def where(t):
        return rem(lax.div(t, PAIRS) + 1, PLANES), rem(t, PAIRS)

    square = fixed(width, width)
    weight = pl.BlockSpec((width, 128), lambda t: (0, rem(t, PAIRS)))
    hbm = pl.BlockSpec(memory_space=pl.ANY)
    flat = out_fixed(tokens, width)
    flat_stat = out_fixed(PAIRS, 2, tokens)
    shapes = courier.out_shape()
    outs = pl.pallas_call(
        kernel,
        grid=(count,),
        out_shape=[rows, rows, rows, stat, rows, wide, rows]
        + [jax.ShapeDtypeStruct((PLANES, PAIRS, 2, tokens), F32), rows, stat]
        + [
            jax.ShapeDtypeStruct((PLANES, keys, 2 * width), BF),
            jax.ShapeDtypeStruct((PLANES, H, keys, tokens), BF),
        ]
        + shapes[:4]
        + shapes[7:],
        in_specs=[fixed(tokens, width), fixed(1, width), fixed(1, width)]
        + [square] * 5
        + [fixed(8, 128), weight, weight, hbm],
        out_specs=[flat] * 3
        + [flat_stat]
        + [flat] * 3
        + [out_fixed(PLANES, PAIRS, 2, tokens), flat, flat_stat]
        + [
            pl.BlockSpec((None, keys, 256), lambda t: (where(t)[0], 0, where(t)[1])),
            pl.BlockSpec((None, 2, keys, tokens), lambda t: where(t) + (0, 0)),
        ]
        + [hbm] * 13,
        scratch_shapes=[
            pltpu.VMEM((keys, width), BF),
            pltpu.VMEM((tokens, width), BF),
            pltpu.VMEM((PLANES, tokens, width), BF),
            pltpu.VMEM((PLANES, PAIRS, 2, tokens), F32),
            pltpu.VMEM((8, 128), jnp.int32),
            pltpu.VMEM((3, 8, 128), jnp.int32),
            pltpu.SemaphoreType.DMA((plane + 1,)),
        ]
        + courier.scratch(),
        compiler_params=pltpu.CompilerParams(
            vmem_limit_bytes=62 * 2**20, collective_id=ident, has_side_effects=True
        ),
    )(inputs, *gains, *weights, lens, key_weight, value_weight, memory)
    saved, (tops, part0, lse0, kv, probs), moved = outs[:7], outs[7:12], outs[12:]
    return dict(
        saved=saved,
        tops=tops,
        keyvals=kv,
        probs=probs,
        rows={r: moved[n] for n, r in enumerate(ORDER)},
        queries={0: saved[6], **{r: moved[3 + r] for r in near}},
        parts=[part0] + [moved[6 + r] for r in near],
        lses=[lse0] + [moved[9 + r] for r in near],
    )


def glu_parts(gate_vals):
    inner = 0.7978845608028654 * (gate_vals + 0.044715 * gate_vals * gate_vals * gate_vals)
    t = jnp.tanh(inner)
    gelu = 0.5 * gate_vals * (1.0 + t)
    slope = 0.5 * (1.0 + t) + 0.5 * gate_vals * (1.0 - t * t) * 0.7978845608028654 * (
        1.0 + 0.134145 * gate_vals * gate_vals
    )
    return gelu, slope


def spread(rows):
    both = [jnp.broadcast_to(rows[h : h + 1], (HD, rows.shape[1])) for h in range(2)]
    return jnp.concatenate(both, axis=0).T


def middle_kernel(*refs, sizes, packed):
    (
        part0,
        part1,
        part2,
        part3,
        lse0,
        lse1,
        lse2,
        lse3,
        h1_ref,
        wo_ref,
        gain_ref,
        cot_ref,
        gate_ref,
        up_ref,
        down_ref,
        out_ref,
        attn_ref,
        two_ref,
        da_ref,
        stats_ref,
        gnorm_ref,
        gwo_ref,
        *grad_refs,
        gdown_ref,
        raw_ref,
        h2_ref,
        n3_ref,
        total_ref,
        dn3_ref,
    ) = refs[: 29 + (not packed)]
    step = pl.program_id(0)
    last = pl.num_programs(0) - 1
    devices = sizes[0] * sizes[1] * sizes[2] * sizes[3]
    if packed:
        wide_ref, wide_got, tall_ref, tall_got, send, receive = refs[29:]
        core = lax.axis_index("c")

    def exchange(n):
        slot = rem(n, 2)
        return [
            pltpu.make_async_remote_copy(
                src_ref=source,
                dst_ref=target,
                send_sem=send.at[n, at],
                recv_sem=receive.at[n, at],
                device_id={"c": 1 - core},
                device_id_type=pl.DeviceIdType.MESH,
            )
            for at, (source, target) in enumerate(
                (
                    (wide_ref.at[slot, :, :, :, 1 - core], wide_got.at[n]),
                    (tall_ref.at[slot, :, :, 1 - core], tall_got.at[n]),
                )
            )
        ]
    parts = (part0, part1, part2, part3)
    lses = (lse0, lse1, lse2, lse3)

    @pl.when(step == 0)
    def _():
        for p in range(PAIRS):
            cols = pl.ds(p * 128, 128)
            values = [ref[p] for ref in lses]
            top = functools.reduce(jnp.maximum, values)
            scales = [jnp.exp(v - top) for v in values]
            total = functools.reduce(jnp.add, scales)
            stats_ref[0, p] = top + jnp.log(total)
            raw = None
            for ref, scale in zip(parts, scales):
                term = spread(scale / total) * ref[:, cols].astype(F32)
                raw = term if raw is None else raw + term
            raw_ref[:, cols] = raw
            attn_ref[:, cols] = raw.astype(BF)
        hidden = h1_ref[...] + dot(attn_ref[...], wo_ref[...], 1, 0)
        h2_ref[...] = hidden
        n3_ref[...] = rms(hidden, gain_ref[...]).astype(BF)
        total_ref[...] = hidden
        dn3_ref[...] = jnp.zeros_like(dn3_ref)
        if packed:
            barrier = pltpu.get_barrier_semaphore()
            pl.semaphore_signal(
                barrier,
                inc=1,
                device_id={"c": 1 - core},
                device_id_type=pl.DeviceIdType.MESH,
            )
            pl.semaphore_wait(barrier, 1)

    def one_chunk():
        normed = n3_ref[...]
        branch = cot_ref[...]
        gate_vals = dot(normed, gate_ref[...], 1, 0)
        up_vals = dot(normed, up_ref[...], 1, 0)
        grad_inner = dot(branch, down_ref[...], 1, 1)
        gelu, slope = glu_parts(gate_vals)
        inner = (gelu * up_vals).astype(BF)
        grad_gate = (grad_inner * up_vals * slope).astype(BF)
        grad_up = (grad_inner * gelu).astype(BF)
        total_ref[...] += dot(inner, down_ref[...], 1, 0)
        dn3_ref[...] += dot(grad_gate, gate_ref[...], 1, 1) + dot(grad_up, up_ref[...], 1, 1)
        terms = [dot(normed, grad_gate, 0, 0), dot(normed, grad_up, 0, 0)]
        if packed:
            shape = (devices, terms[0].shape[0] // devices, terms[0].shape[1])
            both = jnp.concatenate([t.reshape(shape) for t in terms], axis=1).astype(BF)
            slot = rem(step, 2)
            wide_ref[slot] = both.reshape(wide_ref.shape[1:])
            tall_ref[slot] = dot(inner, branch, 0, 0).astype(BF).reshape(tall_ref.shape[1:])
            for copy in exchange(step):
                copy.start()
        else:
            for ref, term in zip(grad_refs, terms):
                ref[...] = term
            gdown_ref[...] = dot(inner, branch, 0, 0).astype(BF).reshape(gdown_ref.shape)

    if packed:

        @pl.when(step < last)
        def _():
            one_chunk()

    else:
        one_chunk()

    @pl.when(step == last)
    def _():
        out_ref[...] = total_ref[...].astype(BF)
        hidden = h2_ref[...]
        grad = dn3_ref[...]
        r = lax.rsqrt(jnp.mean(hidden * hidden, axis=-1, keepdims=True) + EPSILON)
        u = gain_ref[...] * grad
        back = r * u - hidden * (r * r * r) * jnp.mean(u * hidden, axis=-1, keepdims=True)
        gnorm_ref[...] = jnp.sum(grad * hidden * r, axis=0, keepdims=True)
        two = cot_ref[...].astype(F32) + back
        two_ref[...] = two
        low = two.astype(BF)
        da_ref[...] = dot(low, wo_ref[...], 1, 1).astype(BF)
        gwo_ref[...] = dot(attn_ref[...], low, 0, 0).astype(BF)
        for p in range(PAIRS):
            cols = pl.ds(p * 128, 128)
            product = (da_ref[:, cols].astype(F32) * raw_ref[:, cols]).T
            for h in range(2):
                stats_ref[1, p, h : h + 1] = jnp.sum(
                    product[h * HD : (h + 1) * HD], axis=0, keepdims=True
                )

    if packed:

        @pl.when(step > 0)
        def _():
            before = step - 1
            slot = rem(before, 2)
            for copy in exchange(before):
                copy.wait()
            mine = wide_ref[slot, :, :, :, core].astype(F32)
            grad_refs[0][...] = (mine + wide_got[before].astype(F32)).astype(BF)
            mine = tall_ref[slot, :, :, core].astype(F32)
            gdown_ref[0] = (mine + tall_got[before].astype(F32)).astype(BF)


def middle(sizes, parts, lses, hidden, out_weight, gain, cotangent, gate, up, down):
    tokens, width = hidden.shape
    inner = gate.shape[1]
    chunk = 512
    count = inner // chunk
    devices = sizes[0] * sizes[1] * sizes[2] * sizes[3]
    share = width // devices
    down_share = inner // devices
    packed = share % 8 == 0 and chunk * PLANES == inner
    first = lambda p: jnp.minimum(p, count - 1)
    fixed = lambda *shape: pl.BlockSpec(shape, lambda p: (0,) * len(shape))
    whole = fixed(tokens, width)
    square = fixed(width, width)
    stat = fixed(PAIRS, 2, tokens)
    column = pl.BlockSpec((width, chunk), lambda p: (0, first(p)))
    scratch = [
        pltpu.VMEM((tokens, width), F32),
        pltpu.VMEM((tokens, width), F32),
        pltpu.VMEM((tokens, width), BF),
        pltpu.VMEM((tokens, width), F32),
        pltpu.VMEM((tokens, width), F32),
    ]
    params = dict(vmem_limit_bytes=VMEM)
    if packed:
        z, y, x, c = sizes
        wide_shape = (z, y, x, 2 * share)
        tall_shape = (y, x, down_share, width)
        grad_shapes = [
            jax.ShapeDtypeStruct(wide_shape + (inner,), BF),
            jax.ShapeDtypeStruct((z,) + tall_shape, BF),
        ]
        before = lambda p: jnp.maximum(p - 1, 0)
        grad_specs = [
            pl.BlockSpec(wide_shape + (chunk,), lambda p: (0, 0, 0, 0, before(p))),
            pl.BlockSpec((1,) + tall_shape, lambda p: (before(p), 0, 0, 0, 0)),
        ]
        scratch += [
            pltpu.VMEM((2, z, y, x, c, 2 * share, chunk), BF),
            pltpu.VMEM((count,) + wide_shape + (chunk,), BF),
            pltpu.VMEM((2, y, x, c, down_share, width), BF),
            pltpu.VMEM((count,) + tall_shape, BF),
            pltpu.SemaphoreType.DMA((count, 2)),
            pltpu.SemaphoreType.DMA((count, 2)),
        ]
        params.update(collective_id=12, has_side_effects=True)
    else:
        grad_shapes = [jax.ShapeDtypeStruct((width, inner), F32)] * 2
        grad_shapes.append(jax.ShapeDtypeStruct((devices, down_share, width), BF))
        grad_specs = [column] * 2
        grad_specs.append(
            pl.BlockSpec((chunk // down_share, down_share, width), lambda p: (p, 0, 0))
        )
    rows = jax.ShapeDtypeStruct((tokens, width), BF)
    wide = jax.ShapeDtypeStruct((tokens, width), F32)
    return pl.pallas_call(
        functools.partial(middle_kernel, sizes=sizes, packed=packed),
        grid=(count + packed,),
        out_shape=[
            rows,
            rows,
            wide,
            rows,
            jax.ShapeDtypeStruct((2, PAIRS, 2, tokens), F32),
            jax.ShapeDtypeStruct((1, width), F32),
            jax.ShapeDtypeStruct((width, width), BF),
        ]
        + grad_shapes,
        in_specs=[whole] * 4
        + [stat] * 4
        + [whole, square, fixed(1, width), whole]
        + [column, column, pl.BlockSpec((chunk, width), lambda p: (first(p), 0))],
        out_specs=[whole] * 4
        + [fixed(2, PAIRS, 2, tokens), fixed(1, width), square]
        + grad_specs,
        scratch_shapes=scratch,
        compiler_params=pltpu.CompilerParams(**params),
    )(*parts, *lses, hidden, out_weight, gain, cotangent, gate, up, down)


def cross_backward(
    courier, ident, r, queries, grad, keyvals, probs, tops, stats, key_weight, value_weight, summands=()
):
    tokens, keys = queries.shape[0], keyvals.shape[1]
    width = H * HD
    spec = block_specs(tokens, keys)

    def body(ins, outs, scratch):
        q_ref, da_ref, kv_ref, probs_ref, top_ref, stats_ref, wk_ref, wv_ref = ins
        dkv_ref, dq_ref, dm_ref = outs
        (total_ref,) = scratch
        step = pl.program_id(0)

        @pl.when(step == 0)
        def _():
            total_ref[...] = jnp.zeros_like(total_ref)

        def stored(h, keys_h, query_h):
            scale = jnp.exp(top_ref[0, h : h + 1, :] - stats_ref[0, 0, h : h + 1, :])
            return probs_ref[h].astype(F32) * scale

        weights = jnp.concatenate([wk_ref[...], wv_ref[...]], axis=1)
        grad_kv, grad_q = backward_pair(
            q_ref[...],
            da_ref[...],
            kv_ref[:, :128],
            kv_ref[:, 128:],
            stored,
            [stats_ref[1, 0, h : h + 1, :] for h in range(2)],
        )
        dkv_ref[...] = grad_kv
        dq_ref[...] = grad_q
        total_ref[...] += dot(grad_kv, weights, 1, 1)

        @pl.when(step == PAIRS - 1)
        def _():
            dm_ref[...] = total_ref[...].astype(BF)

    return call(
        courier,
        ident,
        body,
        [queries, grad, keyvals, probs, tops, stats, key_weight, value_weight],
        [
            spec["col"],
            spec["col"],
            pl.BlockSpec((None, keys, 256), lambda p: (r, 0, p)),
            pl.BlockSpec((None, 2, keys, tokens), lambda p: (r, p, 0, 0)),
            pl.BlockSpec((None, 1, 2, tokens), lambda p: (rem(r + 3, PLANES), p, 0, 0)),
            pl.BlockSpec((2, 1, 2, tokens), lambda p: (0, p, 0, 0)),
            spec["weight"],
            spec["weight"],
        ],
        [
            jax.ShapeDtypeStruct((keys, 2 * width), BF),
            jax.ShapeDtypeStruct((tokens, width), BF),
            jax.ShapeDtypeStruct((keys, width), BF),
        ],
        [spec["pair"], spec["col"], spec["rows"]],
        [pltpu.VMEM((keys, width), F32)],
        2**35,
        summands,
    )


def weight_terms(courier, ident, rows, grads):
    keys, width = rows[0].shape
    spec = block_specs(keys, keys)
    count = len(rows)

    def body(ins, outs, _):
        total = None
        for rows_ref, grad_ref in zip(ins[:count], ins[count:]):
            term = dot(rows_ref[...], grad_ref[...], 0, 0)
            total = term if total is None else total + term
        outs[0][...] = total[:, :128]
        outs[1][...] = total[:, 128:]

    return call(
        courier,
        ident,
        body,
        list(rows) + list(grads),
        [spec["rows"]] * count + [spec["pair"]] * count,
        [jax.ShapeDtypeStruct((width, width), F32)] * 2,
        [spec["weight"]] * 2,
        [],
        2**34,
    )


def self_backward(courier, ident, queries, grad, keys, values, lse, summand):
    tokens, width = queries.shape
    spec = block_specs(tokens, tokens)

    def body(ins, outs, _):
        q_ref, da_ref, k_ref, v_ref, lse_ref = ins
        dq_ref, dk_ref, dv_ref = outs
        grad_kv, dq_ref[...] = backward_pair(
            q_ref[...],
            da_ref[...],
            k_ref[...],
            v_ref[...],
            causal_probs([lse_ref[0, h : h + 1, :] for h in range(2)]),
            None,
        )
        dk_ref[...] = grad_kv[:, :128]
        dv_ref[...] = grad_kv[:, 128:]

    return call(
        courier,
        ident,
        body,
        [queries, grad, keys, values, lse],
        [spec["col"]] * 4 + [spec["stat"]],
        [jax.ShapeDtypeStruct((tokens, width), BF)] * 3,
        [spec["col"]] * 3,
        [],
        2**33,
        [summand],
    )


def rms_back(values, gain, grad):
    r = lax.rsqrt(jnp.mean(values * values, axis=-1, keepdims=True) + EPSILON)
    u = gain * grad
    back = r * u - values * (r * r * r) * jnp.mean(u * values, axis=-1, keepdims=True)
    return back, jnp.sum(grad * values * r, axis=0, keepdims=True)


def ending(sizes, ident, rows, grads, grad_q, grad_rows, left, two, held, lse, small_in):
    courier = Courier(
        sizes,
        [("line", PLANES - 1, grad_q[-1]), ("return", 0, grad_rows)]
        + [("scatter", 0, value) for value in left],
    )
    courier.lines = list(range(1, PLANES))
    jobs = len(courier.jobs)
    devices = sizes[0] * sizes[1] * sizes[2] * sizes[3]
    keys, width = rows[0].shape
    tokens = two.shape[0]
    share = width // devices
    chunk = 512
    cuts = keys // chunk
    groups = [Resident(sizes, (2 * share, width)) for _ in range(2)]
    groups += [Resident(sizes, (2 * share, 256)) for _ in range(6)]
    small = SmallSum(sizes, (8, width))
    early = [two] + list(held) + list(grad_q[:-1])
    far = list(rows) + list(grads) + early
    counts = (len(far), len(small_in) + 1, jobs, 6, jobs - 1, 4, len(early) - 1, 8, 3, 80, 10)

    def pack(ref, first, second, cols=EVERY):
        lanes = first.shape[1]
        parts = [v.astype(F32).reshape(devices, share, lanes) for v in (first, second)]
        both = jnp.concatenate(parts, axis=1).astype(BF)
        ref[:, :, :, :, :, cols] = both.reshape(tuple(sizes) + both.shape[1:])

    def kernel(*refs):
        far_refs, near, sources, outs, targets, stage, loaded, work, sems, group_refs, rest = (
            split_refs(refs, *counts)
        )
        self_gain, cross_gain, ffn_term, lse_ref = near
        grad_in, *sums, norm_sums = outs
        row_buf, grad_buf, total, load_sems = stage
        dq_got, da_ref, dq1, dk1, dv1, normed_ref, *_ = work
        chunk_sems, early_sems = load_sems, work[6]
        copies = courier.copies(sources, [dq_got] + list(targets), sems)
        courier.greet()
        for copy in copies:
            copy.start()

        def chunk_loads(r, i):
            slot = rem(i, 2)
            where = pl.ds(pl.multiple_of(rem(i, cuts) * chunk, chunk), chunk)
            return [
                pltpu.make_async_copy(
                    far_refs[r].at[where], row_buf.at[slot], chunk_sems.at[slot, 0]
                ),
                pltpu.make_async_copy(
                    far_refs[PLANES + r].at[where], grad_buf.at[slot], chunk_sems.at[slot, 1]
                ),
            ]

        def start_chunk(i):
            for r in range(PLANES):

                @pl.when(lax.div(jnp.int32(i), cuts) == r)
                def _(r=r):
                    for copy in chunk_loads(r, i):
                        copy.start()

        total[...] = jnp.zeros_like(total)
        early_refs = far_refs[2 * PLANES :]
        early_loads = [
            pltpu.make_async_copy(source, target, early_sems.at[n])
            for n, (source, target) in enumerate(zip(early_refs, [grad_in] + list(loaded)))
        ]
        start_chunk(0)
        for copy in early_loads:
            copy.start()

        @pl.loop(0, PLANES * cuts)
        def _(i):
            @pl.when(i + 1 < PLANES * cuts)
            def _():
                start_chunk(i + 1)

            for copy in chunk_loads(0, i):
                copy.wait()
            slot = rem(i, 2)
            total[...] += dot(row_buf[slot], grad_buf[slot], 0, 0)

        bound = [
            one.bind(group_refs[10 * n : 10 * n + 10]) for n, one in enumerate(groups)
        ]
        bits = small.bind(rest)

        @pl.loop(0, PAIRS)
        def _(p):
            at = pl.multiple_of(p * 256, 256)
            pack(
                bound[0].held,
                total[:, pl.ds(at, 128)],
                total[:, pl.ds(at + 128, 128)],
                pl.ds(pl.multiple_of(p * 128, 128), 128),
            )

        bound[0].begin()
        for copy in early_loads:
            copy.wait()
        copies[1].wait()
        x_ref, h1_ref, gco_ref, q_ref, k_ref, v_ref, attn_ref = loaded[:7]
        wq_ref, wk_ref, wv_ref, wo_ref, wc_ref, *dq_refs = loaded[7:]
        grad = dq_got[...].astype(F32)
        for ref in dq_refs:
            grad += ref[...].astype(F32)
        dq_got[...] = grad.astype(BF)
        hidden = h1_ref[...]
        back, cross_norm = rms_back(hidden, cross_gain[...], dot(dq_got[...], wc_ref[...], 1, 1))
        grad_in[...] += back
        dv1[...] = rms(hidden, cross_gain[...]).astype(BF)
        bound[0].after_first()

        @pl.loop(0, 3)
        def _(i):
            cols = pl.ds(pl.multiple_of(i * 256, 256), 256)
            pack(bound[1].held, dot(dv1[...], dq_got[:, cols], 0, 0), gco_ref[:, cols], cols)

        bound[1].begin()
        low_ref = dq_got
        low_ref[...] = grad_in[...].astype(BF)
        da_ref[...] = dot(low_ref[...], wo_ref[...], 1, 1).astype(BF)
        values = x_ref[...].astype(F32)
        normed_ref[...] = rms(values, self_gain[...]).astype(BF)

        for third in range(3):

            @pl.loop(2 * third, 2 * third + 2)
            def _(p):
                cols = pl.ds(pl.multiple_of(p * 128, 128), 128)
                grad_kv, grad_q_p = backward_pair(
                    q_ref[:, cols],
                    da_ref[:, cols],
                    k_ref[:, cols],
                    v_ref[:, cols],
                    causal_probs([lse_ref[p, h : h + 1, :] for h in range(2)]),
                    None,
                )
                dq1[:, cols] = grad_q_p
                dk1[:, cols] = grad_kv[:, :128]
                dv1[:, cols] = grad_kv[:, 128:]

            cols = pl.ds(third * 256, 256)
            near_sum, far_sum = bound[2 + 2 * third], bound[3 + 2 * third]
            normed = normed_ref[...]
            pack(near_sum.held, dot(normed, dq1[:, cols], 0, 0), dot(normed, dk1[:, cols], 0, 0))
            near_sum.begin()
            pack(
                far_sum.held,
                dot(normed, dv1[:, cols], 0, 0),
                dot(attn_ref[...], low_ref[:, cols], 0, 0),
            )
            far_sum.begin()
            if third == 0:
                bound[0].after_second()
                bound[1].after_first()
            if third == 1:
                bound[0].after_third_start()
                bound[1].after_second()
                bound[2].after_first()
                bound[3].after_first()
            if third == 2:
                bound[1].after_third_start()
                bound[2].after_second()
                bound[3].after_second()
                bound[4].after_first()
                bound[5].after_first()
        grad_normed = (
            dot(dq1[...], wq_ref[...], 1, 1)
            + dot(dk1[...], wk_ref[...], 1, 1)
            + dot(dv1[...], wv_ref[...], 1, 1)
        )
        back, self_norm = rms_back(values, self_gain[...], grad_normed)
        grad_in[...] += back
        bits.held[0][...] = jnp.concatenate(
            [self_norm, cross_norm, ffn_term[...], jnp.zeros((5, width), F32)], axis=0
        )
        bits.start(0)
        bound[2].after_third_start()
        bound[3].after_third_start()
        bound[4].after_second()
        bound[5].after_second()
        bound[6].after_first()
        bound[7].after_first()
        bits.advance(0)
        bound[4].after_third_start()
        bound[5].after_third_start()
        bound[6].after_second()
        bound[7].after_second()
        bits.advance(1)
        bound[6].after_third_start()
        bound[7].after_third_start()
        bits.advance(2)
        bound[0].finish(sums[0])
        bound[1].finish(sums[1])
        for n in range(2, 8):
            third, kind = divmod(n - 2, 2)
            bound[n].finish(sums[2 + kind].at[:, pl.ds(third * 256, 256)])
        bits.advance(3, norm_sums)
        for n, copy in enumerate(copies):
            if n != 1:
                copy.wait()

    any_spec = pl.BlockSpec(memory_space=pl.ANY)
    vmem = pl.BlockSpec(memory_space=pltpu.VMEM)
    row = pltpu.VMEM((tokens, width), BF)
    scratch = [
        pltpu.VMEM((2, chunk, width), BF),
        pltpu.VMEM((2, chunk, 2 * width), BF),
        pltpu.VMEM((width, 2 * width), F32),
        pltpu.SemaphoreType.DMA((2, 2)),
    ]
    scratch += [pltpu.VMEM(v.shape, v.dtype) for v in early[1:]]
    scratch += [row] * 6 + [pltpu.SemaphoreType.DMA((len(early),))]
    scratch += [pltpu.SemaphoreType.DMA((1,))] + courier.scratch()
    for one in groups:
        scratch += one.scratch()
    scratch += small.scratch()
    outs = pl.pallas_call(
        kernel,
        out_shape=[jax.ShapeDtypeStruct((tokens, width), F32)]
        + [jax.ShapeDtypeStruct((2 * share, width), F32)] * 4
        + [jax.ShapeDtypeStruct((8, width), F32)]
        + courier.out_shape()[1:],
        in_specs=[any_spec] * len(far) + [vmem] * (len(small_in) + 1) + courier.specs(),
        out_specs=[vmem] * 6 + courier.specs()[1:],
        scratch_shapes=scratch,
        compiler_params=pltpu.CompilerParams(
            vmem_limit_bytes=62 * 2**20, collective_id=ident, has_side_effects=True
        ),
    )(*far, *small_in, lse, *courier.values())
    return outs[0], outs[1:5], outs[5], outs[6:]


def place_kernel(*refs):
    *blocks, out_ref, held, arrive, leave = refs
    z = lax.axis_index("z")
    size = held.shape[1]
    inward = []
    outward = []
    for r, block in enumerate(blocks):
        at = rem(z + r, PLANES) * size
        inward.append(pltpu.make_async_copy(block, held.at[r], arrive.at[r]))
        outward.append(
            pltpu.make_async_copy(held.at[r], out_ref.at[pl.ds(at, size)], leave.at[r])
        )
        inward[r].start()
    for r in range(len(blocks)):
        inward[r].wait()
        outward[r].start()
    for copy in outward:
        copy.wait()


def finish_kernel(*refs):
    blocks = refs[:PLANES]
    left0, got0, left1, got1, out_ref, gate_ref, up_ref, down_ref = refs[PLANES : PLANES + 8]
    held, arrive, leave = refs[PLANES + 8 :]
    z = lax.axis_index("z")
    size = held.shape[1]
    inward = []
    outward = []
    for r, block in enumerate(blocks):
        at = rem(z + r, PLANES) * size
        inward.append(pltpu.make_async_copy(block, held.at[r], arrive.at[r]))
        outward.append(
            pltpu.make_async_copy(held.at[r], out_ref.at[pl.ds(at, size)], leave.at[r])
        )
        inward[r].start()
    for r in range(PLANES):
        inward[r].wait()
        outward[r].start()
    share = gate_ref.shape[0]
    wide = left0[z].astype(F32)
    tall = left1[z].astype(F32)
    for k in range(PLANES - 1):
        wide += got0[k].astype(F32)
        tall += got1[k].astype(F32)
    gate_ref[...] = wide[:share]
    up_ref[...] = wide[share:]
    down_ref[...] = tall
    for copy in outward:
        copy.wait()


def finish(blocks, left0, got0, left1, got1):
    shape = blocks[0].shape
    share, inner = left0.shape[1] // 2, left0.shape[2]
    hbm = pl.BlockSpec(memory_space=pl.ANY)
    vmem = pl.BlockSpec(memory_space=pltpu.VMEM)
    return pl.pallas_call(
        finish_kernel,
        out_shape=[jax.ShapeDtypeStruct((PLANES * shape[0],) + shape[1:], BF)]
        + [jax.ShapeDtypeStruct((share, inner), F32)] * 2
        + [jax.ShapeDtypeStruct(left1.shape[1:], F32)],
        in_specs=[hbm] * PLANES + [vmem] * 4,
        out_specs=[hbm] + [vmem] * 3,
        scratch_shapes=[
            pltpu.VMEM((PLANES,) + shape, BF),
            pltpu.SemaphoreType.DMA((PLANES,)),
            pltpu.SemaphoreType.DMA((PLANES,)),
        ],
        compiler_params=pltpu.CompilerParams(vmem_limit_bytes=VMEM),
    )(*blocks, left0, got0, left1, got1)


def place(blocks):
    shape = blocks[0].shape
    count = len(blocks)
    hbm = pl.BlockSpec(memory_space=pl.ANY)
    return pl.pallas_call(
        place_kernel,
        out_shape=jax.ShapeDtypeStruct((count * shape[0],) + shape[1:], blocks[0].dtype),
        in_specs=[hbm] * count,
        out_specs=hbm,
        scratch_shapes=[
            pltpu.VMEM((count,) + shape, blocks[0].dtype),
            pltpu.SemaphoreType.DMA((count,)),
            pltpu.SemaphoreType.DMA((count,)),
        ],
        compiler_params=pltpu.CompilerParams(vmem_limit_bytes=VMEM),
    )(*blocks)


def norm_apply(values, gain):
    return values * lax.rsqrt(jnp.mean(values * values, axis=-1, keepdims=True) + EPSILON) * gain


def norm_back(values, gain, grad):
    r = lax.rsqrt(jnp.mean(values * values, axis=-1, keepdims=True) + EPSILON)
    u = gain * grad
    dv = r * u - values * (r * r * r) * jnp.mean(u * values, axis=-1, keepdims=True)
    return dv, jnp.sum(grad * values * r, axis=0)


def matmul(left, right):
    return dot(left, right, 1, 0)


def matmul_t(left, right):
    return dot(left, right, 1, 1)


def tmatmul(left, right):
    return dot(left, right, 0, 0)


def on_device(
    sizes,
    decoder_in,
    memory,
    memory_lengths,
    cotangent,
    norm_self,
    self_query,
    self_key,
    self_value,
    self_out,
    norm_cross,
    cross_query,
    cross_key,
    cross_value,
    cross_out,
    norm_ffn,
    ffn_gate,
    ffn_up,
    ffn_down,
):
    devices, positions, width = memory.shape
    plane_size = sizes[1] * sizes[2] * sizes[3]
    z = lax.axis_index("z")

    def flat(blocks):
        return blocks.reshape(plane_size * positions, width)

    def cut(rows):
        return rows.reshape(plane_size, positions, width)

    forward = forward_part(
        sizes,
        0,
        memory,
        jnp.broadcast_to(memory_lengths[None, :], (8, 128)),
        decoder_in[0],
        (norm_self[None], norm_cross[None]),
        (self_query, self_key, self_value, self_out, cross_query),
        cross_key,
        cross_value,
    )
    query_one, key_one, value_one, lse_one, attn_one, hidden_one, _ = forward["saved"]
    queries = forward["queries"]
    rows = {r: flat(forward["rows"][r]) for r in range(PLANES)}

    (
        output,
        attn_two,
        grad_two,
        grad_attn_two,
        stats,
        grad_norm_ffn,
        grad_cross_out,
        *grads_in,
        grad_down,
    ) = middle(
        sizes,
        forward["parts"],
        forward["lses"],
        hidden_one,
        cross_out,
        norm_ffn[None],
        cotangent[0],
        ffn_gate,
        ffn_up,
        ffn_down,
    )
    decoder_out = output[None]
    if len(grads_in) == 2:
        summands = {
            0: [summand_of(sizes, grads_in)],
            1: [grad_down.reshape(tuple(sizes) + grad_down.shape[1:])],
        }
    else:
        summands = {0: [grads_in[0], grad_down]}
    left, got = {}, {}

    grads = {0: grad_attn_two}
    both = {0: stats}
    grad_kv, grad_q, grad_rows, returned = {}, {}, {}, {}
    for r in range(PLANES):
        jobs = []
        if r + 1 < PLANES:
            jobs.append(("line", -(r + 1), grad_attn_two))
            jobs.append(("line", -(r + 1), stats))
        if r >= 1:
            jobs.append(("return", 0, cut(grad_rows[r - 1])))
        if r >= 2:
            jobs.append(("line", r - 1, grad_q[r - 1]))
        (grad_kv[r], grad_q[r], grad_rows[r]), moved = cross_backward(
            Courier(sizes, jobs),
            5 + r,
            r,
            queries[r],
            grads[r],
            forward["keyvals"],
            forward["probs"],
            forward["tops"],
            both[r],
            cross_key,
            cross_value,
            summands.get(r, []),
        )
        moved = list(moved)
        if r in summands:
            for value in moved[len(moved) - len(summands[r]) :]:
                left[len(left)] = value
        if r + 1 < PLANES:
            grads[r + 1], both[r + 1] = moved.pop(0), moved.pop(0)
        if r >= 1:
            returned[r - 1] = moved.pop(0)
        if r >= 2:
            grad_q[r - 1] = moved.pop(0)
    last = PLANES - 1
    part = width // devices
    if part % 8 == 0:
        decoder_in_grad, sums, norm_sums, moved = ending(
            sizes,
            9,
            [rows[r] for r in range(PLANES)],
            [grad_kv[r] for r in range(PLANES)],
            [grad_q[r] for r in range(PLANES)],
            cut(grad_rows[last]),
            [left[0], left[1]],
            grad_two,
            (decoder_in[0], hidden_one, grad_cross_out, query_one, key_one, value_one, attn_one)
            + (self_query, self_key, self_value, self_out, cross_query),
            lse_one,
            (norm_self[None], norm_cross[None], grad_norm_ffn),
        )
        returned[last], got[0], got[1] = moved
        memory_grad, sum_gate, sum_up, sum_down = finish(
            [returned[r] for r in range(PLANES)], left[0], got[0], left[1], got[1]
        )
        here = lax.axis_index(ALL) * part
        norm_self_sum, norm_cross_sum, norm_ffn_sum = (
            lax.dynamic_slice_in_dim(norm_sums[n], here, part) for n in range(3)
        )
        return (
            decoder_out,
            decoder_in_grad[None],
            memory_grad,
            norm_self_sum,
            sums[2][:part],
            sums[2][part:],
            sums[3][:part],
            sums[3][part:],
            norm_cross_sum,
            sums[1][:part],
            sums[0][:part],
            sums[0][part:],
            sums[1][part:],
            norm_ffn_sum,
            sum_gate,
            sum_up,
            sum_down,
        )

    jobs = [
        ("line", last, grad_q[last]),
        ("return", 0, cut(grad_rows[last])),
        ("scatter", 0, left[0]),
        ("scatter", 0, left[1]),
    ]
    (grad_cross_key, grad_cross_value), (grad_q[last], returned[last], got[0], got[1]) = weight_terms(
        Courier(sizes, jobs),
        9,
        [rows[r] for r in range(PLANES)],
        [grad_kv[r] for r in range(PLANES)],
    )
    memory_grad = place([returned[r] for r in range(PLANES)])

    inputs = decoder_in[0].astype(F32)
    normed_one = norm_apply(inputs, norm_self).astype(BF)
    normed_two = norm_apply(hidden_one, norm_cross).astype(BF)
    grad_q_two = sum(grad_q[r].astype(F32) for r in range(PLANES)).astype(BF)
    grad_cross_query = tmatmul(normed_two, grad_q_two)
    grad_normed_two = matmul_t(grad_q_two, cross_query)
    back_one, grad_norm_cross = norm_back(hidden_one, norm_cross, grad_normed_two)
    grad_one = grad_two + back_one
    branch_one = grad_one.astype(BF)
    grad_self_out = tmatmul(attn_one, branch_one)
    grad_attn_one = matmul_t(branch_one, self_out).astype(BF)
    (grad_q_one, grad_k_one, grad_v_one), (cross_left,) = self_backward(
        Courier(sizes, []),
        10,
        query_one,
        grad_attn_one,
        key_one,
        value_one,
        lse_one,
        summand_of(sizes, (grad_cross_key, grad_cross_value)),
    )
    grad_normed_one = (
        matmul_t(grad_q_one, self_query)
        + matmul_t(grad_k_one, self_key)
        + matmul_t(grad_v_one, self_value)
    )
    back_in, grad_norm_self = norm_back(inputs, norm_self, grad_normed_one)
    decoder_in_grad = (grad_one + back_in)[None]
    share_of_norms = width // devices
    norms = jnp.stack(
        [g.reshape(devices, share_of_norms) for g in (grad_norm_self, grad_norm_cross, grad_norm_ffn[0])],
        axis=1,
    ).reshape(devices, 1, 3 * share_of_norms)
    norms = jnp.pad(norms, ((0, 0), (0, 15), (0, 256 - 3 * share_of_norms)))
    (cross_got,), sums = reduce_all(
        sizes,
        11,
        [
            norms.astype(BF).reshape(tuple(sizes) + norms.shape[1:]),
            summand_of(sizes, (grad_cross_query, grad_cross_out.astype(F32))),
            summand_of(sizes, (tmatmul(normed_one, grad_q_one), tmatmul(normed_one, grad_k_one))),
            summand_of(sizes, (tmatmul(normed_one, grad_v_one), grad_self_out)),
        ],
        [cross_left],
    )
    norm_sums = sums[0][0, : 3 * share_of_norms].reshape(3, share_of_norms)
    gate_up = over_z(left[0], got[0])
    cross_kv = over_z(cross_left, cross_got)
    part = share_of_norms
    return (
        decoder_out,
        decoder_in_grad,
        memory_grad,
        norm_sums[0],
        sums[2][:part],
        sums[2][part:],
        sums[3][:part],
        sums[3][part:],
        norm_sums[1],
        sums[1][:part],
        cross_kv[:part],
        cross_kv[part:],
        sums[1][part:],
        norm_sums[2],
        gate_up[:part],
        gate_up[part:],
        over_z(left[1], got[1]),
    )


def solution(mesh):
    dp, seq = mesh.devices.shape
    cores = 2
    lines = dp // PLANES
    split = Mesh(mesh.devices.reshape(PLANES, lines, seq // cores, cores), ALL)
    sizes = split.devices.shape
    first = P(ALL)
    middle = P(None, ALL)
    whole = P()
    return jax.shard_map(
        functools.partial(on_device, sizes),
        mesh=split,
        in_specs=(first, middle, first, first) + (whole,) * 14,
        out_specs=(first, first, middle) + (first,) * 14,
        check_vma=False,
    )
```

```python
import functools

import jax
import jax.numpy as jnp
from jax import lax
from jax.experimental import pallas as pl
from jax.experimental.pallas import tpu as pltpu
from jax.sharding import Mesh
from jax.sharding import PartitionSpec as P

H = 12
HD = 64
PAIRS = 6
PLANES = 4
EPSILON = 1e-06
MASKED = -1e30
VMEM = 56 * 2**20
BF = jnp.bfloat16
F32 = jnp.float32
ALL = ("z", "y", "x", "c")
PLANE = ("y", "x", "c")
EVERY = slice(None)


def dot(left, right, left_dim, right_dim):
    return lax.dot_general(
        left, right, (((left_dim,), (right_dim,)), ((), ())), preferred_element_type=F32
    )


def lane_masks():
    lane = lax.broadcasted_iota(jnp.int32, (1, 2 * HD), 1)
    low = jnp.where(lane < HD, 1.0, 0.0)
    first = jnp.where(lane == HD, 1.0, 0.0)
    second = jnp.where(lane == 0, 1.0, 0.0)
    low, high, first, second = (
        v.astype(BF) for v in (low, 1.0 - low, first, second)
    )
    return ((low, high, first), (high, low, second))


def causal_mask(scores):
    key = lax.broadcasted_iota(jnp.int32, scores.shape, 0)
    query = lax.broadcasted_iota(jnp.int32, scores.shape, 1)
    return jnp.where(key <= query, scores, MASKED)


def rem(value, size):
    return lax.rem(value, size)


class Courier:
    def __init__(self, sizes, jobs):
        self.sizes = sizes
        self.jobs = jobs
        self.plane = sizes[1] * sizes[2] * sizes[3]
        self.in_plane = any(job[0] in ("fetch", "return") for job in jobs)
        self.lines = [job[1] for job in jobs if job[0] == "line"]
        for job in jobs:
            if job[0] == "scatter":
                self.lines += list(range(1, PLANES))

    def out_shape(self):
        shapes = []
        for kind, _, value in self.jobs:
            shape = value.shape
            if kind == "fetch":
                shape = (self.plane,) + shape[1:]
            elif kind == "scatter":
                shape = (PLANES - 1,) + shape[1:]
            shapes.append(jax.ShapeDtypeStruct(shape, value.dtype))
        return shapes

    def specs(self):
        return [pl.BlockSpec(memory_space=pl.ANY)] * len(self.jobs)

    def values(self):
        return [job[2] for job in self.jobs]

    def scratch(self):
        each = {"line": 1, "scatter": PLANES - 1}
        count = max(1, sum(each.get(job[0], self.plane - 1) for job in self.jobs))
        own = max(1, sum(job[0] in ("fetch", "return") for job in self.jobs))
        return [pltpu.SemaphoreType.DMA((n,)) for n in (count, count, own)]

    def params(self, ident):
        return pltpu.CompilerParams(
            vmem_limit_bytes=VMEM, collective_id=ident, has_side_effects=True
        )

    def me(self):
        _, _, x_size, c_size = self.sizes
        y, x, c = (lax.axis_index(name) for name in PLANE)
        return (y * x_size + x) * c_size + c

    def along(self, offset):
        return {"z": rem(lax.axis_index("z") + (offset + PLANES), PLANES)}

    def across(self, offset):
        _, _, x_size, c_size = self.sizes
        other = rem(self.me() + offset, self.plane)
        line = lax.div(other, c_size)
        return other, {"y": lax.div(line, x_size), "x": rem(line, x_size), "c": rem(other, c_size)}

    def greet(self):
        barrier = pltpu.get_barrier_semaphore()
        count = 0
        if self.in_plane:
            for k in range(1, self.plane):
                _, device = self.across(k)
                pl.semaphore_signal(
                    barrier, inc=1, device_id=device, device_id_type=pl.DeviceIdType.MESH
                )
                count += 1
        for offset in self.lines:
            pl.semaphore_signal(
                barrier,
                inc=1,
                device_id=self.along(-offset),
                device_id_type=pl.DeviceIdType.MESH,
            )
            count += 1
        pl.semaphore_wait(barrier, count)

    def copies(self, sources, targets, sems):
        send, receive, own = sems
        remote = []
        local = []

        def add(source, target, device):
            n = len(remote)
            remote.append(
                pltpu.make_async_remote_copy(
                    src_ref=source,
                    dst_ref=target,
                    send_sem=send.at[n],
                    recv_sem=receive.at[n],
                    device_id=device,
                    device_id_type=pl.DeviceIdType.MESH,
                )
            )

        me = self.me()
        for (kind, offset, _), source, target in zip(self.jobs, sources, targets):
            if kind == "line":
                add(source, target, self.along(offset))
                continue
            if kind == "scatter":
                for k in range(1, PLANES):
                    there = rem(lax.axis_index("z") + k, PLANES)
                    add(source.at[there], target.at[k - 1], self.along(k))
                continue
            base = 0
            if kind == "fetch":
                base = rem(lax.axis_index("z") + offset, PLANES) * self.plane
            for k in range(1, self.plane):
                other, device = self.across(k)
                add(source.at[base + other], target.at[me], device)
            local.append(
                pltpu.make_async_copy(source.at[base + me], target.at[me], own.at[len(local)])
            )
        return local + remote

    def start(self, sources, targets, sems):
        self.greet()
        for copy in self.copies(sources, targets, sems):
            copy.start()

    def wait(self, sources, targets, sems):
        for copy in self.copies(sources, targets, sems):
            copy.wait()


class Reducer:
    def __init__(self, sizes, shape):
        self.sizes = sizes
        self.rows, self.lanes = shape[-2:]
        self.half = self.lanes // 2

    def scratch(self):
        z, y, x, _ = self.sizes
        r, w, h = self.rows, self.lanes, self.half
        crossing = x + y - 2
        return [
            pltpu.VMEM((z, y, x, r, w), BF),
            pltpu.VMEM((z, y, x, r, w), BF),
            pltpu.VMEM((x - 1, z, y, r, h), BF),
            pltpu.VMEM((y - 1, z, x, r, h), BF),
            pltpu.VMEM((y - 1, z, r, h), BF),
            pltpu.VMEM((x - 1, z, r, h), BF),
            pltpu.SemaphoreType.DMA((1,)),
            pltpu.SemaphoreType.DMA((1 + 2 * crossing,)),
            pltpu.SemaphoreType.DMA((1 + 2 * crossing,)),
        ]

    def bind(self, source, refs):
        self.source = source
        self.held, self.got0, self.got1x, self.got1y, self.got2y, self.got2x = refs[:6]
        self.local, self.send, self.receive = refs[6:]
        self.z, self.y, self.x, self.c = (lax.axis_index(name) for name in ALL)
        return self

    def index(self, z, y, x, lanes):
        return (z, y, x, EVERY, lanes)

    def slab(self, z, y, x, lanes):
        return self.held.at[self.index(z, y, x, lanes)]

    given = slab

    def remote(self, n, source, target, device):
        return pltpu.make_async_remote_copy(
            src_ref=source,
            dst_ref=target,
            send_sem=self.send.at[n],
            recv_sem=self.receive.at[n],
            device_id=device,
            device_id_type=pl.DeviceIdType.MESH,
        )

    def first(self):
        other = 1 - self.c
        return [
            pltpu.make_async_copy(self.source.at[:, :, :, self.c], self.held, self.local.at[0]),
            self.remote(0, self.source.at[:, :, :, other], self.got0, {"c": other}),
        ]

    def second(self):
        _, y_size, x_size, _ = self.sizes
        left, right = pl.ds(0, self.half), pl.ds(self.half, self.half)
        copies = []
        for k in range(1, x_size):
            there = rem(self.x + k, x_size)
            copies.append((self.given(EVERY, EVERY, there, left), self.got1x.at[k - 1], {"x": there}))
        for k in range(1, y_size):
            there = rem(self.y + k, y_size)
            copies.append((self.given(EVERY, there, EVERY, right), self.got1y.at[k - 1], {"y": there}))
        return [self.remote(1 + n, *copy) for n, copy in enumerate(copies)]

    def third(self):
        _, y_size, x_size, _ = self.sizes
        left, right = pl.ds(0, self.half), pl.ds(self.half, self.half)
        at = 1 + x_size + y_size - 2
        copies = []
        for k in range(1, y_size):
            there = rem(self.y + k, y_size)
            copies.append(
                (self.slab(EVERY, there, self.x, left), self.got2y.at[k - 1], {"y": there})
            )
        for k in range(1, x_size):
            there = rem(self.x + k, x_size)
            copies.append(
                (self.slab(EVERY, self.y, there, right), self.got2x.at[k - 1], {"x": there})
            )
        return [self.remote(at + n, *copy) for n, copy in enumerate(copies)]

    def begin(self):
        for copy in self.first():
            copy.start()

    def after_first(self):
        for copy in self.first():
            copy.wait()

        @pl.loop(0, self.sizes[0])
        def _(z):
            at = self.index(z, EVERY, EVERY, EVERY)
            self.held[at] = (self.held[at].astype(F32) + self.got0[z].astype(F32)).astype(BF)

        for copy in self.second():
            copy.start()

    def after_second(self):
        _, y_size, x_size, _ = self.sizes
        for copy in self.second():
            copy.wait()
        h = self.half

        @pl.loop(0, self.sizes[0])
        def _(z):
            for y in range(y_size):
                at = self.index(z, y, self.x, pl.ds(0, h))
                total = self.held[at].astype(F32)
                for k in range(x_size - 1):
                    total += self.got1x[k, z, y].astype(F32)
                self.held[at] = total.astype(BF)
            for x in range(x_size):
                at = self.index(z, self.y, x, pl.ds(h, h))
                total = self.held[at].astype(F32)
                for k in range(y_size - 1):
                    total += self.got1y[k, z, x].astype(F32)
                self.held[at] = total.astype(BF)

        for copy in self.third():
            copy.start()

    def after_third(self, out_ref):
        _, y_size, x_size, _ = self.sizes
        for copy in self.third():
            copy.wait()
        h = self.half

        @pl.loop(0, self.sizes[0])
        def _(z):
            total = self.held[self.index(z, self.y, self.x, pl.ds(0, h))].astype(F32)
            for k in range(y_size - 1):
                total += self.got2y[k, z].astype(F32)
            out_ref[z, :, :h] = total.astype(BF)
            total = self.held[self.index(z, self.y, self.x, pl.ds(h, h))].astype(F32)
            for k in range(x_size - 1):
                total += self.got2x[k, z].astype(F32)
            out_ref[z, :, h:] = total.astype(BF)


class Halved(Reducer):
    def scratch(self):
        z, y, x, _ = self.sizes
        r, w, h = self.rows, self.lanes, self.half
        crossing = x + y - 2
        return [
            pltpu.VMEM((z, y, x, r, w), BF),
            pltpu.VMEM((x - 1, z, y, r, h), BF),
            pltpu.VMEM((y - 1, z, x, r, h), BF),
            pltpu.VMEM((y - 1, z, r, h), BF),
            pltpu.VMEM((x - 1, z, r, h), BF),
            pltpu.SemaphoreType.DMA((1,)),
            pltpu.SemaphoreType.DMA((1 + 2 * crossing,)),
            pltpu.SemaphoreType.DMA((1 + 2 * crossing,)),
        ]

    def bind(self, source, refs):
        self.source = source
        self.held, self.got1x, self.got1y, self.got2y, self.got2x = refs[:5]
        self.local, self.send, self.receive = refs[5:]
        self.z, self.y, self.x, self.c = (lax.axis_index(name) for name in ALL)
        return self

    def given(self, z, y, x, lanes):
        return self.source.at[self.index(z, y, x, lanes)]

    def first(self):
        return [pltpu.make_async_copy(self.source, self.held, self.local.at[0])]

    def begin(self):
        for copy in self.first() + self.second():
            copy.start()

    def after_first(self):
        pass

    def after_second(self):
        for copy in self.first():
            copy.wait()
        super().after_second()


class Resident(Reducer):
    def scratch(self):
        z, y, x, c = self.sizes
        r, w, h = self.rows, self.lanes, self.half
        count = 1 + 2 * (x + y - 2) + z - 1
        return [
            pltpu.VMEM((z, y, x, c, r, w), BF),
            pltpu.VMEM((z, y, x, r, w), BF),
            pltpu.VMEM((x - 1, z, y, r, h), BF),
            pltpu.VMEM((y - 1, z, x, r, h), BF),
            pltpu.VMEM((y - 1, z, r, h), BF),
            pltpu.VMEM((x - 1, z, r, h), BF),
            pltpu.VMEM((z, r, w), BF),
            pltpu.VMEM((z - 1, r, w), BF),
            pltpu.SemaphoreType.DMA((count,)),
            pltpu.SemaphoreType.DMA((count,)),
        ]

    def bind(self, refs):
        self.held, self.got0, self.got1x, self.got1y, self.got2y, self.got2x = refs[:6]
        self.left, self.got3, self.send, self.receive = refs[6:]
        self.z, self.y, self.x, self.c = (lax.axis_index(name) for name in ALL)
        return self

    def index(self, z, y, x, lanes):
        return (z, y, x, self.c, EVERY, lanes)

    def first(self):
        other = 1 - self.c
        return [self.remote(0, self.held.at[:, :, :, other], self.got0, {"c": other})]

    def fourth(self):
        _, y_size, x_size, _ = self.sizes
        at = 1 + 2 * (x_size + y_size - 2)
        copies = []
        for k in range(1, PLANES):
            there = rem(self.z + k, PLANES)
            copies.append(
                self.remote(at + k - 1, self.left.at[there], self.got3.at[k - 1], {"z": there})
            )
        return copies

    def after_third_start(self):
        self.after_third(self.left)
        for copy in self.fourth():
            copy.start()

    def finish(self, out_ref):
        for copy in self.fourth():
            copy.wait()
        total = self.left[self.z].astype(F32)
        for k in range(PLANES - 1):
            total += self.got3[k].astype(F32)
        out_ref[...] = total


class SmallSum:
    def __init__(self, sizes, shape):
        self.shape = shape
        self.steps = list(zip(("c", "x", "y", "z"), (sizes[3], sizes[2], sizes[1], sizes[0])))

    def scratch(self):
        count = sum(n - 1 for _, n in self.steps)
        return (
            [pltpu.VMEM(self.shape, F32) for _ in range(4)]
            + [pltpu.VMEM((n - 1,) + self.shape, F32) for _, n in self.steps]
            + [pltpu.SemaphoreType.DMA((count,))] * 2
        )

    def bind(self, refs):
        self.held, self.got = refs[:4], refs[4:8]
        self.send, self.receive = refs[8:]
        return self

    def copies(self, step):
        axis, n = self.steps[step]
        at = sum(m - 1 for _, m in self.steps[:step])
        me = lax.axis_index(axis)
        return [
            pltpu.make_async_remote_copy(
                src_ref=self.held[step],
                dst_ref=self.got[step].at[k - 1],
                send_sem=self.send.at[at + k - 1],
                recv_sem=self.receive.at[at + k - 1],
                device_id={axis: rem(me + k, n)},
                device_id_type=pl.DeviceIdType.MESH,
            )
            for k in range(1, n)
        ]

    def start(self, step):
        for copy in self.copies(step):
            copy.start()

    def advance(self, step, out_ref=None):
        for copy in self.copies(step):
            copy.wait()
        total = self.held[step][...]
        for k in range(self.steps[step][1] - 1):
            total += self.got[step][k]
        if step < 3:
            self.held[step + 1][...] = total
            self.start(step + 1)
        else:
            out_ref[...] = total


def forward_pair(queries, keys, values, bias):
    masks = lane_masks()
    all_scores = []
    for mine, other, one in masks:
        if bias is None:
            all_scores.append(causal_mask(dot(keys, queries * mine, 1, 1)))
        else:
            all_scores.append(dot(keys * mine + bias * one, queries * mine + one, 1, 1))
    parts = []
    stats = []
    held = []
    for h in range(2):
        mine, other, _ = masks[h]
        scores = all_scores[h]
        row_max = jnp.max(scores, axis=0, keepdims=True)
        probs = jnp.exp(scores - row_max).astype(BF)
        both = dot(values * mine + other, probs, 0, 0)
        halves = (both[:HD], both[HD:])
        total = halves[1 - h]
        parts.append(halves[h] / total)
        stats.append((row_max + jnp.log(total[0:1]), row_max))
        held.append(probs)
    return jnp.concatenate(parts, axis=0).T.astype(BF), stats, held


def backward_pair(queries, grad, keys, values, probs_of, delta):
    grad_k = None
    grad_v = None
    grad_q = []
    for h, (mine, other, one) in enumerate(lane_masks()):
        query_h = queries * mine
        grad_h = grad * mine
        probs = probs_of(h, keys, query_h)
        grad_p = dot(values, grad_h, 1, 1)
        if delta is None:
            delta_h = jnp.sum(probs * grad_p, axis=0, keepdims=True)
        else:
            delta_h = delta[h]
        grad_s = (probs * (grad_p - delta_h)).astype(BF)
        term_v = dot(probs.astype(BF), grad_h, 1, 0)
        term_k = dot(grad_s, query_h, 1, 0)
        grad_v = term_v if grad_v is None else grad_v + term_v
        grad_k = term_k if grad_k is None else grad_k + term_k
        grad_q.append(dot(keys, grad_s, 0, 0)[h * HD : (h + 1) * HD])
    grad_kv = jnp.concatenate([grad_k, grad_v], axis=1).astype(BF)
    return grad_kv, jnp.concatenate(grad_q, axis=0).T.astype(BF)


def causal_probs(lse):
    return lambda h, keys, query: jnp.exp(causal_mask(dot(keys, query, 1, 1)) - lse[h])


def key_bias(keys, lens):
    row = lax.broadcasted_iota(jnp.int32, (keys, 128), 0) + lax.axis_index("z") * keys
    return jnp.where(row < lens[0:1, :], 0.0, MASKED).astype(BF)


def split_refs(refs, *counts):
    groups = []
    at = 0
    for count in counts:
        groups.append(refs[at : at + count])
        at += count
    return groups


def carried(courier, reducers, body):
    jobs = len(courier.jobs)
    sums = len(reducers)
    parts = [len(one.scratch()) for one in reducers]

    def kernel(ins, outs, scratch, refs):
        own_in, sources, summands, own_out, targets, results, own_scratch, sems, rest = split_refs(
            refs, ins, jobs, sums, outs, jobs, sums, scratch, 3, sum(parts)
        )
        step = pl.program_id(0)
        work = split_refs(rest, *parts)

        def bound():
            return [one.bind(value, refs) for one, value, refs in zip(reducers, summands, work)]

        @pl.when(step == 0)
        def _():
            courier.start(sources, targets, sems)
            for one in bound():
                one.begin()

        body(own_in, own_out, own_scratch)

        if sums:

            @pl.when(step == 1)
            def _():
                for one in bound():
                    one.after_first()

            @pl.when(step == 3)
            def _():
                for one in bound():
                    one.after_second()

        @pl.when(step == PAIRS - 1)
        def _():
            for one, result in zip(bound(), results):
                one.after_third(result)
            courier.wait(sources, targets, sems)

    return kernel


def call(courier, ident, body, args, in_specs, out_shape, out_specs, scratch, flops, summands=()):
    if summands:
        courier.in_plane = True
    reducers = [
        (Halved if value.ndim == 5 else Reducer)(courier.sizes, value.shape) for value in summands
    ]
    shapes = [(PLANES,) + value.shape[-2:] for value in summands]
    kernel = carried(courier, reducers, body)
    counts = (len(args), len(out_shape), len(scratch))
    outs = pl.pallas_call(
        lambda *refs: kernel(*counts, refs),
        grid=(PAIRS,),
        out_shape=out_shape
        + courier.out_shape()
        + [jax.ShapeDtypeStruct(shape, BF) for shape in shapes],
        in_specs=in_specs + courier.specs() + [pl.BlockSpec(memory_space=pl.ANY)] * len(shapes),
        out_specs=out_specs
        + courier.specs()
        + [pl.BlockSpec(shape, lambda p: (0, 0, 0)) for shape in shapes],
        scratch_shapes=scratch
        + courier.scratch()
        + [ref for one in reducers for ref in one.scratch()],
        compiler_params=courier.params(ident),
        cost_estimate=pl.CostEstimate(flops=flops, bytes_accessed=2**24, transcendentals=2**20),
    )(*args, *courier.values(), *summands)
    return outs[: len(out_shape)], outs[len(out_shape) :]


def reduce_all(sizes, ident, summands, scattered):
    courier = Courier(sizes, [("scatter", 0, value) for value in scattered])
    courier.in_plane = True
    courier.lines += list(range(1, PLANES))
    jobs = len(scattered)
    count = len(summands)
    reducers = [Reducer(sizes, value.shape) for value in summands]
    shapes = [value.shape[-2:] for value in summands]

    def kernel(*refs):
        sources, arrays, targets, results, sems, rest = split_refs(
            refs, jobs, count, jobs, count, 3, len(refs) - 2 * jobs - 2 * count - 3
        )
        courier.start(sources, targets, sems)
        bound = []
        last = []
        for n in range(count):
            refs_n = rest[13 * n : 13 * n + 13]
            bound.append(reducers[n].bind(arrays[n], refs_n[:9]))
            last.append(refs_n[9:])

        def leave(n):
            left, got, send, receive = last[n]
            copies = []
            for k in range(1, PLANES):
                copies.append(
                    pltpu.make_async_remote_copy(
                        src_ref=left.at[rem(lax.axis_index("z") + k, PLANES)],
                        dst_ref=got.at[k - 1],
                        send_sem=send.at[k - 1],
                        recv_sem=receive.at[k - 1],
                        device_id=courier.along(k),
                        device_id_type=pl.DeviceIdType.MESH,
                    )
                )
            return copies

        for one in bound:
            one.begin()
        for one in bound:
            one.after_first()
        for one in bound:
            one.after_second()
        for n, one in enumerate(bound):
            one.after_third(last[n][0])
            for copy in leave(n):
                copy.start()
        for n in range(count):
            for copy in leave(n):
                copy.wait()
            left, got = last[n][:2]
            total = left[lax.axis_index("z")].astype(F32)
            for k in range(PLANES - 1):
                total += got[k].astype(F32)
            results[n][...] = total
        courier.wait(sources, targets, sems)

    scratch = []
    for n in range(count):
        scratch += reducers[n].scratch() + [
            pltpu.VMEM((PLANES,) + shapes[n], BF),
            pltpu.VMEM((PLANES - 1,) + shapes[n], BF),
            pltpu.SemaphoreType.DMA((PLANES - 1,)),
            pltpu.SemaphoreType.DMA((PLANES - 1,)),
        ]
    outs = pl.pallas_call(
        kernel,
        out_shape=courier.out_shape() + [jax.ShapeDtypeStruct(shape, F32) for shape in shapes],
        in_specs=courier.specs() + [pl.BlockSpec(memory_space=pl.ANY)] * count,
        out_specs=courier.specs() + [pl.BlockSpec(memory_space=pltpu.VMEM)] * count,
        scratch_shapes=courier.scratch() + scratch,
        compiler_params=courier.params(ident),
    )(*courier.values(), *summands)
    return outs[:jobs], outs[jobs:]


def summand_of(sizes, arrays):
    devices = sizes[0] * sizes[1] * sizes[2] * sizes[3]
    parts = [a.reshape(devices, a.shape[0] // devices, a.shape[1]) for a in arrays]
    joined = parts[0] if len(parts) == 1 else jnp.concatenate(parts, axis=1)
    return joined.astype(BF).reshape(tuple(sizes) + joined.shape[1:])


def over_z(left, got):
    own = lax.dynamic_index_in_dim(left, lax.axis_index("z"), 0, keepdims=False)
    return own.astype(F32) + jnp.sum(got.astype(F32), axis=0)


def block_specs(tokens, keys):
    return dict(
        col=pl.BlockSpec((tokens, 128), lambda p: (0, p)),
        pair=pl.BlockSpec((keys, 256), lambda p: (0, p)),
        rows=pl.BlockSpec((keys, H * HD), lambda p: (0, 0)),
        weight=pl.BlockSpec((H * HD, 128), lambda p: (0, p)),
        stat=pl.BlockSpec((1, 2, tokens), lambda p: (p, 0, 0)),
    )


def rms(values, gain):
    r = lax.rsqrt(jnp.mean(values * values, axis=-1, keepdims=True) + EPSILON)
    return values * r * gain


ORDER = (1, 2, 3, 0)


def forward_part(sizes, ident, memory, lens, inputs, gains, weights, key_weight, value_weight):
    tokens, width = inputs.shape
    positions = memory.shape[1]
    plane = sizes[1] * sizes[2] * sizes[3]
    keys = plane * positions
    rows = jax.ShapeDtypeStruct((tokens, width), BF)
    wide = jax.ShapeDtypeStruct((tokens, width), F32)
    stat = jax.ShapeDtypeStruct((PAIRS, 2, tokens), F32)
    near = range(1, PLANES)
    jobs = [("fetch", r, memory) for r in ORDER]
    jobs += [("line", -r, lens) for r in near] + [("line", -r, rows) for r in near]
    jobs += [("line", r, rows) for r in near] + [("line", r, stat) for r in near]
    courier = Courier(sizes, jobs)
    courier.lines = list(near)
    count = PLANES * PAIRS

    def kernel(*refs):
        ins, sources, outs, parts, targets, work, sems = split_refs(refs, 11, 1, 8, 4, 13, 7, 3)
        x_ref, self_gain, cross_gain, wq_ref, wk_ref, wv_ref, wo_ref, wc_ref = ins[:8]
        lens_ref, key_ref, value_ref = ins[8:]
        (memory_ref,) = sources
        q_ref, k_ref, v_ref, lse_ref, attn_ref, hidden_ref, query_ref, top_ref = outs
        part_ref, part_lse_ref, kv_ref, probs_ref = parts
        row_buf, query_buf, out_buf, lse_buf, lens_buf, near_lens, load_sems = work
        copies = courier.copies(
            [memory_ref] * PLANES
            + [lens_ref] * 3
            + [query_ref] * 3
            + [out_buf.at[n] for n in range(3)]
            + [lse_buf.at[n] for n in range(3)],
            list(targets[:4])
            + [near_lens.at[n] for n in range(3)]
            + list(targets[4:]),
            sems,
        )
        own, remote = copies[:PLANES], copies[PLANES:]
        far = plane - 1
        lines = remote[PLANES * far :]
        lens_lines, query_lines, out_lines, lse_lines = split_refs(lines, 3, 3, 3, 3)
        step = pl.program_id(0)
        me = courier.me()

        def start_fetch(n):
            for copy in [own[n]] + remote[n * far : n * far + far]:
                copy.start()

        @pl.when(step == 0)
        def _():
            courier.greet()
            start_fetch(0)
            for copy in lens_lines:
                copy.start()
            values = x_ref[...].astype(F32)
            normed = rms(values, self_gain[...]).astype(BF)
            q_ref[...] = dot(normed, wq_ref[...], 1, 0).astype(BF)
            k_ref[...] = dot(normed, wk_ref[...], 1, 0).astype(BF)
            v_ref[...] = dot(normed, wv_ref[...], 1, 0).astype(BF)

            @pl.loop(0, PAIRS)
            def _(p):
                cols = pl.ds(pl.multiple_of(p * 128, 128), 128)
                out, stats, _ = forward_pair(q_ref[:, cols], k_ref[:, cols], v_ref[:, cols], None)
                attn_ref[:, cols] = out
                for h in range(2):
                    lse_ref[p, h : h + 1, :] = stats[h][0]

            hidden = values + dot(attn_ref[...], wo_ref[...], 1, 0)
            hidden_ref[...] = hidden
            normed = rms(hidden, cross_gain[...]).astype(BF)
            query_ref[...] = dot(normed, wc_ref[...], 1, 0).astype(BF)
            query_lines[0].start()

        for n, r in enumerate(ORDER):

            @pl.when(step == n * PAIRS)
            def _(n=n, r=r):
                loads = []

                def load(block):
                    at = pl.ds(pl.multiple_of(block * positions, positions), positions)
                    copy = pltpu.make_async_copy(
                        targets[n].at[block], row_buf.at[at], load_sems.at[len(loads)]
                    )
                    copy.start()
                    loads.append(copy)

                own[n].wait()
                load(me)
                for k in range(1, plane):
                    remote[n * far + k - 1].wait()
                    load(rem(me + (plane - k), plane))
                if n + 1 < PLANES:
                    start_fetch(n + 1)
                if r > 0:
                    query_lines[r - 1].wait()
                    copy = pltpu.make_async_copy(
                        targets[3 + r], query_buf, load_sems.at[plane]
                    )
                    copy.start()
                    if r + 1 < PLANES:
                        query_lines[r].start()
                    lens_lines[r - 1].wait()
                    lens_buf[...] = near_lens[r - 1]
                    copy.wait()
                else:
                    query_buf[...] = query_ref[...]
                    lens_buf[...] = lens_ref[...]
                for copy in loads:
                    copy.wait()

        phase = lax.div(step, PAIRS)
        p = rem(step, PAIRS)
        cols = pl.ds(pl.multiple_of(p * 128, 128), 128)
        both = jnp.concatenate([key_ref[...], value_ref[...]], axis=1)
        kv_ref[...] = dot(row_buf[...], both, 1, 0).astype(BF)
        bias = key_bias(keys, lens_buf[...])
        out, stats, held = forward_pair(query_buf[:, cols], kv_ref[:, :128], kv_ref[:, 128:], bias)
        out_buf[phase, :, cols] = out
        for h in range(2):
            probs_ref[h] = held[h]
            lse_buf[phase, p, h : h + 1, :] = stats[h][0]
            top_ref[phase, p, h : h + 1, :] = stats[h][1]

        for n, r in enumerate(ORDER[:-1]):

            @pl.when(step == n * PAIRS + PAIRS - 1)
            def _(r=r):
                out_lines[r - 1].start()
                lse_lines[r - 1].start()

        @pl.when(step == count - 1)
        def _():
            part_ref[...] = out_buf[PLANES - 1]
            part_lse_ref[...] = lse_buf[PLANES - 1]
            for copy in out_lines + lse_lines:
                copy.wait()

    once = pl.Buffered(1)

    def fixed(*shape):
        return pl.BlockSpec(shape, lambda t: (0,) * len(shape), pipeline_mode=once)

    def out_fixed(*shape):
        return pl.BlockSpec(shape, lambda t: (0,) * len(shape))

    def where(t):
        return rem(lax.div(t, PAIRS) + 1, PLANES), rem(t, PAIRS)

    square = fixed(width, width)
    weight = pl.BlockSpec((width, 128), lambda t: (0, rem(t, PAIRS)))
    hbm = pl.BlockSpec(memory_space=pl.ANY)
    flat = out_fixed(tokens, width)
    flat_stat = out_fixed(PAIRS, 2, tokens)
    shapes = courier.out_shape()
    outs = pl.pallas_call(
        kernel,
        grid=(count,),
        out_shape=[rows, rows, rows, stat, rows, wide, rows]
        + [jax.ShapeDtypeStruct((PLANES, PAIRS, 2, tokens), F32), rows, stat]
        + [
            jax.ShapeDtypeStruct((PLANES, keys, 2 * width), BF),
            jax.ShapeDtypeStruct((PLANES, H, keys, tokens), BF),
        ]
        + shapes[:4]
        + shapes[7:],
        in_specs=[fixed(tokens, width), fixed(1, width), fixed(1, width)]
        + [square] * 5
        + [fixed(8, 128), weight, weight, hbm],
        out_specs=[flat] * 3
        + [flat_stat]
        + [flat] * 3
        + [out_fixed(PLANES, PAIRS, 2, tokens), flat, flat_stat]
        + [
            pl.BlockSpec((None, keys, 256), lambda t: (where(t)[0], 0, where(t)[1])),
            pl.BlockSpec((None, 2, keys, tokens), lambda t: where(t) + (0, 0)),
        ]
        + [hbm] * 13,
        scratch_shapes=[
            pltpu.VMEM((keys, width), BF),
            pltpu.VMEM((tokens, width), BF),
            pltpu.VMEM((PLANES, tokens, width), BF),
            pltpu.VMEM((PLANES, PAIRS, 2, tokens), F32),
            pltpu.VMEM((8, 128), jnp.int32),
            pltpu.VMEM((3, 8, 128), jnp.int32),
            pltpu.SemaphoreType.DMA((plane + 1,)),
        ]
        + courier.scratch(),
        compiler_params=pltpu.CompilerParams(
            vmem_limit_bytes=62 * 2**20, collective_id=ident, has_side_effects=True
        ),
    )(inputs, *gains, *weights, lens, key_weight, value_weight, memory)
    saved, (tops, part0, lse0, kv, probs), moved = outs[:7], outs[7:12], outs[12:]
    return dict(
        saved=saved,
        tops=tops,
        keyvals=kv,
        probs=probs,
        rows={r: moved[n] for n, r in enumerate(ORDER)},
        queries={0: saved[6], **{r: moved[3 + r] for r in near}},
        parts=[part0] + [moved[6 + r] for r in near],
        lses=[lse0] + [moved[9 + r] for r in near],
    )


def glu_parts(gate_vals):
    inner = 0.7978845608028654 * (gate_vals + 0.044715 * gate_vals * gate_vals * gate_vals)
    t = jnp.tanh(inner)
    gelu = 0.5 * gate_vals * (1.0 + t)
    slope = 0.5 * (1.0 + t) + 0.5 * gate_vals * (1.0 - t * t) * 0.7978845608028654 * (
        1.0 + 0.134145 * gate_vals * gate_vals
    )
    return gelu, slope


def spread(rows):
    both = [jnp.broadcast_to(rows[h : h + 1], (HD, rows.shape[1])) for h in range(2)]
    return jnp.concatenate(both, axis=0).T


def middle_kernel(*refs, sizes, packed):
    (
        part0,
        part1,
        part2,
        part3,
        lse0,
        lse1,
        lse2,
        lse3,
        h1_ref,
        wo_ref,
        gain_ref,
        cot_ref,
        gate_ref,
        up_ref,
        down_ref,
        out_ref,
        attn_ref,
        two_ref,
        da_ref,
        stats_ref,
        gnorm_ref,
        gwo_ref,
        *grad_refs,
        gdown_ref,
        raw_ref,
        h2_ref,
        n3_ref,
        total_ref,
        dn3_ref,
    ) = refs[: 29 + (not packed)]
    step = pl.program_id(0)
    last = pl.num_programs(0) - 1
    devices = sizes[0] * sizes[1] * sizes[2] * sizes[3]
    if packed:
        wide_ref, wide_got, tall_ref, tall_got, send, receive = refs[29:]
        core = lax.axis_index("c")

    def exchange(n):
        slot = rem(n, 2)
        return [
            pltpu.make_async_remote_copy(
                src_ref=source,
                dst_ref=target,
                send_sem=send.at[n, at],
                recv_sem=receive.at[n, at],
                device_id={"c": 1 - core},
                device_id_type=pl.DeviceIdType.MESH,
            )
            for at, (source, target) in enumerate(
                (
                    (wide_ref.at[slot, :, :, :, 1 - core], wide_got.at[n]),
                    (tall_ref.at[slot, :, :, 1 - core], tall_got.at[n]),
                )
            )
        ]
    parts = (part0, part1, part2, part3)
    lses = (lse0, lse1, lse2, lse3)

    @pl.when(step == 0)
    def _():
        for p in range(PAIRS):
            cols = pl.ds(p * 128, 128)
            values = [ref[p] for ref in lses]
            top = functools.reduce(jnp.maximum, values)
            scales = [jnp.exp(v - top) for v in values]
            total = functools.reduce(jnp.add, scales)
            stats_ref[0, p] = top + jnp.log(total)
            raw = None
            for ref, scale in zip(parts, scales):
                term = spread(scale / total) * ref[:, cols].astype(F32)
                raw = term if raw is None else raw + term
            raw_ref[:, cols] = raw
            attn_ref[:, cols] = raw.astype(BF)
        hidden = h1_ref[...] + dot(attn_ref[...], wo_ref[...], 1, 0)
        h2_ref[...] = hidden
        n3_ref[...] = rms(hidden, gain_ref[...]).astype(BF)
        total_ref[...] = hidden
        dn3_ref[...] = jnp.zeros_like(dn3_ref)
        if packed:
            barrier = pltpu.get_barrier_semaphore()
            pl.semaphore_signal(
                barrier,
                inc=1,
                device_id={"c": 1 - core},
                device_id_type=pl.DeviceIdType.MESH,
            )
            pl.semaphore_wait(barrier, 1)

    def one_chunk():
        normed = n3_ref[...]
        branch = cot_ref[...]
        gate_vals = dot(normed, gate_ref[...], 1, 0)
        up_vals = dot(normed, up_ref[...], 1, 0)
        grad_inner = dot(branch, down_ref[...], 1, 1)
        gelu, slope = glu_parts(gate_vals)
        inner = (gelu * up_vals).astype(BF)
        grad_gate = (grad_inner * up_vals * slope).astype(BF)
        grad_up = (grad_inner * gelu).astype(BF)
        total_ref[...] += dot(inner, down_ref[...], 1, 0)
        dn3_ref[...] += dot(grad_gate, gate_ref[...], 1, 1) + dot(grad_up, up_ref[...], 1, 1)
        terms = [dot(normed, grad_gate, 0, 0), dot(normed, grad_up, 0, 0)]
        if packed:
            shape = (devices, terms[0].shape[0] // devices, terms[0].shape[1])
            both = jnp.concatenate([t.reshape(shape) for t in terms], axis=1).astype(BF)
            slot = rem(step, 2)
            wide_ref[slot] = both.reshape(wide_ref.shape[1:])
            tall_ref[slot] = dot(inner, branch, 0, 0).astype(BF).reshape(tall_ref.shape[1:])
            for copy in exchange(step):
                copy.start()
        else:
            for ref, term in zip(grad_refs, terms):
                ref[...] = term
            gdown_ref[...] = dot(inner, branch, 0, 0).astype(BF).reshape(gdown_ref.shape)

    if packed:

        @pl.when(step < last)
        def _():
            one_chunk()

    else:
        one_chunk()

    @pl.when(step == last)
    def _():
        out_ref[...] = total_ref[...].astype(BF)
        hidden = h2_ref[...]
        grad = dn3_ref[...]
        r = lax.rsqrt(jnp.mean(hidden * hidden, axis=-1, keepdims=True) + EPSILON)
        u = gain_ref[...] * grad
        back = r * u - hidden * (r * r * r) * jnp.mean(u * hidden, axis=-1, keepdims=True)
        gnorm_ref[...] = jnp.sum(grad * hidden * r, axis=0, keepdims=True)
        two = cot_ref[...].astype(F32) + back
        two_ref[...] = two
        low = two.astype(BF)
        da_ref[...] = dot(low, wo_ref[...], 1, 1).astype(BF)
        gwo_ref[...] = dot(attn_ref[...], low, 0, 0).astype(BF)
        for p in range(PAIRS):
            cols = pl.ds(p * 128, 128)
            product = (da_ref[:, cols].astype(F32) * raw_ref[:, cols]).T
            for h in range(2):
                stats_ref[1, p, h : h + 1] = jnp.sum(
                    product[h * HD : (h + 1) * HD], axis=0, keepdims=True
                )

    if packed:

        @pl.when(step > 0)
        def _():
            before = step - 1
            slot = rem(before, 2)
            for copy in exchange(before):
                copy.wait()
            mine = wide_ref[slot, :, :, :, core].astype(F32)
            grad_refs[0][...] = (mine + wide_got[before].astype(F32)).astype(BF)
            mine = tall_ref[slot, :, :, core].astype(F32)
            gdown_ref[0] = (mine + tall_got[before].astype(F32)).astype(BF)


def middle(sizes, parts, lses, hidden, out_weight, gain, cotangent, gate, up, down):
    tokens, width = hidden.shape
    inner = gate.shape[1]
    chunk = 512
    count = inner // chunk
    devices = sizes[0] * sizes[1] * sizes[2] * sizes[3]
    share = width // devices
    down_share = inner // devices
    packed = share % 8 == 0 and chunk * PLANES == inner
    first = lambda p: jnp.minimum(p, count - 1)
    fixed = lambda *shape: pl.BlockSpec(shape, lambda p: (0,) * len(shape))
    whole = fixed(tokens, width)
    square = fixed(width, width)
    stat = fixed(PAIRS, 2, tokens)
    column = pl.BlockSpec((width, chunk), lambda p: (0, first(p)))
    scratch = [
        pltpu.VMEM((tokens, width), F32),
        pltpu.VMEM((tokens, width), F32),
        pltpu.VMEM((tokens, width), BF),
        pltpu.VMEM((tokens, width), F32),
        pltpu.VMEM((tokens, width), F32),
    ]
    params = dict(vmem_limit_bytes=VMEM)
    if packed:
        z, y, x, c = sizes
        wide_shape = (z, y, x, 2 * share)
        tall_shape = (y, x, down_share, width)
        grad_shapes = [
            jax.ShapeDtypeStruct(wide_shape + (inner,), BF),
            jax.ShapeDtypeStruct((z,) + tall_shape, BF),
        ]
        before = lambda p: jnp.maximum(p - 1, 0)
        grad_specs = [
            pl.BlockSpec(wide_shape + (chunk,), lambda p: (0, 0, 0, 0, before(p))),
            pl.BlockSpec((1,) + tall_shape, lambda p: (before(p), 0, 0, 0, 0)),
        ]
        scratch += [
            pltpu.VMEM((2, z, y, x, c, 2 * share, chunk), BF),
            pltpu.VMEM((count,) + wide_shape + (chunk,), BF),
            pltpu.VMEM((2, y, x, c, down_share, width), BF),
            pltpu.VMEM((count,) + tall_shape, BF),
            pltpu.SemaphoreType.DMA((count, 2)),
            pltpu.SemaphoreType.DMA((count, 2)),
        ]
        params.update(collective_id=12, has_side_effects=True)
    else:
        grad_shapes = [jax.ShapeDtypeStruct((width, inner), F32)] * 2
        grad_shapes.append(jax.ShapeDtypeStruct((devices, down_share, width), BF))
        grad_specs = [column] * 2
        grad_specs.append(
            pl.BlockSpec((chunk // down_share, down_share, width), lambda p: (p, 0, 0))
        )
    rows = jax.ShapeDtypeStruct((tokens, width), BF)
    wide = jax.ShapeDtypeStruct((tokens, width), F32)
    return pl.pallas_call(
        functools.partial(middle_kernel, sizes=sizes, packed=packed),
        grid=(count + packed,),
        out_shape=[
            rows,
            rows,
            wide,
            rows,
            jax.ShapeDtypeStruct((2, PAIRS, 2, tokens), F32),
            jax.ShapeDtypeStruct((1, width), F32),
            jax.ShapeDtypeStruct((width, width), BF),
        ]
        + grad_shapes,
        in_specs=[whole] * 4
        + [stat] * 4
        + [whole, square, fixed(1, width), whole]
        + [column, column, pl.BlockSpec((chunk, width), lambda p: (first(p), 0))],
        out_specs=[whole] * 4
        + [fixed(2, PAIRS, 2, tokens), fixed(1, width), square]
        + grad_specs,
        scratch_shapes=scratch,
        compiler_params=pltpu.CompilerParams(**params),
    )(*parts, *lses, hidden, out_weight, gain, cotangent, gate, up, down)


def cross_backward(
    courier, ident, r, queries, grad, keyvals, probs, tops, stats, key_weight, value_weight, summands=()
):
    tokens, keys = queries.shape[0], keyvals.shape[1]
    width = H * HD
    spec = block_specs(tokens, keys)

    def body(ins, outs, scratch):
        q_ref, da_ref, kv_ref, probs_ref, top_ref, stats_ref, wk_ref, wv_ref = ins
        dkv_ref, dq_ref, dm_ref = outs
        (total_ref,) = scratch
        step = pl.program_id(0)

        @pl.when(step == 0)
        def _():
            total_ref[...] = jnp.zeros_like(total_ref)

        def stored(h, keys_h, query_h):
            scale = jnp.exp(top_ref[0, h : h + 1, :] - stats_ref[0, 0, h : h + 1, :])
            return probs_ref[h].astype(F32) * scale

        weights = jnp.concatenate([wk_ref[...], wv_ref[...]], axis=1)
        grad_kv, grad_q = backward_pair(
            q_ref[...],
            da_ref[...],
            kv_ref[:, :128],
            kv_ref[:, 128:],
            stored,
            [stats_ref[1, 0, h : h + 1, :] for h in range(2)],
        )
        dkv_ref[...] = grad_kv
        dq_ref[...] = grad_q
        total_ref[...] += dot(grad_kv, weights, 1, 1)

        @pl.when(step == PAIRS - 1)
        def _():
            dm_ref[...] = total_ref[...].astype(BF)

    return call(
        courier,
        ident,
        body,
        [queries, grad, keyvals, probs, tops, stats, key_weight, value_weight],
        [
            spec["col"],
            spec["col"],
            pl.BlockSpec((None, keys, 256), lambda p: (r, 0, p)),
            pl.BlockSpec((None, 2, keys, tokens), lambda p: (r, p, 0, 0)),
            pl.BlockSpec((None, 1, 2, tokens), lambda p: (rem(r + 3, PLANES), p, 0, 0)),
            pl.BlockSpec((2, 1, 2, tokens), lambda p: (0, p, 0, 0)),
            spec["weight"],
            spec["weight"],
        ],
        [
            jax.ShapeDtypeStruct((keys, 2 * width), BF),
            jax.ShapeDtypeStruct((tokens, width), BF),
            jax.ShapeDtypeStruct((keys, width), BF),
        ],
        [spec["pair"], spec["col"], spec["rows"]],
        [pltpu.VMEM((keys, width), F32)],
        2**35,
        summands,
    )


def backward_part(
    sizes, ident, queries, grad, stats, keyvals, probs, tops, key_weight, value_weight, summands
):
    tokens, width = grad.shape
    plane = sizes[1] * sizes[2] * sizes[3]
    keys = keyvals.shape[1]
    positions = keys // plane
    rows = jax.ShapeDtypeStruct((tokens, width), BF)
    blocks = jax.ShapeDtypeStruct((plane, positions, width), BF)
    near = range(1, PLANES)
    jobs = [("return", 0, blocks)] * 3
    jobs += [("line", -r, rows) for r in near] + [("line", -r, stats) for r in near]
    jobs += [("line", 1, rows), ("line", 2, rows)]
    courier = Courier(sizes, jobs)
    courier.lines = list(near)
    count = PLANES * PAIRS
    reducers = [Halved(sizes, value.shape) for value in summands]
    parts = [len(one.scratch()) for one in reducers]
    sums = len(reducers)

    def kernel(*refs):
        ins, far, arrays, outs, results, targets, work, sems, rest = split_refs(
            refs, 5, 6, sums, 1, sums, 8, 7, 3, sum(parts)
        )
        kv_ref, probs_ref, top_ref, wk_ref, wv_ref = ins
        (dkv_ref,) = outs
        query_all, grad_all, stats_all, dq_all, total_ref, dm_buf, load_sems = work
        dq0, dq_near, dq_next, dq3, back0, back1, back2, rows3 = targets
        copies = courier.copies(
            [dm_buf.at[0], dm_buf.at[1], dm_buf.at[0]]
            + [far[4]] * 3
            + [far[5]] * 3
            + [dq_all.at[1], dq_all.at[2]],
            [back0, back1, back2]
            + [grad_all.at[r] for r in near]
            + [stats_all.at[r] for r in near]
            + [dq_near, dq_next],
            sems,
        )
        own, remote = copies[:3], copies[3:]
        others = plane - 1
        grad_lines, stats_lines, dq_lines = split_refs(remote[3 * others :], 3, 3, 2)
        returns = [[own[n]] + remote[n * others : n * others + others] for n in range(3)]
        work_of = split_refs(rest, *parts)
        step = pl.program_id(0)
        r_now = lax.div(step, PAIRS)
        p = rem(step, PAIRS)

        def bound():
            return [one.bind(v, held) for one, v, held in zip(reducers, arrays, work_of)]

        loads = [
            pltpu.make_async_copy(far[n], query_all.at[n], load_sems.at[n]) for n in range(PLANES)
        ]
        loads.append(pltpu.make_async_copy(far[4], grad_all.at[0], load_sems.at[4]))
        loads.append(pltpu.make_async_copy(far[5], stats_all.at[0], load_sems.at[5]))
        leave = [
            pltpu.make_async_copy(dq_all.at[0], dq0, load_sems.at[6]),
            pltpu.make_async_copy(dq_all.at[3], dq3, load_sems.at[7]),
            pltpu.make_async_copy(dm_buf.at[1], rows3, load_sems.at[8]),
        ]

        @pl.when(step == 0)
        def _():
            for copy in loads:
                copy.start()
            courier.greet()
            grad_lines[0].start()
            stats_lines[0].start()
            for one in bound():
                one.begin()
            for copy in loads:
                copy.wait()

        for r in near:

            @pl.when(step == r * PAIRS)
            def _(r=r):
                grad_lines[r - 1].wait()
                stats_lines[r - 1].wait()
                if r + 1 < PLANES:
                    grad_lines[r].start()
                    stats_lines[r].start()

        @pl.when(p == 0)
        def _():
            total_ref[...] = jnp.zeros_like(total_ref)

        cols = pl.ds(pl.multiple_of(p * 128, 128), 128)
        top_at = rem(r_now + 3, PLANES)

        def stored(h, keys_h, query_h):
            lse = stats_all[r_now, 0, p, h : h + 1, :]
            return probs_ref[h].astype(F32) * jnp.exp(top_ref[top_at, p, h : h + 1, :] - lse)

        weights = jnp.concatenate([wk_ref[...], wv_ref[...]], axis=1)
        grad_kv, grad_q = backward_pair(
            query_all[r_now, :, cols],
            grad_all[r_now, :, cols],
            kv_ref[:, :128],
            kv_ref[:, 128:],
            stored,
            [stats_all[r_now, 1, p, h : h + 1, :] for h in range(2)],
        )
        dkv_ref[...] = grad_kv
        dq_all[r_now, :, cols] = grad_q
        total_ref[...] += dot(grad_kv, weights, 1, 1)

        @pl.when(step == 3)
        def _():
            for one in bound():
                one.after_second()

        @pl.when(step == PAIRS - 1)
        def _():
            for one, result in zip(bound(), results):
                one.after_third(result)

        for r in range(PLANES):

            @pl.when(step == r * PAIRS + PAIRS - 1)
            def _(r=r):
                if r >= 2:
                    for copy in returns[r - 2]:
                        copy.wait()
                dm_buf[r % 2] = total_ref[...].astype(BF).reshape(dm_buf.shape[1:])
                if r < 3:
                    for copy in returns[r]:
                        copy.start()
                if r == 0:
                    leave[0].start()
                elif r < 3:
                    dq_lines[r - 1].start()
                else:
                    leave[1].start()
                    leave[2].start()
                    for copy in returns[2] + list(dq_lines) + leave:
                        copy.wait()

    once = pl.Buffered(1)

    def where(t):
        return lax.div(t, PAIRS), rem(t, PAIRS)

    hbm = pl.BlockSpec(memory_space=pl.ANY)
    weight = pl.BlockSpec((width, 128), lambda t: (0, rem(t, PAIRS)))
    pair = pl.BlockSpec((None, keys, 256), lambda t: (where(t)[0], 0, where(t)[1]))
    shapes = [(PLANES,) + value.shape[-2:] for value in summands]
    scratch = [
        pltpu.VMEM((PLANES, tokens, width), BF),
        pltpu.VMEM((PLANES, tokens, width), BF),
        pltpu.VMEM((PLANES,) + stats.shape, F32),
        pltpu.VMEM((PLANES, tokens, width), BF),
        pltpu.VMEM((keys, width), F32),
        pltpu.VMEM((2, plane, positions, width), BF),
        pltpu.SemaphoreType.DMA((9,)),
    ]
    outs = pl.pallas_call(
        kernel,
        grid=(count,),
        out_shape=[jax.ShapeDtypeStruct((PLANES, keys, 2 * width), BF)]
        + [jax.ShapeDtypeStruct(shape, BF) for shape in shapes]
        + [rows] * 4
        + [blocks] * 4,
        in_specs=[
            pair,
            pl.BlockSpec((None, 2, keys, tokens), lambda t: where(t) + (0, 0)),
            pl.BlockSpec(tops.shape, lambda t: (0, 0, 0, 0), pipeline_mode=once),
            weight,
            weight,
        ]
        + [hbm] * (6 + sums),
        out_specs=[pair] + [pl.BlockSpec(shape, lambda t: (0, 0, 0)) for shape in shapes] + [hbm] * 8,
        scratch_shapes=scratch
        + courier.scratch()
        + [ref for one in reducers for ref in one.scratch()],
        compiler_params=pltpu.CompilerParams(
            vmem_limit_bytes=62 * 2**20, collective_id=ident, has_side_effects=True
        ),
    )(
        keyvals,
        probs,
        tops,
        key_weight,
        value_weight,
        *[queries[r] for r in range(PLANES)],
        grad,
        stats,
        *summands,
    )
    return outs[0], outs[1 : 1 + sums], outs[1 + sums : 5 + sums], outs[5 + sums :]


def weight_terms(courier, ident, rows, grads):
    keys, width = rows[0].shape
    spec = block_specs(keys, keys)
    count = len(rows)

    def body(ins, outs, _):
        total = None
        for rows_ref, grad_ref in zip(ins[:count], ins[count:]):
            term = dot(rows_ref[...], grad_ref[...], 0, 0)
            total = term if total is None else total + term
        outs[0][...] = total[:, :128]
        outs[1][...] = total[:, 128:]

    return call(
        courier,
        ident,
        body,
        list(rows) + list(grads),
        [spec["rows"]] * count + [spec["pair"]] * count,
        [jax.ShapeDtypeStruct((width, width), F32)] * 2,
        [spec["weight"]] * 2,
        [],
        2**34,
    )


def self_backward(courier, ident, queries, grad, keys, values, lse, summand):
    tokens, width = queries.shape
    spec = block_specs(tokens, tokens)

    def body(ins, outs, _):
        q_ref, da_ref, k_ref, v_ref, lse_ref = ins
        dq_ref, dk_ref, dv_ref = outs
        grad_kv, dq_ref[...] = backward_pair(
            q_ref[...],
            da_ref[...],
            k_ref[...],
            v_ref[...],
            causal_probs([lse_ref[0, h : h + 1, :] for h in range(2)]),
            None,
        )
        dk_ref[...] = grad_kv[:, :128]
        dv_ref[...] = grad_kv[:, 128:]

    return call(
        courier,
        ident,
        body,
        [queries, grad, keys, values, lse],
        [spec["col"]] * 4 + [spec["stat"]],
        [jax.ShapeDtypeStruct((tokens, width), BF)] * 3,
        [spec["col"]] * 3,
        [],
        2**33,
        [summand],
    )


def rms_back(values, gain, grad):
    r = lax.rsqrt(jnp.mean(values * values, axis=-1, keepdims=True) + EPSILON)
    u = gain * grad
    back = r * u - values * (r * r * r) * jnp.mean(u * values, axis=-1, keepdims=True)
    return back, jnp.sum(grad * values * r, axis=0, keepdims=True)


def ending(sizes, ident, rows, grads, grad_q, grad_rows, left, two, held, lse, small_in):
    courier = Courier(
        sizes,
        [("line", PLANES - 1, grad_q[-1]), ("return", 0, grad_rows)]
        + [("scatter", 0, value) for value in left],
    )
    courier.lines = list(range(1, PLANES))
    jobs = len(courier.jobs)
    devices = sizes[0] * sizes[1] * sizes[2] * sizes[3]
    keys, width = rows[0].shape
    tokens = two.shape[0]
    share = width // devices
    chunk = 512
    cuts = keys // chunk
    groups = [Resident(sizes, (2 * share, width)) for _ in range(2)]
    groups += [Resident(sizes, (2 * share, 256)) for _ in range(6)]
    small = SmallSum(sizes, (8, width))
    early = [two] + list(held) + list(grad_q[:-1])
    far = list(rows) + [grads] + early
    counts = (len(far), len(small_in) + 1, jobs, 6, jobs - 1, 4, len(early) - 1, 8, 3, 80, 10)

    def pack(ref, first, second, cols=EVERY):
        lanes = first.shape[1]
        parts = [v.astype(F32).reshape(devices, share, lanes) for v in (first, second)]
        both = jnp.concatenate(parts, axis=1).astype(BF)
        ref[:, :, :, :, :, cols] = both.reshape(tuple(sizes) + both.shape[1:])

    def kernel(*refs):
        far_refs, near, sources, outs, targets, stage, loaded, work, sems, group_refs, rest = (
            split_refs(refs, *counts)
        )
        self_gain, cross_gain, ffn_term, lse_ref = near
        grad_in, *sums, norm_sums = outs
        row_buf, grad_buf, total, load_sems = stage
        dq_got, da_ref, dq1, dk1, dv1, normed_ref, *_ = work
        chunk_sems, early_sems = load_sems, work[6]
        copies = courier.copies(sources, [dq_got] + list(targets), sems)
        courier.greet()
        for copy in copies:
            copy.start()

        def chunk_loads(r, i):
            slot = rem(i, 2)
            where = pl.ds(pl.multiple_of(rem(i, cuts) * chunk, chunk), chunk)
            return [
                pltpu.make_async_copy(
                    far_refs[r].at[where], row_buf.at[slot], chunk_sems.at[slot, 0]
                ),
                pltpu.make_async_copy(
                    far_refs[PLANES].at[r, where], grad_buf.at[slot], chunk_sems.at[slot, 1]
                ),
            ]

        def start_chunk(i):
            for r in range(PLANES):

                @pl.when(lax.div(jnp.int32(i), cuts) == r)
                def _(r=r):
                    for copy in chunk_loads(r, i):
                        copy.start()

        total[...] = jnp.zeros_like(total)
        early_refs = far_refs[PLANES + 1 :]
        early_loads = [
            pltpu.make_async_copy(source, target, early_sems.at[n])
            for n, (source, target) in enumerate(zip(early_refs, [grad_in] + list(loaded)))
        ]
        start_chunk(0)
        for copy in early_loads:
            copy.start()

        @pl.loop(0, PLANES * cuts)
        def _(i):
            @pl.when(i + 1 < PLANES * cuts)
            def _():
                start_chunk(i + 1)

            for copy in chunk_loads(0, i):
                copy.wait()
            slot = rem(i, 2)
            total[...] += dot(row_buf[slot], grad_buf[slot], 0, 0)

        bound = [
            one.bind(group_refs[10 * n : 10 * n + 10]) for n, one in enumerate(groups)
        ]
        bits = small.bind(rest)

        @pl.loop(0, PAIRS)
        def _(p):
            at = pl.multiple_of(p * 256, 256)
            pack(
                bound[0].held,
                total[:, pl.ds(at, 128)],
                total[:, pl.ds(at + 128, 128)],
                pl.ds(pl.multiple_of(p * 128, 128), 128),
            )

        bound[0].begin()
        for copy in early_loads:
            copy.wait()
        copies[1].wait()
        x_ref, h1_ref, gco_ref, q_ref, k_ref, v_ref, attn_ref = loaded[:7]
        wq_ref, wk_ref, wv_ref, wo_ref, wc_ref, *dq_refs = loaded[7:]
        grad = dq_got[...].astype(F32)
        for ref in dq_refs:
            grad += ref[...].astype(F32)
        dq_got[...] = grad.astype(BF)
        hidden = h1_ref[...]
        back, cross_norm = rms_back(hidden, cross_gain[...], dot(dq_got[...], wc_ref[...], 1, 1))
        grad_in[...] += back
        dv1[...] = rms(hidden, cross_gain[...]).astype(BF)
        bound[0].after_first()

        @pl.loop(0, 3)
        def _(i):
            cols = pl.ds(pl.multiple_of(i * 256, 256), 256)
            pack(bound[1].held, dot(dv1[...], dq_got[:, cols], 0, 0), gco_ref[:, cols], cols)

        bound[1].begin()
        low_ref = dq_got
        low_ref[...] = grad_in[...].astype(BF)
        da_ref[...] = dot(low_ref[...], wo_ref[...], 1, 1).astype(BF)
        values = x_ref[...].astype(F32)
        normed_ref[...] = rms(values, self_gain[...]).astype(BF)

        for third in range(3):

            @pl.loop(2 * third, 2 * third + 2)
            def _(p):
                cols = pl.ds(pl.multiple_of(p * 128, 128), 128)
                grad_kv, grad_q_p = backward_pair(
                    q_ref[:, cols],
                    da_ref[:, cols],
                    k_ref[:, cols],
                    v_ref[:, cols],
                    causal_probs([lse_ref[p, h : h + 1, :] for h in range(2)]),
                    None,
                )
                dq1[:, cols] = grad_q_p
                dk1[:, cols] = grad_kv[:, :128]
                dv1[:, cols] = grad_kv[:, 128:]

            cols = pl.ds(third * 256, 256)
            near_sum, far_sum = bound[2 + 2 * third], bound[3 + 2 * third]
            normed = normed_ref[...]
            pack(near_sum.held, dot(normed, dq1[:, cols], 0, 0), dot(normed, dk1[:, cols], 0, 0))
            near_sum.begin()
            pack(
                far_sum.held,
                dot(normed, dv1[:, cols], 0, 0),
                dot(attn_ref[...], low_ref[:, cols], 0, 0),
            )
            far_sum.begin()
            if third == 0:
                bound[0].after_second()
                bound[1].after_first()
            if third == 1:
                bound[0].after_third_start()
                bound[1].after_second()
                bound[2].after_first()
                bound[3].after_first()
            if third == 2:
                bound[1].after_third_start()
                bound[2].after_second()
                bound[3].after_second()
                bound[4].after_first()
                bound[5].after_first()
        grad_normed = (
            dot(dq1[...], wq_ref[...], 1, 1)
            + dot(dk1[...], wk_ref[...], 1, 1)
            + dot(dv1[...], wv_ref[...], 1, 1)
        )
        back, self_norm = rms_back(values, self_gain[...], grad_normed)
        grad_in[...] += back
        bits.held[0][...] = jnp.concatenate(
            [self_norm, cross_norm, ffn_term[...], jnp.zeros((5, width), F32)], axis=0
        )
        bits.start(0)
        bound[2].after_third_start()
        bound[3].after_third_start()
        bound[4].after_second()
        bound[5].after_second()
        bound[6].after_first()
        bound[7].after_first()
        bits.advance(0)
        bound[4].after_third_start()
        bound[5].after_third_start()
        bound[6].after_second()
        bound[7].after_second()
        bits.advance(1)
        bound[6].after_third_start()
        bound[7].after_third_start()
        bits.advance(2)
        bound[0].finish(sums[0])
        bound[1].finish(sums[1])
        for n in range(2, 8):
            third, kind = divmod(n - 2, 2)
            bound[n].finish(sums[2 + kind].at[:, pl.ds(third * 256, 256)])
        bits.advance(3, norm_sums)
        for n, copy in enumerate(copies):
            if n != 1:
                copy.wait()

    any_spec = pl.BlockSpec(memory_space=pl.ANY)
    vmem = pl.BlockSpec(memory_space=pltpu.VMEM)
    row = pltpu.VMEM((tokens, width), BF)
    scratch = [
        pltpu.VMEM((2, chunk, width), BF),
        pltpu.VMEM((2, chunk, 2 * width), BF),
        pltpu.VMEM((width, 2 * width), F32),
        pltpu.SemaphoreType.DMA((2, 2)),
    ]
    scratch += [pltpu.VMEM(v.shape, v.dtype) for v in early[1:]]
    scratch += [row] * 6 + [pltpu.SemaphoreType.DMA((len(early),))]
    scratch += [pltpu.SemaphoreType.DMA((1,))] + courier.scratch()
    for one in groups:
        scratch += one.scratch()
    scratch += small.scratch()
    outs = pl.pallas_call(
        kernel,
        out_shape=[jax.ShapeDtypeStruct((tokens, width), F32)]
        + [jax.ShapeDtypeStruct((2 * share, width), F32)] * 4
        + [jax.ShapeDtypeStruct((8, width), F32)]
        + courier.out_shape()[1:],
        in_specs=[any_spec] * len(far) + [vmem] * (len(small_in) + 1) + courier.specs(),
        out_specs=[vmem] * 6 + courier.specs()[1:],
        scratch_shapes=scratch,
        compiler_params=pltpu.CompilerParams(
            vmem_limit_bytes=62 * 2**20, collective_id=ident, has_side_effects=True
        ),
    )(*far, *small_in, lse, *courier.values())
    return outs[0], outs[1:5], outs[5], outs[6:]


def place_kernel(*refs):
    *blocks, out_ref, held, arrive, leave = refs
    z = lax.axis_index("z")
    size = held.shape[1]
    inward = []
    outward = []
    for r, block in enumerate(blocks):
        at = rem(z + r, PLANES) * size
        inward.append(pltpu.make_async_copy(block, held.at[r], arrive.at[r]))
        outward.append(
            pltpu.make_async_copy(held.at[r], out_ref.at[pl.ds(at, size)], leave.at[r])
        )
        inward[r].start()
    for r in range(len(blocks)):
        inward[r].wait()
        outward[r].start()
    for copy in outward:
        copy.wait()


def finish_kernel(*refs):
    blocks = refs[:PLANES]
    left0, got0, left1, got1, out_ref, gate_ref, up_ref, down_ref = refs[PLANES : PLANES + 8]
    held, arrive, leave = refs[PLANES + 8 :]
    z = lax.axis_index("z")
    size = held.shape[1]
    inward = []
    outward = []
    for r, block in enumerate(blocks):
        at = rem(z + r, PLANES) * size
        inward.append(pltpu.make_async_copy(block, held.at[r], arrive.at[r]))
        outward.append(
            pltpu.make_async_copy(held.at[r], out_ref.at[pl.ds(at, size)], leave.at[r])
        )
        inward[r].start()
    for r in range(PLANES):
        inward[r].wait()
        outward[r].start()
    share = gate_ref.shape[0]
    wide = left0[z].astype(F32)
    tall = left1[z].astype(F32)
    for k in range(PLANES - 1):
        wide += got0[k].astype(F32)
        tall += got1[k].astype(F32)
    gate_ref[...] = wide[:share]
    up_ref[...] = wide[share:]
    down_ref[...] = tall
    for copy in outward:
        copy.wait()


def finish(blocks, left0, got0, left1, got1):
    shape = blocks[0].shape
    share, inner = left0.shape[1] // 2, left0.shape[2]
    hbm = pl.BlockSpec(memory_space=pl.ANY)
    vmem = pl.BlockSpec(memory_space=pltpu.VMEM)
    return pl.pallas_call(
        finish_kernel,
        out_shape=[jax.ShapeDtypeStruct((PLANES * shape[0],) + shape[1:], BF)]
        + [jax.ShapeDtypeStruct((share, inner), F32)] * 2
        + [jax.ShapeDtypeStruct(left1.shape[1:], F32)],
        in_specs=[hbm] * PLANES + [vmem] * 4,
        out_specs=[hbm] + [vmem] * 3,
        scratch_shapes=[
            pltpu.VMEM((PLANES,) + shape, BF),
            pltpu.SemaphoreType.DMA((PLANES,)),
            pltpu.SemaphoreType.DMA((PLANES,)),
        ],
        compiler_params=pltpu.CompilerParams(vmem_limit_bytes=VMEM),
    )(*blocks, left0, got0, left1, got1)


def place(blocks):
    shape = blocks[0].shape
    count = len(blocks)
    hbm = pl.BlockSpec(memory_space=pl.ANY)
    return pl.pallas_call(
        place_kernel,
        out_shape=jax.ShapeDtypeStruct((count * shape[0],) + shape[1:], blocks[0].dtype),
        in_specs=[hbm] * count,
        out_specs=hbm,
        scratch_shapes=[
            pltpu.VMEM((count,) + shape, blocks[0].dtype),
            pltpu.SemaphoreType.DMA((count,)),
            pltpu.SemaphoreType.DMA((count,)),
        ],
        compiler_params=pltpu.CompilerParams(vmem_limit_bytes=VMEM),
    )(*blocks)


def norm_apply(values, gain):
    return values * lax.rsqrt(jnp.mean(values * values, axis=-1, keepdims=True) + EPSILON) * gain


def norm_back(values, gain, grad):
    r = lax.rsqrt(jnp.mean(values * values, axis=-1, keepdims=True) + EPSILON)
    u = gain * grad
    dv = r * u - values * (r * r * r) * jnp.mean(u * values, axis=-1, keepdims=True)
    return dv, jnp.sum(grad * values * r, axis=0)


def matmul(left, right):
    return dot(left, right, 1, 0)


def matmul_t(left, right):
    return dot(left, right, 1, 1)


def tmatmul(left, right):
    return dot(left, right, 0, 0)


def on_device(
    sizes,
    decoder_in,
    memory,
    memory_lengths,
    cotangent,
    norm_self,
    self_query,
    self_key,
    self_value,
    self_out,
    norm_cross,
    cross_query,
    cross_key,
    cross_value,
    cross_out,
    norm_ffn,
    ffn_gate,
    ffn_up,
    ffn_down,
):
    devices, positions, width = memory.shape
    plane_size = sizes[1] * sizes[2] * sizes[3]
    z = lax.axis_index("z")

    def flat(blocks):
        return blocks.reshape(plane_size * positions, width)

    def cut(rows):
        return rows.reshape(plane_size, positions, width)

    forward = forward_part(
        sizes,
        0,
        memory,
        jnp.broadcast_to(memory_lengths[None, :], (8, 128)),
        decoder_in[0],
        (norm_self[None], norm_cross[None]),
        (self_query, self_key, self_value, self_out, cross_query),
        cross_key,
        cross_value,
    )
    query_one, key_one, value_one, lse_one, attn_one, hidden_one, _ = forward["saved"]
    queries = forward["queries"]
    rows = {r: flat(forward["rows"][r]) for r in range(PLANES)}

    (
        output,
        attn_two,
        grad_two,
        grad_attn_two,
        stats,
        grad_norm_ffn,
        grad_cross_out,
        *grads_in,
        grad_down,
    ) = middle(
        sizes,
        forward["parts"],
        forward["lses"],
        hidden_one,
        cross_out,
        norm_ffn[None],
        cotangent[0],
        ffn_gate,
        ffn_up,
        ffn_down,
    )
    decoder_out = output[None]
    if len(grads_in) == 2:
        summands = {
            0: [summand_of(sizes, grads_in)],
            1: [grad_down.reshape(tuple(sizes) + grad_down.shape[1:])],
        }
    else:
        summands = {0: [grads_in[0], grad_down]}
    left, got = {}, {}

    last = PLANES - 1
    part = width // devices
    if len(grads_in) == 1:
        grad_kv, left, grad_q, returned = backward_part(
            sizes,
            5,
            queries,
            grad_attn_two,
            stats,
            forward["keyvals"],
            forward["probs"],
            forward["tops"],
            cross_key,
            cross_value,
            summands[0],
        )
        returned = list(returned)
        decoder_in_grad, sums, norm_sums, moved = ending(
            sizes,
            9,
            [rows[r] for r in range(PLANES)],
            grad_kv,
            grad_q,
            returned[last],
            left,
            grad_two,
            (decoder_in[0], hidden_one, grad_cross_out, query_one, key_one, value_one, attn_one)
            + (self_query, self_key, self_value, self_out, cross_query),
            lse_one,
            (norm_self[None], norm_cross[None], grad_norm_ffn),
        )
        returned[last], got_wide, got_tall = moved
        memory_grad, sum_gate, sum_up, sum_down = finish(
            returned, left[0], got_wide, left[1], got_tall
        )
        here = lax.axis_index(ALL) * part
        norm_self_sum, norm_cross_sum, norm_ffn_sum = (
            lax.dynamic_slice_in_dim(norm_sums[n], here, part) for n in range(3)
        )
        return (
            decoder_out,
            decoder_in_grad[None],
            memory_grad,
            norm_self_sum,
            sums[2][:part],
            sums[2][part:],
            sums[3][:part],
            sums[3][part:],
            norm_cross_sum,
            sums[1][:part],
            sums[0][:part],
            sums[0][part:],
            sums[1][part:],
            norm_ffn_sum,
            sum_gate,
            sum_up,
            sum_down,
        )

    grads = {0: grad_attn_two}
    both = {0: stats}
    grad_kv, grad_q, grad_rows, returned = {}, {}, {}, {}
    for r in range(PLANES):
        jobs = []
        if r + 1 < PLANES:
            jobs.append(("line", -(r + 1), grad_attn_two))
            jobs.append(("line", -(r + 1), stats))
        if r >= 1:
            jobs.append(("return", 0, cut(grad_rows[r - 1])))
        if r >= 2:
            jobs.append(("line", r - 1, grad_q[r - 1]))
        (grad_kv[r], grad_q[r], grad_rows[r]), moved = cross_backward(
            Courier(sizes, jobs),
            5 + r,
            r,
            queries[r],
            grads[r],
            forward["keyvals"],
            forward["probs"],
            forward["tops"],
            both[r],
            cross_key,
            cross_value,
            summands.get(r, []),
        )
        moved = list(moved)
        if r in summands:
            for value in moved[len(moved) - len(summands[r]) :]:
                left[len(left)] = value
        if r + 1 < PLANES:
            grads[r + 1], both[r + 1] = moved.pop(0), moved.pop(0)
        if r >= 1:
            returned[r - 1] = moved.pop(0)
        if r >= 2:
            grad_q[r - 1] = moved.pop(0)
    jobs = [
        ("line", last, grad_q[last]),
        ("return", 0, cut(grad_rows[last])),
        ("scatter", 0, left[0]),
        ("scatter", 0, left[1]),
    ]
    (grad_cross_key, grad_cross_value), (grad_q[last], returned[last], got[0], got[1]) = weight_terms(
        Courier(sizes, jobs),
        9,
        [rows[r] for r in range(PLANES)],
        [grad_kv[r] for r in range(PLANES)],
    )
    memory_grad = place([returned[r] for r in range(PLANES)])

    inputs = decoder_in[0].astype(F32)
    normed_one = norm_apply(inputs, norm_self).astype(BF)
    normed_two = norm_apply(hidden_one, norm_cross).astype(BF)
    grad_q_two = sum(grad_q[r].astype(F32) for r in range(PLANES)).astype(BF)
    grad_cross_query = tmatmul(normed_two, grad_q_two)
    grad_normed_two = matmul_t(grad_q_two, cross_query)
    back_one, grad_norm_cross = norm_back(hidden_one, norm_cross, grad_normed_two)
    grad_one = grad_two + back_one
    branch_one = grad_one.astype(BF)
    grad_self_out = tmatmul(attn_one, branch_one)
    grad_attn_one = matmul_t(branch_one, self_out).astype(BF)
    (grad_q_one, grad_k_one, grad_v_one), (cross_left,) = self_backward(
        Courier(sizes, []),
        10,
        query_one,
        grad_attn_one,
        key_one,
        value_one,
        lse_one,
        summand_of(sizes, (grad_cross_key, grad_cross_value)),
    )
    grad_normed_one = (
        matmul_t(grad_q_one, self_query)
        + matmul_t(grad_k_one, self_key)
        + matmul_t(grad_v_one, self_value)
    )
    back_in, grad_norm_self = norm_back(inputs, norm_self, grad_normed_one)
    decoder_in_grad = (grad_one + back_in)[None]
    share_of_norms = width // devices
    norms = jnp.stack(
        [g.reshape(devices, share_of_norms) for g in (grad_norm_self, grad_norm_cross, grad_norm_ffn[0])],
        axis=1,
    ).reshape(devices, 1, 3 * share_of_norms)
    norms = jnp.pad(norms, ((0, 0), (0, 15), (0, 256 - 3 * share_of_norms)))
    (cross_got,), sums = reduce_all(
        sizes,
        11,
        [
            norms.astype(BF).reshape(tuple(sizes) + norms.shape[1:]),
            summand_of(sizes, (grad_cross_query, grad_cross_out.astype(F32))),
            summand_of(sizes, (tmatmul(normed_one, grad_q_one), tmatmul(normed_one, grad_k_one))),
            summand_of(sizes, (tmatmul(normed_one, grad_v_one), grad_self_out)),
        ],
        [cross_left],
    )
    norm_sums = sums[0][0, : 3 * share_of_norms].reshape(3, share_of_norms)
    gate_up = over_z(left[0], got[0])
    cross_kv = over_z(cross_left, cross_got)
    part = share_of_norms
    return (
        decoder_out,
        decoder_in_grad,
        memory_grad,
        norm_sums[0],
        sums[2][:part],
        sums[2][part:],
        sums[3][:part],
        sums[3][part:],
        norm_sums[1],
        sums[1][:part],
        cross_kv[:part],
        cross_kv[part:],
        sums[1][part:],
        norm_sums[2],
        gate_up[:part],
        gate_up[part:],
        over_z(left[1], got[1]),
    )


def solution(mesh):
    dp, seq = mesh.devices.shape
    cores = 2
    lines = dp // PLANES
    split = Mesh(mesh.devices.reshape(PLANES, lines, seq // cores, cores), ALL)
    sizes = split.devices.shape
    first = P(ALL)
    middle = P(None, ALL)
    whole = P()
    return jax.shard_map(
        functools.partial(on_device, sizes),
        mesh=split,
        in_specs=(first, middle, first, first) + (whole,) * 14,
        out_specs=(first, first, middle) + (first,) * 14,
        check_vma=False,
    )
```

```python
import functools

import jax
import jax.numpy as jnp
from jax import lax
from jax.experimental import pallas as pl
from jax.experimental.pallas import tpu as pltpu
from jax.sharding import Mesh
from jax.sharding import PartitionSpec as P

H = 12
HD = 64
PAIRS = 6
PLANES = 4
EPSILON = 1e-06
MASKED = -1e30
VMEM = 56 * 2**20
BF = jnp.bfloat16
F32 = jnp.float32
ALL = ("z", "y", "x", "c")
PLANE = ("y", "x", "c")
EVERY = slice(None)


def dot(left, right, left_dim, right_dim):
    return lax.dot_general(
        left, right, (((left_dim,), (right_dim,)), ((), ())), preferred_element_type=F32
    )


def lane_masks():
    lane = lax.broadcasted_iota(jnp.int32, (1, 2 * HD), 1)
    low = jnp.where(lane < HD, 1.0, 0.0)
    first = jnp.where(lane == HD, 1.0, 0.0)
    second = jnp.where(lane == 0, 1.0, 0.0)
    low, high, first, second = (
        v.astype(BF) for v in (low, 1.0 - low, first, second)
    )
    return ((low, high, first), (high, low, second))


def causal_mask(scores):
    key = lax.broadcasted_iota(jnp.int32, scores.shape, 0)
    query = lax.broadcasted_iota(jnp.int32, scores.shape, 1)
    return jnp.where(key <= query, scores, MASKED)


def rem(value, size):
    return lax.rem(value, size)


class Courier:
    def __init__(self, sizes, jobs):
        self.sizes = sizes
        self.jobs = jobs
        self.plane = sizes[1] * sizes[2] * sizes[3]
        self.in_plane = any(job[0] in ("fetch", "return") for job in jobs)
        self.lines = [job[1] for job in jobs if job[0] == "line"]
        for job in jobs:
            if job[0] == "scatter":
                self.lines += list(range(1, PLANES))

    def out_shape(self):
        shapes = []
        for kind, _, value in self.jobs:
            shape = value.shape
            if kind == "fetch":
                shape = (self.plane,) + shape[1:]
            elif kind == "scatter":
                shape = (PLANES - 1,) + shape[1:]
            shapes.append(jax.ShapeDtypeStruct(shape, value.dtype))
        return shapes

    def specs(self):
        return [pl.BlockSpec(memory_space=pl.ANY)] * len(self.jobs)

    def values(self):
        return [job[2] for job in self.jobs]

    def scratch(self):
        each = {"line": 1, "scatter": PLANES - 1}
        count = max(1, sum(each.get(job[0], self.plane - 1) for job in self.jobs))
        own = max(1, sum(job[0] in ("fetch", "return") for job in self.jobs))
        return [pltpu.SemaphoreType.DMA((n,)) for n in (count, count, own)]

    def params(self, ident):
        return pltpu.CompilerParams(
            vmem_limit_bytes=VMEM, collective_id=ident, has_side_effects=True
        )

    def me(self):
        _, _, x_size, c_size = self.sizes
        y, x, c = (lax.axis_index(name) for name in PLANE)
        return (y * x_size + x) * c_size + c

    def along(self, offset):
        return {"z": rem(lax.axis_index("z") + (offset + PLANES), PLANES)}

    def across(self, offset):
        _, _, x_size, c_size = self.sizes
        other = rem(self.me() + offset, self.plane)
        line = lax.div(other, c_size)
        return other, {"y": lax.div(line, x_size), "x": rem(line, x_size), "c": rem(other, c_size)}

    def greet(self):
        barrier = pltpu.get_barrier_semaphore()
        count = 0
        if self.in_plane:
            for k in range(1, self.plane):
                _, device = self.across(k)
                pl.semaphore_signal(
                    barrier, inc=1, device_id=device, device_id_type=pl.DeviceIdType.MESH
                )
                count += 1
        for offset in self.lines:
            pl.semaphore_signal(
                barrier,
                inc=1,
                device_id=self.along(-offset),
                device_id_type=pl.DeviceIdType.MESH,
            )
            count += 1
        pl.semaphore_wait(barrier, count)

    def copies(self, sources, targets, sems):
        send, receive, own = sems
        remote = []
        local = []

        def add(source, target, device):
            n = len(remote)
            remote.append(
                pltpu.make_async_remote_copy(
                    src_ref=source,
                    dst_ref=target,
                    send_sem=send.at[n],
                    recv_sem=receive.at[n],
                    device_id=device,
                    device_id_type=pl.DeviceIdType.MESH,
                )
            )

        me = self.me()
        for (kind, offset, _), source, target in zip(self.jobs, sources, targets):
            if kind == "line":
                add(source, target, self.along(offset))
                continue
            if kind == "scatter":
                for k in range(1, PLANES):
                    there = rem(lax.axis_index("z") + k, PLANES)
                    add(source.at[there], target.at[k - 1], self.along(k))
                continue
            base = 0
            if kind == "fetch":
                base = rem(lax.axis_index("z") + offset, PLANES) * self.plane
            for k in range(1, self.plane):
                other, device = self.across(k)
                add(source.at[base + other], target.at[me], device)
            local.append(
                pltpu.make_async_copy(source.at[base + me], target.at[me], own.at[len(local)])
            )
        return local + remote

    def start(self, sources, targets, sems):
        self.greet()
        for copy in self.copies(sources, targets, sems):
            copy.start()

    def wait(self, sources, targets, sems):
        for copy in self.copies(sources, targets, sems):
            copy.wait()


class Reducer:
    def __init__(self, sizes, shape):
        self.sizes = sizes
        self.rows, self.lanes = shape[-2:]
        self.half = self.lanes // 2

    def scratch(self):
        z, y, x, _ = self.sizes
        r, w, h = self.rows, self.lanes, self.half
        crossing = x + y - 2
        return [
            pltpu.VMEM((z, y, x, r, w), BF),
            pltpu.VMEM((z, y, x, r, w), BF),
            pltpu.VMEM((x - 1, z, y, r, h), BF),
            pltpu.VMEM((y - 1, z, x, r, h), BF),
            pltpu.VMEM((y - 1, z, r, h), BF),
            pltpu.VMEM((x - 1, z, r, h), BF),
            pltpu.SemaphoreType.DMA((1,)),
            pltpu.SemaphoreType.DMA((1 + 2 * crossing,)),
            pltpu.SemaphoreType.DMA((1 + 2 * crossing,)),
        ]

    def bind(self, source, refs):
        self.source = source
        self.held, self.got0, self.got1x, self.got1y, self.got2y, self.got2x = refs[:6]
        self.local, self.send, self.receive = refs[6:]
        self.z, self.y, self.x, self.c = (lax.axis_index(name) for name in ALL)
        return self

    def index(self, z, y, x, lanes):
        return (z, y, x, EVERY, lanes)

    def slab(self, z, y, x, lanes):
        return self.held.at[self.index(z, y, x, lanes)]

    given = slab

    def remote(self, n, source, target, device):
        return pltpu.make_async_remote_copy(
            src_ref=source,
            dst_ref=target,
            send_sem=self.send.at[n],
            recv_sem=self.receive.at[n],
            device_id=device,
            device_id_type=pl.DeviceIdType.MESH,
        )

    def first(self):
        other = 1 - self.c
        return [
            pltpu.make_async_copy(self.source.at[:, :, :, self.c], self.held, self.local.at[0]),
            self.remote(0, self.source.at[:, :, :, other], self.got0, {"c": other}),
        ]

    def second(self):
        _, y_size, x_size, _ = self.sizes
        left, right = pl.ds(0, self.half), pl.ds(self.half, self.half)
        copies = []
        for k in range(1, x_size):
            there = rem(self.x + k, x_size)
            copies.append((self.given(EVERY, EVERY, there, left), self.got1x.at[k - 1], {"x": there}))
        for k in range(1, y_size):
            there = rem(self.y + k, y_size)
            copies.append((self.given(EVERY, there, EVERY, right), self.got1y.at[k - 1], {"y": there}))
        return [self.remote(1 + n, *copy) for n, copy in enumerate(copies)]

    def third(self):
        _, y_size, x_size, _ = self.sizes
        left, right = pl.ds(0, self.half), pl.ds(self.half, self.half)
        at = 1 + x_size + y_size - 2
        copies = []
        for k in range(1, y_size):
            there = rem(self.y + k, y_size)
            copies.append(
                (self.slab(EVERY, there, self.x, left), self.got2y.at[k - 1], {"y": there})
            )
        for k in range(1, x_size):
            there = rem(self.x + k, x_size)
            copies.append(
                (self.slab(EVERY, self.y, there, right), self.got2x.at[k - 1], {"x": there})
            )
        return [self.remote(at + n, *copy) for n, copy in enumerate(copies)]

    def begin(self):
        for copy in self.first():
            copy.start()

    def after_first(self):
        for copy in self.first():
            copy.wait()

        @pl.loop(0, self.sizes[0])
        def _(z):
            at = self.index(z, EVERY, EVERY, EVERY)
            self.held[at] = (self.held[at].astype(F32) + self.got0[z].astype(F32)).astype(BF)

        for copy in self.second():
            copy.start()

    def after_second(self):
        _, y_size, x_size, _ = self.sizes
        for copy in self.second():
            copy.wait()
        h = self.half

        @pl.loop(0, self.sizes[0])
        def _(z):
            for y in range(y_size):
                at = self.index(z, y, self.x, pl.ds(0, h))
                total = self.held[at].astype(F32)
                for k in range(x_size - 1):
                    total += self.got1x[k, z, y].astype(F32)
                self.held[at] = total.astype(BF)
            for x in range(x_size):
                at = self.index(z, self.y, x, pl.ds(h, h))
                total = self.held[at].astype(F32)
                for k in range(y_size - 1):
                    total += self.got1y[k, z, x].astype(F32)
                self.held[at] = total.astype(BF)

        for copy in self.third():
            copy.start()

    def after_third(self, out_ref):
        _, y_size, x_size, _ = self.sizes
        for copy in self.third():
            copy.wait()
        h = self.half

        @pl.loop(0, self.sizes[0])
        def _(z):
            total = self.held[self.index(z, self.y, self.x, pl.ds(0, h))].astype(F32)
            for k in range(y_size - 1):
                total += self.got2y[k, z].astype(F32)
            out_ref[z, :, :h] = total.astype(BF)
            total = self.held[self.index(z, self.y, self.x, pl.ds(h, h))].astype(F32)
            for k in range(x_size - 1):
                total += self.got2x[k, z].astype(F32)
            out_ref[z, :, h:] = total.astype(BF)


class Halved(Reducer):
    def scratch(self):
        z, y, x, _ = self.sizes
        r, w, h = self.rows, self.lanes, self.half
        crossing = x + y - 2
        return [
            pltpu.VMEM((z, y, x, r, w), BF),
            pltpu.VMEM((x - 1, z, y, r, h), BF),
            pltpu.VMEM((y - 1, z, x, r, h), BF),
            pltpu.VMEM((y - 1, z, r, h), BF),
            pltpu.VMEM((x - 1, z, r, h), BF),
            pltpu.SemaphoreType.DMA((1,)),
            pltpu.SemaphoreType.DMA((1 + 2 * crossing,)),
            pltpu.SemaphoreType.DMA((1 + 2 * crossing,)),
        ]

    def bind(self, source, refs):
        self.source = source
        self.held, self.got1x, self.got1y, self.got2y, self.got2x = refs[:5]
        self.local, self.send, self.receive = refs[5:]
        self.z, self.y, self.x, self.c = (lax.axis_index(name) for name in ALL)
        return self

    def given(self, z, y, x, lanes):
        return self.source.at[self.index(z, y, x, lanes)]

    def first(self):
        return [pltpu.make_async_copy(self.source, self.held, self.local.at[0])]

    def begin(self):
        for copy in self.first() + self.second():
            copy.start()

    def after_first(self):
        pass

    def after_second(self):
        for copy in self.first():
            copy.wait()
        super().after_second()


class Resident(Reducer):
    def scratch(self):
        z, y, x, c = self.sizes
        r, w, h = self.rows, self.lanes, self.half
        count = 1 + 2 * (x + y - 2) + z - 1
        return [
            pltpu.VMEM((z, y, x, c, r, w), BF),
            pltpu.VMEM((z, y, x, r, w), BF),
            pltpu.VMEM((x - 1, z, y, r, h), BF),
            pltpu.VMEM((y - 1, z, x, r, h), BF),
            pltpu.VMEM((y - 1, z, r, h), BF),
            pltpu.VMEM((x - 1, z, r, h), BF),
            pltpu.VMEM((z, r, w), BF),
            pltpu.VMEM((z - 1, r, w), BF),
            pltpu.SemaphoreType.DMA((count,)),
            pltpu.SemaphoreType.DMA((count,)),
        ]

    def bind(self, refs):
        self.held, self.got0, self.got1x, self.got1y, self.got2y, self.got2x = refs[:6]
        self.left, self.got3, self.send, self.receive = refs[6:]
        self.z, self.y, self.x, self.c = (lax.axis_index(name) for name in ALL)
        return self

    def index(self, z, y, x, lanes):
        return (z, y, x, self.c, EVERY, lanes)

    def first(self):
        other = 1 - self.c
        return [self.remote(0, self.held.at[:, :, :, other], self.got0, {"c": other})]

    def fourth(self):
        _, y_size, x_size, _ = self.sizes
        at = 1 + 2 * (x_size + y_size - 2)
        copies = []
        for k in range(1, PLANES):
            there = rem(self.z + k, PLANES)
            copies.append(
                self.remote(at + k - 1, self.left.at[there], self.got3.at[k - 1], {"z": there})
            )
        return copies

    def after_third_start(self):
        self.after_third(self.left)
        for copy in self.fourth():
            copy.start()

    def finish(self, out_ref):
        for copy in self.fourth():
            copy.wait()
        total = self.left[self.z].astype(F32)
        for k in range(PLANES - 1):
            total += self.got3[k].astype(F32)
        out_ref[...] = total


class SmallSum:
    def __init__(self, sizes, shape):
        self.shape = shape
        self.steps = list(zip(("c", "x", "y", "z"), (sizes[3], sizes[2], sizes[1], sizes[0])))

    def scratch(self):
        count = sum(n - 1 for _, n in self.steps)
        return (
            [pltpu.VMEM(self.shape, F32) for _ in range(4)]
            + [pltpu.VMEM((n - 1,) + self.shape, F32) for _, n in self.steps]
            + [pltpu.SemaphoreType.DMA((count,))] * 2
        )

    def bind(self, refs):
        self.held, self.got = refs[:4], refs[4:8]
        self.send, self.receive = refs[8:]
        return self

    def copies(self, step):
        axis, n = self.steps[step]
        at = sum(m - 1 for _, m in self.steps[:step])
        me = lax.axis_index(axis)
        return [
            pltpu.make_async_remote_copy(
                src_ref=self.held[step],
                dst_ref=self.got[step].at[k - 1],
                send_sem=self.send.at[at + k - 1],
                recv_sem=self.receive.at[at + k - 1],
                device_id={axis: rem(me + k, n)},
                device_id_type=pl.DeviceIdType.MESH,
            )
            for k in range(1, n)
        ]

    def start(self, step):
        for copy in self.copies(step):
            copy.start()

    def advance(self, step, out_ref=None):
        for copy in self.copies(step):
            copy.wait()
        total = self.held[step][...]
        for k in range(self.steps[step][1] - 1):
            total += self.got[step][k]
        if step < 3:
            self.held[step + 1][...] = total
            self.start(step + 1)
        else:
            out_ref[...] = total


def forward_pair(queries, keys, values, bias):
    masks = lane_masks()
    all_scores = []
    for mine, other, one in masks:
        if bias is None:
            all_scores.append(causal_mask(dot(keys, queries * mine, 1, 1)))
        else:
            all_scores.append(dot(keys * mine + bias * one, queries * mine + one, 1, 1))
    parts = []
    stats = []
    held = []
    for h in range(2):
        mine, other, _ = masks[h]
        scores = all_scores[h]
        row_max = jnp.max(scores, axis=0, keepdims=True)
        probs = jnp.exp(scores - row_max).astype(BF)
        both = dot(values * mine + other, probs, 0, 0)
        halves = (both[:HD], both[HD:])
        total = halves[1 - h]
        parts.append(halves[h] / total)
        stats.append((row_max + jnp.log(total[0:1]), row_max))
        held.append(probs)
    return jnp.concatenate(parts, axis=0).T.astype(BF), stats, held


def backward_pair(queries, grad, keys, values, probs_of, delta):
    grad_k = None
    grad_v = None
    grad_q = []
    for h, (mine, other, one) in enumerate(lane_masks()):
        query_h = queries * mine
        grad_h = grad * mine
        probs = probs_of(h, keys, query_h)
        grad_p = dot(values, grad_h, 1, 1)
        if delta is None:
            delta_h = jnp.sum(probs * grad_p, axis=0, keepdims=True)
        else:
            delta_h = delta[h]
        grad_s = (probs * (grad_p - delta_h)).astype(BF)
        term_v = dot(probs.astype(BF), grad_h, 1, 0)
        term_k = dot(grad_s, query_h, 1, 0)
        grad_v = term_v if grad_v is None else grad_v + term_v
        grad_k = term_k if grad_k is None else grad_k + term_k
        grad_q.append(dot(keys, grad_s, 0, 0)[h * HD : (h + 1) * HD])
    grad_kv = jnp.concatenate([grad_k, grad_v], axis=1).astype(BF)
    return grad_kv, jnp.concatenate(grad_q, axis=0).T.astype(BF)


def causal_probs(lse):
    return lambda h, keys, query: jnp.exp(causal_mask(dot(keys, query, 1, 1)) - lse[h])


def key_bias(keys, lens):
    row = lax.broadcasted_iota(jnp.int32, (keys, 128), 0) + lax.axis_index("z") * keys
    return jnp.where(row < lens[0:1, :], 0.0, MASKED).astype(BF)


def split_refs(refs, *counts):
    groups = []
    at = 0
    for count in counts:
        groups.append(refs[at : at + count])
        at += count
    return groups


def carried(courier, reducers, body):
    jobs = len(courier.jobs)
    sums = len(reducers)
    parts = [len(one.scratch()) for one in reducers]

    def kernel(ins, outs, scratch, refs):
        own_in, sources, summands, own_out, targets, results, own_scratch, sems, rest = split_refs(
            refs, ins, jobs, sums, outs, jobs, sums, scratch, 3, sum(parts)
        )
        step = pl.program_id(0)
        work = split_refs(rest, *parts)

        def bound():
            return [one.bind(value, refs) for one, value, refs in zip(reducers, summands, work)]

        @pl.when(step == 0)
        def _():
            courier.start(sources, targets, sems)
            for one in bound():
                one.begin()

        body(own_in, own_out, own_scratch)

        for n in range(sums):

            @pl.when(step == 1)
            def _(n=n):
                bound()[n].after_first()

            @pl.when(step == (2 + n if sums > 1 else 3))
            def _(n=n):
                bound()[n].after_second()

            @pl.when(step == PAIRS - sums + n)
            def _(n=n):
                bound()[n].after_third(results[n])

        @pl.when(step == PAIRS - 1)
        def _():
            courier.wait(sources, targets, sems)

    return kernel


def call(courier, ident, body, args, in_specs, out_shape, out_specs, scratch, flops, summands=()):
    if summands:
        courier.in_plane = True
    reducers = [
        (Halved if value.ndim == 5 else Reducer)(courier.sizes, value.shape) for value in summands
    ]
    shapes = [(PLANES,) + value.shape[-2:] for value in summands]
    kernel = carried(courier, reducers, body)
    counts = (len(args), len(out_shape), len(scratch))
    outs = pl.pallas_call(
        lambda *refs: kernel(*counts, refs),
        grid=(PAIRS,),
        out_shape=out_shape
        + courier.out_shape()
        + [jax.ShapeDtypeStruct(shape, BF) for shape in shapes],
        in_specs=in_specs + courier.specs() + [pl.BlockSpec(memory_space=pl.ANY)] * len(shapes),
        out_specs=out_specs
        + courier.specs()
        + [pl.BlockSpec(shape, lambda p: (0, 0, 0)) for shape in shapes],
        scratch_shapes=scratch
        + courier.scratch()
        + [ref for one in reducers for ref in one.scratch()],
        compiler_params=courier.params(ident),
        cost_estimate=pl.CostEstimate(flops=flops, bytes_accessed=2**24, transcendentals=2**20),
    )(*args, *courier.values(), *summands)
    return outs[: len(out_shape)], outs[len(out_shape) :]


def reduce_all(sizes, ident, summands, scattered):
    courier = Courier(sizes, [("scatter", 0, value) for value in scattered])
    courier.in_plane = True
    courier.lines += list(range(1, PLANES))
    jobs = len(scattered)
    count = len(summands)
    reducers = [Reducer(sizes, value.shape) for value in summands]
    shapes = [value.shape[-2:] for value in summands]

    def kernel(*refs):
        sources, arrays, targets, results, sems, rest = split_refs(
            refs, jobs, count, jobs, count, 3, len(refs) - 2 * jobs - 2 * count - 3
        )
        courier.start(sources, targets, sems)
        bound = []
        last = []
        for n in range(count):
            refs_n = rest[13 * n : 13 * n + 13]
            bound.append(reducers[n].bind(arrays[n], refs_n[:9]))
            last.append(refs_n[9:])

        def leave(n):
            left, got, send, receive = last[n]
            copies = []
            for k in range(1, PLANES):
                copies.append(
                    pltpu.make_async_remote_copy(
                        src_ref=left.at[rem(lax.axis_index("z") + k, PLANES)],
                        dst_ref=got.at[k - 1],
                        send_sem=send.at[k - 1],
                        recv_sem=receive.at[k - 1],
                        device_id=courier.along(k),
                        device_id_type=pl.DeviceIdType.MESH,
                    )
                )
            return copies

        for one in bound:
            one.begin()
        for one in bound:
            one.after_first()
        for one in bound:
            one.after_second()
        for n, one in enumerate(bound):
            one.after_third(last[n][0])
            for copy in leave(n):
                copy.start()
        for n in range(count):
            for copy in leave(n):
                copy.wait()
            left, got = last[n][:2]
            total = left[lax.axis_index("z")].astype(F32)
            for k in range(PLANES - 1):
                total += got[k].astype(F32)
            results[n][...] = total
        courier.wait(sources, targets, sems)

    scratch = []
    for n in range(count):
        scratch += reducers[n].scratch() + [
            pltpu.VMEM((PLANES,) + shapes[n], BF),
            pltpu.VMEM((PLANES - 1,) + shapes[n], BF),
            pltpu.SemaphoreType.DMA((PLANES - 1,)),
            pltpu.SemaphoreType.DMA((PLANES - 1,)),
        ]
    outs = pl.pallas_call(
        kernel,
        out_shape=courier.out_shape() + [jax.ShapeDtypeStruct(shape, F32) for shape in shapes],
        in_specs=courier.specs() + [pl.BlockSpec(memory_space=pl.ANY)] * count,
        out_specs=courier.specs() + [pl.BlockSpec(memory_space=pltpu.VMEM)] * count,
        scratch_shapes=courier.scratch() + scratch,
        compiler_params=courier.params(ident),
    )(*courier.values(), *summands)
    return outs[:jobs], outs[jobs:]


def summand_of(sizes, arrays):
    devices = sizes[0] * sizes[1] * sizes[2] * sizes[3]
    parts = [a.reshape(devices, a.shape[0] // devices, a.shape[1]) for a in arrays]
    joined = parts[0] if len(parts) == 1 else jnp.concatenate(parts, axis=1)
    return joined.astype(BF).reshape(tuple(sizes) + joined.shape[1:])


def over_z(left, got):
    own = lax.dynamic_index_in_dim(left, lax.axis_index("z"), 0, keepdims=False)
    return own.astype(F32) + jnp.sum(got.astype(F32), axis=0)


def block_specs(tokens, keys):
    return dict(
        col=pl.BlockSpec((tokens, 128), lambda p: (0, p)),
        pair=pl.BlockSpec((keys, 256), lambda p: (0, p)),
        rows=pl.BlockSpec((keys, H * HD), lambda p: (0, 0)),
        weight=pl.BlockSpec((H * HD, 128), lambda p: (0, p)),
        stat=pl.BlockSpec((1, 2, tokens), lambda p: (p, 0, 0)),
    )


def rms(values, gain):
    r = lax.rsqrt(jnp.mean(values * values, axis=-1, keepdims=True) + EPSILON)
    return values * r * gain


ORDER = (1, 2, 3, 0)


def forward_part(sizes, ident, memory, lens, inputs, gains, weights, key_weight, value_weight):
    tokens, width = inputs.shape
    positions = memory.shape[1]
    plane = sizes[1] * sizes[2] * sizes[3]
    keys = plane * positions
    rows = jax.ShapeDtypeStruct((tokens, width), BF)
    wide = jax.ShapeDtypeStruct((tokens, width), F32)
    stat = jax.ShapeDtypeStruct((PAIRS, 2, tokens), F32)
    near = range(1, PLANES)
    jobs = [("fetch", r, memory) for r in ORDER]
    jobs += [("line", -r, lens) for r in near] + [("line", -r, rows) for r in near]
    jobs += [("line", r, rows) for r in near] + [("line", r, stat) for r in near]
    courier = Courier(sizes, jobs)
    courier.lines = list(near)
    count = PLANES * PAIRS

    def kernel(*refs):
        ins, sources, outs, parts, targets, work, sems = split_refs(refs, 11, 1, 8, 4, 13, 7, 3)
        x_ref, self_gain, cross_gain, wq_ref, wk_ref, wv_ref, wo_ref, wc_ref = ins[:8]
        lens_ref, key_ref, value_ref = ins[8:]
        (memory_ref,) = sources
        q_ref, k_ref, v_ref, lse_ref, attn_ref, hidden_ref, query_ref, top_ref = outs
        part_ref, part_lse_ref, kv_ref, probs_ref = parts
        row_buf, query_buf, out_buf, lse_buf, lens_buf, near_lens, load_sems = work
        copies = courier.copies(
            [memory_ref] * PLANES
            + [lens_ref] * 3
            + [query_ref] * 3
            + [out_buf.at[n] for n in range(3)]
            + [lse_buf.at[n] for n in range(3)],
            list(targets[:4])
            + [near_lens.at[n] for n in range(3)]
            + list(targets[4:]),
            sems,
        )
        own, remote = copies[:PLANES], copies[PLANES:]
        far = plane - 1
        lines = remote[PLANES * far :]
        lens_lines, query_lines, out_lines, lse_lines = split_refs(lines, 3, 3, 3, 3)
        step = pl.program_id(0)
        me = courier.me()

        def start_fetch(n):
            for copy in [own[n]] + remote[n * far : n * far + far]:
                copy.start()

        @pl.when(step == 0)
        def _():
            courier.greet()
            start_fetch(0)
            for copy in lens_lines:
                copy.start()
            values = x_ref[...].astype(F32)
            normed = rms(values, self_gain[...]).astype(BF)
            q_ref[...] = dot(normed, wq_ref[...], 1, 0).astype(BF)
            k_ref[...] = dot(normed, wk_ref[...], 1, 0).astype(BF)
            v_ref[...] = dot(normed, wv_ref[...], 1, 0).astype(BF)

            @pl.loop(0, PAIRS)
            def _(p):
                cols = pl.ds(pl.multiple_of(p * 128, 128), 128)
                out, stats, _ = forward_pair(q_ref[:, cols], k_ref[:, cols], v_ref[:, cols], None)
                attn_ref[:, cols] = out
                for h in range(2):
                    lse_ref[p, h : h + 1, :] = stats[h][0]

            hidden = values + dot(attn_ref[...], wo_ref[...], 1, 0)
            hidden_ref[...] = hidden
            normed = rms(hidden, cross_gain[...]).astype(BF)
            query_ref[...] = dot(normed, wc_ref[...], 1, 0).astype(BF)
            query_lines[0].start()

        for n, r in enumerate(ORDER):

            @pl.when(step == n * PAIRS)
            def _(n=n, r=r):
                loads = []

                def load(block):
                    at = pl.ds(pl.multiple_of(block * positions, positions), positions)
                    copy = pltpu.make_async_copy(
                        targets[n].at[block], row_buf.at[at], load_sems.at[len(loads)]
                    )
                    copy.start()
                    loads.append(copy)

                own[n].wait()
                load(me)
                for k in range(1, plane):
                    remote[n * far + k - 1].wait()
                    load(rem(me + (plane - k), plane))
                if n + 1 < PLANES:
                    start_fetch(n + 1)
                if r > 0:
                    query_lines[r - 1].wait()
                    copy = pltpu.make_async_copy(
                        targets[3 + r], query_buf, load_sems.at[plane]
                    )
                    copy.start()
                    if r + 1 < PLANES:
                        query_lines[r].start()
                    lens_lines[r - 1].wait()
                    lens_buf[...] = near_lens[r - 1]
                    copy.wait()
                else:
                    query_buf[...] = query_ref[...]
                    lens_buf[...] = lens_ref[...]
                for copy in loads:
                    copy.wait()

        phase = lax.div(step, PAIRS)
        p = rem(step, PAIRS)
        cols = pl.ds(pl.multiple_of(p * 128, 128), 128)
        both = jnp.concatenate([key_ref[...], value_ref[...]], axis=1)
        kv_ref[...] = dot(row_buf[...], both, 1, 0).astype(BF)
        bias = key_bias(keys, lens_buf[...])
        out, stats, held = forward_pair(query_buf[:, cols], kv_ref[:, :128], kv_ref[:, 128:], bias)
        out_buf[phase, :, cols] = out
        for h in range(2):
            probs_ref[h] = held[h]
            lse_buf[phase, p, h : h + 1, :] = stats[h][0]
            top_ref[phase, p, h : h + 1, :] = stats[h][1]

        for n, r in enumerate(ORDER[:-1]):

            @pl.when(step == n * PAIRS + PAIRS - 1)
            def _(r=r):
                out_lines[r - 1].start()
                lse_lines[r - 1].start()

        @pl.when(step == count - 1)
        def _():
            part_ref[...] = out_buf[PLANES - 1]
            part_lse_ref[...] = lse_buf[PLANES - 1]
            for copy in out_lines + lse_lines:
                copy.wait()

    once = pl.Buffered(1)

    def fixed(*shape):
        return pl.BlockSpec(shape, lambda t: (0,) * len(shape), pipeline_mode=once)

    def out_fixed(*shape):
        return pl.BlockSpec(shape, lambda t: (0,) * len(shape))

    def where(t):
        return rem(lax.div(t, PAIRS) + 1, PLANES), rem(t, PAIRS)

    square = fixed(width, width)
    weight = pl.BlockSpec((width, 128), lambda t: (0, rem(t, PAIRS)))
    hbm = pl.BlockSpec(memory_space=pl.ANY)
    flat = out_fixed(tokens, width)
    flat_stat = out_fixed(PAIRS, 2, tokens)
    shapes = courier.out_shape()
    outs = pl.pallas_call(
        kernel,
        grid=(count,),
        out_shape=[rows, rows, rows, stat, rows, wide, rows]
        + [jax.ShapeDtypeStruct((PLANES, PAIRS, 2, tokens), F32), rows, stat]
        + [
            jax.ShapeDtypeStruct((PLANES, keys, 2 * width), BF),
            jax.ShapeDtypeStruct((PLANES, H, keys, tokens), BF),
        ]
        + shapes[:4]
        + shapes[7:],
        in_specs=[fixed(tokens, width), fixed(1, width), fixed(1, width)]
        + [square] * 5
        + [fixed(8, 128), weight, weight, hbm],
        out_specs=[flat] * 3
        + [flat_stat]
        + [flat] * 3
        + [out_fixed(PLANES, PAIRS, 2, tokens), flat, flat_stat]
        + [
            pl.BlockSpec((None, keys, 256), lambda t: (where(t)[0], 0, where(t)[1])),
            pl.BlockSpec((None, 2, keys, tokens), lambda t: where(t) + (0, 0)),
        ]
        + [hbm] * 13,
        scratch_shapes=[
            pltpu.VMEM((keys, width), BF),
            pltpu.VMEM((tokens, width), BF),
            pltpu.VMEM((PLANES, tokens, width), BF),
            pltpu.VMEM((PLANES, PAIRS, 2, tokens), F32),
            pltpu.VMEM((8, 128), jnp.int32),
            pltpu.VMEM((3, 8, 128), jnp.int32),
            pltpu.SemaphoreType.DMA((plane + 1,)),
        ]
        + courier.scratch(),
        compiler_params=pltpu.CompilerParams(
            vmem_limit_bytes=62 * 2**20, collective_id=ident, has_side_effects=True
        ),
    )(inputs, *gains, *weights, lens, key_weight, value_weight, memory)
    saved, (tops, part0, lse0, kv, probs), moved = outs[:7], outs[7:12], outs[12:]
    return dict(
        saved=saved,
        tops=tops,
        keyvals=kv,
        probs=probs,
        rows={r: moved[n] for n, r in enumerate(ORDER)},
        queries={0: saved[6], **{r: moved[3 + r] for r in near}},
        parts=[part0] + [moved[6 + r] for r in near],
        lses=[lse0] + [moved[9 + r] for r in near],
    )


def glu_parts(gate_vals):
    inner = 0.7978845608028654 * (gate_vals + 0.044715 * gate_vals * gate_vals * gate_vals)
    t = jnp.tanh(inner)
    gelu = 0.5 * gate_vals * (1.0 + t)
    slope = 0.5 * (1.0 + t) + 0.5 * gate_vals * (1.0 - t * t) * 0.7978845608028654 * (
        1.0 + 0.134145 * gate_vals * gate_vals
    )
    return gelu, slope


def spread(rows):
    both = [jnp.broadcast_to(rows[h : h + 1], (HD, rows.shape[1])) for h in range(2)]
    return jnp.concatenate(both, axis=0).T


def middle_kernel(*refs, sizes, packed):
    (
        part0,
        part1,
        part2,
        part3,
        lse0,
        lse1,
        lse2,
        lse3,
        h1_ref,
        wo_ref,
        gain_ref,
        cot_ref,
        gate_ref,
        up_ref,
        down_ref,
        out_ref,
        attn_ref,
        two_ref,
        da_ref,
        stats_ref,
        gnorm_ref,
        gwo_ref,
        *grad_refs,
        gdown_ref,
        raw_ref,
        h2_ref,
        n3_ref,
        total_ref,
        dn3_ref,
    ) = refs[: 29 + (not packed)]
    step = pl.program_id(0)
    last = pl.num_programs(0) - 1
    devices = sizes[0] * sizes[1] * sizes[2] * sizes[3]
    if packed:
        wide_ref, wide_got, tall_ref, tall_got, send, receive = refs[29:]
        core = lax.axis_index("c")

    def exchange(n):
        slot = rem(n, 2)
        return [
            pltpu.make_async_remote_copy(
                src_ref=source,
                dst_ref=target,
                send_sem=send.at[n, at],
                recv_sem=receive.at[n, at],
                device_id={"c": 1 - core},
                device_id_type=pl.DeviceIdType.MESH,
            )
            for at, (source, target) in enumerate(
                (
                    (wide_ref.at[slot, :, :, :, 1 - core], wide_got.at[n]),
                    (tall_ref.at[slot, :, :, 1 - core], tall_got.at[n]),
                )
            )
        ]
    parts = (part0, part1, part2, part3)
    lses = (lse0, lse1, lse2, lse3)

    @pl.when(step == 0)
    def _():
        for p in range(PAIRS):
            cols = pl.ds(p * 128, 128)
            values = [ref[p] for ref in lses]
            top = functools.reduce(jnp.maximum, values)
            scales = [jnp.exp(v - top) for v in values]
            total = functools.reduce(jnp.add, scales)
            stats_ref[0, p] = top + jnp.log(total)
            raw = None
            for ref, scale in zip(parts, scales):
                term = spread(scale / total) * ref[:, cols].astype(F32)
                raw = term if raw is None else raw + term
            raw_ref[:, cols] = raw
            attn_ref[:, cols] = raw.astype(BF)
        hidden = h1_ref[...] + dot(attn_ref[...], wo_ref[...], 1, 0)
        h2_ref[...] = hidden
        n3_ref[...] = rms(hidden, gain_ref[...]).astype(BF)
        total_ref[...] = hidden
        dn3_ref[...] = jnp.zeros_like(dn3_ref)
        if packed:
            barrier = pltpu.get_barrier_semaphore()
            pl.semaphore_signal(
                barrier,
                inc=1,
                device_id={"c": 1 - core},
                device_id_type=pl.DeviceIdType.MESH,
            )
            pl.semaphore_wait(barrier, 1)

    def one_chunk():
        normed = n3_ref[...]
        branch = cot_ref[...]
        gate_vals = dot(normed, gate_ref[...], 1, 0)
        up_vals = dot(normed, up_ref[...], 1, 0)
        grad_inner = dot(branch, down_ref[...], 1, 1)
        gelu, slope = glu_parts(gate_vals)
        inner = (gelu * up_vals).astype(BF)
        grad_gate = (grad_inner * up_vals * slope).astype(BF)
        grad_up = (grad_inner * gelu).astype(BF)
        total_ref[...] += dot(inner, down_ref[...], 1, 0)
        dn3_ref[...] += dot(grad_gate, gate_ref[...], 1, 1) + dot(grad_up, up_ref[...], 1, 1)
        terms = [dot(normed, grad_gate, 0, 0), dot(normed, grad_up, 0, 0)]
        if packed:
            shape = (devices, terms[0].shape[0] // devices, terms[0].shape[1])
            both = jnp.concatenate([t.reshape(shape) for t in terms], axis=1).astype(BF)
            slot = rem(step, 2)
            wide_ref[slot] = both.reshape(wide_ref.shape[1:])
            tall_ref[slot] = dot(inner, branch, 0, 0).astype(BF).reshape(tall_ref.shape[1:])
            for copy in exchange(step):
                copy.start()
        else:
            for ref, term in zip(grad_refs, terms):
                ref[...] = term
            gdown_ref[...] = dot(inner, branch, 0, 0).astype(BF).reshape(gdown_ref.shape)

    if packed:

        @pl.when(step < last)
        def _():
            one_chunk()

    else:
        one_chunk()

    @pl.when(step == last)
    def _():
        out_ref[...] = total_ref[...].astype(BF)
        hidden = h2_ref[...]
        grad = dn3_ref[...]
        r = lax.rsqrt(jnp.mean(hidden * hidden, axis=-1, keepdims=True) + EPSILON)
        u = gain_ref[...] * grad
        back = r * u - hidden * (r * r * r) * jnp.mean(u * hidden, axis=-1, keepdims=True)
        gnorm_ref[...] = jnp.sum(grad * hidden * r, axis=0, keepdims=True)
        two = cot_ref[...].astype(F32) + back
        two_ref[...] = two
        low = two.astype(BF)
        da_ref[...] = dot(low, wo_ref[...], 1, 1).astype(BF)
        gwo_ref[...] = dot(attn_ref[...], low, 0, 0).astype(BF)
        for p in range(PAIRS):
            cols = pl.ds(p * 128, 128)
            product = (da_ref[:, cols].astype(F32) * raw_ref[:, cols]).T
            for h in range(2):
                stats_ref[1, p, h : h + 1] = jnp.sum(
                    product[h * HD : (h + 1) * HD], axis=0, keepdims=True
                )

    if packed:

        @pl.when(step > 0)
        def _():
            before = step - 1
            slot = rem(before, 2)
            for copy in exchange(before):
                copy.wait()
            mine = wide_ref[slot, :, :, :, core].astype(F32)
            grad_refs[0][...] = (mine + wide_got[before].astype(F32)).astype(BF)
            mine = tall_ref[slot, :, :, core].astype(F32)
            gdown_ref[0] = (mine + tall_got[before].astype(F32)).astype(BF)


def middle(sizes, parts, lses, hidden, out_weight, gain, cotangent, gate, up, down):
    tokens, width = hidden.shape
    inner = gate.shape[1]
    chunk = 512
    count = inner // chunk
    devices = sizes[0] * sizes[1] * sizes[2] * sizes[3]
    share = width // devices
    down_share = inner // devices
    packed = share % 8 == 0 and chunk * PLANES == inner
    first = lambda p: jnp.minimum(p, count - 1)
    fixed = lambda *shape: pl.BlockSpec(shape, lambda p: (0,) * len(shape))
    whole = fixed(tokens, width)
    square = fixed(width, width)
    stat = fixed(PAIRS, 2, tokens)
    column = pl.BlockSpec((width, chunk), lambda p: (0, first(p)))
    scratch = [
        pltpu.VMEM((tokens, width), F32),
        pltpu.VMEM((tokens, width), F32),
        pltpu.VMEM((tokens, width), BF),
        pltpu.VMEM((tokens, width), F32),
        pltpu.VMEM((tokens, width), F32),
    ]
    params = dict(vmem_limit_bytes=VMEM)
    if packed:
        z, y, x, c = sizes
        wide_shape = (z, y, x, 2 * share)
        tall_shape = (y, x, down_share, width)
        grad_shapes = [
            jax.ShapeDtypeStruct(wide_shape + (inner,), BF),
            jax.ShapeDtypeStruct((z,) + tall_shape, BF),
        ]
        before = lambda p: jnp.maximum(p - 1, 0)
        grad_specs = [
            pl.BlockSpec(wide_shape + (chunk,), lambda p: (0, 0, 0, 0, before(p))),
            pl.BlockSpec((1,) + tall_shape, lambda p: (before(p), 0, 0, 0, 0)),
        ]
        scratch += [
            pltpu.VMEM((2, z, y, x, c, 2 * share, chunk), BF),
            pltpu.VMEM((count,) + wide_shape + (chunk,), BF),
            pltpu.VMEM((2, y, x, c, down_share, width), BF),
            pltpu.VMEM((count,) + tall_shape, BF),
            pltpu.SemaphoreType.DMA((count, 2)),
            pltpu.SemaphoreType.DMA((count, 2)),
        ]
        params.update(collective_id=12, has_side_effects=True)
    else:
        grad_shapes = [jax.ShapeDtypeStruct((width, inner), F32)] * 2
        grad_shapes.append(jax.ShapeDtypeStruct((devices, down_share, width), BF))
        grad_specs = [column] * 2
        grad_specs.append(
            pl.BlockSpec((chunk // down_share, down_share, width), lambda p: (p, 0, 0))
        )
    rows = jax.ShapeDtypeStruct((tokens, width), BF)
    wide = jax.ShapeDtypeStruct((tokens, width), F32)
    return pl.pallas_call(
        functools.partial(middle_kernel, sizes=sizes, packed=packed),
        grid=(count + packed,),
        out_shape=[
            rows,
            rows,
            wide,
            rows,
            jax.ShapeDtypeStruct((2, PAIRS, 2, tokens), F32),
            jax.ShapeDtypeStruct((1, width), F32),
            jax.ShapeDtypeStruct((width, width), BF),
        ]
        + grad_shapes,
        in_specs=[whole] * 4
        + [stat] * 4
        + [whole, square, fixed(1, width), whole]
        + [column, column, pl.BlockSpec((chunk, width), lambda p: (first(p), 0))],
        out_specs=[whole] * 4
        + [fixed(2, PAIRS, 2, tokens), fixed(1, width), square]
        + grad_specs,
        scratch_shapes=scratch,
        compiler_params=pltpu.CompilerParams(**params),
    )(*parts, *lses, hidden, out_weight, gain, cotangent, gate, up, down)


def cross_backward(
    courier, ident, r, queries, grad, keyvals, probs, tops, stats, key_weight, value_weight,
    summands=(), before=()
):
    tokens, keys = queries.shape[0], keyvals.shape[1]
    width = H * HD
    spec = block_specs(tokens, keys)
    earlier = [
        pl.BlockSpec((keys, width), lambda p: (0, 0), pipeline_mode=pl.Buffered(1)),
        spec["pair"],
        pl.BlockSpec((width, 256), lambda p: (0, p)),
    ]

    def body(ins, outs, scratch):
        q_ref, da_ref, kv_ref, probs_ref, top_ref, stats_ref, wk_ref, wv_ref = ins[:8]
        dkv_ref, dq_ref, dm_ref = outs[:3]
        (total_ref,) = scratch
        step = pl.program_id(0)

        @pl.when(step == 0)
        def _():
            total_ref[...] = jnp.zeros_like(total_ref)

        def stored(h, keys_h, query_h):
            scale = jnp.exp(top_ref[0, h : h + 1, :] - stats_ref[0, 0, h : h + 1, :])
            return probs_ref[h].astype(F32) * scale

        weights = jnp.concatenate([wk_ref[...], wv_ref[...]], axis=1)
        grad_kv, grad_q = backward_pair(
            q_ref[...],
            da_ref[...],
            kv_ref[:, :128],
            kv_ref[:, 128:],
            stored,
            [stats_ref[1, 0, h : h + 1, :] for h in range(2)],
        )
        dkv_ref[...] = grad_kv
        dq_ref[...] = grad_q
        total_ref[...] += dot(grad_kv, weights, 1, 1)
        if before:
            term = dot(ins[8][...], ins[9][...], 0, 0)
            outs[3][...] = term if len(before) == 2 else term + ins[10][...]

        @pl.when(step == PAIRS - 1)
        def _():
            dm_ref[...] = total_ref[...].astype(BF)

    return call(
        courier,
        ident,
        body,
        [queries, grad, keyvals, probs, tops, stats, key_weight, value_weight] + list(before),
        [
            spec["col"],
            spec["col"],
            pl.BlockSpec((None, keys, 256), lambda p: (r, 0, p)),
            pl.BlockSpec((None, 2, keys, tokens), lambda p: (r, p, 0, 0)),
            pl.BlockSpec((None, 1, 2, tokens), lambda p: (rem(r + 3, PLANES), p, 0, 0)),
            pl.BlockSpec((2, 1, 2, tokens), lambda p: (0, p, 0, 0)),
            spec["weight"],
            spec["weight"],
        ]
        + earlier[: len(before)],
        [
            jax.ShapeDtypeStruct((keys, 2 * width), BF),
            jax.ShapeDtypeStruct((tokens, width), BF),
            jax.ShapeDtypeStruct((keys, width), BF),
        ]
        + [jax.ShapeDtypeStruct((width, 2 * width), F32)] * bool(before),
        [spec["pair"], spec["col"], spec["rows"]] + [earlier[2]] * bool(before),
        [pltpu.VMEM((keys, width), F32)],
        2**35,
        summands,
    )


def weight_terms(courier, ident, rows, grads):
    keys, width = rows[0].shape
    spec = block_specs(keys, keys)
    count = len(rows)

    def body(ins, outs, _):
        total = None
        for rows_ref, grad_ref in zip(ins[:count], ins[count:]):
            term = dot(rows_ref[...], grad_ref[...], 0, 0)
            total = term if total is None else total + term
        outs[0][...] = total[:, :128]
        outs[1][...] = total[:, 128:]

    return call(
        courier,
        ident,
        body,
        list(rows) + list(grads),
        [spec["rows"]] * count + [spec["pair"]] * count,
        [jax.ShapeDtypeStruct((width, width), F32)] * 2,
        [spec["weight"]] * 2,
        [],
        2**34,
    )


def self_backward(courier, ident, queries, grad, keys, values, lse, summand):
    tokens, width = queries.shape
    spec = block_specs(tokens, tokens)

    def body(ins, outs, _):
        q_ref, da_ref, k_ref, v_ref, lse_ref = ins
        dq_ref, dk_ref, dv_ref = outs
        grad_kv, dq_ref[...] = backward_pair(
            q_ref[...],
            da_ref[...],
            k_ref[...],
            v_ref[...],
            causal_probs([lse_ref[0, h : h + 1, :] for h in range(2)]),
            None,
        )
        dk_ref[...] = grad_kv[:, :128]
        dv_ref[...] = grad_kv[:, 128:]

    return call(
        courier,
        ident,
        body,
        [queries, grad, keys, values, lse],
        [spec["col"]] * 4 + [spec["stat"]],
        [jax.ShapeDtypeStruct((tokens, width), BF)] * 3,
        [spec["col"]] * 3,
        [],
        2**33,
        [summand],
    )


def rms_back(values, gain, grad):
    r = lax.rsqrt(jnp.mean(values * values, axis=-1, keepdims=True) + EPSILON)
    u = gain * grad
    back = r * u - values * (r * r * r) * jnp.mean(u * values, axis=-1, keepdims=True)
    return back, jnp.sum(grad * values * r, axis=0, keepdims=True)


def ending(sizes, ident, rows, grads, summed, grad_q, grad_rows, left, two, held, lse, small_in):
    courier = Courier(
        sizes,
        [("line", PLANES - 1, grad_q[-1]), ("return", 0, grad_rows)]
        + [("scatter", 0, value) for value in left],
    )
    courier.lines = list(range(1, PLANES))
    jobs = len(courier.jobs)
    devices = sizes[0] * sizes[1] * sizes[2] * sizes[3]
    keys, width = rows[0].shape
    tokens = two.shape[0]
    share = width // devices
    chunk = 512
    cuts = keys // chunk
    groups = [Resident(sizes, (2 * share, width)) for _ in range(2)]
    groups += [Resident(sizes, (2 * share, 256)) for _ in range(6)]
    small = SmallSum(sizes, (8, width))
    early = [two] + list(held) + list(grad_q[:-1])
    count = len(rows)
    far = list(rows) + list(grads) + [summed] + early
    counts = (len(far), len(small_in) + 1, jobs, 6, jobs - 1, 4, len(early) - 1, 8, 3, 80, 10)

    def pack(ref, first, second, cols=EVERY):
        lanes = first.shape[1]
        parts = [v.astype(F32).reshape(devices, share, lanes) for v in (first, second)]
        both = jnp.concatenate(parts, axis=1).astype(BF)
        ref[:, :, :, :, :, cols] = both.reshape(tuple(sizes) + both.shape[1:])

    def kernel(*refs):
        far_refs, near, sources, outs, targets, stage, loaded, work, sems, group_refs, rest = (
            split_refs(refs, *counts)
        )
        self_gain, cross_gain, ffn_term, lse_ref = near
        grad_in, *sums, norm_sums = outs
        row_buf, grad_buf, total, load_sems = stage
        dq_got, da_ref, dq1, dk1, dv1, normed_ref, _, norm_all = work
        chunk_sems, early_sems = load_sems, work[6]
        copies = courier.copies(sources, [dq_got] + list(targets), sems)
        courier.greet()
        for copy in copies:
            copy.start()

        def chunk_loads(r, i):
            slot = rem(i, 2)
            where = pl.ds(pl.multiple_of(rem(i, cuts) * chunk, chunk), chunk)
            return [
                pltpu.make_async_copy(
                    far_refs[r].at[where], row_buf.at[slot], chunk_sems.at[slot, 0]
                ),
                pltpu.make_async_copy(
                    far_refs[count + r].at[where], grad_buf.at[slot], chunk_sems.at[slot, 1]
                ),
            ]

        def start_chunk(i):
            for r in range(count):

                @pl.when(lax.div(jnp.int32(i), cuts) == r)
                def _(r=r):
                    for copy in chunk_loads(r, i):
                        copy.start()

        begin = pltpu.make_async_copy(far_refs[2 * count], total, early_sems.at[len(early)])
        begin.start()
        early_refs = far_refs[2 * count + 1 :]
        early_loads = [
            pltpu.make_async_copy(source, target, early_sems.at[n])
            for n, (source, target) in enumerate(zip(early_refs, [grad_in] + list(loaded)))
        ]
        start_chunk(0)
        for copy in early_loads:
            copy.start()

        begin.wait()

        @pl.loop(0, count * cuts)
        def _(i):
            @pl.when(i + 1 < count * cuts)
            def _():
                start_chunk(i + 1)

            for copy in chunk_loads(0, i):
                copy.wait()
            slot = rem(i, 2)
            total[...] += dot(row_buf[slot], grad_buf[slot], 0, 0)

        bound = [
            one.bind(group_refs[10 * n : 10 * n + 10]) for n, one in enumerate(groups)
        ]
        bits = small.bind(rest)

        @pl.loop(0, PAIRS)
        def _(p):
            at = pl.multiple_of(p * 256, 256)
            pack(
                bound[0].held,
                total[:, pl.ds(at, 128)],
                total[:, pl.ds(at + 128, 128)],
                pl.ds(pl.multiple_of(p * 128, 128), 128),
            )

        bound[0].begin()
        for copy in early_loads:
            copy.wait()
        copies[1].wait()
        x_ref, h1_ref, gco_ref, q_ref, k_ref, v_ref, attn_ref = loaded[:7]
        wq_ref, wk_ref, wv_ref, wo_ref, wc_ref, *dq_refs = loaded[7:]
        grad = dq_got[...].astype(F32)
        for ref in dq_refs:
            grad += ref[...].astype(F32)
        dq_got[...] = grad.astype(BF)
        hidden = h1_ref[...]
        back, cross_norm = rms_back(hidden, cross_gain[...], dot(dq_got[...], wc_ref[...], 1, 1))
        grad_in[...] += back
        dv1[...] = rms(hidden, cross_gain[...]).astype(BF)
        bound[0].after_first()

        @pl.loop(0, 3)
        def _(i):
            cols = pl.ds(pl.multiple_of(i * 256, 256), 256)
            pack(bound[1].held, dot(dv1[...], dq_got[:, cols], 0, 0), gco_ref[:, cols], cols)

        bound[1].begin()
        low_ref = dq_got
        low_ref[...] = grad_in[...].astype(BF)
        da_ref[...] = dot(low_ref[...], wo_ref[...], 1, 1).astype(BF)
        values = x_ref[...].astype(F32)
        normed_ref[...] = rms(values, self_gain[...]).astype(BF)

        for third in range(3):

            @pl.loop(2 * third, 2 * third + 2)
            def _(p):
                cols = pl.ds(pl.multiple_of(p * 128, 128), 128)
                grad_kv, grad_q_p = backward_pair(
                    q_ref[:, cols],
                    da_ref[:, cols],
                    k_ref[:, cols],
                    v_ref[:, cols],
                    causal_probs([lse_ref[p, h : h + 1, :] for h in range(2)]),
                    None,
                )
                dq1[:, cols] = grad_q_p
                dk1[:, cols] = grad_kv[:, :128]
                dv1[:, cols] = grad_kv[:, 128:]

            cols = pl.ds(third * 256, 256)
            near_sum, far_sum = bound[2 + 2 * third], bound[3 + 2 * third]
            normed = normed_ref[...]
            pack(near_sum.held, dot(normed, dq1[:, cols], 0, 0), dot(normed, dk1[:, cols], 0, 0))
            near_sum.begin()
            pack(
                far_sum.held,
                dot(normed, dv1[:, cols], 0, 0),
                dot(attn_ref[...], low_ref[:, cols], 0, 0),
            )
            far_sum.begin()
            if third == 0:
                bound[0].after_second()
                bound[1].after_first()
            if third == 1:
                bound[0].after_third_start()
                bound[1].after_second()
                bound[2].after_first()
                bound[3].after_first()
            if third == 2:
                bound[1].after_third_start()
                bound[2].after_second()
                bound[3].after_second()
                bound[4].after_first()
                bound[5].after_first()
        grad_normed = (
            dot(dq1[...], wq_ref[...], 1, 1)
            + dot(dk1[...], wk_ref[...], 1, 1)
            + dot(dv1[...], wv_ref[...], 1, 1)
        )
        back, self_norm = rms_back(values, self_gain[...], grad_normed)
        grad_in[...] += back
        bits.held[0][...] = jnp.concatenate(
            [self_norm, cross_norm, ffn_term[...], jnp.zeros((5, width), F32)], axis=0
        )
        bits.start(0)
        bound[2].after_third_start()
        bound[3].after_third_start()
        bound[4].after_second()
        bound[5].after_second()
        bound[6].after_first()
        bound[7].after_first()
        bits.advance(0)
        bound[4].after_third_start()
        bound[5].after_third_start()
        bound[6].after_second()
        bound[7].after_second()
        bits.advance(1)
        bound[6].after_third_start()
        bound[7].after_third_start()
        bits.advance(2)
        bound[0].finish(sums[0])
        bound[1].finish(sums[1])
        for n in range(2, 8):
            third, kind = divmod(n - 2, 2)
            bound[n].finish(sums[2 + kind].at[:, pl.ds(third * 256, 256)])
        bits.advance(3, norm_all)
        device = lax.axis_index("z") * courier.plane + courier.me()
        lane = lax.broadcasted_iota(jnp.int32, (width, 128), 0)
        place_of = lax.broadcasted_iota(jnp.int32, (width, 128), 1) + device * share
        pick = jnp.where(lane == place_of, 1.0, 0.0)
        norm_sums[...] = lax.dot_general(
            norm_all[...],
            pick,
            (((1,), (0,)), ((), ())),
            precision=lax.Precision.HIGHEST,
            preferred_element_type=F32,
        )
        for n, copy in enumerate(copies):
            if n != 1:
                copy.wait()

    any_spec = pl.BlockSpec(memory_space=pl.ANY)
    vmem = pl.BlockSpec(memory_space=pltpu.VMEM)
    row = pltpu.VMEM((tokens, width), BF)
    scratch = [
        pltpu.VMEM((2, chunk, width), BF),
        pltpu.VMEM((2, chunk, 2 * width), BF),
        pltpu.VMEM((width, 2 * width), F32),
        pltpu.SemaphoreType.DMA((2, 2)),
    ]
    scratch += [pltpu.VMEM(v.shape, v.dtype) for v in early[1:]]
    scratch += [row] * 6 + [pltpu.SemaphoreType.DMA((len(early) + 1,))]
    scratch += [pltpu.VMEM((8, width), F32)] + courier.scratch()
    for one in groups:
        scratch += one.scratch()
    scratch += small.scratch()
    outs = pl.pallas_call(
        kernel,
        out_shape=[jax.ShapeDtypeStruct((tokens, width), F32)]
        + [jax.ShapeDtypeStruct((2 * share, width), F32)] * 4
        + [jax.ShapeDtypeStruct((8, 128), F32)]
        + courier.out_shape()[1:],
        in_specs=[any_spec] * len(far) + [vmem] * (len(small_in) + 1) + courier.specs(),
        out_specs=[vmem] * 6 + courier.specs()[1:],
        scratch_shapes=scratch,
        compiler_params=pltpu.CompilerParams(
            vmem_limit_bytes=62 * 2**20, collective_id=ident, has_side_effects=True
        ),
    )(*far, *small_in, lse, *courier.values())
    return outs[0], outs[1:5], outs[5], outs[6:]


def place_kernel(*refs):
    *blocks, out_ref, held, arrive, leave = refs
    z = lax.axis_index("z")
    size = held.shape[1]
    inward = []
    outward = []
    for r, block in enumerate(blocks):
        at = rem(z + r, PLANES) * size
        inward.append(pltpu.make_async_copy(block, held.at[r], arrive.at[r]))
        outward.append(
            pltpu.make_async_copy(held.at[r], out_ref.at[pl.ds(at, size)], leave.at[r])
        )
        inward[r].start()
    for r in range(len(blocks)):
        inward[r].wait()
        outward[r].start()
    for copy in outward:
        copy.wait()


def finish_kernel(*refs):
    blocks = refs[:PLANES]
    left0, got0, left1, got1, out_ref, gate_ref, up_ref, down_ref = refs[PLANES : PLANES + 8]
    held, arrive, leave = refs[PLANES + 8 :]
    z = lax.axis_index("z")
    size = held.shape[1]
    inward = []
    outward = []
    for r, block in enumerate(blocks):
        at = rem(z + r, PLANES) * size
        inward.append(pltpu.make_async_copy(block, held.at[r], arrive.at[r]))
        outward.append(
            pltpu.make_async_copy(held.at[r], out_ref.at[pl.ds(at, size)], leave.at[r])
        )
        inward[r].start()
    for r in range(PLANES):
        inward[r].wait()
        outward[r].start()
    share = gate_ref.shape[0]
    wide = left0[z].astype(F32)
    tall = left1[z].astype(F32)
    for k in range(PLANES - 1):
        wide += got0[k].astype(F32)
        tall += got1[k].astype(F32)
    gate_ref[...] = wide[:share]
    up_ref[...] = wide[share:]
    down_ref[...] = tall
    for copy in outward:
        copy.wait()


def finish(blocks, left0, got0, left1, got1):
    shape = blocks[0].shape
    share, inner = left0.shape[1] // 2, left0.shape[2]
    hbm = pl.BlockSpec(memory_space=pl.ANY)
    vmem = pl.BlockSpec(memory_space=pltpu.VMEM)
    return pl.pallas_call(
        finish_kernel,
        out_shape=[jax.ShapeDtypeStruct((PLANES * shape[0],) + shape[1:], BF)]
        + [jax.ShapeDtypeStruct((share, inner), F32)] * 2
        + [jax.ShapeDtypeStruct(left1.shape[1:], F32)],
        in_specs=[hbm] * PLANES + [vmem] * 4,
        out_specs=[hbm] + [vmem] * 3,
        scratch_shapes=[
            pltpu.VMEM((PLANES,) + shape, BF),
            pltpu.SemaphoreType.DMA((PLANES,)),
            pltpu.SemaphoreType.DMA((PLANES,)),
        ],
        compiler_params=pltpu.CompilerParams(vmem_limit_bytes=VMEM),
    )(*blocks, left0, got0, left1, got1)


def place(blocks):
    shape = blocks[0].shape
    count = len(blocks)
    hbm = pl.BlockSpec(memory_space=pl.ANY)
    return pl.pallas_call(
        place_kernel,
        out_shape=jax.ShapeDtypeStruct((count * shape[0],) + shape[1:], blocks[0].dtype),
        in_specs=[hbm] * count,
        out_specs=hbm,
        scratch_shapes=[
            pltpu.VMEM((count,) + shape, blocks[0].dtype),
            pltpu.SemaphoreType.DMA((count,)),
            pltpu.SemaphoreType.DMA((count,)),
        ],
        compiler_params=pltpu.CompilerParams(vmem_limit_bytes=VMEM),
    )(*blocks)


def norm_apply(values, gain):
    return values * lax.rsqrt(jnp.mean(values * values, axis=-1, keepdims=True) + EPSILON) * gain


def norm_back(values, gain, grad):
    r = lax.rsqrt(jnp.mean(values * values, axis=-1, keepdims=True) + EPSILON)
    u = gain * grad
    dv = r * u - values * (r * r * r) * jnp.mean(u * values, axis=-1, keepdims=True)
    return dv, jnp.sum(grad * values * r, axis=0)


def matmul(left, right):
    return dot(left, right, 1, 0)


def matmul_t(left, right):
    return dot(left, right, 1, 1)


def tmatmul(left, right):
    return dot(left, right, 0, 0)


def on_device(
    sizes,
    decoder_in,
    memory,
    memory_lengths,
    cotangent,
    norm_self,
    self_query,
    self_key,
    self_value,
    self_out,
    norm_cross,
    cross_query,
    cross_key,
    cross_value,
    cross_out,
    norm_ffn,
    ffn_gate,
    ffn_up,
    ffn_down,
):
    devices, positions, width = memory.shape
    plane_size = sizes[1] * sizes[2] * sizes[3]
    z = lax.axis_index("z")

    def flat(blocks):
        return blocks.reshape(plane_size * positions, width)

    def cut(rows):
        return rows.reshape(plane_size, positions, width)

    forward = forward_part(
        sizes,
        0,
        memory,
        jnp.broadcast_to(memory_lengths[None, :], (8, 128)),
        decoder_in[0],
        (norm_self[None], norm_cross[None]),
        (self_query, self_key, self_value, self_out, cross_query),
        cross_key,
        cross_value,
    )
    query_one, key_one, value_one, lse_one, attn_one, hidden_one, _ = forward["saved"]
    queries = forward["queries"]
    rows = {r: flat(forward["rows"][r]) for r in range(PLANES)}

    (
        output,
        attn_two,
        grad_two,
        grad_attn_two,
        stats,
        grad_norm_ffn,
        grad_cross_out,
        *grads_in,
        grad_down,
    ) = middle(
        sizes,
        forward["parts"],
        forward["lses"],
        hidden_one,
        cross_out,
        norm_ffn[None],
        cotangent[0],
        ffn_gate,
        ffn_up,
        ffn_down,
    )
    decoder_out = output[None]
    if len(grads_in) == 2:
        summands = {
            0: [summand_of(sizes, grads_in)],
            1: [grad_down.reshape(tuple(sizes) + grad_down.shape[1:])],
        }
    else:
        summands = {0: [grads_in[0], grad_down]}
    part = width // devices
    terms = ()
    left, got = {}, {}

    grads = {0: grad_attn_two}
    both = {0: stats}
    grad_kv, grad_q, grad_rows, returned = {}, {}, {}, {}
    for r in range(PLANES):
        jobs = []
        if r + 1 < PLANES:
            jobs.append(("line", -(r + 1), grad_attn_two))
            jobs.append(("line", -(r + 1), stats))
        if r >= 1:
            jobs.append(("return", 0, cut(grad_rows[r - 1])))
        if r >= 2:
            jobs.append(("line", r - 1, grad_q[r - 1]))
        before = ()
        if part % 8 == 0 and r in (1, 2):
            before = (rows[r - 1], grad_kv[r - 1]) + terms
        (grad_kv[r], grad_q[r], grad_rows[r], *terms), moved = cross_backward(
            Courier(sizes, jobs),
            5 + r,
            r,
            queries[r],
            grads[r],
            forward["keyvals"],
            forward["probs"],
            forward["tops"],
            both[r],
            cross_key,
            cross_value,
            summands.get(r, []),
            before,
        )
        terms = tuple(terms)
        if terms:
            summed = terms[0]
        moved = list(moved)
        if r in summands:
            for value in moved[len(moved) - len(summands[r]) :]:
                left[len(left)] = value
        if r + 1 < PLANES:
            grads[r + 1], both[r + 1] = moved.pop(0), moved.pop(0)
        if r >= 1:
            returned[r - 1] = moved.pop(0)
        if r >= 2:
            grad_q[r - 1] = moved.pop(0)
    last = PLANES - 1
    if part % 8 == 0:
        decoder_in_grad, sums, norm_sums, moved = ending(
            sizes,
            9,
            [rows[r] for r in (2, 3)],
            [grad_kv[r] for r in (2, 3)],
            summed,
            [grad_q[r] for r in range(PLANES)],
            cut(grad_rows[last]),
            [left[0], left[1]],
            grad_two,
            (decoder_in[0], hidden_one, grad_cross_out, query_one, key_one, value_one, attn_one)
            + (self_query, self_key, self_value, self_out, cross_query),
            lse_one,
            (norm_self[None], norm_cross[None], grad_norm_ffn),
        )
        returned[last], got[0], got[1] = moved
        memory_grad, sum_gate, sum_up, sum_down = finish(
            [returned[r] for r in range(PLANES)], left[0], got[0], left[1], got[1]
        )
        norm_self_sum, norm_cross_sum, norm_ffn_sum = (norm_sums[n, :part] for n in range(3))
        return (
            decoder_out,
            decoder_in_grad[None],
            memory_grad,
            norm_self_sum,
            sums[2][:part],
            sums[2][part:],
            sums[3][:part],
            sums[3][part:],
            norm_cross_sum,
            sums[1][:part],
            sums[0][:part],
            sums[0][part:],
            sums[1][part:],
            norm_ffn_sum,
            sum_gate,
            sum_up,
            sum_down,
        )

    jobs = [
        ("line", last, grad_q[last]),
        ("return", 0, cut(grad_rows[last])),
        ("scatter", 0, left[0]),
        ("scatter", 0, left[1]),
    ]
    (grad_cross_key, grad_cross_value), (grad_q[last], returned[last], got[0], got[1]) = weight_terms(
        Courier(sizes, jobs),
        9,
        [rows[r] for r in range(PLANES)],
        [grad_kv[r] for r in range(PLANES)],
    )
    memory_grad = place([returned[r] for r in range(PLANES)])

    inputs = decoder_in[0].astype(F32)
    normed_one = norm_apply(inputs, norm_self).astype(BF)
    normed_two = norm_apply(hidden_one, norm_cross).astype(BF)
    grad_q_two = sum(grad_q[r].astype(F32) for r in range(PLANES)).astype(BF)
    grad_cross_query = tmatmul(normed_two, grad_q_two)
    grad_normed_two = matmul_t(grad_q_two, cross_query)
    back_one, grad_norm_cross = norm_back(hidden_one, norm_cross, grad_normed_two)
    grad_one = grad_two + back_one
    branch_one = grad_one.astype(BF)
    grad_self_out = tmatmul(attn_one, branch_one)
    grad_attn_one = matmul_t(branch_one, self_out).astype(BF)
    (grad_q_one, grad_k_one, grad_v_one), (cross_left,) = self_backward(
        Courier(sizes, []),
        10,
        query_one,
        grad_attn_one,
        key_one,
        value_one,
        lse_one,
        summand_of(sizes, (grad_cross_key, grad_cross_value)),
    )
    grad_normed_one = (
        matmul_t(grad_q_one, self_query)
        + matmul_t(grad_k_one, self_key)
        + matmul_t(grad_v_one, self_value)
    )
    back_in, grad_norm_self = norm_back(inputs, norm_self, grad_normed_one)
    decoder_in_grad = (grad_one + back_in)[None]
    share_of_norms = width // devices
    norms = jnp.stack(
        [g.reshape(devices, share_of_norms) for g in (grad_norm_self, grad_norm_cross, grad_norm_ffn[0])],
        axis=1,
    ).reshape(devices, 1, 3 * share_of_norms)
    norms = jnp.pad(norms, ((0, 0), (0, 15), (0, 256 - 3 * share_of_norms)))
    (cross_got,), sums = reduce_all(
        sizes,
        11,
        [
            norms.astype(BF).reshape(tuple(sizes) + norms.shape[1:]),
            summand_of(sizes, (grad_cross_query, grad_cross_out.astype(F32))),
            summand_of(sizes, (tmatmul(normed_one, grad_q_one), tmatmul(normed_one, grad_k_one))),
            summand_of(sizes, (tmatmul(normed_one, grad_v_one), grad_self_out)),
        ],
        [cross_left],
    )
    norm_sums = sums[0][0, : 3 * share_of_norms].reshape(3, share_of_norms)
    gate_up = over_z(left[0], got[0])
    cross_kv = over_z(cross_left, cross_got)
    part = share_of_norms
    return (
        decoder_out,
        decoder_in_grad,
        memory_grad,
        norm_sums[0],
        sums[2][:part],
        sums[2][part:],
        sums[3][:part],
        sums[3][part:],
        norm_sums[1],
        sums[1][:part],
        cross_kv[:part],
        cross_kv[part:],
        sums[1][part:],
        norm_sums[2],
        gate_up[:part],
        gate_up[part:],
        over_z(left[1], got[1]),
    )


def solution(mesh):
    dp, seq = mesh.devices.shape
    cores = 2
    lines = dp // PLANES
    split = Mesh(mesh.devices.reshape(PLANES, lines, seq // cores, cores), ALL)
    sizes = split.devices.shape
    first = P(ALL)
    middle = P(None, ALL)
    whole = P()
    return jax.shard_map(
        functools.partial(on_device, sizes),
        mesh=split,
        in_specs=(first, middle, first, first) + (whole,) * 14,
        out_specs=(first, first, middle) + (first,) * 14,
        check_vma=False,
    )
```

```python
import functools

import jax
import jax.numpy as jnp
from jax import lax
from jax.experimental import pallas as pl
from jax.experimental.pallas import tpu as pltpu
from jax.sharding import Mesh
from jax.sharding import PartitionSpec as P

H = 12
HD = 64
PAIRS = 6
PLANES = 4
EPSILON = 1e-06
MASKED = -1e30
VMEM = 56 * 2**20
BF = jnp.bfloat16
F32 = jnp.float32
ALL = ("z", "y", "x", "c")
PLANE = ("y", "x", "c")
EVERY = slice(None)


def dot(left, right, left_dim, right_dim):
    return lax.dot_general(
        left, right, (((left_dim,), (right_dim,)), ((), ())), preferred_element_type=F32
    )


def lane_masks():
    lane = lax.broadcasted_iota(jnp.int32, (1, 2 * HD), 1)
    low = jnp.where(lane < HD, 1.0, 0.0)
    first = jnp.where(lane == HD, 1.0, 0.0)
    second = jnp.where(lane == 0, 1.0, 0.0)
    low, high, first, second = (
        v.astype(BF) for v in (low, 1.0 - low, first, second)
    )
    return ((low, high, first), (high, low, second))


def causal_mask(scores):
    key = lax.broadcasted_iota(jnp.int32, scores.shape, 0)
    query = lax.broadcasted_iota(jnp.int32, scores.shape, 1)
    return jnp.where(key <= query, scores, MASKED)


def rem(value, size):
    return lax.rem(value, size)


class Courier:
    def __init__(self, sizes, jobs):
        self.sizes = sizes
        self.jobs = jobs
        self.plane = sizes[1] * sizes[2] * sizes[3]
        self.in_plane = any(job[0] in ("fetch", "return") for job in jobs)
        self.lines = [job[1] for job in jobs if job[0] == "line"]
        for job in jobs:
            if job[0] == "scatter":
                self.lines += list(range(1, PLANES))

    def out_shape(self):
        shapes = []
        for kind, _, value in self.jobs:
            shape = value.shape
            if kind == "fetch":
                shape = (self.plane,) + shape[1:]
            elif kind == "scatter":
                shape = (PLANES - 1,) + shape[1:]
            shapes.append(jax.ShapeDtypeStruct(shape, value.dtype))
        return shapes

    def specs(self):
        return [pl.BlockSpec(memory_space=pl.ANY)] * len(self.jobs)

    def values(self):
        return [job[2] for job in self.jobs]

    def scratch(self):
        each = {"line": 1, "scatter": PLANES - 1}
        count = max(1, sum(each.get(job[0], self.plane - 1) for job in self.jobs))
        own = max(1, sum(job[0] in ("fetch", "return") for job in self.jobs))
        return [pltpu.SemaphoreType.DMA((n,)) for n in (count, count, own)]

    def params(self, ident):
        return pltpu.CompilerParams(
            vmem_limit_bytes=VMEM, collective_id=ident, has_side_effects=True
        )

    def me(self):
        _, _, x_size, c_size = self.sizes
        y, x, c = (lax.axis_index(name) for name in PLANE)
        return (y * x_size + x) * c_size + c

    def along(self, offset):
        return {"z": rem(lax.axis_index("z") + (offset + PLANES), PLANES)}

    def across(self, offset):
        _, _, x_size, c_size = self.sizes
        other = rem(self.me() + offset, self.plane)
        line = lax.div(other, c_size)
        return other, {"y": lax.div(line, x_size), "x": rem(line, x_size), "c": rem(other, c_size)}

    def greet(self):
        barrier = pltpu.get_barrier_semaphore()
        count = 0
        if self.in_plane:
            for k in range(1, self.plane):
                _, device = self.across(k)
                pl.semaphore_signal(
                    barrier, inc=1, device_id=device, device_id_type=pl.DeviceIdType.MESH
                )
                count += 1
        for offset in self.lines:
            pl.semaphore_signal(
                barrier,
                inc=1,
                device_id=self.along(-offset),
                device_id_type=pl.DeviceIdType.MESH,
            )
            count += 1
        pl.semaphore_wait(barrier, count)

    def copies(self, sources, targets, sems):
        send, receive, own = sems
        remote = []
        local = []

        def add(source, target, device):
            n = len(remote)
            remote.append(
                pltpu.make_async_remote_copy(
                    src_ref=source,
                    dst_ref=target,
                    send_sem=send.at[n],
                    recv_sem=receive.at[n],
                    device_id=device,
                    device_id_type=pl.DeviceIdType.MESH,
                )
            )

        me = self.me()
        for (kind, offset, _), source, target in zip(self.jobs, sources, targets):
            if kind == "line":
                add(source, target, self.along(offset))
                continue
            if kind == "scatter":
                for k in range(1, PLANES):
                    there = rem(lax.axis_index("z") + k, PLANES)
                    add(source.at[there], target.at[k - 1], self.along(k))
                continue
            base = 0
            if kind == "fetch":
                base = rem(lax.axis_index("z") + offset, PLANES) * self.plane
            for k in range(1, self.plane):
                other, device = self.across(k)
                add(source.at[base + other], target.at[me], device)
            local.append(
                pltpu.make_async_copy(source.at[base + me], target.at[me], own.at[len(local)])
            )
        return local + remote

    def start(self, sources, targets, sems):
        self.greet()
        for copy in self.copies(sources, targets, sems):
            copy.start()

    def wait(self, sources, targets, sems):
        for copy in self.copies(sources, targets, sems):
            copy.wait()


class Reducer:
    def __init__(self, sizes, shape):
        self.sizes = sizes
        self.rows, self.lanes = shape[-2:]
        self.half = self.lanes // 2

    def scratch(self):
        z, y, x, _ = self.sizes
        r, w, h = self.rows, self.lanes, self.half
        crossing = x + y - 2
        return [
            pltpu.VMEM((z, y, x, r, w), BF),
            pltpu.VMEM((z, y, x, r, w), BF),
            pltpu.VMEM((x - 1, z, y, r, h), BF),
            pltpu.VMEM((y - 1, z, x, r, h), BF),
            pltpu.VMEM((y - 1, z, r, h), BF),
            pltpu.VMEM((x - 1, z, r, h), BF),
            pltpu.SemaphoreType.DMA((1,)),
            pltpu.SemaphoreType.DMA((1 + 2 * crossing,)),
            pltpu.SemaphoreType.DMA((1 + 2 * crossing,)),
        ]

    def bind(self, source, refs):
        self.source = source
        self.held, self.got0, self.got1x, self.got1y, self.got2y, self.got2x = refs[:6]
        self.local, self.send, self.receive = refs[6:]
        self.z, self.y, self.x, self.c = (lax.axis_index(name) for name in ALL)
        return self

    def index(self, z, y, x, lanes):
        return (z, y, x, EVERY, lanes)

    def slab(self, z, y, x, lanes):
        return self.held.at[self.index(z, y, x, lanes)]

    given = slab

    def remote(self, n, source, target, device):
        return pltpu.make_async_remote_copy(
            src_ref=source,
            dst_ref=target,
            send_sem=self.send.at[n],
            recv_sem=self.receive.at[n],
            device_id=device,
            device_id_type=pl.DeviceIdType.MESH,
        )

    def first(self):
        other = 1 - self.c
        return [
            pltpu.make_async_copy(self.source.at[:, :, :, self.c], self.held, self.local.at[0]),
            self.remote(0, self.source.at[:, :, :, other], self.got0, {"c": other}),
        ]

    def second(self):
        _, y_size, x_size, _ = self.sizes
        left, right = pl.ds(0, self.half), pl.ds(self.half, self.half)
        copies = []
        for k in range(1, x_size):
            there = rem(self.x + k, x_size)
            copies.append((self.given(EVERY, EVERY, there, left), self.got1x.at[k - 1], {"x": there}))
        for k in range(1, y_size):
            there = rem(self.y + k, y_size)
            copies.append((self.given(EVERY, there, EVERY, right), self.got1y.at[k - 1], {"y": there}))
        return [self.remote(1 + n, *copy) for n, copy in enumerate(copies)]

    def third(self):
        _, y_size, x_size, _ = self.sizes
        left, right = pl.ds(0, self.half), pl.ds(self.half, self.half)
        at = 1 + x_size + y_size - 2
        copies = []
        for k in range(1, y_size):
            there = rem(self.y + k, y_size)
            copies.append(
                (self.slab(EVERY, there, self.x, left), self.got2y.at[k - 1], {"y": there})
            )
        for k in range(1, x_size):
            there = rem(self.x + k, x_size)
            copies.append(
                (self.slab(EVERY, self.y, there, right), self.got2x.at[k - 1], {"x": there})
            )
        return [self.remote(at + n, *copy) for n, copy in enumerate(copies)]

    def begin(self):
        for copy in self.first():
            copy.start()

    def after_first(self):
        for copy in self.first():
            copy.wait()

        @pl.loop(0, self.sizes[0])
        def _(z):
            at = self.index(z, EVERY, EVERY, EVERY)
            self.held[at] = (self.held[at].astype(F32) + self.got0[z].astype(F32)).astype(BF)

        for copy in self.second():
            copy.start()

    def after_second(self):
        _, y_size, x_size, _ = self.sizes
        for copy in self.second():
            copy.wait()
        h = self.half

        @pl.loop(0, self.sizes[0])
        def _(z):
            for y in range(y_size):
                at = self.index(z, y, self.x, pl.ds(0, h))
                total = self.held[at].astype(F32)
                for k in range(x_size - 1):
                    total += self.got1x[k, z, y].astype(F32)
                self.held[at] = total.astype(BF)
            for x in range(x_size):
                at = self.index(z, self.y, x, pl.ds(h, h))
                total = self.held[at].astype(F32)
                for k in range(y_size - 1):
                    total += self.got1y[k, z, x].astype(F32)
                self.held[at] = total.astype(BF)

        for copy in self.third():
            copy.start()

    def after_third(self, out_ref):
        _, y_size, x_size, _ = self.sizes
        for copy in self.third():
            copy.wait()
        h = self.half

        @pl.loop(0, self.sizes[0])
        def _(z):
            total = self.held[self.index(z, self.y, self.x, pl.ds(0, h))].astype(F32)
            for k in range(y_size - 1):
                total += self.got2y[k, z].astype(F32)
            out_ref[z, :, :h] = total.astype(BF)
            total = self.held[self.index(z, self.y, self.x, pl.ds(h, h))].astype(F32)
            for k in range(x_size - 1):
                total += self.got2x[k, z].astype(F32)
            out_ref[z, :, h:] = total.astype(BF)


class Halved(Reducer):
    def scratch(self):
        z, y, x, _ = self.sizes
        r, w, h = self.rows, self.lanes, self.half
        crossing = x + y - 2
        return [
            pltpu.VMEM((z, y, x, r, w), BF),
            pltpu.VMEM((x - 1, z, y, r, h), BF),
            pltpu.VMEM((y - 1, z, x, r, h), BF),
            pltpu.VMEM((y - 1, z, r, h), BF),
            pltpu.VMEM((x - 1, z, r, h), BF),
            pltpu.SemaphoreType.DMA((1,)),
            pltpu.SemaphoreType.DMA((1 + 2 * crossing,)),
            pltpu.SemaphoreType.DMA((1 + 2 * crossing,)),
        ]

    def bind(self, source, refs):
        self.source = source
        self.held, self.got1x, self.got1y, self.got2y, self.got2x = refs[:5]
        self.local, self.send, self.receive = refs[5:]
        self.z, self.y, self.x, self.c = (lax.axis_index(name) for name in ALL)
        return self

    def given(self, z, y, x, lanes):
        return self.source.at[self.index(z, y, x, lanes)]

    def first(self):
        return [pltpu.make_async_copy(self.source, self.held, self.local.at[0])]

    def begin(self):
        for copy in self.first() + self.second():
            copy.start()

    def after_first(self):
        pass

    def after_second(self):
        for copy in self.first():
            copy.wait()
        super().after_second()


class Resident(Reducer):
    def scratch(self):
        z, y, x, c = self.sizes
        r, w, h = self.rows, self.lanes, self.half
        count = 1 + 2 * (x + y - 2) + z - 1
        return [
            pltpu.VMEM((z, y, x, c, r, w), BF),
            pltpu.VMEM((z, y, x, r, w), BF),
            pltpu.VMEM((x - 1, z, y, r, h), BF),
            pltpu.VMEM((y - 1, z, x, r, h), BF),
            pltpu.VMEM((y - 1, z, r, h), BF),
            pltpu.VMEM((x - 1, z, r, h), BF),
            pltpu.VMEM((z, r, w), BF),
            pltpu.VMEM((z - 1, r, w), BF),
            pltpu.SemaphoreType.DMA((count,)),
            pltpu.SemaphoreType.DMA((count,)),
        ]

    def bind(self, refs):
        self.held, self.got0, self.got1x, self.got1y, self.got2y, self.got2x = refs[:6]
        self.left, self.got3, self.send, self.receive = refs[6:]
        self.z, self.y, self.x, self.c = (lax.axis_index(name) for name in ALL)
        return self

    def index(self, z, y, x, lanes):
        return (z, y, x, self.c, EVERY, lanes)

    def first(self):
        other = 1 - self.c
        return [self.remote(0, self.held.at[:, :, :, other], self.got0, {"c": other})]

    def fourth(self):
        _, y_size, x_size, _ = self.sizes
        at = 1 + 2 * (x_size + y_size - 2)
        copies = []
        for k in range(1, PLANES):
            there = rem(self.z + k, PLANES)
            copies.append(
                self.remote(at + k - 1, self.left.at[there], self.got3.at[k - 1], {"z": there})
            )
        return copies

    def after_third_start(self):
        self.after_third(self.left)
        for copy in self.fourth():
            copy.start()

    def finish(self, out_ref):
        for copy in self.fourth():
            copy.wait()
        total = self.left[self.z].astype(F32)
        for k in range(PLANES - 1):
            total += self.got3[k].astype(F32)
        out_ref[...] = total


class SmallSum:
    def __init__(self, sizes, shape):
        self.shape = shape
        self.steps = list(zip(("c", "x", "y", "z"), (sizes[3], sizes[2], sizes[1], sizes[0])))

    def scratch(self):
        count = sum(n - 1 for _, n in self.steps)
        return (
            [pltpu.VMEM(self.shape, F32) for _ in range(4)]
            + [pltpu.VMEM((n - 1,) + self.shape, F32) for _, n in self.steps]
            + [pltpu.SemaphoreType.DMA((count,))] * 2
        )

    def bind(self, refs):
        self.held, self.got = refs[:4], refs[4:8]
        self.send, self.receive = refs[8:]
        return self

    def copies(self, step):
        axis, n = self.steps[step]
        at = sum(m - 1 for _, m in self.steps[:step])
        me = lax.axis_index(axis)
        return [
            pltpu.make_async_remote_copy(
                src_ref=self.held[step],
                dst_ref=self.got[step].at[k - 1],
                send_sem=self.send.at[at + k - 1],
                recv_sem=self.receive.at[at + k - 1],
                device_id={axis: rem(me + k, n)},
                device_id_type=pl.DeviceIdType.MESH,
            )
            for k in range(1, n)
        ]

    def start(self, step):
        for copy in self.copies(step):
            copy.start()

    def advance(self, step, out_ref=None):
        for copy in self.copies(step):
            copy.wait()
        total = self.held[step][...]
        for k in range(self.steps[step][1] - 1):
            total += self.got[step][k]
        if step < 3:
            self.held[step + 1][...] = total
            self.start(step + 1)
        else:
            out_ref[...] = total


def forward_pair(queries, keys, values, bias):
    masks = lane_masks()
    all_scores = []
    for mine, other, one in masks:
        if bias is None:
            all_scores.append(causal_mask(dot(keys, queries * mine, 1, 1)))
        else:
            all_scores.append(dot(keys * mine + bias * one, queries * mine + one, 1, 1))
    parts = []
    lse = []
    for h in range(2):
        mine, other, _ = masks[h]
        scores = all_scores[h]
        row_max = jnp.max(scores, axis=0, keepdims=True)
        probs = jnp.exp(scores - row_max).astype(BF)
        both = dot(values * mine + other, probs, 0, 0)
        halves = (both[:HD], both[HD:])
        total = halves[1 - h]
        parts.append(halves[h] / total)
        lse.append(row_max + jnp.log(total[0:1]))
    return jnp.concatenate(parts, axis=0).T.astype(BF), lse


def backward_pair(queries, grad, keys, values, probs_of, delta):
    grad_k = None
    grad_v = None
    grad_q = []
    for h, (mine, other, one) in enumerate(lane_masks()):
        query_h = queries * mine
        grad_h = grad * mine
        probs = probs_of(h, keys, query_h)
        grad_p = dot(values, grad_h, 1, 1)
        if delta is None:
            delta_h = jnp.sum(probs * grad_p, axis=0, keepdims=True)
        else:
            delta_h = delta[h]
        grad_s = (probs * (grad_p - delta_h)).astype(BF)
        term_v = dot(probs.astype(BF), grad_h, 1, 0)
        term_k = dot(grad_s, query_h, 1, 0)
        grad_v = term_v if grad_v is None else grad_v + term_v
        grad_k = term_k if grad_k is None else grad_k + term_k
        grad_q.append(dot(keys, grad_s, 0, 0)[h * HD : (h + 1) * HD])
    grad_kv = jnp.concatenate([grad_k, grad_v], axis=1).astype(BF)
    return grad_kv, jnp.concatenate(grad_q, axis=0).T.astype(BF)


def causal_probs(lse):
    return lambda h, keys, query: jnp.exp(causal_mask(dot(keys, query, 1, 1)) - lse[h])


def key_bias(keys, lens):
    row = lax.broadcasted_iota(jnp.int32, (keys, 128), 0) + lax.axis_index("z") * keys
    return jnp.where(row < lens[0:1, :], 0.0, MASKED).astype(BF)


def split_refs(refs, *counts):
    groups = []
    at = 0
    for count in counts:
        groups.append(refs[at : at + count])
        at += count
    return groups


def carried(courier, reducers, body):
    jobs = len(courier.jobs)
    sums = len(reducers)
    parts = [len(one.scratch()) for one in reducers]

    def kernel(ins, outs, scratch, refs):
        own_in, sources, summands, own_out, targets, results, own_scratch, sems, rest = split_refs(
            refs, ins, jobs, sums, outs, jobs, sums, scratch, 3, sum(parts)
        )
        step = pl.program_id(0)
        work = split_refs(rest, *parts)

        def bound():
            return [one.bind(value, refs) for one, value, refs in zip(reducers, summands, work)]

        @pl.when(step == 0)
        def _():
            courier.start(sources, targets, sems)
            for one in bound():
                one.begin()

        body(own_in, own_out, own_scratch)

        if sums:

            @pl.when(step == 1)
            def _():
                for one in bound():
                    one.after_first()

            @pl.when(step == 3)
            def _():
                for one in bound():
                    one.after_second()

        @pl.when(step == PAIRS - 1)
        def _():
            for one, result in zip(bound(), results):
                one.after_third(result)
            courier.wait(sources, targets, sems)

    return kernel


def call(courier, ident, body, args, in_specs, out_shape, out_specs, scratch, flops, summands=()):
    if summands:
        courier.in_plane = True
    reducers = [
        (Halved if value.ndim == 5 else Reducer)(courier.sizes, value.shape) for value in summands
    ]
    shapes = [(PLANES,) + value.shape[-2:] for value in summands]
    kernel = carried(courier, reducers, body)
    counts = (len(args), len(out_shape), len(scratch))
    outs = pl.pallas_call(
        lambda *refs: kernel(*counts, refs),
        grid=(PAIRS,),
        out_shape=out_shape
        + courier.out_shape()
        + [jax.ShapeDtypeStruct(shape, BF) for shape in shapes],
        in_specs=in_specs + courier.specs() + [pl.BlockSpec(memory_space=pl.ANY)] * len(shapes),
        out_specs=out_specs
        + courier.specs()
        + [pl.BlockSpec(shape, lambda p: (0, 0, 0)) for shape in shapes],
        scratch_shapes=scratch
        + courier.scratch()
        + [ref for one in reducers for ref in one.scratch()],
        compiler_params=courier.params(ident),
        cost_estimate=pl.CostEstimate(flops=flops, bytes_accessed=2**24, transcendentals=2**20),
    )(*args, *courier.values(), *summands)
    return outs[: len(out_shape)], outs[len(out_shape) :]


def reduce_all(sizes, ident, summands, scattered):
    courier = Courier(sizes, [("scatter", 0, value) for value in scattered])
    courier.in_plane = True
    courier.lines += list(range(1, PLANES))
    jobs = len(scattered)
    count = len(summands)
    reducers = [Reducer(sizes, value.shape) for value in summands]
    shapes = [value.shape[-2:] for value in summands]

    def kernel(*refs):
        sources, arrays, targets, results, sems, rest = split_refs(
            refs, jobs, count, jobs, count, 3, len(refs) - 2 * jobs - 2 * count - 3
        )
        courier.start(sources, targets, sems)
        bound = []
        last = []
        for n in range(count):
            refs_n = rest[13 * n : 13 * n + 13]
            bound.append(reducers[n].bind(arrays[n], refs_n[:9]))
            last.append(refs_n[9:])

        def leave(n):
            left, got, send, receive = last[n]
            copies = []
            for k in range(1, PLANES):
                copies.append(
                    pltpu.make_async_remote_copy(
                        src_ref=left.at[rem(lax.axis_index("z") + k, PLANES)],
                        dst_ref=got.at[k - 1],
                        send_sem=send.at[k - 1],
                        recv_sem=receive.at[k - 1],
                        device_id=courier.along(k),
                        device_id_type=pl.DeviceIdType.MESH,
                    )
                )
            return copies

        for one in bound:
            one.begin()
        for one in bound:
            one.after_first()
        for one in bound:
            one.after_second()
        for n, one in enumerate(bound):
            one.after_third(last[n][0])
            for copy in leave(n):
                copy.start()
        for n in range(count):
            for copy in leave(n):
                copy.wait()
            left, got = last[n][:2]
            total = left[lax.axis_index("z")].astype(F32)
            for k in range(PLANES - 1):
                total += got[k].astype(F32)
            results[n][...] = total
        courier.wait(sources, targets, sems)

    scratch = []
    for n in range(count):
        scratch += reducers[n].scratch() + [
            pltpu.VMEM((PLANES,) + shapes[n], BF),
            pltpu.VMEM((PLANES - 1,) + shapes[n], BF),
            pltpu.SemaphoreType.DMA((PLANES - 1,)),
            pltpu.SemaphoreType.DMA((PLANES - 1,)),
        ]
    outs = pl.pallas_call(
        kernel,
        out_shape=courier.out_shape() + [jax.ShapeDtypeStruct(shape, F32) for shape in shapes],
        in_specs=courier.specs() + [pl.BlockSpec(memory_space=pl.ANY)] * count,
        out_specs=courier.specs() + [pl.BlockSpec(memory_space=pltpu.VMEM)] * count,
        scratch_shapes=courier.scratch() + scratch,
        compiler_params=courier.params(ident),
    )(*courier.values(), *summands)
    return outs[:jobs], outs[jobs:]


def summand_of(sizes, arrays):
    devices = sizes[0] * sizes[1] * sizes[2] * sizes[3]
    parts = [a.reshape(devices, a.shape[0] // devices, a.shape[1]) for a in arrays]
    joined = parts[0] if len(parts) == 1 else jnp.concatenate(parts, axis=1)
    return joined.astype(BF).reshape(tuple(sizes) + joined.shape[1:])


def over_z(left, got):
    own = lax.dynamic_index_in_dim(left, lax.axis_index("z"), 0, keepdims=False)
    return own.astype(F32) + jnp.sum(got.astype(F32), axis=0)


def block_specs(tokens, keys):
    return dict(
        col=pl.BlockSpec((tokens, 128), lambda p: (0, p)),
        pair=pl.BlockSpec((keys, 256), lambda p: (0, p)),
        rows=pl.BlockSpec((keys, H * HD), lambda p: (0, 0)),
        weight=pl.BlockSpec((H * HD, 128), lambda p: (0, p)),
        stat=pl.BlockSpec((1, 2, tokens), lambda p: (p, 0, 0)),
    )


def rms(values, gain):
    r = lax.rsqrt(jnp.mean(values * values, axis=-1, keepdims=True) + EPSILON)
    return values * r * gain


ORDER = (1, 2, 3, 0)


def forward_part(sizes, ident, memory, lens, inputs, gains, weights, key_weight, value_weight):
    tokens, width = inputs.shape
    positions = memory.shape[1]
    plane = sizes[1] * sizes[2] * sizes[3]
    keys = plane * positions
    rows = jax.ShapeDtypeStruct((tokens, width), BF)
    wide = jax.ShapeDtypeStruct((tokens, width), F32)
    stat = jax.ShapeDtypeStruct((PAIRS, 2, tokens), F32)
    near = range(1, PLANES)
    jobs = [("fetch", r, memory) for r in ORDER]
    jobs += [("line", -r, lens) for r in near] + [("line", -r, rows) for r in near]
    jobs += [("line", r, rows) for r in near] + [("line", r, stat) for r in near]
    courier = Courier(sizes, jobs)
    courier.lines = list(near)
    count = PLANES * PAIRS

    def kernel(*refs):
        ins, sources, outs, parts, targets, work, sems = split_refs(refs, 11, 1, 8, 3, 13, 7, 3)
        x_ref, self_gain, cross_gain, wq_ref, wk_ref, wv_ref, wo_ref, wc_ref = ins[:8]
        lens_ref, key_ref, value_ref = ins[8:]
        (memory_ref,) = sources
        q_ref, k_ref, v_ref, lse_ref, attn_ref, hidden_ref, query_ref, lens_out = outs
        part_ref, part_lse_ref, kv_ref = parts
        row_buf, query_buf, out_buf, lse_buf, lens_buf, near_lens, load_sems = work
        copies = courier.copies(
            [memory_ref] * PLANES
            + [lens_ref] * 3
            + [query_ref] * 3
            + [out_buf.at[n] for n in range(3)]
            + [lse_buf.at[n] for n in range(3)],
            list(targets[:4])
            + [near_lens.at[n] for n in range(3)]
            + list(targets[4:]),
            sems,
        )
        own, remote = copies[:PLANES], copies[PLANES:]
        far = plane - 1
        lines = remote[PLANES * far :]
        lens_lines, query_lines, out_lines, lse_lines = split_refs(lines, 3, 3, 3, 3)
        step = pl.program_id(0)
        me = courier.me()

        def start_fetch(n):
            for copy in [own[n]] + remote[n * far : n * far + far]:
                copy.start()

        @pl.when(step == 0)
        def _():
            courier.greet()
            start_fetch(0)
            for copy in lens_lines:
                copy.start()
            values = x_ref[...].astype(F32)
            normed = rms(values, self_gain[...]).astype(BF)
            q_ref[...] = dot(normed, wq_ref[...], 1, 0).astype(BF)
            k_ref[...] = dot(normed, wk_ref[...], 1, 0).astype(BF)
            v_ref[...] = dot(normed, wv_ref[...], 1, 0).astype(BF)

            @pl.loop(0, PAIRS)
            def _(p):
                cols = pl.ds(pl.multiple_of(p * 128, 128), 128)
                out, lse = forward_pair(q_ref[:, cols], k_ref[:, cols], v_ref[:, cols], None)
                attn_ref[:, cols] = out
                for h in range(2):
                    lse_ref[p, h : h + 1, :] = lse[h]

            hidden = values + dot(attn_ref[...], wo_ref[...], 1, 0)
            hidden_ref[...] = hidden
            normed = rms(hidden, cross_gain[...]).astype(BF)
            query_ref[...] = dot(normed, wc_ref[...], 1, 0).astype(BF)
            query_lines[0].start()

        for n, r in enumerate(ORDER):

            @pl.when(step == n * PAIRS)
            def _(n=n, r=r):
                loads = []

                def load(block):
                    at = pl.ds(pl.multiple_of(block * positions, positions), positions)
                    copy = pltpu.make_async_copy(
                        targets[n].at[block], row_buf.at[at], load_sems.at[len(loads)]
                    )
                    copy.start()
                    loads.append(copy)

                own[n].wait()
                load(me)
                for k in range(1, plane):
                    remote[n * far + k - 1].wait()
                    load(rem(me + (plane - k), plane))
                if n + 1 < PLANES:
                    start_fetch(n + 1)
                if r > 0:
                    query_lines[r - 1].wait()
                    copy = pltpu.make_async_copy(
                        targets[3 + r], query_buf, load_sems.at[plane]
                    )
                    copy.start()
                    if r + 1 < PLANES:
                        query_lines[r].start()
                    lens_lines[r - 1].wait()
                    lens_buf[...] = near_lens[r - 1]
                    copy.wait()
                else:
                    query_buf[...] = query_ref[...]
                    lens_buf[...] = lens_ref[...]
                for copy in loads:
                    copy.wait()

        phase = lax.div(step, PAIRS)
        p = rem(step, PAIRS)
        cols = pl.ds(pl.multiple_of(p * 128, 128), 128)
        both = jnp.concatenate([key_ref[...], value_ref[...]], axis=1)
        kv_ref[...] = dot(row_buf[...], both, 1, 0).astype(BF)
        bias = key_bias(keys, lens_buf[...])
        out, lse = forward_pair(query_buf[:, cols], kv_ref[:, :128], kv_ref[:, 128:], bias)
        out_buf[phase, :, cols] = out
        for h in range(2):
            lse_buf[phase, p, h : h + 1, :] = lse[h]

        for n, r in enumerate(ORDER[:-1]):

            @pl.when(step == n * PAIRS + PAIRS - 1)
            def _(r=r):
                out_lines[r - 1].start()
                lse_lines[r - 1].start()

        @pl.when(step == count - 1)
        def _():
            lens_out[0] = lens_ref[...]
            for r in near:
                lens_out[r] = near_lens[r - 1]
            part_ref[...] = out_buf[PLANES - 1]
            part_lse_ref[...] = lse_buf[PLANES - 1]
            for copy in out_lines + lse_lines:
                copy.wait()

    once = pl.Buffered(1)

    def fixed(*shape):
        return pl.BlockSpec(shape, lambda t: (0,) * len(shape), pipeline_mode=once)

    def out_fixed(*shape):
        return pl.BlockSpec(shape, lambda t: (0,) * len(shape))

    def where(t):
        return rem(lax.div(t, PAIRS) + 1, PLANES), rem(t, PAIRS)

    square = fixed(width, width)
    weight = pl.BlockSpec((width, 128), lambda t: (0, rem(t, PAIRS)))
    hbm = pl.BlockSpec(memory_space=pl.ANY)
    flat = out_fixed(tokens, width)
    flat_stat = out_fixed(PAIRS, 2, tokens)
    shapes = courier.out_shape()
    outs = pl.pallas_call(
        kernel,
        grid=(count,),
        out_shape=[rows, rows, rows, stat, rows, wide, rows]
        + [jax.ShapeDtypeStruct((PLANES, 8, 128), jnp.int32), rows, stat]
        + [jax.ShapeDtypeStruct((PLANES, keys, 2 * width), BF)]
        + shapes[:4]
        + shapes[7:],
        in_specs=[fixed(tokens, width), fixed(1, width), fixed(1, width)]
        + [square] * 5
        + [fixed(8, 128), weight, weight, hbm],
        out_specs=[flat] * 3
        + [flat_stat]
        + [flat] * 3
        + [out_fixed(PLANES, 8, 128), flat, flat_stat]
        + [pl.BlockSpec((None, keys, 256), lambda t: (where(t)[0], 0, where(t)[1]))]
        + [hbm] * 13,
        scratch_shapes=[
            pltpu.VMEM((keys, width), BF),
            pltpu.VMEM((tokens, width), BF),
            pltpu.VMEM((PLANES, tokens, width), BF),
            pltpu.VMEM((PLANES, PAIRS, 2, tokens), F32),
            pltpu.VMEM((8, 128), jnp.int32),
            pltpu.VMEM((3, 8, 128), jnp.int32),
            pltpu.SemaphoreType.DMA((plane + 1,)),
        ]
        + courier.scratch(),
        compiler_params=pltpu.CompilerParams(
            vmem_limit_bytes=62 * 2**20, collective_id=ident, has_side_effects=True
        ),
    )(inputs, *gains, *weights, lens, key_weight, value_weight, memory)
    saved, (all_lens, part0, lse0, kv), moved = outs[:7], outs[7:11], outs[11:]
    return dict(
        saved=saved,
        lens=all_lens,
        keyvals=kv,
        rows={r: moved[n] for n, r in enumerate(ORDER)},
        queries={0: saved[6], **{r: moved[3 + r] for r in near}},
        parts=[part0] + [moved[6 + r] for r in near],
        lses=[lse0] + [moved[9 + r] for r in near],
    )


def glu_parts(gate_vals):
    inner = 0.7978845608028654 * (gate_vals + 0.044715 * gate_vals * gate_vals * gate_vals)
    t = jnp.tanh(inner)
    gelu = 0.5 * gate_vals * (1.0 + t)
    slope = 0.5 * (1.0 + t) + 0.5 * gate_vals * (1.0 - t * t) * 0.7978845608028654 * (
        1.0 + 0.134145 * gate_vals * gate_vals
    )
    return gelu, slope


def spread(rows):
    both = [jnp.broadcast_to(rows[h : h + 1], (HD, rows.shape[1])) for h in range(2)]
    return jnp.concatenate(both, axis=0).T


def middle_kernel(*refs, sizes, packed):
    (
        part0,
        part1,
        part2,
        part3,
        lse0,
        lse1,
        lse2,
        lse3,
        h1_ref,
        wo_ref,
        gain_ref,
        cot_ref,
        gate_ref,
        up_ref,
        down_ref,
        out_ref,
        attn_ref,
        two_ref,
        da_ref,
        stats_ref,
        gnorm_ref,
        gwo_ref,
        *grad_refs,
        gdown_ref,
        raw_ref,
        h2_ref,
        n3_ref,
        total_ref,
        dn3_ref,
    ) = refs[: 29 + (not packed)]
    step = pl.program_id(0)
    last = pl.num_programs(0) - 1
    devices = sizes[0] * sizes[1] * sizes[2] * sizes[3]
    if packed:
        wide_ref, wide_got, tall_ref, tall_got, send, receive = refs[29:]
        core = lax.axis_index("c")

    def exchange(n):
        slot = rem(n, 2)
        return [
            pltpu.make_async_remote_copy(
                src_ref=source,
                dst_ref=target,
                send_sem=send.at[n, at],
                recv_sem=receive.at[n, at],
                device_id={"c": 1 - core},
                device_id_type=pl.DeviceIdType.MESH,
            )
            for at, (source, target) in enumerate(
                (
                    (wide_ref.at[slot, :, :, :, 1 - core], wide_got.at[n]),
                    (tall_ref.at[slot, :, :, 1 - core], tall_got.at[n]),
                )
            )
        ]
    parts = (part0, part1, part2, part3)
    lses = (lse0, lse1, lse2, lse3)

    @pl.when(step == 0)
    def _():
        for p in range(PAIRS):
            cols = pl.ds(p * 128, 128)
            values = [ref[p] for ref in lses]
            top = functools.reduce(jnp.maximum, values)
            scales = [jnp.exp(v - top) for v in values]
            total = functools.reduce(jnp.add, scales)
            stats_ref[0, p] = top + jnp.log(total)
            raw = None
            for ref, scale in zip(parts, scales):
                term = spread(scale / total) * ref[:, cols].astype(F32)
                raw = term if raw is None else raw + term
            raw_ref[:, cols] = raw
            attn_ref[:, cols] = raw.astype(BF)
        hidden = h1_ref[...] + dot(attn_ref[...], wo_ref[...], 1, 0)
        h2_ref[...] = hidden
        n3_ref[...] = rms(hidden, gain_ref[...]).astype(BF)
        total_ref[...] = hidden
        dn3_ref[...] = jnp.zeros_like(dn3_ref)
        if packed:
            barrier = pltpu.get_barrier_semaphore()
            pl.semaphore_signal(
                barrier,
                inc=1,
                device_id={"c": 1 - core},
                device_id_type=pl.DeviceIdType.MESH,
            )
            pl.semaphore_wait(barrier, 1)

    def one_chunk():
        normed = n3_ref[...]
        branch = cot_ref[...]
        gate_vals = dot(normed, gate_ref[...], 1, 0)
        up_vals = dot(normed, up_ref[...], 1, 0)
        grad_inner = dot(branch, down_ref[...], 1, 1)
        gelu, slope = glu_parts(gate_vals)
        inner = (gelu * up_vals).astype(BF)
        grad_gate = (grad_inner * up_vals * slope).astype(BF)
        grad_up = (grad_inner * gelu).astype(BF)
        total_ref[...] += dot(inner, down_ref[...], 1, 0)
        dn3_ref[...] += dot(grad_gate, gate_ref[...], 1, 1) + dot(grad_up, up_ref[...], 1, 1)
        terms = [dot(normed, grad_gate, 0, 0), dot(normed, grad_up, 0, 0)]
        if packed:
            shape = (devices, terms[0].shape[0] // devices, terms[0].shape[1])
            both = jnp.concatenate([t.reshape(shape) for t in terms], axis=1).astype(BF)
            slot = rem(step, 2)
            wide_ref[slot] = both.reshape(wide_ref.shape[1:])
            tall_ref[slot] = dot(inner, branch, 0, 0).astype(BF).reshape(tall_ref.shape[1:])
            for copy in exchange(step):
                copy.start()
        else:
            for ref, term in zip(grad_refs, terms):
                ref[...] = term
            gdown_ref[...] = dot(inner, branch, 0, 0).astype(BF).reshape(gdown_ref.shape)

    if packed:

        @pl.when(step < last)
        def _():
            one_chunk()

    else:
        one_chunk()

    @pl.when(step == last)
    def _():
        out_ref[...] = total_ref[...].astype(BF)
        hidden = h2_ref[...]
        grad = dn3_ref[...]
        r = lax.rsqrt(jnp.mean(hidden * hidden, axis=-1, keepdims=True) + EPSILON)
        u = gain_ref[...] * grad
        back = r * u - hidden * (r * r * r) * jnp.mean(u * hidden, axis=-1, keepdims=True)
        gnorm_ref[...] = jnp.sum(grad * hidden * r, axis=0, keepdims=True)
        two = cot_ref[...].astype(F32) + back
        two_ref[...] = two
        low = two.astype(BF)
        da_ref[...] = dot(low, wo_ref[...], 1, 1).astype(BF)
        gwo_ref[...] = dot(attn_ref[...], low, 0, 0).astype(BF)
        for p in range(PAIRS):
            cols = pl.ds(p * 128, 128)
            product = (da_ref[:, cols].astype(F32) * raw_ref[:, cols]).T
            for h in range(2):
                stats_ref[1, p, h : h + 1] = jnp.sum(
                    product[h * HD : (h + 1) * HD], axis=0, keepdims=True
                )

    if packed:

        @pl.when(step > 0)
        def _():
            before = step - 1
            slot = rem(before, 2)
            for copy in exchange(before):
                copy.wait()
            mine = wide_ref[slot, :, :, :, core].astype(F32)
            grad_refs[0][...] = (mine + wide_got[before].astype(F32)).astype(BF)
            mine = tall_ref[slot, :, :, core].astype(F32)
            gdown_ref[0] = (mine + tall_got[before].astype(F32)).astype(BF)


def middle(sizes, parts, lses, hidden, out_weight, gain, cotangent, gate, up, down):
    tokens, width = hidden.shape
    inner = gate.shape[1]
    chunk = 512
    count = inner // chunk
    devices = sizes[0] * sizes[1] * sizes[2] * sizes[3]
    share = width // devices
    down_share = inner // devices
    packed = share % 8 == 0 and chunk * PLANES == inner
    first = lambda p: jnp.minimum(p, count - 1)
    fixed = lambda *shape: pl.BlockSpec(shape, lambda p: (0,) * len(shape))
    whole = fixed(tokens, width)
    square = fixed(width, width)
    stat = fixed(PAIRS, 2, tokens)
    column = pl.BlockSpec((width, chunk), lambda p: (0, first(p)))
    scratch = [
        pltpu.VMEM((tokens, width), F32),
        pltpu.VMEM((tokens, width), F32),
        pltpu.VMEM((tokens, width), BF),
        pltpu.VMEM((tokens, width), F32),
        pltpu.VMEM((tokens, width), F32),
    ]
    params = dict(vmem_limit_bytes=VMEM)
    if packed:
        z, y, x, c = sizes
        wide_shape = (z, y, x, 2 * share)
        tall_shape = (y, x, down_share, width)
        grad_shapes = [
            jax.ShapeDtypeStruct(wide_shape + (inner,), BF),
            jax.ShapeDtypeStruct((z,) + tall_shape, BF),
        ]
        before = lambda p: jnp.maximum(p - 1, 0)
        grad_specs = [
            pl.BlockSpec(wide_shape + (chunk,), lambda p: (0, 0, 0, 0, before(p))),
            pl.BlockSpec((1,) + tall_shape, lambda p: (before(p), 0, 0, 0, 0)),
        ]
        scratch += [
            pltpu.VMEM((2, z, y, x, c, 2 * share, chunk), BF),
            pltpu.VMEM((count,) + wide_shape + (chunk,), BF),
            pltpu.VMEM((2, y, x, c, down_share, width), BF),
            pltpu.VMEM((count,) + tall_shape, BF),
            pltpu.SemaphoreType.DMA((count, 2)),
            pltpu.SemaphoreType.DMA((count, 2)),
        ]
        params.update(collective_id=12, has_side_effects=True)
    else:
        grad_shapes = [jax.ShapeDtypeStruct((width, inner), F32)] * 2
        grad_shapes.append(jax.ShapeDtypeStruct((devices, down_share, width), BF))
        grad_specs = [column] * 2
        grad_specs.append(
            pl.BlockSpec((chunk // down_share, down_share, width), lambda p: (p, 0, 0))
        )
    rows = jax.ShapeDtypeStruct((tokens, width), BF)
    wide = jax.ShapeDtypeStruct((tokens, width), F32)
    return pl.pallas_call(
        functools.partial(middle_kernel, sizes=sizes, packed=packed),
        grid=(count + packed,),
        out_shape=[
            rows,
            rows,
            wide,
            rows,
            jax.ShapeDtypeStruct((2, PAIRS, 2, tokens), F32),
            jax.ShapeDtypeStruct((1, width), F32),
            jax.ShapeDtypeStruct((width, width), BF),
        ]
        + grad_shapes,
        in_specs=[whole] * 4
        + [stat] * 4
        + [whole, square, fixed(1, width), whole]
        + [column, column, pl.BlockSpec((chunk, width), lambda p: (first(p), 0))],
        out_specs=[whole] * 4
        + [fixed(2, PAIRS, 2, tokens), fixed(1, width), square]
        + grad_specs,
        scratch_shapes=scratch,
        compiler_params=pltpu.CompilerParams(**params),
    )(*parts, *lses, hidden, out_weight, gain, cotangent, gate, up, down)


def cross_backward(
    courier, ident, r, queries, grad, keyvals, lens, stats, key_weight, value_weight, summands=()
):
    tokens, keys = queries.shape[0], keyvals.shape[1]
    width = H * HD
    spec = block_specs(tokens, keys)

    def body(ins, outs, scratch):
        q_ref, da_ref, kv_ref, lens_ref, stats_ref, wk_ref, wv_ref = ins
        dkv_ref, dq_ref, dm_ref = outs
        (total_ref,) = scratch
        step = pl.program_id(0)

        @pl.when(step == 0)
        def _():
            total_ref[...] = jnp.zeros_like(total_ref)

        bias = key_bias(keys, lens_ref[...])

        def again(h, keys_h, query_h):
            mine, _, one = lane_masks()[h]
            scores = dot(keys_h * mine + bias * one, query_h + one, 1, 1)
            return jnp.exp(scores - stats_ref[0, 0, h : h + 1, :])

        weights = jnp.concatenate([wk_ref[...], wv_ref[...]], axis=1)
        grad_kv, grad_q = backward_pair(
            q_ref[...],
            da_ref[...],
            kv_ref[:, :128],
            kv_ref[:, 128:],
            again,
            [stats_ref[1, 0, h : h + 1, :] for h in range(2)],
        )
        dkv_ref[...] = grad_kv
        dq_ref[...] = grad_q
        total_ref[...] += dot(grad_kv, weights, 1, 1)

        @pl.when(step == PAIRS - 1)
        def _():
            dm_ref[...] = total_ref[...].astype(BF)

    return call(
        courier,
        ident,
        body,
        [queries, grad, keyvals, lens, stats, key_weight, value_weight],
        [
            spec["col"],
            spec["col"],
            pl.BlockSpec((None, keys, 256), lambda p: (r, 0, p)),
            pl.BlockSpec((None, 8, 128), lambda p: (r, 0, 0)),
            pl.BlockSpec((2, 1, 2, tokens), lambda p: (0, p, 0, 0)),
            spec["weight"],
            spec["weight"],
        ],
        [
            jax.ShapeDtypeStruct((keys, 2 * width), BF),
            jax.ShapeDtypeStruct((tokens, width), BF),
            jax.ShapeDtypeStruct((keys, width), BF),
        ],
        [spec["pair"], spec["col"], spec["rows"]],
        [pltpu.VMEM((keys, width), F32)],
        2**35,
        summands,
    )


def weight_terms(courier, ident, rows, grads):
    keys, width = rows[0].shape
    spec = block_specs(keys, keys)
    count = len(rows)

    def body(ins, outs, _):
        total = None
        for rows_ref, grad_ref in zip(ins[:count], ins[count:]):
            term = dot(rows_ref[...], grad_ref[...], 0, 0)
            total = term if total is None else total + term
        outs[0][...] = total[:, :128]
        outs[1][...] = total[:, 128:]

    return call(
        courier,
        ident,
        body,
        list(rows) + list(grads),
        [spec["rows"]] * count + [spec["pair"]] * count,
        [jax.ShapeDtypeStruct((width, width), F32)] * 2,
        [spec["weight"]] * 2,
        [],
        2**34,
    )


def self_backward(courier, ident, queries, grad, keys, values, lse, summand):
    tokens, width = queries.shape
    spec = block_specs(tokens, tokens)

    def body(ins, outs, _):
        q_ref, da_ref, k_ref, v_ref, lse_ref = ins
        dq_ref, dk_ref, dv_ref = outs
        grad_kv, dq_ref[...] = backward_pair(
            q_ref[...],
            da_ref[...],
            k_ref[...],
            v_ref[...],
            causal_probs([lse_ref[0, h : h + 1, :] for h in range(2)]),
            None,
        )
        dk_ref[...] = grad_kv[:, :128]
        dv_ref[...] = grad_kv[:, 128:]

    return call(
        courier,
        ident,
        body,
        [queries, grad, keys, values, lse],
        [spec["col"]] * 4 + [spec["stat"]],
        [jax.ShapeDtypeStruct((tokens, width), BF)] * 3,
        [spec["col"]] * 3,
        [],
        2**33,
        [summand],
    )


def rms_back(values, gain, grad):
    r = lax.rsqrt(jnp.mean(values * values, axis=-1, keepdims=True) + EPSILON)
    u = gain * grad
    back = r * u - values * (r * r * r) * jnp.mean(u * values, axis=-1, keepdims=True)
    return back, jnp.sum(grad * values * r, axis=0, keepdims=True)


def ending(sizes, ident, rows, grads, grad_q, grad_rows, left, two, held, lse, small_in):
    courier = Courier(
        sizes,
        [("line", PLANES - 1, grad_q[-1]), ("return", 0, grad_rows)]
        + [("scatter", 0, value) for value in left],
    )
    courier.lines = list(range(1, PLANES))
    jobs = len(courier.jobs)
    devices = sizes[0] * sizes[1] * sizes[2] * sizes[3]
    keys, width = rows[0].shape
    tokens = two.shape[0]
    share = width // devices
    chunk = 512
    cuts = keys // chunk
    groups = [Resident(sizes, (2 * share, width)) for _ in range(2)]
    groups += [Resident(sizes, (2 * share, 256)) for _ in range(6)]
    small = SmallSum(sizes, (8, width))
    early = [two] + list(held) + list(grad_q[:-1])
    far = list(rows) + list(grads) + early
    counts = (len(far), len(small_in) + 1, jobs, 6, jobs - 1, 4, len(early) - 1, 8, 3, 80, 10)

    def pack(ref, first, second, cols=EVERY):
        lanes = first.shape[1]
        parts = [v.astype(F32).reshape(devices, share, lanes) for v in (first, second)]
        both = jnp.concatenate(parts, axis=1).astype(BF)
        ref[:, :, :, :, :, cols] = both.reshape(tuple(sizes) + both.shape[1:])

    def kernel(*refs):
        far_refs, near, sources, outs, targets, stage, loaded, work, sems, group_refs, rest = (
            split_refs(refs, *counts)
        )
        self_gain, cross_gain, ffn_term, lse_ref = near
        grad_in, *sums, norm_sums = outs
        row_buf, grad_buf, total, load_sems = stage
        dq_got, da_ref, dq1, dk1, dv1, normed_ref, _, norm_all = work
        chunk_sems, early_sems = load_sems, work[6]
        copies = courier.copies(sources, [dq_got] + list(targets), sems)
        courier.greet()
        for copy in copies:
            copy.start()

        def chunk_loads(r, i):
            slot = rem(i, 2)
            where = pl.ds(pl.multiple_of(rem(i, cuts) * chunk, chunk), chunk)
            return [
                pltpu.make_async_copy(
                    far_refs[r].at[where], row_buf.at[slot], chunk_sems.at[slot, 0]
                ),
                pltpu.make_async_copy(
                    far_refs[PLANES + r].at[where], grad_buf.at[slot], chunk_sems.at[slot, 1]
                ),
            ]

        def start_chunk(i):
            for r in range(PLANES):

                @pl.when(lax.div(jnp.int32(i), cuts) == r)
                def _(r=r):
                    for copy in chunk_loads(r, i):
                        copy.start()

        total[...] = jnp.zeros_like(total)
        early_refs = far_refs[2 * PLANES :]
        early_loads = [
            pltpu.make_async_copy(source, target, early_sems.at[n])
            for n, (source, target) in enumerate(zip(early_refs, [grad_in] + list(loaded)))
        ]
        start_chunk(0)
        for copy in early_loads:
            copy.start()

        @pl.loop(0, PLANES * cuts)
        def _(i):
            @pl.when(i + 1 < PLANES * cuts)
            def _():
                start_chunk(i + 1)

            for copy in chunk_loads(0, i):
                copy.wait()
            slot = rem(i, 2)
            total[...] += dot(row_buf[slot], grad_buf[slot], 0, 0)

        bound = [
            one.bind(group_refs[10 * n : 10 * n + 10]) for n, one in enumerate(groups)
        ]
        bits = small.bind(rest)

        @pl.loop(0, PAIRS)
        def _(p):
            at = pl.multiple_of(p * 256, 256)
            pack(
                bound[0].held,
                total[:, pl.ds(at, 128)],
                total[:, pl.ds(at + 128, 128)],
                pl.ds(pl.multiple_of(p * 128, 128), 128),
            )

        bound[0].begin()
        for copy in early_loads:
            copy.wait()
        copies[1].wait()
        x_ref, h1_ref, gco_ref, q_ref, k_ref, v_ref, attn_ref = loaded[:7]
        wq_ref, wk_ref, wv_ref, wo_ref, wc_ref, *dq_refs = loaded[7:]
        grad = dq_got[...].astype(F32)
        for ref in dq_refs:
            grad += ref[...].astype(F32)
        dq_got[...] = grad.astype(BF)
        hidden = h1_ref[...]
        back, cross_norm = rms_back(hidden, cross_gain[...], dot(dq_got[...], wc_ref[...], 1, 1))
        grad_in[...] += back
        dv1[...] = rms(hidden, cross_gain[...]).astype(BF)
        bound[0].after_first()

        @pl.loop(0, 3)
        def _(i):
            cols = pl.ds(pl.multiple_of(i * 256, 256), 256)
            pack(bound[1].held, dot(dv1[...], dq_got[:, cols], 0, 0), gco_ref[:, cols], cols)

        bound[1].begin()
        low_ref = dq_got
        low_ref[...] = grad_in[...].astype(BF)
        da_ref[...] = dot(low_ref[...], wo_ref[...], 1, 1).astype(BF)
        values = x_ref[...].astype(F32)
        normed_ref[...] = rms(values, self_gain[...]).astype(BF)

        for third in range(3):

            @pl.loop(2 * third, 2 * third + 2)
            def _(p):
                cols = pl.ds(pl.multiple_of(p * 128, 128), 128)
                grad_kv, grad_q_p = backward_pair(
                    q_ref[:, cols],
                    da_ref[:, cols],
                    k_ref[:, cols],
                    v_ref[:, cols],
                    causal_probs([lse_ref[p, h : h + 1, :] for h in range(2)]),
                    None,
                )
                dq1[:, cols] = grad_q_p
                dk1[:, cols] = grad_kv[:, :128]
                dv1[:, cols] = grad_kv[:, 128:]

            cols = pl.ds(third * 256, 256)
            near_sum, far_sum = bound[2 + 2 * third], bound[3 + 2 * third]
            normed = normed_ref[...]
            pack(near_sum.held, dot(normed, dq1[:, cols], 0, 0), dot(normed, dk1[:, cols], 0, 0))
            near_sum.begin()
            pack(
                far_sum.held,
                dot(normed, dv1[:, cols], 0, 0),
                dot(attn_ref[...], low_ref[:, cols], 0, 0),
            )
            far_sum.begin()
            if third == 0:
                bound[0].after_second()
                bound[1].after_first()
            if third == 1:
                bound[0].after_third_start()
                bound[1].after_second()
                bound[2].after_first()
                bound[3].after_first()
            if third == 2:
                bound[1].after_third_start()
                bound[2].after_second()
                bound[3].after_second()
                bound[4].after_first()
                bound[5].after_first()
        grad_normed = dot(dq1[...], wq_ref[...], 1, 1) + dot(dk1[...], wk_ref[...], 1, 1)
        bound[6].after_first()
        bound[7].after_first()
        bound[2].after_third_start()
        bound[3].after_third_start()
        grad_normed += dot(dv1[...], wv_ref[...], 1, 1)
        back, self_norm = rms_back(values, self_gain[...], grad_normed)
        bound[4].after_second()
        bound[5].after_second()
        bound[6].after_second()
        bound[7].after_second()
        grad_in[...] += back
        bits.held[0][...] = jnp.concatenate(
            [self_norm, cross_norm, ffn_term[...], jnp.zeros((5, width), F32)], axis=0
        )
        bits.start(0)
        bound[4].after_third_start()
        bound[5].after_third_start()
        bits.advance(0)
        bound[6].after_third_start()
        bound[7].after_third_start()
        bits.advance(1)
        bits.advance(2)
        bound[0].finish(sums[0])
        bound[1].finish(sums[1])
        for n in range(2, 8):
            third, kind = divmod(n - 2, 2)
            bound[n].finish(sums[2 + kind].at[:, pl.ds(third * 256, 256)])
        bits.advance(3, norm_all)
        device = lax.axis_index("z") * courier.plane + courier.me()
        lane = lax.broadcasted_iota(jnp.int32, (width, 128), 0)
        place_of = lax.broadcasted_iota(jnp.int32, (width, 128), 1) + device * share
        pick = jnp.where(lane == place_of, 1.0, 0.0)
        norm_sums[...] = lax.dot_general(
            norm_all[...],
            pick,
            (((1,), (0,)), ((), ())),
            precision=lax.Precision.HIGHEST,
            preferred_element_type=F32,
        )
        for n, copy in enumerate(copies):
            if n != 1:
                copy.wait()

    any_spec = pl.BlockSpec(memory_space=pl.ANY)
    vmem = pl.BlockSpec(memory_space=pltpu.VMEM)
    row = pltpu.VMEM((tokens, width), BF)
    scratch = [
        pltpu.VMEM((2, chunk, width), BF),
        pltpu.VMEM((2, chunk, 2 * width), BF),
        pltpu.VMEM((width, 2 * width), F32),
        pltpu.SemaphoreType.DMA((2, 2)),
    ]
    scratch += [pltpu.VMEM(v.shape, v.dtype) for v in early[1:]]
    scratch += [row] * 6 + [pltpu.SemaphoreType.DMA((len(early),))]
    scratch += [pltpu.VMEM((8, width), F32)] + courier.scratch()
    for one in groups:
        scratch += one.scratch()
    scratch += small.scratch()
    outs = pl.pallas_call(
        kernel,
        out_shape=[jax.ShapeDtypeStruct((tokens, width), F32)]
        + [jax.ShapeDtypeStruct((2 * share, width), F32)] * 4
        + [jax.ShapeDtypeStruct((8, 128), F32)]
        + courier.out_shape()[1:],
        in_specs=[any_spec] * len(far) + [vmem] * (len(small_in) + 1) + courier.specs(),
        out_specs=[vmem] * 6 + courier.specs()[1:],
        scratch_shapes=scratch,
        compiler_params=pltpu.CompilerParams(
            vmem_limit_bytes=62 * 2**20, collective_id=ident, has_side_effects=True
        ),
    )(*far, *small_in, lse, *courier.values())
    return outs[0], outs[1:5], outs[5], outs[6:]


def place_kernel(*refs):
    *blocks, out_ref, held, arrive, leave = refs
    z = lax.axis_index("z")
    size = held.shape[1]
    inward = []
    outward = []
    for r, block in enumerate(blocks):
        at = rem(z + r, PLANES) * size
        inward.append(pltpu.make_async_copy(block, held.at[r], arrive.at[r]))
        outward.append(
            pltpu.make_async_copy(held.at[r], out_ref.at[pl.ds(at, size)], leave.at[r])
        )
        inward[r].start()
    for r in range(len(blocks)):
        inward[r].wait()
        outward[r].start()
    for copy in outward:
        copy.wait()


def finish_kernel(*refs, pieces):
    ins, far, outs, far_outs, work = split_refs(refs, 9, PLANES + 2, 14, 3, 5)
    left0, got0, left1, got1, *sums, norms = ins
    gate_ref, up_ref, down_ref, *halves = outs
    halves, norm_outs = halves[:8], halves[8:]
    blocks, others = far[:PLANES], far[PLANES:]
    out_ref, *other_outs = far_outs
    held, held_in, held_out, arrive, leave = work
    z = lax.axis_index("z")
    size = held.shape[1]
    part = size // pieces
    moves = []
    for r, block in enumerate(blocks):
        at = rem(z + r, PLANES) * size
        for n in range(pieces):
            rows = pl.ds(n * part, part)
            moves.append((block.at[rows], held.at[r, rows], out_ref.at[pl.ds(at + n * part, part)]))
    moves.append((others[0], held_in, other_outs[0]))
    moves.append((others[1], held_out, other_outs[1]))
    inward = []
    outward = []
    for n, (source, middle_ref, target) in enumerate(moves):
        inward.append(pltpu.make_async_copy(source, middle_ref, arrive.at[n]))
        outward.append(pltpu.make_async_copy(middle_ref, target, leave.at[n]))
        inward[n].start()
    for n in range(len(moves)):
        inward[n].wait()
        outward[n].start()
    share = gate_ref.shape[0]
    wide = left0[z].astype(F32)
    tall = left1[z].astype(F32)
    for k in range(PLANES - 1):
        wide += got0[k].astype(F32)
        tall += got1[k].astype(F32)
    gate_ref[...] = wide[:share]
    up_ref[...] = wide[share:]
    down_ref[...] = tall
    for n, ref in enumerate(sums):
        halves[2 * n][...] = ref[:share]
        halves[2 * n + 1][...] = ref[share:]
    for n, ref in enumerate(norm_outs):
        ref[...] = norms[n : n + 1]
    for copy in outward:
        copy.wait()


def finish(blocks, left0, got0, left1, got1, sums, norms, grad_in, output):
    shape = blocks[0].shape
    pieces = 4 if shape[0] % 4 == 0 else 1
    share, inner = left0.shape[1] // 2, left0.shape[2]
    width = sums[0].shape[1]
    hbm = pl.BlockSpec(memory_space=pl.ANY)
    vmem = pl.BlockSpec(memory_space=pltpu.VMEM)
    moves = PLANES * pieces + 2
    outs = pl.pallas_call(
        functools.partial(finish_kernel, pieces=pieces),
        out_shape=[jax.ShapeDtypeStruct((share, inner), F32)] * 2
        + [jax.ShapeDtypeStruct(left1.shape[1:], F32)]
        + [jax.ShapeDtypeStruct((share, width), F32)] * 8
        + [jax.ShapeDtypeStruct((1, norms.shape[1]), F32)] * 3
        + [jax.ShapeDtypeStruct((PLANES * shape[0],) + shape[1:], BF)]
        + [jax.ShapeDtypeStruct(v.shape, v.dtype) for v in (grad_in, output)],
        in_specs=[vmem] * 9 + [hbm] * (PLANES + 2),
        out_specs=[vmem] * 14 + [hbm] * 3,
        scratch_shapes=[
            pltpu.VMEM((PLANES,) + shape, BF),
            pltpu.VMEM(grad_in.shape, grad_in.dtype),
            pltpu.VMEM(output.shape, output.dtype),
            pltpu.SemaphoreType.DMA((moves,)),
            pltpu.SemaphoreType.DMA((moves,)),
        ],
        compiler_params=pltpu.CompilerParams(vmem_limit_bytes=VMEM),
    )(left0, got0, left1, got1, *sums, norms, *blocks, grad_in, output)
    return outs[:3], outs[3:11], outs[11:14], outs[14:]


def place(blocks):
    shape = blocks[0].shape
    count = len(blocks)
    hbm = pl.BlockSpec(memory_space=pl.ANY)
    return pl.pallas_call(
        place_kernel,
        out_shape=jax.ShapeDtypeStruct((count * shape[0],) + shape[1:], blocks[0].dtype),
        in_specs=[hbm] * count,
        out_specs=hbm,
        scratch_shapes=[
            pltpu.VMEM((count,) + shape, blocks[0].dtype),
            pltpu.SemaphoreType.DMA((count,)),
            pltpu.SemaphoreType.DMA((count,)),
        ],
        compiler_params=pltpu.CompilerParams(vmem_limit_bytes=VMEM),
    )(*blocks)


def norm_apply(values, gain):
    return values * lax.rsqrt(jnp.mean(values * values, axis=-1, keepdims=True) + EPSILON) * gain


def norm_back(values, gain, grad):
    r = lax.rsqrt(jnp.mean(values * values, axis=-1, keepdims=True) + EPSILON)
    u = gain * grad
    dv = r * u - values * (r * r * r) * jnp.mean(u * values, axis=-1, keepdims=True)
    return dv, jnp.sum(grad * values * r, axis=0)


def matmul(left, right):
    return dot(left, right, 1, 0)


def matmul_t(left, right):
    return dot(left, right, 1, 1)


def tmatmul(left, right):
    return dot(left, right, 0, 0)


def on_device(
    sizes,
    decoder_in,
    memory,
    memory_lengths,
    cotangent,
    norm_self,
    self_query,
    self_key,
    self_value,
    self_out,
    norm_cross,
    cross_query,
    cross_key,
    cross_value,
    cross_out,
    norm_ffn,
    ffn_gate,
    ffn_up,
    ffn_down,
):
    devices, positions, width = memory.shape
    plane_size = sizes[1] * sizes[2] * sizes[3]
    z = lax.axis_index("z")

    def flat(blocks):
        return blocks.reshape(plane_size * positions, width)

    def cut(rows):
        return rows.reshape(plane_size, positions, width)

    forward = forward_part(
        sizes,
        0,
        memory,
        jnp.broadcast_to(memory_lengths[None, :], (8, 128)),
        decoder_in[0],
        (norm_self[None], norm_cross[None]),
        (self_query, self_key, self_value, self_out, cross_query),
        cross_key,
        cross_value,
    )
    query_one, key_one, value_one, lse_one, attn_one, hidden_one, _ = forward["saved"]
    queries = forward["queries"]
    rows = {r: flat(forward["rows"][r]) for r in range(PLANES)}

    (
        output,
        attn_two,
        grad_two,
        grad_attn_two,
        stats,
        grad_norm_ffn,
        grad_cross_out,
        *grads_in,
        grad_down,
    ) = middle(
        sizes,
        forward["parts"],
        forward["lses"],
        hidden_one,
        cross_out,
        norm_ffn[None],
        cotangent[0],
        ffn_gate,
        ffn_up,
        ffn_down,
    )
    decoder_out = output[None]
    if len(grads_in) == 2:
        summands = {
            0: [summand_of(sizes, grads_in)],
            1: [grad_down.reshape(tuple(sizes) + grad_down.shape[1:])],
        }
    else:
        summands = {0: [grads_in[0], grad_down]}
    left, got = {}, {}

    grads = {0: grad_attn_two}
    both = {0: stats}
    grad_kv, grad_q, grad_rows, returned = {}, {}, {}, {}
    for r in range(PLANES):
        jobs = []
        if r + 1 < PLANES:
            jobs.append(("line", -(r + 1), grad_attn_two))
            jobs.append(("line", -(r + 1), stats))
        if r >= 1:
            jobs.append(("return", 0, cut(grad_rows[r - 1])))
        if r >= 2:
            jobs.append(("line", r - 1, grad_q[r - 1]))
        (grad_kv[r], grad_q[r], grad_rows[r]), moved = cross_backward(
            Courier(sizes, jobs),
            5 + r,
            r,
            queries[r],
            grads[r],
            forward["keyvals"],
            forward["lens"],
            both[r],
            cross_key,
            cross_value,
            summands.get(r, []),
        )
        moved = list(moved)
        if r in summands:
            for value in moved[len(moved) - len(summands[r]) :]:
                left[len(left)] = value
        if r + 1 < PLANES:
            grads[r + 1], both[r + 1] = moved.pop(0), moved.pop(0)
        if r >= 1:
            returned[r - 1] = moved.pop(0)
        if r >= 2:
            grad_q[r - 1] = moved.pop(0)
    last = PLANES - 1
    part = width // devices
    if part % 8 == 0:
        decoder_in_grad, sums, norm_sums, moved = ending(
            sizes,
            9,
            [rows[r] for r in range(PLANES)],
            [grad_kv[r] for r in range(PLANES)],
            [grad_q[r] for r in range(PLANES)],
            cut(grad_rows[last]),
            [left[0], left[1]],
            grad_two,
            (decoder_in[0], hidden_one, grad_cross_out, query_one, key_one, value_one, attn_one)
            + (self_query, self_key, self_value, self_out, cross_query),
            lse_one,
            (norm_self[None], norm_cross[None], grad_norm_ffn),
        )
        returned[last], got[0], got[1] = moved
        ffn, halves, norm_rows, whole = finish(
            [returned[r] for r in range(PLANES)],
            left[0],
            got[0],
            left[1],
            got[1],
            sums,
            norm_sums,
            decoder_in_grad,
            output,
        )
        memory_grad, decoder_in_grad, output = whole
        norm_self_sum, norm_cross_sum, norm_ffn_sum = (v[0, :part] for v in norm_rows)
        sum_cross_key, sum_cross_value, sum_cross_query, sum_cross_out = halves[:4]
        return (
            output[None],
            decoder_in_grad[None],
            memory_grad,
            norm_self_sum,
            *halves[4:],
            norm_cross_sum,
            sum_cross_query,
            sum_cross_key,
            sum_cross_value,
            sum_cross_out,
            norm_ffn_sum,
            *ffn,
        )

    jobs = [
        ("line", last, grad_q[last]),
        ("return", 0, cut(grad_rows[last])),
        ("scatter", 0, left[0]),
        ("scatter", 0, left[1]),
    ]
    (grad_cross_key, grad_cross_value), (grad_q[last], returned[last], got[0], got[1]) = weight_terms(
        Courier(sizes, jobs),
        9,
        [rows[r] for r in range(PLANES)],
        [grad_kv[r] for r in range(PLANES)],
    )
    memory_grad = place([returned[r] for r in range(PLANES)])

    inputs = decoder_in[0].astype(F32)
    normed_one = norm_apply(inputs, norm_self).astype(BF)
    normed_two = norm_apply(hidden_one, norm_cross).astype(BF)
    grad_q_two = sum(grad_q[r].astype(F32) for r in range(PLANES)).astype(BF)
    grad_cross_query = tmatmul(normed_two, grad_q_two)
    grad_normed_two = matmul_t(grad_q_two, cross_query)
    back_one, grad_norm_cross = norm_back(hidden_one, norm_cross, grad_normed_two)
    grad_one = grad_two + back_one
    branch_one = grad_one.astype(BF)
    grad_self_out = tmatmul(attn_one, branch_one)
    grad_attn_one = matmul_t(branch_one, self_out).astype(BF)
    (grad_q_one, grad_k_one, grad_v_one), (cross_left,) = self_backward(
        Courier(sizes, []),
        10,
        query_one,
        grad_attn_one,
        key_one,
        value_one,
        lse_one,
        summand_of(sizes, (grad_cross_key, grad_cross_value)),
    )
    grad_normed_one = (
        matmul_t(grad_q_one, self_query)
        + matmul_t(grad_k_one, self_key)
        + matmul_t(grad_v_one, self_value)
    )
    back_in, grad_norm_self = norm_back(inputs, norm_self, grad_normed_one)
    decoder_in_grad = (grad_one + back_in)[None]
    share_of_norms = width // devices
    norms = jnp.stack(
        [g.reshape(devices, share_of_norms) for g in (grad_norm_self, grad_norm_cross, grad_norm_ffn[0])],
        axis=1,
    ).reshape(devices, 1, 3 * share_of_norms)
    norms = jnp.pad(norms, ((0, 0), (0, 15), (0, 256 - 3 * share_of_norms)))
    (cross_got,), sums = reduce_all(
        sizes,
        11,
        [
            norms.astype(BF).reshape(tuple(sizes) + norms.shape[1:]),
            summand_of(sizes, (grad_cross_query, grad_cross_out.astype(F32))),
            summand_of(sizes, (tmatmul(normed_one, grad_q_one), tmatmul(normed_one, grad_k_one))),
            summand_of(sizes, (tmatmul(normed_one, grad_v_one), grad_self_out)),
        ],
        [cross_left],
    )
    norm_sums = sums[0][0, : 3 * share_of_norms].reshape(3, share_of_norms)
    gate_up = over_z(left[0], got[0])
    cross_kv = over_z(cross_left, cross_got)
    part = share_of_norms
    return (
        decoder_out,
        decoder_in_grad,
        memory_grad,
        norm_sums[0],
        sums[2][:part],
        sums[2][part:],
        sums[3][:part],
        sums[3][part:],
        norm_sums[1],
        sums[1][:part],
        cross_kv[:part],
        cross_kv[part:],
        sums[1][part:],
        norm_sums[2],
        gate_up[:part],
        gate_up[part:],
        over_z(left[1], got[1]),
    )


def solution(mesh):
    dp, seq = mesh.devices.shape
    cores = 2
    lines = dp // PLANES
    split = Mesh(mesh.devices.reshape(PLANES, lines, seq // cores, cores), ALL)
    sizes = split.devices.shape
    first = P(ALL)
    middle = P(None, ALL)
    whole = P()
    return jax.shard_map(
        functools.partial(on_device, sizes),
        mesh=split,
        in_specs=(first, middle, first, first) + (whole,) * 14,
        out_specs=(first, first, middle) + (first,) * 14,
        check_vma=False,
    )
```

```python
import functools

import jax
import jax.numpy as jnp
from jax import lax
from jax.experimental import pallas as pl
from jax.experimental.pallas import tpu as pltpu
from jax.sharding import Mesh
from jax.sharding import PartitionSpec as P

H = 12
HD = 64
PAIRS = 6
PLANES = 4
EPSILON = 1e-06
MASKED = -1e30
VMEM = 56 * 2**20
BF = jnp.bfloat16
F32 = jnp.float32
ALL = ("z", "y", "x", "c")
PLANE = ("y", "x", "c")
EVERY = slice(None)


def dot(left, right, left_dim, right_dim):
    return lax.dot_general(
        left, right, (((left_dim,), (right_dim,)), ((), ())), preferred_element_type=F32
    )


def lane_masks():
    lane = lax.broadcasted_iota(jnp.int32, (1, 2 * HD), 1)
    low = jnp.where(lane < HD, 1.0, 0.0)
    first = jnp.where(lane == HD, 1.0, 0.0)
    second = jnp.where(lane == 0, 1.0, 0.0)
    low, high, first, second = (
        v.astype(BF) for v in (low, 1.0 - low, first, second)
    )
    return ((low, high, first), (high, low, second))


def causal_mask(scores):
    key = lax.broadcasted_iota(jnp.int32, scores.shape, 0)
    query = lax.broadcasted_iota(jnp.int32, scores.shape, 1)
    return jnp.where(key <= query, scores, MASKED)


def rem(value, size):
    return lax.rem(value, size)


class Courier:
    def __init__(self, sizes, jobs):
        self.sizes = sizes
        self.jobs = jobs
        self.plane = sizes[1] * sizes[2] * sizes[3]
        self.in_plane = any(job[0] in ("fetch", "return") for job in jobs)
        self.lines = [job[1] for job in jobs if job[0] == "line"]
        for job in jobs:
            if job[0] == "scatter":
                self.lines += list(range(1, PLANES))

    def out_shape(self):
        shapes = []
        for kind, _, value in self.jobs:
            shape = value.shape
            if kind == "fetch":
                shape = (self.plane,) + shape[1:]
            elif kind == "scatter":
                shape = (PLANES - 1,) + shape[1:]
            shapes.append(jax.ShapeDtypeStruct(shape, value.dtype))
        return shapes

    def specs(self):
        return [pl.BlockSpec(memory_space=pl.ANY)] * len(self.jobs)

    def values(self):
        return [job[2] for job in self.jobs]

    def scratch(self):
        each = {"line": 1, "scatter": PLANES - 1}
        count = max(1, sum(each.get(job[0], self.plane - 1) for job in self.jobs))
        own = max(1, sum(job[0] in ("fetch", "return") for job in self.jobs))
        return [pltpu.SemaphoreType.DMA((n,)) for n in (count, count, own)]

    def params(self, ident):
        return pltpu.CompilerParams(
            vmem_limit_bytes=VMEM, collective_id=ident, has_side_effects=True
        )

    def me(self):
        _, _, x_size, c_size = self.sizes
        y, x, c = (lax.axis_index(name) for name in PLANE)
        return (y * x_size + x) * c_size + c

    def along(self, offset):
        return {"z": rem(lax.axis_index("z") + (offset + PLANES), PLANES)}

    def across(self, offset):
        _, _, x_size, c_size = self.sizes
        other = rem(self.me() + offset, self.plane)
        line = lax.div(other, c_size)
        return other, {"y": lax.div(line, x_size), "x": rem(line, x_size), "c": rem(other, c_size)}

    def greet(self):
        barrier = pltpu.get_barrier_semaphore()
        count = 0
        if self.in_plane:
            for k in range(1, self.plane):
                _, device = self.across(k)
                pl.semaphore_signal(
                    barrier, inc=1, device_id=device, device_id_type=pl.DeviceIdType.MESH
                )
                count += 1
        for offset in self.lines:
            pl.semaphore_signal(
                barrier,
                inc=1,
                device_id=self.along(-offset),
                device_id_type=pl.DeviceIdType.MESH,
            )
            count += 1
        pl.semaphore_wait(barrier, count)

    def copies(self, sources, targets, sems):
        send, receive, own = sems
        remote = []
        local = []

        def add(source, target, device):
            n = len(remote)
            remote.append(
                pltpu.make_async_remote_copy(
                    src_ref=source,
                    dst_ref=target,
                    send_sem=send.at[n],
                    recv_sem=receive.at[n],
                    device_id=device,
                    device_id_type=pl.DeviceIdType.MESH,
                )
            )

        me = self.me()
        for (kind, offset, _), source, target in zip(self.jobs, sources, targets):
            if kind == "line":
                add(source, target, self.along(offset))
                continue
            if kind == "scatter":
                for k in range(1, PLANES):
                    there = rem(lax.axis_index("z") + k, PLANES)
                    add(source.at[there], target.at[k - 1], self.along(k))
                continue
            base = 0
            if kind == "fetch":
                base = rem(lax.axis_index("z") + offset, PLANES) * self.plane
            for k in range(1, self.plane):
                other, device = self.across(k)
                add(source.at[base + other], target.at[me], device)
            local.append(
                pltpu.make_async_copy(source.at[base + me], target.at[me], own.at[len(local)])
            )
        return local + remote

    def start(self, sources, targets, sems):
        self.greet()
        for copy in self.copies(sources, targets, sems):
            copy.start()

    def wait(self, sources, targets, sems):
        for copy in self.copies(sources, targets, sems):
            copy.wait()


class Reducer:
    def __init__(self, sizes, shape):
        self.sizes = sizes
        self.rows, self.lanes = shape[-2:]
        self.half = self.lanes // 2

    def scratch(self):
        z, y, x, _ = self.sizes
        r, w, h = self.rows, self.lanes, self.half
        crossing = x + y - 2
        return [
            pltpu.VMEM((z, y, x, r, w), BF),
            pltpu.VMEM((z, y, x, r, w), BF),
            pltpu.VMEM((x - 1, z, y, r, h), BF),
            pltpu.VMEM((y - 1, z, x, r, h), BF),
            pltpu.VMEM((y - 1, z, r, h), BF),
            pltpu.VMEM((x - 1, z, r, h), BF),
            pltpu.SemaphoreType.DMA((1,)),
            pltpu.SemaphoreType.DMA((1 + 2 * crossing,)),
            pltpu.SemaphoreType.DMA((1 + 2 * crossing,)),
        ]

    def bind(self, source, refs):
        self.source = source
        self.held, self.got0, self.got1x, self.got1y, self.got2y, self.got2x = refs[:6]
        self.local, self.send, self.receive = refs[6:]
        self.z, self.y, self.x, self.c = (lax.axis_index(name) for name in ALL)
        return self

    def index(self, z, y, x, lanes):
        return (z, y, x, EVERY, lanes)

    def slab(self, z, y, x, lanes):
        return self.held.at[self.index(z, y, x, lanes)]

    given = slab

    def remote(self, n, source, target, device):
        return pltpu.make_async_remote_copy(
            src_ref=source,
            dst_ref=target,
            send_sem=self.send.at[n],
            recv_sem=self.receive.at[n],
            device_id=device,
            device_id_type=pl.DeviceIdType.MESH,
        )

    def first(self):
        other = 1 - self.c
        return [
            pltpu.make_async_copy(self.source.at[:, :, :, self.c], self.held, self.local.at[0]),
            self.remote(0, self.source.at[:, :, :, other], self.got0, {"c": other}),
        ]

    def second(self):
        _, y_size, x_size, _ = self.sizes
        left, right = pl.ds(0, self.half), pl.ds(self.half, self.half)
        copies = []
        for k in range(1, x_size):
            there = rem(self.x + k, x_size)
            copies.append((self.given(EVERY, EVERY, there, left), self.got1x.at[k - 1], {"x": there}))
        for k in range(1, y_size):
            there = rem(self.y + k, y_size)
            copies.append((self.given(EVERY, there, EVERY, right), self.got1y.at[k - 1], {"y": there}))
        return [self.remote(1 + n, *copy) for n, copy in enumerate(copies)]

    def third(self):
        _, y_size, x_size, _ = self.sizes
        left, right = pl.ds(0, self.half), pl.ds(self.half, self.half)
        at = 1 + x_size + y_size - 2
        copies = []
        for k in range(1, y_size):
            there = rem(self.y + k, y_size)
            copies.append(
                (self.slab(EVERY, there, self.x, left), self.got2y.at[k - 1], {"y": there})
            )
        for k in range(1, x_size):
            there = rem(self.x + k, x_size)
            copies.append(
                (self.slab(EVERY, self.y, there, right), self.got2x.at[k - 1], {"x": there})
            )
        return [self.remote(at + n, *copy) for n, copy in enumerate(copies)]

    def begin(self):
        for copy in self.first():
            copy.start()

    def after_first(self):
        for copy in self.first():
            copy.wait()

        @pl.loop(0, self.sizes[0])
        def _(z):
            at = self.index(z, EVERY, EVERY, EVERY)
            self.held[at] = (self.held[at].astype(F32) + self.got0[z].astype(F32)).astype(BF)

        for copy in self.second():
            copy.start()

    def after_second(self):
        _, y_size, x_size, _ = self.sizes
        for copy in self.second():
            copy.wait()
        h = self.half

        @pl.loop(0, self.sizes[0])
        def _(z):
            for y in range(y_size):
                at = self.index(z, y, self.x, pl.ds(0, h))
                total = self.held[at].astype(F32)
                for k in range(x_size - 1):
                    total += self.got1x[k, z, y].astype(F32)
                self.held[at] = total.astype(BF)
            for x in range(x_size):
                at = self.index(z, self.y, x, pl.ds(h, h))
                total = self.held[at].astype(F32)
                for k in range(y_size - 1):
                    total += self.got1y[k, z, x].astype(F32)
                self.held[at] = total.astype(BF)

        for copy in self.third():
            copy.start()

    def after_third(self, out_ref):
        _, y_size, x_size, _ = self.sizes
        for copy in self.third():
            copy.wait()
        h = self.half

        @pl.loop(0, self.sizes[0])
        def _(z):
            total = self.held[self.index(z, self.y, self.x, pl.ds(0, h))].astype(F32)
            for k in range(y_size - 1):
                total += self.got2y[k, z].astype(F32)
            out_ref[z, :, :h] = total.astype(BF)
            total = self.held[self.index(z, self.y, self.x, pl.ds(h, h))].astype(F32)
            for k in range(x_size - 1):
                total += self.got2x[k, z].astype(F32)
            out_ref[z, :, h:] = total.astype(BF)


class Halved(Reducer):
    def scratch(self):
        z, y, x, _ = self.sizes
        r, w, h = self.rows, self.lanes, self.half
        crossing = x + y - 2
        return [
            pltpu.VMEM((z, y, x, r, w), BF),
            pltpu.VMEM((x - 1, z, y, r, h), BF),
            pltpu.VMEM((y - 1, z, x, r, h), BF),
            pltpu.VMEM((y - 1, z, r, h), BF),
            pltpu.VMEM((x - 1, z, r, h), BF),
            pltpu.SemaphoreType.DMA((1,)),
            pltpu.SemaphoreType.DMA((1 + 2 * crossing,)),
            pltpu.SemaphoreType.DMA((1 + 2 * crossing,)),
        ]

    def bind(self, source, refs):
        self.source = source
        self.held, self.got1x, self.got1y, self.got2y, self.got2x = refs[:5]
        self.local, self.send, self.receive = refs[5:]
        self.z, self.y, self.x, self.c = (lax.axis_index(name) for name in ALL)
        return self

    def given(self, z, y, x, lanes):
        return self.source.at[self.index(z, y, x, lanes)]

    def first(self):
        return [pltpu.make_async_copy(self.source, self.held, self.local.at[0])]

    def begin(self):
        for copy in self.first() + self.second():
            copy.start()

    def after_first(self):
        pass

    def after_second(self):
        for copy in self.first():
            copy.wait()
        super().after_second()


class Resident(Reducer):
    def scratch(self):
        z, y, x, c = self.sizes
        r, w, h = self.rows, self.lanes, self.half
        count = 1 + 2 * (x + y - 2) + z - 1
        return [
            pltpu.VMEM((z, y, x, c, r, w), BF),
            pltpu.VMEM((z, y, x, r, w), BF),
            pltpu.VMEM((x - 1, z, y, r, h), BF),
            pltpu.VMEM((y - 1, z, x, r, h), BF),
            pltpu.VMEM((y - 1, z, r, h), BF),
            pltpu.VMEM((x - 1, z, r, h), BF),
            pltpu.VMEM((z, r, w), BF),
            pltpu.VMEM((z - 1, r, w), BF),
            pltpu.SemaphoreType.DMA((count,)),
            pltpu.SemaphoreType.DMA((count,)),
        ]

    def bind(self, refs):
        self.held, self.got0, self.got1x, self.got1y, self.got2y, self.got2x = refs[:6]
        self.left, self.got3, self.send, self.receive = refs[6:]
        self.z, self.y, self.x, self.c = (lax.axis_index(name) for name in ALL)
        return self

    def index(self, z, y, x, lanes):
        return (z, y, x, self.c, EVERY, lanes)

    def first(self):
        other = 1 - self.c
        return [self.remote(0, self.held.at[:, :, :, other], self.got0, {"c": other})]

    def fourth(self):
        _, y_size, x_size, _ = self.sizes
        at = 1 + 2 * (x_size + y_size - 2)
        copies = []
        for k in range(1, PLANES):
            there = rem(self.z + k, PLANES)
            copies.append(
                self.remote(at + k - 1, self.left.at[there], self.got3.at[k - 1], {"z": there})
            )
        return copies

    def after_third_start(self):
        self.after_third(self.left)
        for copy in self.fourth():
            copy.start()

    def finish(self, out_ref):
        for copy in self.fourth():
            copy.wait()
        total = self.left[self.z].astype(F32)
        for k in range(PLANES - 1):
            total += self.got3[k].astype(F32)
        out_ref[...] = total


class SmallSum:
    def __init__(self, sizes, shape):
        self.shape = shape
        self.steps = list(zip(("c", "x", "y", "z"), (sizes[3], sizes[2], sizes[1], sizes[0])))

    def scratch(self):
        count = sum(n - 1 for _, n in self.steps)
        return (
            [pltpu.VMEM(self.shape, F32) for _ in range(4)]
            + [pltpu.VMEM((n - 1,) + self.shape, F32) for _, n in self.steps]
            + [pltpu.SemaphoreType.DMA((count,))] * 2
        )

    def bind(self, refs):
        self.held, self.got = refs[:4], refs[4:8]
        self.send, self.receive = refs[8:]
        return self

    def copies(self, step):
        axis, n = self.steps[step]
        at = sum(m - 1 for _, m in self.steps[:step])
        me = lax.axis_index(axis)
        return [
            pltpu.make_async_remote_copy(
                src_ref=self.held[step],
                dst_ref=self.got[step].at[k - 1],
                send_sem=self.send.at[at + k - 1],
                recv_sem=self.receive.at[at + k - 1],
                device_id={axis: rem(me + k, n)},
                device_id_type=pl.DeviceIdType.MESH,
            )
            for k in range(1, n)
        ]

    def start(self, step):
        for copy in self.copies(step):
            copy.start()

    def advance(self, step, out_ref=None):
        for copy in self.copies(step):
            copy.wait()
        total = self.held[step][...]
        for k in range(self.steps[step][1] - 1):
            total += self.got[step][k]
        if step < 3:
            self.held[step + 1][...] = total
            self.start(step + 1)
        else:
            out_ref[...] = total


def forward_pair(queries, keys, values, bias):
    masks = lane_masks()
    all_scores = []
    for mine, other, one in masks:
        if bias is None:
            all_scores.append(causal_mask(dot(keys, queries * mine, 1, 1)))
        else:
            all_scores.append(dot(keys * mine + bias * one, queries * mine + one, 1, 1))
    parts = []
    stats = []
    held = []
    for h in range(2):
        mine, other, _ = masks[h]
        scores = all_scores[h]
        row_max = jnp.max(scores, axis=0, keepdims=True)
        probs = jnp.exp(scores - row_max).astype(BF)
        both = dot(values * mine + other, probs, 0, 0)
        halves = (both[:HD], both[HD:])
        total = halves[1 - h]
        parts.append(halves[h] / total)
        stats.append((row_max + jnp.log(total[0:1]), row_max))
        held.append(probs)
    return jnp.concatenate(parts, axis=0).T.astype(BF), stats, held


def backward_pair(queries, grad, keys, values, probs_of, delta):
    grad_k = None
    grad_v = None
    grad_q = []
    for h, (mine, other, one) in enumerate(lane_masks()):
        query_h = queries * mine
        grad_h = grad * mine
        probs = probs_of(h, keys, query_h)
        grad_p = dot(values, grad_h, 1, 1)
        if delta is None:
            delta_h = jnp.sum(probs * grad_p, axis=0, keepdims=True)
        else:
            delta_h = delta[h]
        grad_s = (probs * (grad_p - delta_h)).astype(BF)
        term_v = dot(probs.astype(BF), grad_h, 1, 0)
        term_k = dot(grad_s, query_h, 1, 0)
        grad_v = term_v if grad_v is None else grad_v + term_v
        grad_k = term_k if grad_k is None else grad_k + term_k
        grad_q.append(dot(keys, grad_s, 0, 0)[h * HD : (h + 1) * HD])
    grad_kv = jnp.concatenate([grad_k, grad_v], axis=1).astype(BF)
    return grad_kv, jnp.concatenate(grad_q, axis=0).T.astype(BF)


def causal_probs(lse):
    return lambda h, keys, query: jnp.exp(causal_mask(dot(keys, query, 1, 1)) - lse[h])


def key_bias(keys, lens):
    row = lax.broadcasted_iota(jnp.int32, (keys, 128), 0) + lax.axis_index("z") * keys
    return jnp.where(row < lens[0:1, :], 0.0, MASKED).astype(BF)


def split_refs(refs, *counts):
    groups = []
    at = 0
    for count in counts:
        groups.append(refs[at : at + count])
        at += count
    return groups


def carried(courier, reducers, body):
    jobs = len(courier.jobs)
    sums = len(reducers)
    parts = [len(one.scratch()) for one in reducers]

    def kernel(ins, outs, scratch, refs):
        own_in, sources, summands, own_out, targets, results, own_scratch, sems, rest = split_refs(
            refs, ins, jobs, sums, outs, jobs, sums, scratch, 3, sum(parts)
        )
        step = pl.program_id(0)
        work = split_refs(rest, *parts)

        def bound():
            return [one.bind(value, refs) for one, value, refs in zip(reducers, summands, work)]

        @pl.when(step == 0)
        def _():
            courier.start(sources, targets, sems)
            for one in bound():
                one.begin()

        body(own_in, own_out, own_scratch)

        if sums:

            @pl.when(step == 1)
            def _():
                for one in bound():
                    one.after_first()

            @pl.when(step == 3)
            def _():
                for one in bound():
                    one.after_second()

        @pl.when(step == PAIRS - 1)
        def _():
            for one, result in zip(bound(), results):
                one.after_third(result)
            courier.wait(sources, targets, sems)

    return kernel


def call(courier, ident, body, args, in_specs, out_shape, out_specs, scratch, flops, summands=()):
    if summands:
        courier.in_plane = True
    reducers = [
        (Halved if value.ndim == 5 else Reducer)(courier.sizes, value.shape) for value in summands
    ]
    shapes = [(PLANES,) + value.shape[-2:] for value in summands]
    kernel = carried(courier, reducers, body)
    counts = (len(args), len(out_shape), len(scratch))
    outs = pl.pallas_call(
        lambda *refs: kernel(*counts, refs),
        grid=(PAIRS,),
        out_shape=out_shape
        + courier.out_shape()
        + [jax.ShapeDtypeStruct(shape, BF) for shape in shapes],
        in_specs=in_specs + courier.specs() + [pl.BlockSpec(memory_space=pl.ANY)] * len(shapes),
        out_specs=out_specs
        + courier.specs()
        + [pl.BlockSpec(shape, lambda p: (0, 0, 0)) for shape in shapes],
        scratch_shapes=scratch
        + courier.scratch()
        + [ref for one in reducers for ref in one.scratch()],
        compiler_params=courier.params(ident),
        cost_estimate=pl.CostEstimate(flops=flops, bytes_accessed=2**24, transcendentals=2**20),
    )(*args, *courier.values(), *summands)
    return outs[: len(out_shape)], outs[len(out_shape) :]


def reduce_all(sizes, ident, summands, scattered):
    courier = Courier(sizes, [("scatter", 0, value) for value in scattered])
    courier.in_plane = True
    courier.lines += list(range(1, PLANES))
    jobs = len(scattered)
    count = len(summands)
    reducers = [Reducer(sizes, value.shape) for value in summands]
    shapes = [value.shape[-2:] for value in summands]

    def kernel(*refs):
        sources, arrays, targets, results, sems, rest = split_refs(
            refs, jobs, count, jobs, count, 3, len(refs) - 2 * jobs - 2 * count - 3
        )
        courier.start(sources, targets, sems)
        bound = []
        last = []
        for n in range(count):
            refs_n = rest[13 * n : 13 * n + 13]
            bound.append(reducers[n].bind(arrays[n], refs_n[:9]))
            last.append(refs_n[9:])

        def leave(n):
            left, got, send, receive = last[n]
            copies = []
            for k in range(1, PLANES):
                copies.append(
                    pltpu.make_async_remote_copy(
                        src_ref=left.at[rem(lax.axis_index("z") + k, PLANES)],
                        dst_ref=got.at[k - 1],
                        send_sem=send.at[k - 1],
                        recv_sem=receive.at[k - 1],
                        device_id=courier.along(k),
                        device_id_type=pl.DeviceIdType.MESH,
                    )
                )
            return copies

        for one in bound:
            one.begin()
        for one in bound:
            one.after_first()
        for one in bound:
            one.after_second()
        for n, one in enumerate(bound):
            one.after_third(last[n][0])
            for copy in leave(n):
                copy.start()
        for n in range(count):
            for copy in leave(n):
                copy.wait()
            left, got = last[n][:2]
            total = left[lax.axis_index("z")].astype(F32)
            for k in range(PLANES - 1):
                total += got[k].astype(F32)
            results[n][...] = total
        courier.wait(sources, targets, sems)

    scratch = []
    for n in range(count):
        scratch += reducers[n].scratch() + [
            pltpu.VMEM((PLANES,) + shapes[n], BF),
            pltpu.VMEM((PLANES - 1,) + shapes[n], BF),
            pltpu.SemaphoreType.DMA((PLANES - 1,)),
            pltpu.SemaphoreType.DMA((PLANES - 1,)),
        ]
    outs = pl.pallas_call(
        kernel,
        out_shape=courier.out_shape() + [jax.ShapeDtypeStruct(shape, F32) for shape in shapes],
        in_specs=courier.specs() + [pl.BlockSpec(memory_space=pl.ANY)] * count,
        out_specs=courier.specs() + [pl.BlockSpec(memory_space=pltpu.VMEM)] * count,
        scratch_shapes=courier.scratch() + scratch,
        compiler_params=courier.params(ident),
    )(*courier.values(), *summands)
    return outs[:jobs], outs[jobs:]


def summand_of(sizes, arrays):
    devices = sizes[0] * sizes[1] * sizes[2] * sizes[3]
    parts = [a.reshape(devices, a.shape[0] // devices, a.shape[1]) for a in arrays]
    joined = parts[0] if len(parts) == 1 else jnp.concatenate(parts, axis=1)
    return joined.astype(BF).reshape(tuple(sizes) + joined.shape[1:])


def over_z(left, got):
    own = lax.dynamic_index_in_dim(left, lax.axis_index("z"), 0, keepdims=False)
    return own.astype(F32) + jnp.sum(got.astype(F32), axis=0)


def block_specs(tokens, keys):
    return dict(
        col=pl.BlockSpec((tokens, 128), lambda p: (0, p)),
        pair=pl.BlockSpec((keys, 256), lambda p: (0, p)),
        rows=pl.BlockSpec((keys, H * HD), lambda p: (0, 0)),
        weight=pl.BlockSpec((H * HD, 128), lambda p: (0, p)),
        stat=pl.BlockSpec((1, 2, tokens), lambda p: (p, 0, 0)),
    )


def rms(values, gain):
    r = lax.rsqrt(jnp.mean(values * values, axis=-1, keepdims=True) + EPSILON)
    return values * r * gain


ORDER = (1, 2, 3, 0)


def forward_part(sizes, ident, memory, length, inputs, gains, weights, key_weight, value_weight):
    tokens, width = inputs.shape
    positions = memory.shape[1]
    plane = sizes[1] * sizes[2] * sizes[3]
    keys = plane * positions
    rows = jax.ShapeDtypeStruct((tokens, width), BF)
    wide = jax.ShapeDtypeStruct((tokens, width), F32)
    stat = jax.ShapeDtypeStruct((PAIRS, 2, tokens), F32)
    near = range(1, PLANES)
    lens = jax.ShapeDtypeStruct((8, 128), jnp.int32)
    jobs = [("fetch", r, memory) for r in ORDER]
    jobs += [("line", -r, lens) for r in near] + [("line", -r, rows) for r in near]
    jobs += [("line", r, rows) for r in near] + [("line", r, stat) for r in near]
    courier = Courier(sizes, jobs)
    courier.lines = list(near)
    count = PLANES * PAIRS

    def kernel(*refs):
        ins, sources, outs, parts, targets, work, sems = split_refs(refs, 11, 1, 8, 4, 13, 8, 3)
        x_ref, self_gain, cross_gain, wq_ref, wk_ref, wv_ref, wo_ref, wc_ref = ins[:8]
        length_ref, key_ref, value_ref = ins[8:]
        (memory_ref,) = sources
        q_ref, k_ref, v_ref, lse_ref, attn_ref, hidden_ref, query_ref, top_ref = outs
        part_ref, part_lse_ref, kv_ref, probs_ref = parts
        row_buf, query_buf, out_buf, lse_buf, lens_buf, near_lens, lens_ref, load_sems = work
        copies = courier.copies(
            [memory_ref] * PLANES
            + [lens_ref] * 3
            + [query_ref] * 3
            + [out_buf.at[n] for n in range(3)]
            + [lse_buf.at[n] for n in range(3)],
            list(targets[:4])
            + [near_lens.at[n] for n in range(3)]
            + list(targets[4:]),
            sems,
        )
        own, remote = copies[:PLANES], copies[PLANES:]
        far = plane - 1
        lines = remote[PLANES * far :]
        lens_lines, query_lines, out_lines, lse_lines = split_refs(lines, 3, 3, 3, 3)
        step = pl.program_id(0)
        me = courier.me()

        def start_fetch(n):
            for copy in [own[n]] + remote[n * far : n * far + far]:
                copy.start()

        @pl.when(step == 0)
        def _():
            courier.greet()
            start_fetch(0)
            lens_ref[...] = jnp.full((8, 128), length_ref[0], jnp.int32)
            for copy in lens_lines:
                copy.start()
            values = x_ref[...].astype(F32)
            normed = rms(values, self_gain[...]).astype(BF)
            q_ref[...] = dot(normed, wq_ref[...], 1, 0).astype(BF)
            k_ref[...] = dot(normed, wk_ref[...], 1, 0).astype(BF)
            v_ref[...] = dot(normed, wv_ref[...], 1, 0).astype(BF)

            @pl.loop(0, PAIRS)
            def _(p):
                cols = pl.ds(pl.multiple_of(p * 128, 128), 128)
                out, stats, _ = forward_pair(q_ref[:, cols], k_ref[:, cols], v_ref[:, cols], None)
                attn_ref[:, cols] = out
                for h in range(2):
                    lse_ref[p, h : h + 1, :] = stats[h][0]

            hidden = values + dot(attn_ref[...], wo_ref[...], 1, 0)
            hidden_ref[...] = hidden
            normed = rms(hidden, cross_gain[...]).astype(BF)
            query_ref[...] = dot(normed, wc_ref[...], 1, 0).astype(BF)
            query_lines[0].start()

        for n, r in enumerate(ORDER):

            @pl.when(step == n * PAIRS)
            def _(n=n, r=r):
                loads = []

                def load(block):
                    at = pl.ds(pl.multiple_of(block * positions, positions), positions)
                    copy = pltpu.make_async_copy(
                        targets[n].at[block], row_buf.at[at], load_sems.at[len(loads)]
                    )
                    copy.start()
                    loads.append(copy)

                own[n].wait()
                load(me)
                for k in range(1, plane):
                    remote[n * far + k - 1].wait()
                    load(rem(me + (plane - k), plane))
                if n + 1 < PLANES:
                    start_fetch(n + 1)
                if r > 0:
                    query_lines[r - 1].wait()
                    copy = pltpu.make_async_copy(
                        targets[3 + r], query_buf, load_sems.at[plane]
                    )
                    copy.start()
                    if r + 1 < PLANES:
                        query_lines[r].start()
                    lens_lines[r - 1].wait()
                    lens_buf[...] = near_lens[r - 1]
                    copy.wait()
                else:
                    query_buf[...] = query_ref[...]
                    lens_buf[...] = lens_ref[...]
                for copy in loads:
                    copy.wait()

        phase = lax.div(step, PAIRS)
        p = rem(step, PAIRS)
        cols = pl.ds(pl.multiple_of(p * 128, 128), 128)
        both = jnp.concatenate([key_ref[...], value_ref[...]], axis=1)
        kv_ref[...] = dot(row_buf[...], both, 1, 0).astype(BF)
        bias = key_bias(keys, lens_buf[...])
        out, stats, held = forward_pair(query_buf[:, cols], kv_ref[:, :128], kv_ref[:, 128:], bias)
        out_buf[phase, :, cols] = out
        for h in range(2):
            probs_ref[h] = held[h]
            lse_buf[phase, p, h : h + 1, :] = stats[h][0]
            top_ref[phase, p, h : h + 1, :] = stats[h][1]

        for n, r in enumerate(ORDER[:-1]):

            @pl.when(step == n * PAIRS + PAIRS - 1)
            def _(r=r):
                out_lines[r - 1].start()
                lse_lines[r - 1].start()

        @pl.when(step == count - 1)
        def _():
            part_ref[...] = out_buf[PLANES - 1]
            part_lse_ref[...] = lse_buf[PLANES - 1]
            for copy in out_lines + lse_lines:
                copy.wait()

    once = pl.Buffered(1)

    def fixed(*shape):
        return pl.BlockSpec(shape, lambda t: (0,) * len(shape), pipeline_mode=once)

    def out_fixed(*shape):
        return pl.BlockSpec(shape, lambda t: (0,) * len(shape))

    def where(t):
        return rem(lax.div(t, PAIRS) + 1, PLANES), rem(t, PAIRS)

    square = fixed(width, width)
    weight = pl.BlockSpec((width, 128), lambda t: (0, rem(t, PAIRS)))
    hbm = pl.BlockSpec(memory_space=pl.ANY)
    flat = out_fixed(tokens, width)
    flat_stat = out_fixed(PAIRS, 2, tokens)
    shapes = courier.out_shape()
    outs = pl.pallas_call(
        kernel,
        grid=(count,),
        out_shape=[rows, rows, rows, stat, rows, wide, rows]
        + [jax.ShapeDtypeStruct((PLANES, PAIRS, 2, tokens), F32), rows, stat]
        + [
            jax.ShapeDtypeStruct((PLANES, keys, 2 * width), BF),
            jax.ShapeDtypeStruct((PLANES, H, keys, tokens), BF),
        ]
        + shapes[:4]
        + shapes[7:],
        in_specs=[fixed(tokens, width), fixed(width), fixed(width)]
        + [square] * 5
        + [pl.BlockSpec(memory_space=pltpu.SMEM), weight, weight, hbm],
        out_specs=[flat] * 3
        + [flat_stat]
        + [flat] * 3
        + [out_fixed(PLANES, PAIRS, 2, tokens), flat, flat_stat]
        + [
            pl.BlockSpec((None, keys, 256), lambda t: (where(t)[0], 0, where(t)[1])),
            pl.BlockSpec((None, 2, keys, tokens), lambda t: where(t) + (0, 0)),
        ]
        + [hbm] * 13,
        scratch_shapes=[
            pltpu.VMEM((keys, width), BF),
            pltpu.VMEM((tokens, width), BF),
            pltpu.VMEM((PLANES, tokens, width), BF),
            pltpu.VMEM((PLANES, PAIRS, 2, tokens), F32),
            pltpu.VMEM((8, 128), jnp.int32),
            pltpu.VMEM((3, 8, 128), jnp.int32),
            pltpu.VMEM((8, 128), jnp.int32),
            pltpu.SemaphoreType.DMA((plane + 1,)),
        ]
        + courier.scratch(),
        compiler_params=pltpu.CompilerParams(
            vmem_limit_bytes=62 * 2**20, collective_id=ident, has_side_effects=True
        ),
    )(inputs, *gains, *weights, length, key_weight, value_weight, memory)
    saved, (tops, part0, lse0, kv, probs), moved = outs[:7], outs[7:12], outs[12:]
    return dict(
        saved=saved,
        tops=tops,
        keyvals=kv,
        probs=probs,
        rows={r: moved[n] for n, r in enumerate(ORDER)},
        queries={0: saved[6], **{r: moved[3 + r] for r in near}},
        parts=[part0] + [moved[6 + r] for r in near],
        lses=[lse0] + [moved[9 + r] for r in near],
    )


def glu_parts(gate_vals):
    inner = 0.7978845608028654 * (gate_vals + 0.044715 * gate_vals * gate_vals * gate_vals)
    t = jnp.tanh(inner)
    gelu = 0.5 * gate_vals * (1.0 + t)
    slope = 0.5 * (1.0 + t) + 0.5 * gate_vals * (1.0 - t * t) * 0.7978845608028654 * (
        1.0 + 0.134145 * gate_vals * gate_vals
    )
    return gelu, slope


def spread(rows):
    both = [jnp.broadcast_to(rows[h : h + 1], (HD, rows.shape[1])) for h in range(2)]
    return jnp.concatenate(both, axis=0).T


def middle_kernel(*refs, sizes, packed):
    (
        part0,
        part1,
        part2,
        part3,
        lse0,
        lse1,
        lse2,
        lse3,
        h1_ref,
        wo_ref,
        gain_ref,
        cot_ref,
        gate_ref,
        up_ref,
        down_ref,
        out_ref,
        attn_ref,
        two_ref,
        da_ref,
        stats_ref,
        gnorm_ref,
        gwo_ref,
        *grad_refs,
        gdown_ref,
        raw_ref,
        h2_ref,
        n3_ref,
        total_ref,
        dn3_ref,
    ) = refs[: 29 + (not packed)]
    step = pl.program_id(0)
    last = pl.num_programs(0) - 1
    devices = sizes[0] * sizes[1] * sizes[2] * sizes[3]
    if packed:
        wide_ref, wide_got, tall_ref, tall_got, send, receive = refs[29:]
        core = lax.axis_index("c")

    def exchange(n):
        slot = rem(n, 2)
        return [
            pltpu.make_async_remote_copy(
                src_ref=source,
                dst_ref=target,
                send_sem=send.at[n, at],
                recv_sem=receive.at[n, at],
                device_id={"c": 1 - core},
                device_id_type=pl.DeviceIdType.MESH,
            )
            for at, (source, target) in enumerate(
                (
                    (wide_ref.at[slot, :, :, :, 1 - core], wide_got.at[n]),
                    (tall_ref.at[slot, :, :, 1 - core], tall_got.at[n]),
                )
            )
        ]
    parts = (part0, part1, part2, part3)
    lses = (lse0, lse1, lse2, lse3)

    @pl.when(step == 0)
    def _():
        for p in range(PAIRS):
            cols = pl.ds(p * 128, 128)
            values = [ref[p] for ref in lses]
            top = functools.reduce(jnp.maximum, values)
            scales = [jnp.exp(v - top) for v in values]
            total = functools.reduce(jnp.add, scales)
            stats_ref[0, p] = top + jnp.log(total)
            raw = None
            for ref, scale in zip(parts, scales):
                term = spread(scale / total) * ref[:, cols].astype(F32)
                raw = term if raw is None else raw + term
            raw_ref[:, cols] = raw
            attn_ref[:, cols] = raw.astype(BF)
        hidden = h1_ref[...] + dot(attn_ref[...], wo_ref[...], 1, 0)
        h2_ref[...] = hidden
        n3_ref[...] = rms(hidden, gain_ref[...]).astype(BF)
        total_ref[...] = hidden
        dn3_ref[...] = jnp.zeros_like(dn3_ref)
        if packed:
            barrier = pltpu.get_barrier_semaphore()
            pl.semaphore_signal(
                barrier,
                inc=1,
                device_id={"c": 1 - core},
                device_id_type=pl.DeviceIdType.MESH,
            )
            pl.semaphore_wait(barrier, 1)

    def one_chunk():
        normed = n3_ref[...]
        branch = cot_ref[...]
        gate_vals = dot(normed, gate_ref[...], 1, 0)
        up_vals = dot(normed, up_ref[...], 1, 0)
        grad_inner = dot(branch, down_ref[...], 1, 1)
        gelu, slope = glu_parts(gate_vals)
        inner = (gelu * up_vals).astype(BF)
        grad_gate = (grad_inner * up_vals * slope).astype(BF)
        grad_up = (grad_inner * gelu).astype(BF)
        total_ref[...] += dot(inner, down_ref[...], 1, 0)
        dn3_ref[...] += dot(grad_gate, gate_ref[...], 1, 1) + dot(grad_up, up_ref[...], 1, 1)
        terms = [dot(normed, grad_gate, 0, 0), dot(normed, grad_up, 0, 0)]
        if packed:
            shape = (devices, terms[0].shape[0] // devices, terms[0].shape[1])
            both = jnp.concatenate([t.reshape(shape) for t in terms], axis=1).astype(BF)
            slot = rem(step, 2)
            wide_ref[slot] = both.reshape(wide_ref.shape[1:])
            tall_ref[slot] = dot(inner, branch, 0, 0).astype(BF).reshape(tall_ref.shape[1:])
            for copy in exchange(step):
                copy.start()
        else:
            for ref, term in zip(grad_refs, terms):
                ref[...] = term
            gdown_ref[...] = dot(inner, branch, 0, 0).astype(BF).reshape(gdown_ref.shape)

    if packed:

        @pl.when(step < last)
        def _():
            one_chunk()

    else:
        one_chunk()

    @pl.when(step == last)
    def _():
        out_ref[...] = total_ref[...].astype(BF)
        hidden = h2_ref[...]
        grad = dn3_ref[...]
        r = lax.rsqrt(jnp.mean(hidden * hidden, axis=-1, keepdims=True) + EPSILON)
        u = gain_ref[...] * grad
        back = r * u - hidden * (r * r * r) * jnp.mean(u * hidden, axis=-1, keepdims=True)
        gnorm_ref[...] = jnp.sum(grad * hidden * r, axis=0, keepdims=True)
        two = cot_ref[...].astype(F32) + back
        two_ref[...] = two
        low = two.astype(BF)
        da_ref[...] = dot(low, wo_ref[...], 1, 1).astype(BF)
        gwo_ref[...] = dot(attn_ref[...], low, 0, 0).astype(BF)
        for p in range(PAIRS):
            cols = pl.ds(p * 128, 128)
            product = (da_ref[:, cols].astype(F32) * raw_ref[:, cols]).T
            for h in range(2):
                stats_ref[1, p, h : h + 1] = jnp.sum(
                    product[h * HD : (h + 1) * HD], axis=0, keepdims=True
                )

    if packed:

        @pl.when(step > 0)
        def _():
            before = step - 1
            slot = rem(before, 2)
            for copy in exchange(before):
                copy.wait()
            mine = wide_ref[slot, :, :, :, core].astype(F32)
            grad_refs[0][...] = (mine + wide_got[before].astype(F32)).astype(BF)
            mine = tall_ref[slot, :, :, core].astype(F32)
            gdown_ref[0] = (mine + tall_got[before].astype(F32)).astype(BF)


def middle(sizes, parts, lses, hidden, out_weight, gain, cotangent, gate, up, down):
    tokens, width = hidden.shape
    inner = gate.shape[1]
    chunk = 512
    count = inner // chunk
    devices = sizes[0] * sizes[1] * sizes[2] * sizes[3]
    share = width // devices
    down_share = inner // devices
    packed = share % 8 == 0 and chunk * PLANES == inner
    first = lambda p: jnp.minimum(p, count - 1)
    fixed = lambda *shape: pl.BlockSpec(shape, lambda p: (0,) * len(shape))
    whole = fixed(tokens, width)
    square = fixed(width, width)
    stat = fixed(PAIRS, 2, tokens)
    column = pl.BlockSpec((width, chunk), lambda p: (0, first(p)))
    scratch = [
        pltpu.VMEM((tokens, width), F32),
        pltpu.VMEM((tokens, width), F32),
        pltpu.VMEM((tokens, width), BF),
        pltpu.VMEM((tokens, width), F32),
        pltpu.VMEM((tokens, width), F32),
    ]
    params = dict(vmem_limit_bytes=VMEM)
    if packed:
        z, y, x, c = sizes
        wide_shape = (z, y, x, 2 * share)
        tall_shape = (y, x, down_share, width)
        grad_shapes = [
            jax.ShapeDtypeStruct(wide_shape + (inner,), BF),
            jax.ShapeDtypeStruct((z,) + tall_shape, BF),
        ]
        before = lambda p: jnp.maximum(p - 1, 0)
        grad_specs = [
            pl.BlockSpec(wide_shape + (chunk,), lambda p: (0, 0, 0, 0, before(p))),
            pl.BlockSpec((1,) + tall_shape, lambda p: (before(p), 0, 0, 0, 0)),
        ]
        scratch += [
            pltpu.VMEM((2, z, y, x, c, 2 * share, chunk), BF),
            pltpu.VMEM((count,) + wide_shape + (chunk,), BF),
            pltpu.VMEM((2, y, x, c, down_share, width), BF),
            pltpu.VMEM((count,) + tall_shape, BF),
            pltpu.SemaphoreType.DMA((count, 2)),
            pltpu.SemaphoreType.DMA((count, 2)),
        ]
        params.update(collective_id=12, has_side_effects=True)
    else:
        grad_shapes = [jax.ShapeDtypeStruct((width, inner), F32)] * 2
        grad_shapes.append(jax.ShapeDtypeStruct((devices, down_share, width), BF))
        grad_specs = [column] * 2
        grad_specs.append(
            pl.BlockSpec((chunk // down_share, down_share, width), lambda p: (p, 0, 0))
        )
    rows = jax.ShapeDtypeStruct((tokens, width), BF)
    wide = jax.ShapeDtypeStruct((tokens, width), F32)
    return pl.pallas_call(
        functools.partial(middle_kernel, sizes=sizes, packed=packed),
        grid=(count + packed,),
        out_shape=[
            rows,
            rows,
            wide,
            rows,
            jax.ShapeDtypeStruct((2, PAIRS, 2, tokens), F32),
            jax.ShapeDtypeStruct((1, width), F32),
            jax.ShapeDtypeStruct((width, width), BF),
        ]
        + grad_shapes,
        in_specs=[whole] * 4
        + [stat] * 4
        + [whole, square, fixed(width), whole]
        + [column, column, pl.BlockSpec((chunk, width), lambda p: (first(p), 0))],
        out_specs=[whole] * 4
        + [fixed(2, PAIRS, 2, tokens), fixed(1, width), square]
        + grad_specs,
        scratch_shapes=scratch,
        compiler_params=pltpu.CompilerParams(**params),
    )(*parts, *lses, hidden, out_weight, gain, cotangent, gate, up, down)


def cross_backward(
    courier, ident, r, queries, grad, keyvals, probs, tops, stats, key_weight, value_weight, summands=()
):
    tokens, keys = queries.shape[0], keyvals.shape[1]
    width = H * HD
    spec = block_specs(tokens, keys)

    def body(ins, outs, scratch):
        q_ref, da_ref, kv_ref, probs_ref, top_ref, stats_ref, wk_ref, wv_ref = ins
        dkv_ref, dq_ref, dm_ref = outs
        (total_ref,) = scratch
        step = pl.program_id(0)

        @pl.when(step == 0)
        def _():
            total_ref[...] = jnp.zeros_like(total_ref)

        def stored(h, keys_h, query_h):
            scale = jnp.exp(top_ref[0, h : h + 1, :] - stats_ref[0, 0, h : h + 1, :])
            return probs_ref[h].astype(F32) * scale

        weights = jnp.concatenate([wk_ref[...], wv_ref[...]], axis=1)
        grad_kv, grad_q = backward_pair(
            q_ref[...],
            da_ref[...],
            kv_ref[:, :128],
            kv_ref[:, 128:],
            stored,
            [stats_ref[1, 0, h : h + 1, :] for h in range(2)],
        )
        dkv_ref[...] = grad_kv
        dq_ref[...] = grad_q
        total_ref[...] += dot(grad_kv, weights, 1, 1)

        @pl.when(step == PAIRS - 1)
        def _():
            dm_ref[...] = total_ref[...].astype(BF)

    return call(
        courier,
        ident,
        body,
        [queries, grad, keyvals, probs, tops, stats, key_weight, value_weight],
        [
            spec["col"],
            spec["col"],
            pl.BlockSpec((None, keys, 256), lambda p: (r, 0, p)),
            pl.BlockSpec((None, 2, keys, tokens), lambda p: (r, p, 0, 0)),
            pl.BlockSpec((None, 1, 2, tokens), lambda p: (rem(r + 3, PLANES), p, 0, 0)),
            pl.BlockSpec((2, 1, 2, tokens), lambda p: (0, p, 0, 0)),
            spec["weight"],
            spec["weight"],
        ],
        [
            jax.ShapeDtypeStruct((keys, 2 * width), BF),
            jax.ShapeDtypeStruct((tokens, width), BF),
            jax.ShapeDtypeStruct((keys, width), BF),
        ],
        [spec["pair"], spec["col"], spec["rows"]],
        [pltpu.VMEM((keys, width), F32)],
        2**35,
        summands,
    )


def weight_terms(courier, ident, rows, grads):
    keys, width = rows[0].shape
    spec = block_specs(keys, keys)
    count = len(rows)

    def body(ins, outs, _):
        total = None
        for rows_ref, grad_ref in zip(ins[:count], ins[count:]):
            term = dot(rows_ref[...], grad_ref[...], 0, 0)
            total = term if total is None else total + term
        outs[0][...] = total[:, :128]
        outs[1][...] = total[:, 128:]

    return call(
        courier,
        ident,
        body,
        list(rows) + list(grads),
        [spec["rows"]] * count + [spec["pair"]] * count,
        [jax.ShapeDtypeStruct((width, width), F32)] * 2,
        [spec["weight"]] * 2,
        [],
        2**34,
    )


def self_backward(courier, ident, queries, grad, keys, values, lse, summand):
    tokens, width = queries.shape
    spec = block_specs(tokens, tokens)

    def body(ins, outs, _):
        q_ref, da_ref, k_ref, v_ref, lse_ref = ins
        dq_ref, dk_ref, dv_ref = outs
        grad_kv, dq_ref[...] = backward_pair(
            q_ref[...],
            da_ref[...],
            k_ref[...],
            v_ref[...],
            causal_probs([lse_ref[0, h : h + 1, :] for h in range(2)]),
            None,
        )
        dk_ref[...] = grad_kv[:, :128]
        dv_ref[...] = grad_kv[:, 128:]

    return call(
        courier,
        ident,
        body,
        [queries, grad, keys, values, lse],
        [spec["col"]] * 4 + [spec["stat"]],
        [jax.ShapeDtypeStruct((tokens, width), BF)] * 3,
        [spec["col"]] * 3,
        [],
        2**33,
        [summand],
    )


def rms_back(values, gain, grad):
    r = lax.rsqrt(jnp.mean(values * values, axis=-1, keepdims=True) + EPSILON)
    u = gain * grad
    back = r * u - values * (r * r * r) * jnp.mean(u * values, axis=-1, keepdims=True)
    return back, jnp.sum(grad * values * r, axis=0, keepdims=True)


def ending(sizes, ident, rows, grads, grad_q, grad_rows, left, two, held, lse, small_in):
    courier = Courier(
        sizes,
        [("line", PLANES - 1, grad_q[-1]), ("return", 0, grad_rows)]
        + [("scatter", 0, value) for value in left],
    )
    courier.lines = list(range(1, PLANES))
    jobs = len(courier.jobs)
    devices = sizes[0] * sizes[1] * sizes[2] * sizes[3]
    keys, width = rows[0].shape
    tokens = two.shape[0]
    share = width // devices
    chunk = 512
    cuts = keys // chunk
    groups = [Resident(sizes, (2 * share, width)) for _ in range(2)]
    groups += [Resident(sizes, (2 * share, 256)) for _ in range(6)]
    small = SmallSum(sizes, (8, width))
    early = [two] + list(held) + list(grad_q[:-1])
    far = list(rows) + list(grads) + early
    counts = (len(far), len(small_in) + 1, jobs, 6, jobs - 1, 4, len(early) - 1, 8, 3, 80, 10)

    def pack(ref, first, second, cols=EVERY):
        lanes = first.shape[1]
        parts = [v.astype(F32).reshape(devices, share, lanes) for v in (first, second)]
        both = jnp.concatenate(parts, axis=1).astype(BF)
        ref[:, :, :, :, :, cols] = both.reshape(tuple(sizes) + both.shape[1:])

    def kernel(*refs):
        far_refs, near, sources, outs, targets, stage, loaded, work, sems, group_refs, rest = (
            split_refs(refs, *counts)
        )
        self_gain, cross_gain, ffn_term, lse_ref = near
        grad_in, *sums, norm_sums = outs
        row_buf, grad_buf, total, load_sems = stage
        dq_got, da_ref, dq1, dk1, dv1, normed_ref, _, norm_all = work
        chunk_sems, early_sems = load_sems, work[6]
        copies = courier.copies(sources, [dq_got] + list(targets), sems)
        courier.greet()
        later = copies[6 : 1 + courier.plane]
        for n, copy in enumerate(copies):
            if not 6 <= n < 1 + courier.plane:
                copy.start()

        def chunk_loads(r, i):
            slot = rem(i, 2)
            where = pl.ds(pl.multiple_of(rem(i, cuts) * chunk, chunk), chunk)
            return [
                pltpu.make_async_copy(
                    far_refs[r].at[where], row_buf.at[slot], chunk_sems.at[slot, 0]
                ),
                pltpu.make_async_copy(
                    far_refs[PLANES + r].at[where], grad_buf.at[slot], chunk_sems.at[slot, 1]
                ),
            ]

        def start_chunk(i):
            for r in range(PLANES):

                @pl.when(lax.div(jnp.int32(i), cuts) == r)
                def _(r=r):
                    for copy in chunk_loads(r, i):
                        copy.start()

        total[...] = jnp.zeros_like(total)
        early_refs = far_refs[2 * PLANES :]
        early_loads = [
            pltpu.make_async_copy(source, target, early_sems.at[n])
            for n, (source, target) in enumerate(zip(early_refs, [grad_in] + list(loaded)))
        ]
        start_chunk(0)
        for copy in early_loads:
            copy.start()

        @pl.loop(0, PLANES * cuts)
        def _(i):
            @pl.when(i + 1 < PLANES * cuts)
            def _():
                start_chunk(i + 1)

            for copy in chunk_loads(0, i):
                copy.wait()
            slot = rem(i, 2)
            total[...] += dot(row_buf[slot], grad_buf[slot], 0, 0)

        bound = [
            one.bind(group_refs[10 * n : 10 * n + 10]) for n, one in enumerate(groups)
        ]
        bits = small.bind(rest)

        @pl.loop(0, PAIRS)
        def _(p):
            at = pl.multiple_of(p * 256, 256)
            pack(
                bound[0].held,
                total[:, pl.ds(at, 128)],
                total[:, pl.ds(at + 128, 128)],
                pl.ds(pl.multiple_of(p * 128, 128), 128),
            )

        later[0].start()
        bound[0].begin()
        for copy in early_loads:
            copy.wait()
        copies[1].wait()
        x_ref, h1_ref, gco_ref, q_ref, k_ref, v_ref, attn_ref = loaded[:7]
        wq_ref, wk_ref, wv_ref, wo_ref, wc_ref, *dq_refs = loaded[7:]
        grad = dq_got[...].astype(F32)
        for ref in dq_refs:
            grad += ref[...].astype(F32)
        dq_got[...] = grad.astype(BF)
        hidden = h1_ref[...]
        back, cross_norm = rms_back(hidden, cross_gain[...], dot(dq_got[...], wc_ref[...], 1, 1))
        grad_in[...] += back
        dv1[...] = rms(hidden, cross_gain[...]).astype(BF)
        bound[0].after_first()

        @pl.loop(0, 3)
        def _(i):
            cols = pl.ds(pl.multiple_of(i * 256, 256), 256)
            pack(bound[1].held, dot(dv1[...], dq_got[:, cols], 0, 0), gco_ref[:, cols], cols)

        bound[1].begin()
        low_ref = dq_got
        low_ref[...] = grad_in[...].astype(BF)
        da_ref[...] = dot(low_ref[...], wo_ref[...], 1, 1).astype(BF)
        values = x_ref[...].astype(F32)
        normed_ref[...] = rms(values, self_gain[...]).astype(BF)

        for third in range(3):

            @pl.loop(2 * third, 2 * third + 2)
            def _(p):
                cols = pl.ds(pl.multiple_of(p * 128, 128), 128)
                grad_kv, grad_q_p = backward_pair(
                    q_ref[:, cols],
                    da_ref[:, cols],
                    k_ref[:, cols],
                    v_ref[:, cols],
                    causal_probs([lse_ref[p, h : h + 1, :] for h in range(2)]),
                    None,
                )
                dq1[:, cols] = grad_q_p
                dk1[:, cols] = grad_kv[:, :128]
                dv1[:, cols] = grad_kv[:, 128:]

            cols = pl.ds(third * 256, 256)
            near_sum, far_sum = bound[2 + 2 * third], bound[3 + 2 * third]
            normed = normed_ref[...]
            pack(near_sum.held, dot(normed, dq1[:, cols], 0, 0), dot(normed, dk1[:, cols], 0, 0))
            near_sum.begin()
            pack(
                far_sum.held,
                dot(normed, dv1[:, cols], 0, 0),
                dot(attn_ref[...], low_ref[:, cols], 0, 0),
            )
            far_sum.begin()
            if third == 0:
                later[1].start()
                bound[0].after_second()
                bound[1].after_first()
            if third == 1:
                for copy in later[2:]:
                    copy.start()
                bound[0].after_third_start()
                bound[1].after_second()
                bound[2].after_first()
                bound[3].after_first()
            if third == 2:
                bound[1].after_third_start()
                bound[2].after_second()
                bound[3].after_second()
                bound[4].after_first()
                bound[5].after_first()
        grad_normed = (
            dot(dq1[...], wq_ref[...], 1, 1)
            + dot(dk1[...], wk_ref[...], 1, 1)
            + dot(dv1[...], wv_ref[...], 1, 1)
        )
        back, self_norm = rms_back(values, self_gain[...], grad_normed)
        grad_in[...] += back
        bits.held[0][...] = jnp.concatenate(
            [self_norm, cross_norm, ffn_term[...], jnp.zeros((5, width), F32)], axis=0
        )
        bits.start(0)
        bound[2].after_third_start()
        bound[3].after_third_start()
        bound[4].after_second()
        bound[5].after_second()
        bound[6].after_first()
        bound[7].after_first()
        bits.advance(0)
        bound[4].after_third_start()
        bound[5].after_third_start()
        bound[6].after_second()
        bound[7].after_second()
        bits.advance(1)
        bound[6].after_third_start()
        bound[7].after_third_start()
        bits.advance(2)
        bound[0].finish(sums[0])
        bound[1].finish(sums[1])
        for n in range(2, 8):
            third, kind = divmod(n - 2, 2)
            bound[n].finish(sums[2 + kind].at[:, pl.ds(third * 256, 256)])
        bits.advance(3, norm_all)
        device = lax.axis_index("z") * courier.plane + courier.me()
        lane = lax.broadcasted_iota(jnp.int32, (width, 128), 0)
        place_of = lax.broadcasted_iota(jnp.int32, (width, 128), 1) + device * share
        pick = jnp.where(lane == place_of, 1.0, 0.0)
        norm_sums[...] = lax.dot_general(
            norm_all[...],
            pick,
            (((1,), (0,)), ((), ())),
            precision=lax.Precision.HIGHEST,
            preferred_element_type=F32,
        )
        for n, copy in enumerate(copies):
            if n != 1:
                copy.wait()

    any_spec = pl.BlockSpec(memory_space=pl.ANY)
    vmem = pl.BlockSpec(memory_space=pltpu.VMEM)
    row = pltpu.VMEM((tokens, width), BF)
    scratch = [
        pltpu.VMEM((2, chunk, width), BF),
        pltpu.VMEM((2, chunk, 2 * width), BF),
        pltpu.VMEM((width, 2 * width), F32),
        pltpu.SemaphoreType.DMA((2, 2)),
    ]
    scratch += [pltpu.VMEM(v.shape, v.dtype) for v in early[1:]]
    scratch += [row] * 6 + [pltpu.SemaphoreType.DMA((len(early),))]
    scratch += [pltpu.VMEM((8, width), F32)] + courier.scratch()
    for one in groups:
        scratch += one.scratch()
    scratch += small.scratch()
    outs = pl.pallas_call(
        kernel,
        out_shape=[jax.ShapeDtypeStruct((tokens, width), F32)]
        + [jax.ShapeDtypeStruct((2 * share, width), F32)] * 4
        + [jax.ShapeDtypeStruct((8, 128), F32)]
        + courier.out_shape()[1:],
        in_specs=[any_spec] * len(far) + [vmem] * (len(small_in) + 1) + courier.specs(),
        out_specs=[vmem] * 6 + courier.specs()[1:],
        scratch_shapes=scratch,
        compiler_params=pltpu.CompilerParams(
            vmem_limit_bytes=62 * 2**20, collective_id=ident, has_side_effects=True
        ),
    )(*far, *small_in, lse, *courier.values())
    return outs[0], outs[1:5], outs[5], outs[6:]


def place_kernel(*refs):
    *blocks, out_ref, held, arrive, leave = refs
    z = lax.axis_index("z")
    size = held.shape[1]
    inward = []
    outward = []
    for r, block in enumerate(blocks):
        at = rem(z + r, PLANES) * size
        inward.append(pltpu.make_async_copy(block, held.at[r], arrive.at[r]))
        outward.append(
            pltpu.make_async_copy(held.at[r], out_ref.at[pl.ds(at, size)], leave.at[r])
        )
        inward[r].start()
    for r in range(len(blocks)):
        inward[r].wait()
        outward[r].start()
    for copy in outward:
        copy.wait()


def finish_kernel(*refs, pieces):
    ins, far, outs, far_outs, work = split_refs(refs, 9, PLANES + 2, 14, 3, 5)
    left0, got0, left1, got1, *sums, norms = ins
    gate_ref, up_ref, down_ref, *halves = outs
    halves, norm_outs = halves[:8], halves[8:]
    blocks, others = far[:PLANES], far[PLANES:]
    out_ref, *other_outs = far_outs
    held, held_in, held_out, arrive, leave = work
    z = lax.axis_index("z")
    size = held.shape[1]
    part = size // pieces
    moves = []
    for r, block in enumerate(blocks):
        at = rem(z + r, PLANES) * size
        for n in range(pieces):
            rows = pl.ds(n * part, part)
            moves.append((block.at[rows], held.at[r, rows], out_ref.at[pl.ds(at + n * part, part)]))
    moves.append((others[0], held_in, other_outs[0]))
    moves.append((others[1], held_out, other_outs[1]))
    inward = []
    outward = []
    for n, (source, middle_ref, target) in enumerate(moves):
        inward.append(pltpu.make_async_copy(source, middle_ref, arrive.at[n]))
        outward.append(pltpu.make_async_copy(middle_ref, target, leave.at[n]))
        inward[n].start()
    for n in range(len(moves)):
        inward[n].wait()
        outward[n].start()
    share = gate_ref.shape[0]
    wide = left0[z].astype(F32)
    tall = left1[z].astype(F32)
    for k in range(PLANES - 1):
        wide += got0[k].astype(F32)
        tall += got1[k].astype(F32)
    gate_ref[...] = wide[:share]
    up_ref[...] = wide[share:]
    down_ref[...] = tall
    for n, ref in enumerate(sums):
        halves[2 * n][...] = ref[:share]
        halves[2 * n + 1][...] = ref[share:]
    for n, ref in enumerate(norm_outs):
        ref[...] = norms[n : n + 1]
    for copy in outward:
        copy.wait()


def finish(blocks, left0, got0, left1, got1, sums, norms, grad_in, output):
    shape = blocks[0].shape
    pieces = 4 if shape[0] % 4 == 0 else 1
    share, inner = left0.shape[1] // 2, left0.shape[2]
    width = sums[0].shape[1]
    hbm = pl.BlockSpec(memory_space=pl.ANY)
    vmem = pl.BlockSpec(memory_space=pltpu.VMEM)
    moves = PLANES * pieces + 2
    outs = pl.pallas_call(
        functools.partial(finish_kernel, pieces=pieces),
        out_shape=[jax.ShapeDtypeStruct((share, inner), F32)] * 2
        + [jax.ShapeDtypeStruct(left1.shape[1:], F32)]
        + [jax.ShapeDtypeStruct((share, width), F32)] * 8
        + [jax.ShapeDtypeStruct((1, norms.shape[1]), F32)] * 3
        + [jax.ShapeDtypeStruct((PLANES * shape[0],) + shape[1:], BF)]
        + [jax.ShapeDtypeStruct(v.shape, v.dtype) for v in (grad_in, output)],
        in_specs=[vmem] * 9 + [hbm] * (PLANES + 2),
        out_specs=[vmem] * 14 + [hbm] * 3,
        scratch_shapes=[
            pltpu.VMEM((PLANES,) + shape, BF),
            pltpu.VMEM(grad_in.shape, grad_in.dtype),
            pltpu.VMEM(output.shape, output.dtype),
            pltpu.SemaphoreType.DMA((moves,)),
            pltpu.SemaphoreType.DMA((moves,)),
        ],
        compiler_params=pltpu.CompilerParams(vmem_limit_bytes=VMEM),
    )(left0, got0, left1, got1, *sums, norms, *blocks, grad_in, output)
    return outs[:3], outs[3:11], outs[11:14], outs[14:]


def place(blocks):
    shape = blocks[0].shape
    count = len(blocks)
    hbm = pl.BlockSpec(memory_space=pl.ANY)
    return pl.pallas_call(
        place_kernel,
        out_shape=jax.ShapeDtypeStruct((count * shape[0],) + shape[1:], blocks[0].dtype),
        in_specs=[hbm] * count,
        out_specs=hbm,
        scratch_shapes=[
            pltpu.VMEM((count,) + shape, blocks[0].dtype),
            pltpu.SemaphoreType.DMA((count,)),
            pltpu.SemaphoreType.DMA((count,)),
        ],
        compiler_params=pltpu.CompilerParams(vmem_limit_bytes=VMEM),
    )(*blocks)


def norm_apply(values, gain):
    return values * lax.rsqrt(jnp.mean(values * values, axis=-1, keepdims=True) + EPSILON) * gain


def norm_back(values, gain, grad):
    r = lax.rsqrt(jnp.mean(values * values, axis=-1, keepdims=True) + EPSILON)
    u = gain * grad
    dv = r * u - values * (r * r * r) * jnp.mean(u * values, axis=-1, keepdims=True)
    return dv, jnp.sum(grad * values * r, axis=0)


def matmul(left, right):
    return dot(left, right, 1, 0)


def matmul_t(left, right):
    return dot(left, right, 1, 1)


def tmatmul(left, right):
    return dot(left, right, 0, 0)


def on_device(
    sizes,
    decoder_in,
    memory,
    memory_lengths,
    cotangent,
    norm_self,
    self_query,
    self_key,
    self_value,
    self_out,
    norm_cross,
    cross_query,
    cross_key,
    cross_value,
    cross_out,
    norm_ffn,
    ffn_gate,
    ffn_up,
    ffn_down,
):
    devices, positions, width = memory.shape
    plane_size = sizes[1] * sizes[2] * sizes[3]
    z = lax.axis_index("z")

    def flat(blocks):
        return blocks.reshape(plane_size * positions, width)

    def cut(rows):
        return rows.reshape(plane_size, positions, width)

    forward = forward_part(
        sizes,
        0,
        memory,
        memory_lengths,
        decoder_in[0],
        (norm_self, norm_cross),
        (self_query, self_key, self_value, self_out, cross_query),
        cross_key,
        cross_value,
    )
    query_one, key_one, value_one, lse_one, attn_one, hidden_one, _ = forward["saved"]
    queries = forward["queries"]
    rows = {r: flat(forward["rows"][r]) for r in range(PLANES)}

    (
        output,
        attn_two,
        grad_two,
        grad_attn_two,
        stats,
        grad_norm_ffn,
        grad_cross_out,
        *grads_in,
        grad_down,
    ) = middle(
        sizes,
        forward["parts"],
        forward["lses"],
        hidden_one,
        cross_out,
        norm_ffn,
        cotangent[0],
        ffn_gate,
        ffn_up,
        ffn_down,
    )
    decoder_out = output[None]
    if len(grads_in) == 2:
        summands = {
            0: [summand_of(sizes, grads_in)],
            1: [grad_down.reshape(tuple(sizes) + grad_down.shape[1:])],
        }
    else:
        summands = {0: [grads_in[0], grad_down]}
    left, got = {}, {}

    grads = {0: grad_attn_two}
    both = {0: stats}
    grad_kv, grad_q, grad_rows, returned = {}, {}, {}, {}
    for r in range(PLANES):
        jobs = []
        if r + 1 < PLANES:
            jobs.append(("line", -(r + 1), grad_attn_two))
            jobs.append(("line", -(r + 1), stats))
        if r >= 1:
            jobs.append(("return", 0, cut(grad_rows[r - 1])))
        if r >= 2:
            jobs.append(("line", r - 1, grad_q[r - 1]))
        (grad_kv[r], grad_q[r], grad_rows[r]), moved = cross_backward(
            Courier(sizes, jobs),
            5 + r,
            r,
            queries[r],
            grads[r],
            forward["keyvals"],
            forward["probs"],
            forward["tops"],
            both[r],
            cross_key,
            cross_value,
            summands.get(r, []),
        )
        moved = list(moved)
        if r in summands:
            for value in moved[len(moved) - len(summands[r]) :]:
                left[len(left)] = value
        if r + 1 < PLANES:
            grads[r + 1], both[r + 1] = moved.pop(0), moved.pop(0)
        if r >= 1:
            returned[r - 1] = moved.pop(0)
        if r >= 2:
            grad_q[r - 1] = moved.pop(0)
    last = PLANES - 1
    part = width // devices
    if part % 8 == 0:
        decoder_in_grad, sums, norm_sums, moved = ending(
            sizes,
            9,
            [rows[r] for r in range(PLANES)],
            [grad_kv[r] for r in range(PLANES)],
            [grad_q[r] for r in range(PLANES)],
            cut(grad_rows[last]),
            [left[0], left[1]],
            grad_two,
            (decoder_in[0], hidden_one, grad_cross_out, query_one, key_one, value_one, attn_one)
            + (self_query, self_key, self_value, self_out, cross_query),
            lse_one,
            (norm_self, norm_cross, grad_norm_ffn),
        )
        returned[last], got[0], got[1] = moved
        ffn, halves, norm_rows, whole = finish(
            [returned[r] for r in range(PLANES)],
            left[0],
            got[0],
            left[1],
            got[1],
            sums,
            norm_sums,
            decoder_in_grad,
            output,
        )
        memory_grad, decoder_in_grad, output = whole
        norm_self_sum, norm_cross_sum, norm_ffn_sum = (v[0, :part] for v in norm_rows)
        sum_cross_key, sum_cross_value, sum_cross_query, sum_cross_out = halves[:4]
        return (
            output[None],
            decoder_in_grad[None],
            memory_grad,
            norm_self_sum,
            *halves[4:],
            norm_cross_sum,
            sum_cross_query,
            sum_cross_key,
            sum_cross_value,
            sum_cross_out,
            norm_ffn_sum,
            *ffn,
        )

    jobs = [
        ("line", last, grad_q[last]),
        ("return", 0, cut(grad_rows[last])),
        ("scatter", 0, left[0]),
        ("scatter", 0, left[1]),
    ]
    (grad_cross_key, grad_cross_value), (grad_q[last], returned[last], got[0], got[1]) = weight_terms(
        Courier(sizes, jobs),
        9,
        [rows[r] for r in range(PLANES)],
        [grad_kv[r] for r in range(PLANES)],
    )
    memory_grad = place([returned[r] for r in range(PLANES)])

    inputs = decoder_in[0].astype(F32)
    normed_one = norm_apply(inputs, norm_self).astype(BF)
    normed_two = norm_apply(hidden_one, norm_cross).astype(BF)
    grad_q_two = sum(grad_q[r].astype(F32) for r in range(PLANES)).astype(BF)
    grad_cross_query = tmatmul(normed_two, grad_q_two)
    grad_normed_two = matmul_t(grad_q_two, cross_query)
    back_one, grad_norm_cross = norm_back(hidden_one, norm_cross, grad_normed_two)
    grad_one = grad_two + back_one
    branch_one = grad_one.astype(BF)
    grad_self_out = tmatmul(attn_one, branch_one)
    grad_attn_one = matmul_t(branch_one, self_out).astype(BF)
    (grad_q_one, grad_k_one, grad_v_one), (cross_left,) = self_backward(
        Courier(sizes, []),
        10,
        query_one,
        grad_attn_one,
        key_one,
        value_one,
        lse_one,
        summand_of(sizes, (grad_cross_key, grad_cross_value)),
    )
    grad_normed_one = (
        matmul_t(grad_q_one, self_query)
        + matmul_t(grad_k_one, self_key)
        + matmul_t(grad_v_one, self_value)
    )
    back_in, grad_norm_self = norm_back(inputs, norm_self, grad_normed_one)
    decoder_in_grad = (grad_one + back_in)[None]
    share_of_norms = width // devices
    norms = jnp.stack(
        [g.reshape(devices, share_of_norms) for g in (grad_norm_self, grad_norm_cross, grad_norm_ffn[0])],
        axis=1,
    ).reshape(devices, 1, 3 * share_of_norms)
    norms = jnp.pad(norms, ((0, 0), (0, 15), (0, 256 - 3 * share_of_norms)))
    (cross_got,), sums = reduce_all(
        sizes,
        11,
        [
            norms.astype(BF).reshape(tuple(sizes) + norms.shape[1:]),
            summand_of(sizes, (grad_cross_query, grad_cross_out.astype(F32))),
            summand_of(sizes, (tmatmul(normed_one, grad_q_one), tmatmul(normed_one, grad_k_one))),
            summand_of(sizes, (tmatmul(normed_one, grad_v_one), grad_self_out)),
        ],
        [cross_left],
    )
    norm_sums = sums[0][0, : 3 * share_of_norms].reshape(3, share_of_norms)
    gate_up = over_z(left[0], got[0])
    cross_kv = over_z(cross_left, cross_got)
    part = share_of_norms
    return (
        decoder_out,
        decoder_in_grad,
        memory_grad,
        norm_sums[0],
        sums[2][:part],
        sums[2][part:],
        sums[3][:part],
        sums[3][part:],
        norm_sums[1],
        sums[1][:part],
        cross_kv[:part],
        cross_kv[part:],
        sums[1][part:],
        norm_sums[2],
        gate_up[:part],
        gate_up[part:],
        over_z(left[1], got[1]),
    )


def solution(mesh):
    dp, seq = mesh.devices.shape
    cores = 2
    lines = dp // PLANES
    split = Mesh(mesh.devices.reshape(PLANES, lines, seq // cores, cores), ALL)
    sizes = split.devices.shape
    first = P(ALL)
    middle = P(None, ALL)
    whole = P()
    return jax.shard_map(
        functools.partial(on_device, sizes),
        mesh=split,
        in_specs=(first, middle, first, first) + (whole,) * 14,
        out_specs=(first, first, middle) + (first,) * 14,
        check_vma=False,
    )
```

```python
import functools

import jax
import jax.numpy as jnp
from jax import lax
from jax.experimental import pallas as pl
from jax.experimental.pallas import tpu as pltpu
from jax.sharding import Mesh
from jax.sharding import PartitionSpec as P

H = 12
HD = 64
PAIRS = 6
PLANES = 4
EPSILON = 1e-06
MASKED = -1e30
VMEM = 56 * 2**20
BF = jnp.bfloat16
F32 = jnp.float32
ALL = ("z", "y", "x", "c")
PLANE = ("y", "x", "c")
EVERY = slice(None)


def dot(left, right, left_dim, right_dim):
    return lax.dot_general(
        left, right, (((left_dim,), (right_dim,)), ((), ())), preferred_element_type=F32
    )


def lane_masks():
    lane = lax.broadcasted_iota(jnp.int32, (1, 2 * HD), 1)
    low = jnp.where(lane < HD, 1.0, 0.0)
    first = jnp.where(lane == HD, 1.0, 0.0)
    second = jnp.where(lane == 0, 1.0, 0.0)
    low, high, first, second = (
        v.astype(BF) for v in (low, 1.0 - low, first, second)
    )
    return ((low, high, first), (high, low, second))


def causal_mask(scores):
    key = lax.broadcasted_iota(jnp.int32, scores.shape, 0)
    query = lax.broadcasted_iota(jnp.int32, scores.shape, 1)
    return jnp.where(key <= query, scores, MASKED)


def rem(value, size):
    return lax.rem(value, size)


class Courier:
    def __init__(self, sizes, jobs):
        self.sizes = sizes
        self.jobs = jobs
        self.plane = sizes[1] * sizes[2] * sizes[3]
        self.in_plane = any(job[0] in ("fetch", "return") for job in jobs)
        self.lines = [job[1] for job in jobs if job[0] == "line"]
        for job in jobs:
            if job[0] == "scatter":
                self.lines += list(range(1, PLANES))

    def out_shape(self):
        shapes = []
        for kind, _, value in self.jobs:
            shape = value.shape
            if kind == "fetch":
                shape = (self.plane,) + shape[1:]
            elif kind == "scatter":
                shape = (PLANES - 1,) + shape[1:]
            shapes.append(jax.ShapeDtypeStruct(shape, value.dtype))
        return shapes

    def specs(self):
        return [pl.BlockSpec(memory_space=pl.ANY)] * len(self.jobs)

    def values(self):
        return [job[2] for job in self.jobs]

    def scratch(self):
        each = {"line": 1, "scatter": PLANES - 1}
        count = max(1, sum(each.get(job[0], self.plane - 1) for job in self.jobs))
        own = max(1, sum(job[0] in ("fetch", "return") for job in self.jobs))
        return [pltpu.SemaphoreType.DMA((n,)) for n in (count, count, own)]

    def params(self, ident):
        return pltpu.CompilerParams(
            vmem_limit_bytes=VMEM, collective_id=ident, has_side_effects=True
        )

    def me(self):
        _, _, x_size, c_size = self.sizes
        y, x, c = (lax.axis_index(name) for name in PLANE)
        return (y * x_size + x) * c_size + c

    def along(self, offset):
        return {"z": rem(lax.axis_index("z") + (offset + PLANES), PLANES)}

    def across(self, offset):
        _, _, x_size, c_size = self.sizes
        other = rem(self.me() + offset, self.plane)
        line = lax.div(other, c_size)
        return other, {"y": lax.div(line, x_size), "x": rem(line, x_size), "c": rem(other, c_size)}

    def greet(self):
        barrier = pltpu.get_barrier_semaphore()
        count = 0
        if self.in_plane:
            for k in range(1, self.plane):
                _, device = self.across(k)
                pl.semaphore_signal(
                    barrier, inc=1, device_id=device, device_id_type=pl.DeviceIdType.MESH
                )
                count += 1
        for offset in self.lines:
            pl.semaphore_signal(
                barrier,
                inc=1,
                device_id=self.along(-offset),
                device_id_type=pl.DeviceIdType.MESH,
            )
            count += 1
        pl.semaphore_wait(barrier, count)

    def copies(self, sources, targets, sems):
        send, receive, own = sems
        remote = []
        local = []

        def add(source, target, device):
            n = len(remote)
            remote.append(
                pltpu.make_async_remote_copy(
                    src_ref=source,
                    dst_ref=target,
                    send_sem=send.at[n],
                    recv_sem=receive.at[n],
                    device_id=device,
                    device_id_type=pl.DeviceIdType.MESH,
                )
            )

        me = self.me()
        for (kind, offset, _), source, target in zip(self.jobs, sources, targets):
            if kind == "line":
                add(source, target, self.along(offset))
                continue
            if kind == "scatter":
                for k in range(1, PLANES):
                    there = rem(lax.axis_index("z") + k, PLANES)
                    add(source.at[there], target.at[k - 1], self.along(k))
                continue
            base = 0
            if kind == "fetch":
                base = rem(lax.axis_index("z") + offset, PLANES) * self.plane
            for k in range(1, self.plane):
                other, device = self.across(k)
                add(source.at[base + other], target.at[me], device)
            local.append(
                pltpu.make_async_copy(source.at[base + me], target.at[me], own.at[len(local)])
            )
        return local + remote

    def start(self, sources, targets, sems):
        self.greet()
        for copy in self.copies(sources, targets, sems):
            copy.start()

    def wait(self, sources, targets, sems):
        for copy in self.copies(sources, targets, sems):
            copy.wait()


class Reducer:
    def __init__(self, sizes, shape):
        self.sizes = sizes
        self.rows, self.lanes = shape[-2:]
        self.half = self.lanes // 2

    def scratch(self):
        z, y, x, _ = self.sizes
        r, w, h = self.rows, self.lanes, self.half
        crossing = x + y - 2
        return [
            pltpu.VMEM((z, y, x, r, w), BF),
            pltpu.VMEM((z, y, x, r, w), BF),
            pltpu.VMEM((x - 1, z, y, r, h), BF),
            pltpu.VMEM((y - 1, z, x, r, h), BF),
            pltpu.VMEM((y - 1, z, r, h), BF),
            pltpu.VMEM((x - 1, z, r, h), BF),
            pltpu.SemaphoreType.DMA((1,)),
            pltpu.SemaphoreType.DMA((1 + 2 * crossing,)),
            pltpu.SemaphoreType.DMA((1 + 2 * crossing,)),
        ]

    def bind(self, source, refs):
        self.source = source
        self.held, self.got0, self.got1x, self.got1y, self.got2y, self.got2x = refs[:6]
        self.local, self.send, self.receive = refs[6:]
        self.z, self.y, self.x, self.c = (lax.axis_index(name) for name in ALL)
        return self

    def index(self, z, y, x, lanes):
        return (z, y, x, EVERY, lanes)

    def slab(self, z, y, x, lanes):
        return self.held.at[self.index(z, y, x, lanes)]

    given = slab

    def remote(self, n, source, target, device):
        return pltpu.make_async_remote_copy(
            src_ref=source,
            dst_ref=target,
            send_sem=self.send.at[n],
            recv_sem=self.receive.at[n],
            device_id=device,
            device_id_type=pl.DeviceIdType.MESH,
        )

    def first(self):
        other = 1 - self.c
        return [
            pltpu.make_async_copy(self.source.at[:, :, :, self.c], self.held, self.local.at[0]),
            self.remote(0, self.source.at[:, :, :, other], self.got0, {"c": other}),
        ]

    def second(self):
        _, y_size, x_size, _ = self.sizes
        left, right = pl.ds(0, self.half), pl.ds(self.half, self.half)
        copies = []
        for k in range(1, x_size):
            there = rem(self.x + k, x_size)
            copies.append((self.given(EVERY, EVERY, there, left), self.got1x.at[k - 1], {"x": there}))
        for k in range(1, y_size):
            there = rem(self.y + k, y_size)
            copies.append((self.given(EVERY, there, EVERY, right), self.got1y.at[k - 1], {"y": there}))
        return [self.remote(1 + n, *copy) for n, copy in enumerate(copies)]

    def third(self):
        _, y_size, x_size, _ = self.sizes
        left, right = pl.ds(0, self.half), pl.ds(self.half, self.half)
        at = 1 + x_size + y_size - 2
        copies = []
        for k in range(1, y_size):
            there = rem(self.y + k, y_size)
            copies.append(
                (self.slab(EVERY, there, self.x, left), self.got2y.at[k - 1], {"y": there})
            )
        for k in range(1, x_size):
            there = rem(self.x + k, x_size)
            copies.append(
                (self.slab(EVERY, self.y, there, right), self.got2x.at[k - 1], {"x": there})
            )
        return [self.remote(at + n, *copy) for n, copy in enumerate(copies)]

    def begin(self):
        for copy in self.first():
            copy.start()

    def after_first(self):
        for copy in self.first():
            copy.wait()

        @pl.loop(0, self.sizes[0])
        def _(z):
            at = self.index(z, EVERY, EVERY, EVERY)
            self.held[at] = (self.held[at].astype(F32) + self.got0[z].astype(F32)).astype(BF)

        for copy in self.second():
            copy.start()

    def after_second(self):
        _, y_size, x_size, _ = self.sizes
        for copy in self.second():
            copy.wait()
        h = self.half

        @pl.loop(0, self.sizes[0])
        def _(z):
            for y in range(y_size):
                at = self.index(z, y, self.x, pl.ds(0, h))
                total = self.held[at].astype(F32)
                for k in range(x_size - 1):
                    total += self.got1x[k, z, y].astype(F32)
                self.held[at] = total.astype(BF)
            for x in range(x_size):
                at = self.index(z, self.y, x, pl.ds(h, h))
                total = self.held[at].astype(F32)
                for k in range(y_size - 1):
                    total += self.got1y[k, z, x].astype(F32)
                self.held[at] = total.astype(BF)

        for copy in self.third():
            copy.start()

    def after_third(self, out_ref):
        _, y_size, x_size, _ = self.sizes
        for copy in self.third():
            copy.wait()
        h = self.half

        @pl.loop(0, self.sizes[0])
        def _(z):
            total = self.held[self.index(z, self.y, self.x, pl.ds(0, h))].astype(F32)
            for k in range(y_size - 1):
                total += self.got2y[k, z].astype(F32)
            out_ref[z, :, :h] = total.astype(BF)
            total = self.held[self.index(z, self.y, self.x, pl.ds(h, h))].astype(F32)
            for k in range(x_size - 1):
                total += self.got2x[k, z].astype(F32)
            out_ref[z, :, h:] = total.astype(BF)


class Halved(Reducer):
    def scratch(self):
        z, y, x, _ = self.sizes
        r, w, h = self.rows, self.lanes, self.half
        crossing = x + y - 2
        return [
            pltpu.VMEM((z, y, x, r, w), BF),
            pltpu.VMEM((x - 1, z, y, r, h), BF),
            pltpu.VMEM((y - 1, z, x, r, h), BF),
            pltpu.VMEM((y - 1, z, r, h), BF),
            pltpu.VMEM((x - 1, z, r, h), BF),
            pltpu.SemaphoreType.DMA((1,)),
            pltpu.SemaphoreType.DMA((1 + 2 * crossing,)),
            pltpu.SemaphoreType.DMA((1 + 2 * crossing,)),
        ]

    def bind(self, source, refs):
        self.source = source
        self.held, self.got1x, self.got1y, self.got2y, self.got2x = refs[:5]
        self.local, self.send, self.receive = refs[5:]
        self.z, self.y, self.x, self.c = (lax.axis_index(name) for name in ALL)
        return self

    def given(self, z, y, x, lanes):
        return self.source.at[self.index(z, y, x, lanes)]

    def first(self):
        return [pltpu.make_async_copy(self.source, self.held, self.local.at[0])]

    def begin(self):
        for copy in self.first() + self.second():
            copy.start()

    def after_first(self):
        pass

    def after_second(self):
        for copy in self.first():
            copy.wait()
        super().after_second()


class Resident(Reducer):
    def scratch(self):
        z, y, x, c = self.sizes
        r, w, h = self.rows, self.lanes, self.half
        count = 1 + 2 * (x + y - 2) + z - 1
        return [
            pltpu.VMEM((z, y, x, c, r, w), BF),
            pltpu.VMEM((z, y, x, r, w), BF),
            pltpu.VMEM((x - 1, z, y, r, h), BF),
            pltpu.VMEM((y - 1, z, x, r, h), BF),
            pltpu.VMEM((y - 1, z, r, h), BF),
            pltpu.VMEM((x - 1, z, r, h), BF),
            pltpu.VMEM((z, r, w), BF),
            pltpu.VMEM((z - 1, r, w), BF),
            pltpu.SemaphoreType.DMA((count,)),
            pltpu.SemaphoreType.DMA((count,)),
        ]

    def bind(self, refs):
        self.held, self.got0, self.got1x, self.got1y, self.got2y, self.got2x = refs[:6]
        self.left, self.got3, self.send, self.receive = refs[6:]
        self.z, self.y, self.x, self.c = (lax.axis_index(name) for name in ALL)
        return self

    def index(self, z, y, x, lanes):
        return (z, y, x, self.c, EVERY, lanes)

    def first(self):
        other = 1 - self.c
        return [self.remote(0, self.held.at[:, :, :, other], self.got0, {"c": other})]

    def fourth(self):
        _, y_size, x_size, _ = self.sizes
        at = 1 + 2 * (x_size + y_size - 2)
        copies = []
        for k in range(1, PLANES):
            there = rem(self.z + k, PLANES)
            copies.append(
                self.remote(at + k - 1, self.left.at[there], self.got3.at[k - 1], {"z": there})
            )
        return copies

    def after_third_start(self):
        self.after_third(self.left)
        for copy in self.fourth():
            copy.start()

    def finish(self, out_ref):
        for copy in self.fourth():
            copy.wait()
        total = self.left[self.z].astype(F32)
        for k in range(PLANES - 1):
            total += self.got3[k].astype(F32)
        out_ref[...] = total


class SmallSum:
    def __init__(self, sizes, shape):
        self.shape = shape
        self.steps = list(zip(("c", "x", "y", "z"), (sizes[3], sizes[2], sizes[1], sizes[0])))

    def scratch(self):
        count = sum(n - 1 for _, n in self.steps)
        return (
            [pltpu.VMEM(self.shape, F32) for _ in range(4)]
            + [pltpu.VMEM((n - 1,) + self.shape, F32) for _, n in self.steps]
            + [pltpu.SemaphoreType.DMA((count,))] * 2
        )

    def bind(self, refs):
        self.held, self.got = refs[:4], refs[4:8]
        self.send, self.receive = refs[8:]
        return self

    def copies(self, step):
        axis, n = self.steps[step]
        at = sum(m - 1 for _, m in self.steps[:step])
        me = lax.axis_index(axis)
        return [
            pltpu.make_async_remote_copy(
                src_ref=self.held[step],
                dst_ref=self.got[step].at[k - 1],
                send_sem=self.send.at[at + k - 1],
                recv_sem=self.receive.at[at + k - 1],
                device_id={axis: rem(me + k, n)},
                device_id_type=pl.DeviceIdType.MESH,
            )
            for k in range(1, n)
        ]

    def start(self, step):
        for copy in self.copies(step):
            copy.start()

    def advance(self, step, out_ref=None):
        for copy in self.copies(step):
            copy.wait()
        total = self.held[step][...]
        for k in range(self.steps[step][1] - 1):
            total += self.got[step][k]
        if step < 3:
            self.held[step + 1][...] = total
            self.start(step + 1)
        else:
            out_ref[...] = total


def forward_pair(queries, keys, values, bias):
    masks = lane_masks()
    all_scores = []
    for mine, other, one in masks:
        if bias is None:
            all_scores.append(causal_mask(dot(keys, queries * mine, 1, 1)))
        else:
            all_scores.append(dot(keys * mine + bias * one, queries * mine + one, 1, 1))
    parts = []
    stats = []
    held = []
    for h in range(2):
        mine, other, _ = masks[h]
        scores = all_scores[h]
        row_max = jnp.max(scores, axis=0, keepdims=True)
        probs = jnp.exp(scores - row_max).astype(BF)
        both = dot(values * mine + other, probs, 0, 0)
        halves = (both[:HD], both[HD:])
        total = halves[1 - h]
        parts.append(halves[h] / total)
        stats.append((row_max + jnp.log(total[0:1]), row_max))
        held.append(probs)
    return jnp.concatenate(parts, axis=0).T.astype(BF), stats, held


def backward_pair(queries, grad, keys, values, probs_of, delta):
    grad_k = None
    grad_v = None
    grad_q = []
    for h, (mine, other, one) in enumerate(lane_masks()):
        query_h = queries * mine
        grad_h = grad * mine
        probs = probs_of(h, keys, query_h)
        grad_p = dot(values, grad_h, 1, 1)
        if delta is None:
            delta_h = jnp.sum(probs * grad_p, axis=0, keepdims=True)
        else:
            delta_h = delta[h]
        grad_s = (probs * (grad_p - delta_h)).astype(BF)
        term_v = dot(probs.astype(BF), grad_h, 1, 0)
        term_k = dot(grad_s, query_h, 1, 0)
        grad_v = term_v if grad_v is None else grad_v + term_v
        grad_k = term_k if grad_k is None else grad_k + term_k
        grad_q.append(dot(keys, grad_s, 0, 0)[h * HD : (h + 1) * HD])
    grad_kv = jnp.concatenate([grad_k, grad_v], axis=1).astype(BF)
    return grad_kv, jnp.concatenate(grad_q, axis=0).T.astype(BF)


def causal_probs(lse):
    return lambda h, keys, query: jnp.exp(causal_mask(dot(keys, query, 1, 1)) - lse[h])


def key_bias(keys, lens):
    row = lax.broadcasted_iota(jnp.int32, (keys, 128), 0) + lax.axis_index("z") * keys
    return jnp.where(row < lens[0:1, :], 0.0, MASKED).astype(BF)


def split_refs(refs, *counts):
    groups = []
    at = 0
    for count in counts:
        groups.append(refs[at : at + count])
        at += count
    return groups


def carried(courier, reducers, body):
    jobs = len(courier.jobs)
    sums = len(reducers)
    parts = [len(one.scratch()) for one in reducers]

    def kernel(ins, outs, scratch, refs):
        own_in, sources, summands, own_out, targets, results, own_scratch, sems, rest = split_refs(
            refs, ins, jobs, sums, outs, jobs, sums, scratch, 3, sum(parts)
        )
        step = pl.program_id(0)
        work = split_refs(rest, *parts)

        def bound():
            return [one.bind(value, refs) for one, value, refs in zip(reducers, summands, work)]

        @pl.when(step == 0)
        def _():
            courier.start(sources, targets, sems)
            for one in bound():
                one.begin()

        body(own_in, own_out, own_scratch)

        if sums:

            @pl.when(step == 1)
            def _():
                for one in bound():
                    one.after_first()

            @pl.when(step == 3)
            def _():
                for one in bound():
                    one.after_second()

        @pl.when(step == PAIRS - 1)
        def _():
            for one, result in zip(bound(), results):
                one.after_third(result)
            courier.wait(sources, targets, sems)

    return kernel


def call(courier, ident, body, args, in_specs, out_shape, out_specs, scratch, flops, summands=()):
    if summands:
        courier.in_plane = True
    reducers = [
        (Halved if value.ndim == 5 else Reducer)(courier.sizes, value.shape) for value in summands
    ]
    shapes = [(PLANES,) + value.shape[-2:] for value in summands]
    kernel = carried(courier, reducers, body)
    counts = (len(args), len(out_shape), len(scratch))
    outs = pl.pallas_call(
        lambda *refs: kernel(*counts, refs),
        grid=(PAIRS,),
        out_shape=out_shape
        + courier.out_shape()
        + [jax.ShapeDtypeStruct(shape, BF) for shape in shapes],
        in_specs=in_specs + courier.specs() + [pl.BlockSpec(memory_space=pl.ANY)] * len(shapes),
        out_specs=out_specs
        + courier.specs()
        + [pl.BlockSpec(shape, lambda p: (0, 0, 0)) for shape in shapes],
        scratch_shapes=scratch
        + courier.scratch()
        + [ref for one in reducers for ref in one.scratch()],
        compiler_params=courier.params(ident),
        cost_estimate=pl.CostEstimate(flops=flops, bytes_accessed=2**24, transcendentals=2**20),
    )(*args, *courier.values(), *summands)
    return outs[: len(out_shape)], outs[len(out_shape) :]


def reduce_all(sizes, ident, summands, scattered):
    courier = Courier(sizes, [("scatter", 0, value) for value in scattered])
    courier.in_plane = True
    courier.lines += list(range(1, PLANES))
    jobs = len(scattered)
    count = len(summands)
    reducers = [Reducer(sizes, value.shape) for value in summands]
    shapes = [value.shape[-2:] for value in summands]

    def kernel(*refs):
        sources, arrays, targets, results, sems, rest = split_refs(
            refs, jobs, count, jobs, count, 3, len(refs) - 2 * jobs - 2 * count - 3
        )
        courier.start(sources, targets, sems)
        bound = []
        last = []
        for n in range(count):
            refs_n = rest[13 * n : 13 * n + 13]
            bound.append(reducers[n].bind(arrays[n], refs_n[:9]))
            last.append(refs_n[9:])

        def leave(n):
            left, got, send, receive = last[n]
            copies = []
            for k in range(1, PLANES):
                copies.append(
                    pltpu.make_async_remote_copy(
                        src_ref=left.at[rem(lax.axis_index("z") + k, PLANES)],
                        dst_ref=got.at[k - 1],
                        send_sem=send.at[k - 1],
                        recv_sem=receive.at[k - 1],
                        device_id=courier.along(k),
                        device_id_type=pl.DeviceIdType.MESH,
                    )
                )
            return copies

        for one in bound:
            one.begin()
        for one in bound:
            one.after_first()
        for one in bound:
            one.after_second()
        for n, one in enumerate(bound):
            one.after_third(last[n][0])
            for copy in leave(n):
                copy.start()
        for n in range(count):
            for copy in leave(n):
                copy.wait()
            left, got = last[n][:2]
            total = left[lax.axis_index("z")].astype(F32)
            for k in range(PLANES - 1):
                total += got[k].astype(F32)
            results[n][...] = total
        courier.wait(sources, targets, sems)

    scratch = []
    for n in range(count):
        scratch += reducers[n].scratch() + [
            pltpu.VMEM((PLANES,) + shapes[n], BF),
            pltpu.VMEM((PLANES - 1,) + shapes[n], BF),
            pltpu.SemaphoreType.DMA((PLANES - 1,)),
            pltpu.SemaphoreType.DMA((PLANES - 1,)),
        ]
    outs = pl.pallas_call(
        kernel,
        out_shape=courier.out_shape() + [jax.ShapeDtypeStruct(shape, F32) for shape in shapes],
        in_specs=courier.specs() + [pl.BlockSpec(memory_space=pl.ANY)] * count,
        out_specs=courier.specs() + [pl.BlockSpec(memory_space=pltpu.VMEM)] * count,
        scratch_shapes=courier.scratch() + scratch,
        compiler_params=courier.params(ident),
    )(*courier.values(), *summands)
    return outs[:jobs], outs[jobs:]


def summand_of(sizes, arrays):
    devices = sizes[0] * sizes[1] * sizes[2] * sizes[3]
    parts = [a.reshape(devices, a.shape[0] // devices, a.shape[1]) for a in arrays]
    joined = parts[0] if len(parts) == 1 else jnp.concatenate(parts, axis=1)
    return joined.astype(BF).reshape(tuple(sizes) + joined.shape[1:])


def over_z(left, got):
    own = lax.dynamic_index_in_dim(left, lax.axis_index("z"), 0, keepdims=False)
    return own.astype(F32) + jnp.sum(got.astype(F32), axis=0)


def block_specs(tokens, keys):
    return dict(
        col=pl.BlockSpec((tokens, 128), lambda p: (0, p)),
        pair=pl.BlockSpec((keys, 256), lambda p: (0, p)),
        rows=pl.BlockSpec((keys, H * HD), lambda p: (0, 0)),
        weight=pl.BlockSpec((H * HD, 128), lambda p: (0, p)),
        stat=pl.BlockSpec((1, 2, tokens), lambda p: (p, 0, 0)),
    )


def rms(values, gain):
    r = lax.rsqrt(jnp.mean(values * values, axis=-1, keepdims=True) + EPSILON)
    return values * r * gain


ORDER = (1, 2, 3, 0)


def forward_part(sizes, ident, memory, length, inputs, gains, weights, key_weight, value_weight):
    tokens, width = inputs.shape
    positions = memory.shape[1]
    plane = sizes[1] * sizes[2] * sizes[3]
    keys = plane * positions
    rows = jax.ShapeDtypeStruct((tokens, width), BF)
    wide = jax.ShapeDtypeStruct((tokens, width), F32)
    stat = jax.ShapeDtypeStruct((PAIRS, 2, tokens), F32)
    near = range(1, PLANES)
    lens = jax.ShapeDtypeStruct((8, 128), jnp.int32)
    jobs = [("fetch", r, memory) for r in ORDER]
    jobs += [("line", -r, lens) for r in near] + [("line", -r, rows) for r in near]
    jobs += [("line", r, rows) for r in near] + [("line", r, stat) for r in near]
    courier = Courier(sizes, jobs)
    courier.lines = list(near)
    count = PLANES * PAIRS

    def kernel(*refs):
        ins, sources, outs, parts, targets, work, sems = split_refs(refs, 11, 1, 8, 4, 13, 8, 3)
        x_ref, self_gain, cross_gain, wq_ref, wk_ref, wv_ref, wo_ref, wc_ref = ins[:8]
        length_ref, key_ref, value_ref = ins[8:]
        (memory_ref,) = sources
        q_ref, k_ref, v_ref, lse_ref, attn_ref, hidden_ref, query_ref, top_ref = outs
        part_ref, part_lse_ref, kv_ref, probs_ref = parts
        row_buf, query_buf, out_buf, lse_buf, lens_buf, near_lens, lens_ref, load_sems = work
        copies = courier.copies(
            [memory_ref] * PLANES
            + [lens_ref] * 3
            + [query_ref] * 3
            + [out_buf.at[n] for n in range(3)]
            + [lse_buf.at[n] for n in range(3)],
            list(targets[:4])
            + [near_lens.at[n] for n in range(3)]
            + list(targets[4:]),
            sems,
        )
        own, remote = copies[:PLANES], copies[PLANES:]
        far = plane - 1
        lines = remote[PLANES * far :]
        lens_lines, query_lines, out_lines, lse_lines = split_refs(lines, 3, 3, 3, 3)
        step = pl.program_id(0)
        me = courier.me()

        def start_fetch(n):
            for copy in [own[n]] + remote[n * far : n * far + far]:
                copy.start()

        @pl.when(step == 0)
        def _():
            courier.greet()
            start_fetch(0)
            lens_ref[...] = jnp.full((8, 128), length_ref[0], jnp.int32)
            for copy in lens_lines:
                copy.start()
            values = x_ref[...].astype(F32)
            normed = rms(values, self_gain[...]).astype(BF)
            q_ref[...] = dot(normed, wq_ref[...], 1, 0).astype(BF)
            k_ref[...] = dot(normed, wk_ref[...], 1, 0).astype(BF)
            v_ref[...] = dot(normed, wv_ref[...], 1, 0).astype(BF)

            @pl.loop(0, PAIRS)
            def _(p):
                cols = pl.ds(pl.multiple_of(p * 128, 128), 128)
                out, stats, _ = forward_pair(q_ref[:, cols], k_ref[:, cols], v_ref[:, cols], None)
                attn_ref[:, cols] = out
                for h in range(2):
                    lse_ref[p, h : h + 1, :] = stats[h][0]

            hidden = values + dot(attn_ref[...], wo_ref[...], 1, 0)
            hidden_ref[...] = hidden
            normed = rms(hidden, cross_gain[...]).astype(BF)
            query_ref[...] = dot(normed, wc_ref[...], 1, 0).astype(BF)
            query_lines[0].start()

        for n, r in enumerate(ORDER):

            @pl.when(step == n * PAIRS)
            def _(n=n, r=r):
                loads = []

                def load(block):
                    at = pl.ds(pl.multiple_of(block * positions, positions), positions)
                    copy = pltpu.make_async_copy(
                        targets[n].at[block], row_buf.at[at], load_sems.at[len(loads)]
                    )
                    copy.start()
                    loads.append(copy)

                own[n].wait()
                load(me)
                for k in range(1, plane):
                    remote[n * far + k - 1].wait()
                    load(rem(me + (plane - k), plane))
                if n + 1 < PLANES:
                    start_fetch(n + 1)
                if r > 0:
                    query_lines[r - 1].wait()
                    copy = pltpu.make_async_copy(
                        targets[3 + r], query_buf, load_sems.at[plane]
                    )
                    copy.start()
                    if r + 1 < PLANES:
                        query_lines[r].start()
                    lens_lines[r - 1].wait()
                    lens_buf[...] = near_lens[r - 1]
                    copy.wait()
                else:
                    query_buf[...] = query_ref[...]
                    lens_buf[...] = lens_ref[...]
                for copy in loads:
                    copy.wait()

        phase = lax.div(step, PAIRS)
        p = rem(step, PAIRS)
        cols = pl.ds(pl.multiple_of(p * 128, 128), 128)
        both = jnp.concatenate([key_ref[...], value_ref[...]], axis=1)
        kv_ref[...] = dot(row_buf[...], both, 1, 0).astype(BF)
        bias = key_bias(keys, lens_buf[...])
        out, stats, held = forward_pair(query_buf[:, cols], kv_ref[:, :128], kv_ref[:, 128:], bias)
        out_buf[phase, :, cols] = out
        for h in range(2):
            probs_ref[h] = held[h]
            lse_buf[phase, p, h : h + 1, :] = stats[h][0]
            top_ref[phase, p, h : h + 1, :] = stats[h][1]

        for n, r in enumerate(ORDER[:-1]):

            @pl.when(step == n * PAIRS + PAIRS - 1)
            def _(r=r):
                out_lines[r - 1].start()
                lse_lines[r - 1].start()

        @pl.when(step == count - 1)
        def _():
            part_ref[...] = out_buf[PLANES - 1]
            part_lse_ref[...] = lse_buf[PLANES - 1]
            for copy in out_lines + lse_lines:
                copy.wait()

    once = pl.Buffered(1)

    def fixed(*shape):
        return pl.BlockSpec(shape, lambda t: (0,) * len(shape), pipeline_mode=once)

    def out_fixed(*shape):
        return pl.BlockSpec(shape, lambda t: (0,) * len(shape))

    def where(t):
        return rem(lax.div(t, PAIRS) + 1, PLANES), rem(t, PAIRS)

    square = fixed(width, width)
    weight = pl.BlockSpec((width, 128), lambda t: (0, rem(t, PAIRS)))
    hbm = pl.BlockSpec(memory_space=pl.ANY)
    flat = out_fixed(tokens, width)
    flat_stat = out_fixed(PAIRS, 2, tokens)
    shapes = courier.out_shape()
    outs = pl.pallas_call(
        kernel,
        grid=(count,),
        out_shape=[rows, rows, rows, stat, rows, wide, rows]
        + [jax.ShapeDtypeStruct((PLANES, PAIRS, 2, tokens), F32), rows, stat]
        + [
            jax.ShapeDtypeStruct((PLANES, keys, 2 * width), BF),
            jax.ShapeDtypeStruct((PLANES, H, keys, tokens), BF),
        ]
        + shapes[:4]
        + shapes[7:],
        in_specs=[fixed(tokens, width), fixed(width), fixed(width)]
        + [square] * 5
        + [pl.BlockSpec(memory_space=pltpu.SMEM), weight, weight, hbm],
        out_specs=[flat] * 3
        + [flat_stat]
        + [flat] * 3
        + [out_fixed(PLANES, PAIRS, 2, tokens), flat, flat_stat]
        + [
            pl.BlockSpec((None, keys, 256), lambda t: (where(t)[0], 0, where(t)[1])),
            pl.BlockSpec((None, 2, keys, tokens), lambda t: where(t) + (0, 0)),
        ]
        + [hbm] * 13,
        scratch_shapes=[
            pltpu.VMEM((keys, width), BF),
            pltpu.VMEM((tokens, width), BF),
            pltpu.VMEM((PLANES, tokens, width), BF),
            pltpu.VMEM((PLANES, PAIRS, 2, tokens), F32),
            pltpu.VMEM((8, 128), jnp.int32),
            pltpu.VMEM((3, 8, 128), jnp.int32),
            pltpu.VMEM((8, 128), jnp.int32),
            pltpu.SemaphoreType.DMA((plane + 1,)),
        ]
        + courier.scratch(),
        compiler_params=pltpu.CompilerParams(
            vmem_limit_bytes=62 * 2**20, collective_id=ident, has_side_effects=True
        ),
    )(inputs, *gains, *weights, length, key_weight, value_weight, memory)
    saved, (tops, part0, lse0, kv, probs), moved = outs[:7], outs[7:12], outs[12:]
    return dict(
        saved=saved,
        tops=tops,
        keyvals=kv,
        probs=probs,
        rows={r: moved[n] for n, r in enumerate(ORDER)},
        queries={0: saved[6], **{r: moved[3 + r] for r in near}},
        parts=[part0] + [moved[6 + r] for r in near],
        lses=[lse0] + [moved[9 + r] for r in near],
    )


def glu_parts(gate_vals):
    inner = 0.7978845608028654 * (gate_vals + 0.044715 * gate_vals * gate_vals * gate_vals)
    t = jnp.tanh(inner)
    gelu = 0.5 * gate_vals * (1.0 + t)
    slope = 0.5 * (1.0 + t) + 0.5 * gate_vals * (1.0 - t * t) * 0.7978845608028654 * (
        1.0 + 0.134145 * gate_vals * gate_vals
    )
    return gelu, slope


def spread(rows):
    both = [jnp.broadcast_to(rows[h : h + 1], (HD, rows.shape[1])) for h in range(2)]
    return jnp.concatenate(both, axis=0).T


def middle_kernel(*refs, sizes, packed):
    (
        part0,
        part1,
        part2,
        part3,
        lse0,
        lse1,
        lse2,
        lse3,
        h1_ref,
        wo_ref,
        gain_ref,
        cot_ref,
        gate_ref,
        up_ref,
        down_ref,
        out_ref,
        attn_ref,
        two_ref,
        da_ref,
        stats_ref,
        gnorm_ref,
        gwo_ref,
        *grad_refs,
        gdown_ref,
        raw_ref,
        h2_ref,
        n3_ref,
        total_ref,
        dn3_ref,
    ) = refs[: 29 + (not packed)]
    step = pl.program_id(0)
    last = pl.num_programs(0) - 1
    devices = sizes[0] * sizes[1] * sizes[2] * sizes[3]
    if packed:
        wide_ref, wide_got, tall_ref, tall_got, send, receive = refs[29:]
        core = lax.axis_index("c")

    def exchange(n):
        slot = rem(n, 2)
        return [
            pltpu.make_async_remote_copy(
                src_ref=source,
                dst_ref=target,
                send_sem=send.at[n, at],
                recv_sem=receive.at[n, at],
                device_id={"c": 1 - core},
                device_id_type=pl.DeviceIdType.MESH,
            )
            for at, (source, target) in enumerate(
                (
                    (wide_ref.at[slot, :, :, :, 1 - core], wide_got.at[n]),
                    (tall_ref.at[slot, :, :, 1 - core], tall_got.at[n]),
                )
            )
        ]
    parts = (part0, part1, part2, part3)
    lses = (lse0, lse1, lse2, lse3)

    @pl.when(step == 0)
    def _():
        for p in range(PAIRS):
            cols = pl.ds(p * 128, 128)
            values = [ref[p] for ref in lses]
            top = functools.reduce(jnp.maximum, values)
            scales = [jnp.exp(v - top) for v in values]
            total = functools.reduce(jnp.add, scales)
            stats_ref[0, p] = top + jnp.log(total)
            raw = None
            for ref, scale in zip(parts, scales):
                term = spread(scale / total) * ref[:, cols].astype(F32)
                raw = term if raw is None else raw + term
            raw_ref[:, cols] = raw
            attn_ref[:, cols] = raw.astype(BF)
        hidden = h1_ref[...] + dot(attn_ref[...], wo_ref[...], 1, 0)
        h2_ref[...] = hidden
        n3_ref[...] = rms(hidden, gain_ref[...]).astype(BF)
        total_ref[...] = hidden
        dn3_ref[...] = jnp.zeros_like(dn3_ref)
        if packed:
            barrier = pltpu.get_barrier_semaphore()
            pl.semaphore_signal(
                barrier,
                inc=1,
                device_id={"c": 1 - core},
                device_id_type=pl.DeviceIdType.MESH,
            )
            pl.semaphore_wait(barrier, 1)

    def one_chunk():
        normed = n3_ref[...]
        branch = cot_ref[...]
        gate_vals = dot(normed, gate_ref[...], 1, 0)
        up_vals = dot(normed, up_ref[...], 1, 0)
        grad_inner = dot(branch, down_ref[...], 1, 1)
        gelu, slope = glu_parts(gate_vals)
        inner = (gelu * up_vals).astype(BF)
        grad_gate = (grad_inner * up_vals * slope).astype(BF)
        grad_up = (grad_inner * gelu).astype(BF)
        total_ref[...] += dot(inner, down_ref[...], 1, 0)
        dn3_ref[...] += dot(grad_gate, gate_ref[...], 1, 1) + dot(grad_up, up_ref[...], 1, 1)
        terms = [dot(normed, grad_gate, 0, 0), dot(normed, grad_up, 0, 0)]
        if packed:
            shape = (devices, terms[0].shape[0] // devices, terms[0].shape[1])
            both = jnp.concatenate([t.reshape(shape) for t in terms], axis=1).astype(BF)
            slot = rem(step, 2)
            wide_ref[slot] = both.reshape(wide_ref.shape[1:])
            tall_ref[slot] = dot(inner, branch, 0, 0).astype(BF).reshape(tall_ref.shape[1:])
            for copy in exchange(step):
                copy.start()
        else:
            for ref, term in zip(grad_refs, terms):
                ref[...] = term
            gdown_ref[...] = dot(inner, branch, 0, 0).astype(BF).reshape(gdown_ref.shape)

    if packed:

        @pl.when(step < last)
        def _():
            one_chunk()

    else:
        one_chunk()

    @pl.when(step == last)
    def _():
        out_ref[...] = total_ref[...].astype(BF)
        hidden = h2_ref[...]
        grad = dn3_ref[...]
        r = lax.rsqrt(jnp.mean(hidden * hidden, axis=-1, keepdims=True) + EPSILON)
        u = gain_ref[...] * grad
        back = r * u - hidden * (r * r * r) * jnp.mean(u * hidden, axis=-1, keepdims=True)
        gnorm_ref[...] = jnp.sum(grad * hidden * r, axis=0, keepdims=True)
        two = cot_ref[...].astype(F32) + back
        two_ref[...] = two
        low = two.astype(BF)
        da_ref[...] = dot(low, wo_ref[...], 1, 1).astype(BF)
        gwo_ref[...] = dot(attn_ref[...], low, 0, 0).astype(BF)
        for p in range(PAIRS):
            cols = pl.ds(p * 128, 128)
            product = (da_ref[:, cols].astype(F32) * raw_ref[:, cols]).T
            for h in range(2):
                stats_ref[1, p, h : h + 1] = jnp.sum(
                    product[h * HD : (h + 1) * HD], axis=0, keepdims=True
                )

    if packed:

        @pl.when(step > 0)
        def _():
            before = step - 1
            slot = rem(before, 2)
            for copy in exchange(before):
                copy.wait()
            mine = wide_ref[slot, :, :, :, core].astype(F32)
            grad_refs[0][...] = (mine + wide_got[before].astype(F32)).astype(BF)
            mine = tall_ref[slot, :, :, core].astype(F32)
            gdown_ref[0] = (mine + tall_got[before].astype(F32)).astype(BF)


def middle(sizes, parts, lses, hidden, out_weight, gain, cotangent, gate, up, down):
    tokens, width = hidden.shape
    inner = gate.shape[1]
    chunk = 512
    count = inner // chunk
    devices = sizes[0] * sizes[1] * sizes[2] * sizes[3]
    share = width // devices
    down_share = inner // devices
    packed = share % 8 == 0 and chunk * PLANES == inner
    first = lambda p: jnp.minimum(p, count - 1)
    fixed = lambda *shape: pl.BlockSpec(shape, lambda p: (0,) * len(shape))
    whole = fixed(tokens, width)
    square = fixed(width, width)
    stat = fixed(PAIRS, 2, tokens)
    column = pl.BlockSpec((width, chunk), lambda p: (0, first(p)))
    scratch = [
        pltpu.VMEM((tokens, width), F32),
        pltpu.VMEM((tokens, width), F32),
        pltpu.VMEM((tokens, width), BF),
        pltpu.VMEM((tokens, width), F32),
        pltpu.VMEM((tokens, width), F32),
    ]
    params = dict(vmem_limit_bytes=VMEM)
    if packed:
        z, y, x, c = sizes
        wide_shape = (z, y, x, 2 * share)
        tall_shape = (y, x, down_share, width)
        grad_shapes = [
            jax.ShapeDtypeStruct(wide_shape + (inner,), BF),
            jax.ShapeDtypeStruct((z,) + tall_shape, BF),
        ]
        before = lambda p: jnp.maximum(p - 1, 0)
        grad_specs = [
            pl.BlockSpec(wide_shape + (chunk,), lambda p: (0, 0, 0, 0, before(p))),
            pl.BlockSpec((1,) + tall_shape, lambda p: (before(p), 0, 0, 0, 0)),
        ]
        scratch += [
            pltpu.VMEM((2, z, y, x, c, 2 * share, chunk), BF),
            pltpu.VMEM((count,) + wide_shape + (chunk,), BF),
            pltpu.VMEM((2, y, x, c, down_share, width), BF),
            pltpu.VMEM((count,) + tall_shape, BF),
            pltpu.SemaphoreType.DMA((count, 2)),
            pltpu.SemaphoreType.DMA((count, 2)),
        ]
        params.update(collective_id=12, has_side_effects=True)
    else:
        grad_shapes = [jax.ShapeDtypeStruct((width, inner), F32)] * 2
        grad_shapes.append(jax.ShapeDtypeStruct((devices, down_share, width), BF))
        grad_specs = [column] * 2
        grad_specs.append(
            pl.BlockSpec((chunk // down_share, down_share, width), lambda p: (p, 0, 0))
        )
    rows = jax.ShapeDtypeStruct((tokens, width), BF)
    wide = jax.ShapeDtypeStruct((tokens, width), F32)
    return pl.pallas_call(
        functools.partial(middle_kernel, sizes=sizes, packed=packed),
        grid=(count + packed,),
        out_shape=[
            rows,
            rows,
            wide,
            rows,
            jax.ShapeDtypeStruct((2, PAIRS, 2, tokens), F32),
            jax.ShapeDtypeStruct((1, width), F32),
            jax.ShapeDtypeStruct((width, width), BF),
        ]
        + grad_shapes,
        in_specs=[whole] * 4
        + [stat] * 4
        + [whole, square, fixed(width), whole]
        + [column, column, pl.BlockSpec((chunk, width), lambda p: (first(p), 0))],
        out_specs=[whole] * 4
        + [fixed(2, PAIRS, 2, tokens), fixed(1, width), square]
        + grad_specs,
        scratch_shapes=scratch,
        compiler_params=pltpu.CompilerParams(**params),
    )(*parts, *lses, hidden, out_weight, gain, cotangent, gate, up, down)


def cross_backward(
    courier, ident, r, queries, grad, keyvals, probs, tops, stats, key_weight, value_weight, summands=()
):
    tokens, keys = queries.shape[0], keyvals.shape[1]
    width = H * HD
    spec = block_specs(tokens, keys)

    def body(ins, outs, scratch):
        q_ref, da_ref, kv_ref, probs_ref, top_ref, stats_ref, wk_ref, wv_ref = ins
        dkv_ref, dq_ref, dm_ref = outs
        (total_ref,) = scratch
        step = pl.program_id(0)

        @pl.when(step == 0)
        def _():
            total_ref[...] = jnp.zeros_like(total_ref)

        def stored(h, keys_h, query_h):
            scale = jnp.exp(top_ref[0, h : h + 1, :] - stats_ref[0, 0, h : h + 1, :])
            return probs_ref[h].astype(F32) * scale

        weights = jnp.concatenate([wk_ref[...], wv_ref[...]], axis=1)
        grad_kv, grad_q = backward_pair(
            q_ref[...],
            da_ref[...],
            kv_ref[:, :128],
            kv_ref[:, 128:],
            stored,
            [stats_ref[1, 0, h : h + 1, :] for h in range(2)],
        )
        dkv_ref[...] = grad_kv
        dq_ref[...] = grad_q
        total_ref[...] += dot(grad_kv, weights, 1, 1)

        @pl.when(step == PAIRS - 1)
        def _():
            dm_ref[...] = total_ref[...].astype(BF)

    return call(
        courier,
        ident,
        body,
        [queries, grad, keyvals, probs, tops, stats, key_weight, value_weight],
        [
            spec["col"],
            spec["col"],
            pl.BlockSpec((None, keys, 256), lambda p: (r, 0, p)),
            pl.BlockSpec((None, 2, keys, tokens), lambda p: (r, p, 0, 0)),
            pl.BlockSpec((None, 1, 2, tokens), lambda p: (rem(r + 3, PLANES), p, 0, 0)),
            pl.BlockSpec((2, 1, 2, tokens), lambda p: (0, p, 0, 0)),
            spec["weight"],
            spec["weight"],
        ],
        [
            jax.ShapeDtypeStruct((keys, 2 * width), BF),
            jax.ShapeDtypeStruct((tokens, width), BF),
            jax.ShapeDtypeStruct((keys, width), BF),
        ],
        [spec["pair"], spec["col"], spec["rows"]],
        [pltpu.VMEM((keys, width), F32)],
        2**35,
        summands,
    )


def weight_terms(courier, ident, rows, grads):
    keys, width = rows[0].shape
    spec = block_specs(keys, keys)
    count = len(rows)

    def body(ins, outs, _):
        total = None
        for rows_ref, grad_ref in zip(ins[:count], ins[count:]):
            term = dot(rows_ref[...], grad_ref[...], 0, 0)
            total = term if total is None else total + term
        outs[0][...] = total[:, :128]
        outs[1][...] = total[:, 128:]

    return call(
        courier,
        ident,
        body,
        list(rows) + list(grads),
        [spec["rows"]] * count + [spec["pair"]] * count,
        [jax.ShapeDtypeStruct((width, width), F32)] * 2,
        [spec["weight"]] * 2,
        [],
        2**34,
    )


def self_backward(courier, ident, queries, grad, keys, values, lse, summand):
    tokens, width = queries.shape
    spec = block_specs(tokens, tokens)

    def body(ins, outs, _):
        q_ref, da_ref, k_ref, v_ref, lse_ref = ins
        dq_ref, dk_ref, dv_ref = outs
        grad_kv, dq_ref[...] = backward_pair(
            q_ref[...],
            da_ref[...],
            k_ref[...],
            v_ref[...],
            causal_probs([lse_ref[0, h : h + 1, :] for h in range(2)]),
            None,
        )
        dk_ref[...] = grad_kv[:, :128]
        dv_ref[...] = grad_kv[:, 128:]

    return call(
        courier,
        ident,
        body,
        [queries, grad, keys, values, lse],
        [spec["col"]] * 4 + [spec["stat"]],
        [jax.ShapeDtypeStruct((tokens, width), BF)] * 3,
        [spec["col"]] * 3,
        [],
        2**33,
        [summand],
    )


def rms_back(values, gain, grad):
    r = lax.rsqrt(jnp.mean(values * values, axis=-1, keepdims=True) + EPSILON)
    u = gain * grad
    back = r * u - values * (r * r * r) * jnp.mean(u * values, axis=-1, keepdims=True)
    return back, jnp.sum(grad * values * r, axis=0, keepdims=True)


def ending(sizes, ident, rows, grads, grad_q, grad_rows, left, two, held, lse, small_in):
    courier = Courier(
        sizes,
        [("line", PLANES - 1, grad_q[-1]), ("return", 0, grad_rows)]
        + [("scatter", 0, value) for value in left],
    )
    courier.lines = list(range(1, PLANES))
    jobs = len(courier.jobs)
    devices = sizes[0] * sizes[1] * sizes[2] * sizes[3]
    keys, width = rows[0].shape
    tokens = two.shape[0]
    share = width // devices
    chunk = 512
    cuts = keys // chunk
    groups = [Resident(sizes, (2 * share, width)) for _ in range(2)]
    groups += [Resident(sizes, (2 * share, 256)) for _ in range(6)]
    small = SmallSum(sizes, (8, width))
    early = [two] + list(held) + list(grad_q[:-1])
    far = list(rows) + list(grads) + early
    counts = (len(far), len(small_in) + 1, jobs, 6, jobs - 1, 4, len(early) - 1, 8, 3, 80, 10)

    def pack(ref, first, second, cols=EVERY):
        lanes = first.shape[1]
        parts = [v.astype(F32).reshape(devices, share, lanes) for v in (first, second)]
        both = jnp.concatenate(parts, axis=1).astype(BF)
        ref[:, :, :, :, :, cols] = both.reshape(tuple(sizes) + both.shape[1:])

    def kernel(*refs):
        far_refs, near, sources, outs, targets, stage, loaded, work, sems, group_refs, rest = (
            split_refs(refs, *counts)
        )
        self_gain, cross_gain, ffn_term, lse_ref = near
        grad_in, *sums, norm_sums = outs
        row_buf, grad_buf, total, load_sems = stage
        dq_got, da_ref, dq1, dk1, dv1, normed_ref, _, norm_all = work
        chunk_sems, early_sems = load_sems, work[6]
        copies = courier.copies(sources, [dq_got] + list(targets), sems)
        courier.greet()
        for copy in copies:
            copy.start()

        def chunk_loads(r, i):
            slot = rem(i, 2)
            where = pl.ds(pl.multiple_of(rem(i, cuts) * chunk, chunk), chunk)
            return [
                pltpu.make_async_copy(
                    far_refs[r].at[where], row_buf.at[slot], chunk_sems.at[slot, 0]
                ),
                pltpu.make_async_copy(
                    far_refs[PLANES + r].at[where], grad_buf.at[slot], chunk_sems.at[slot, 1]
                ),
            ]

        def start_chunk(i):
            for r in range(PLANES):

                @pl.when(lax.div(jnp.int32(i), cuts) == r)
                def _(r=r):
                    for copy in chunk_loads(r, i):
                        copy.start()

        total[...] = jnp.zeros_like(total)
        early_refs = far_refs[2 * PLANES :]
        early_loads = [
            pltpu.make_async_copy(source, target, early_sems.at[n])
            for n, (source, target) in enumerate(zip(early_refs, [grad_in] + list(loaded)))
        ]
        start_chunk(0)
        for copy in early_loads:
            copy.start()

        @pl.loop(0, PLANES * cuts)
        def _(i):
            @pl.when(i + 1 < PLANES * cuts)
            def _():
                start_chunk(i + 1)

            for copy in chunk_loads(0, i):
                copy.wait()
            slot = rem(i, 2)
            total[...] += dot(row_buf[slot], grad_buf[slot], 0, 0)

        bound = [
            one.bind(group_refs[10 * n : 10 * n + 10]) for n, one in enumerate(groups)
        ]
        bits = small.bind(rest)

        @pl.loop(0, PAIRS)
        def _(p):
            at = pl.multiple_of(p * 256, 256)
            pack(
                bound[0].held,
                total[:, pl.ds(at, 128)],
                total[:, pl.ds(at + 128, 128)],
                pl.ds(pl.multiple_of(p * 128, 128), 128),
            )

        bound[0].begin()
        for copy in early_loads:
            copy.wait()
        copies[1].wait()
        x_ref, h1_ref, gco_ref, q_ref, k_ref, v_ref, attn_ref = loaded[:7]
        wq_ref, wk_ref, wv_ref, wo_ref, wc_ref, *dq_refs = loaded[7:]
        grad = dq_got[...].astype(F32)
        for ref in dq_refs:
            grad += ref[...].astype(F32)
        dq_got[...] = grad.astype(BF)
        hidden = h1_ref[...]
        back, cross_norm = rms_back(hidden, cross_gain[...], dot(dq_got[...], wc_ref[...], 1, 1))
        grad_in[...] += back
        dv1[...] = rms(hidden, cross_gain[...]).astype(BF)
        bound[0].after_first()

        @pl.loop(0, 3)
        def _(i):
            cols = pl.ds(pl.multiple_of(i * 256, 256), 256)
            pack(bound[1].held, dot(dv1[...], dq_got[:, cols], 0, 0), gco_ref[:, cols], cols)

        bound[1].begin()
        low_ref = dq_got
        low_ref[...] = grad_in[...].astype(BF)
        da_ref[...] = dot(low_ref[...], wo_ref[...], 1, 1).astype(BF)
        values = x_ref[...].astype(F32)
        normed_ref[...] = rms(values, self_gain[...]).astype(BF)

        for third in range(3):

            @pl.loop(2 * third, 2 * third + 2)
            def _(p):
                cols = pl.ds(pl.multiple_of(p * 128, 128), 128)
                grad_kv, grad_q_p = backward_pair(
                    q_ref[:, cols],
                    da_ref[:, cols],
                    k_ref[:, cols],
                    v_ref[:, cols],
                    causal_probs([lse_ref[p, h : h + 1, :] for h in range(2)]),
                    None,
                )
                dq1[:, cols] = grad_q_p
                dk1[:, cols] = grad_kv[:, :128]
                dv1[:, cols] = grad_kv[:, 128:]

            cols = pl.ds(third * 256, 256)
            near_sum, far_sum = bound[2 + 2 * third], bound[3 + 2 * third]
            normed = normed_ref[...]
            pack(near_sum.held, dot(normed, dq1[:, cols], 0, 0), dot(normed, dk1[:, cols], 0, 0))
            near_sum.begin()
            pack(
                far_sum.held,
                dot(normed, dv1[:, cols], 0, 0),
                dot(attn_ref[...], low_ref[:, cols], 0, 0),
            )
            far_sum.begin()
            if third == 0:
                bound[0].after_second()
                bound[1].after_first()
            if third == 1:
                bound[0].after_third_start()
                bound[1].after_second()
                bound[2].after_first()
                bound[3].after_first()
            if third == 2:
                bound[1].after_third_start()
                bound[2].after_second()
                bound[3].after_second()
                bound[4].after_first()
                bound[5].after_first()
        grad_normed = (
            dot(dq1[...], wq_ref[...], 1, 1)
            + dot(dk1[...], wk_ref[...], 1, 1)
            + dot(dv1[...], wv_ref[...], 1, 1)
        )
        back, self_norm = rms_back(values, self_gain[...], grad_normed)
        grad_in[...] += back
        bits.held[0][...] = jnp.concatenate(
            [self_norm, cross_norm, ffn_term[...], jnp.zeros((5, width), F32)], axis=0
        )
        bits.start(0)
        bound[2].after_third_start()
        bound[3].after_third_start()
        bound[4].after_second()
        bound[5].after_second()
        bound[6].after_first()
        bound[7].after_first()
        bits.advance(0)
        bound[4].after_third_start()
        bound[5].after_third_start()
        bound[6].after_second()
        bound[7].after_second()
        bits.advance(1)
        bound[6].after_third_start()
        bound[7].after_third_start()
        bits.advance(2)
        bound[0].finish(sums[0])
        bound[1].finish(sums[1])
        for n in range(2, 8):
            third, kind = divmod(n - 2, 2)
            bound[n].finish(sums[2 + kind].at[:, pl.ds(third * 256, 256)])
        bits.advance(3, norm_all)
        device = lax.axis_index("z") * courier.plane + courier.me()
        lane = lax.broadcasted_iota(jnp.int32, (width, 128), 0)
        place_of = lax.broadcasted_iota(jnp.int32, (width, 128), 1) + device * share
        pick = jnp.where(lane == place_of, 1.0, 0.0)
        norm_sums[...] = lax.dot_general(
            norm_all[...],
            pick,
            (((1,), (0,)), ((), ())),
            precision=lax.Precision.HIGHEST,
            preferred_element_type=F32,
        )
        for n, copy in enumerate(copies):
            if n != 1:
                copy.wait()

    any_spec = pl.BlockSpec(memory_space=pl.ANY)
    vmem = pl.BlockSpec(memory_space=pltpu.VMEM)
    row = pltpu.VMEM((tokens, width), BF)
    scratch = [
        pltpu.VMEM((2, chunk, width), BF),
        pltpu.VMEM((2, chunk, 2 * width), BF),
        pltpu.VMEM((width, 2 * width), F32),
        pltpu.SemaphoreType.DMA((2, 2)),
    ]
    scratch += [pltpu.VMEM(v.shape, v.dtype) for v in early[1:]]
    scratch += [row] * 6 + [pltpu.SemaphoreType.DMA((len(early),))]
    scratch += [pltpu.VMEM((8, width), F32)] + courier.scratch()
    for one in groups:
        scratch += one.scratch()
    scratch += small.scratch()
    outs = pl.pallas_call(
        kernel,
        out_shape=[jax.ShapeDtypeStruct((tokens, width), F32)]
        + [jax.ShapeDtypeStruct((2 * share, width), F32)] * 4
        + [jax.ShapeDtypeStruct((8, 128), F32)]
        + courier.out_shape()[1:],
        in_specs=[any_spec] * len(far) + [vmem] * (len(small_in) + 1) + courier.specs(),
        out_specs=[vmem] * 6 + courier.specs()[1:],
        scratch_shapes=scratch,
        compiler_params=pltpu.CompilerParams(
            vmem_limit_bytes=62 * 2**20, collective_id=ident, has_side_effects=True
        ),
    )(*far, *small_in, lse, *courier.values())
    return outs[0], outs[1:5], outs[5], outs[6:]


def place_kernel(*refs):
    *blocks, out_ref, held, arrive, leave = refs
    z = lax.axis_index("z")
    size = held.shape[1]
    inward = []
    outward = []
    for r, block in enumerate(blocks):
        at = rem(z + r, PLANES) * size
        inward.append(pltpu.make_async_copy(block, held.at[r], arrive.at[r]))
        outward.append(
            pltpu.make_async_copy(held.at[r], out_ref.at[pl.ds(at, size)], leave.at[r])
        )
        inward[r].start()
    for r in range(len(blocks)):
        inward[r].wait()
        outward[r].start()
    for copy in outward:
        copy.wait()


def finish_kernel(*refs, pieces):
    ins, far, outs, far_outs, work = split_refs(refs, 9, PLANES + 2, 14, 3, 5)
    left0, got0, left1, got1, *sums, norms = ins
    gate_ref, up_ref, down_ref, *halves = outs
    halves, norm_outs = halves[:8], halves[8:]
    blocks, others = far[:PLANES], far[PLANES:]
    out_ref, *other_outs = far_outs
    held, held_in, held_out, arrive, leave = work
    z = lax.axis_index("z")
    size = held.shape[1]
    part = size // pieces
    moves = []
    for r, block in enumerate(blocks):
        at = rem(z + r, PLANES) * size
        for n in range(pieces):
            rows = pl.ds(n * part, part)
            moves.append((block.at[rows], held.at[r, rows], out_ref.at[pl.ds(at + n * part, part)]))
    moves.append((others[0], held_in, other_outs[0]))
    moves.append((others[1], held_out, other_outs[1]))
    inward = []
    outward = []
    for n, (source, middle_ref, target) in enumerate(moves):
        inward.append(pltpu.make_async_copy(source, middle_ref, arrive.at[n]))
        outward.append(pltpu.make_async_copy(middle_ref, target, leave.at[n]))
        inward[n].start()
    for n in range(len(moves)):
        inward[n].wait()
        outward[n].start()
    share = gate_ref.shape[0]
    wide = left0[z].astype(F32)
    tall = left1[z].astype(F32)
    for k in range(PLANES - 1):
        wide += got0[k].astype(F32)
        tall += got1[k].astype(F32)
    gate_ref[...] = wide[:share]
    up_ref[...] = wide[share:]
    down_ref[...] = tall
    for n, ref in enumerate(sums):
        halves[2 * n][...] = ref[:share]
        halves[2 * n + 1][...] = ref[share:]
    for n, ref in enumerate(norm_outs):
        ref[...] = norms[n : n + 1]
    for copy in outward:
        copy.wait()


def finish(blocks, left0, got0, left1, got1, sums, norms, grad_in, output):
    shape = blocks[0].shape
    pieces = 4 if shape[0] % 4 == 0 else 1
    share, inner = left0.shape[1] // 2, left0.shape[2]
    width = sums[0].shape[1]
    hbm = pl.BlockSpec(memory_space=pl.ANY)
    vmem = pl.BlockSpec(memory_space=pltpu.VMEM)
    moves = PLANES * pieces + 2
    outs = pl.pallas_call(
        functools.partial(finish_kernel, pieces=pieces),
        out_shape=[jax.ShapeDtypeStruct((share, inner), F32)] * 2
        + [jax.ShapeDtypeStruct(left1.shape[1:], F32)]
        + [jax.ShapeDtypeStruct((share, width), F32)] * 8
        + [jax.ShapeDtypeStruct((1, norms.shape[1]), F32)] * 3
        + [jax.ShapeDtypeStruct((PLANES * shape[0],) + shape[1:], BF)]
        + [jax.ShapeDtypeStruct(v.shape, v.dtype) for v in (grad_in, output)],
        in_specs=[vmem] * 9 + [hbm] * (PLANES + 2),
        out_specs=[vmem] * 14 + [hbm] * 3,
        scratch_shapes=[
            pltpu.VMEM((PLANES,) + shape, BF),
            pltpu.VMEM(grad_in.shape, grad_in.dtype),
            pltpu.VMEM(output.shape, output.dtype),
            pltpu.SemaphoreType.DMA((moves,)),
            pltpu.SemaphoreType.DMA((moves,)),
        ],
        compiler_params=pltpu.CompilerParams(vmem_limit_bytes=VMEM),
    )(left0, got0, left1, got1, *sums, norms, *blocks, grad_in, output)
    return outs[:3], outs[3:11], outs[11:14], outs[14:]


def place(blocks):
    shape = blocks[0].shape
    count = len(blocks)
    hbm = pl.BlockSpec(memory_space=pl.ANY)
    return pl.pallas_call(
        place_kernel,
        out_shape=jax.ShapeDtypeStruct((count * shape[0],) + shape[1:], blocks[0].dtype),
        in_specs=[hbm] * count,
        out_specs=hbm,
        scratch_shapes=[
            pltpu.VMEM((count,) + shape, blocks[0].dtype),
            pltpu.SemaphoreType.DMA((count,)),
            pltpu.SemaphoreType.DMA((count,)),
        ],
        compiler_params=pltpu.CompilerParams(vmem_limit_bytes=VMEM),
    )(*blocks)


def norm_apply(values, gain):
    return values * lax.rsqrt(jnp.mean(values * values, axis=-1, keepdims=True) + EPSILON) * gain


def norm_back(values, gain, grad):
    r = lax.rsqrt(jnp.mean(values * values, axis=-1, keepdims=True) + EPSILON)
    u = gain * grad
    dv = r * u - values * (r * r * r) * jnp.mean(u * values, axis=-1, keepdims=True)
    return dv, jnp.sum(grad * values * r, axis=0)


def matmul(left, right):
    return dot(left, right, 1, 0)


def matmul_t(left, right):
    return dot(left, right, 1, 1)


def tmatmul(left, right):
    return dot(left, right, 0, 0)


def on_device(
    sizes,
    decoder_in,
    memory,
    memory_lengths,
    cotangent,
    norm_self,
    self_query,
    self_key,
    self_value,
    self_out,
    norm_cross,
    cross_query,
    cross_key,
    cross_value,
    cross_out,
    norm_ffn,
    ffn_gate,
    ffn_up,
    ffn_down,
):
    devices, positions, width = memory.shape
    plane_size = sizes[1] * sizes[2] * sizes[3]
    z = lax.axis_index("z")

    def flat(blocks):
        return blocks.reshape(plane_size * positions, width)

    def cut(rows):
        return rows.reshape(plane_size, positions, width)

    forward = forward_part(
        sizes,
        0,
        memory,
        memory_lengths,
        decoder_in[0],
        (norm_self, norm_cross),
        (self_query, self_key, self_value, self_out, cross_query),
        cross_key,
        cross_value,
    )
    query_one, key_one, value_one, lse_one, attn_one, hidden_one, _ = forward["saved"]
    queries = forward["queries"]
    rows = {r: flat(forward["rows"][r]) for r in range(PLANES)}

    (
        output,
        attn_two,
        grad_two,
        grad_attn_two,
        stats,
        grad_norm_ffn,
        grad_cross_out,
        *grads_in,
        grad_down,
    ) = middle(
        sizes,
        forward["parts"],
        forward["lses"],
        hidden_one,
        cross_out,
        norm_ffn,
        cotangent[0],
        ffn_gate,
        ffn_up,
        ffn_down,
    )
    decoder_out = output[None]
    if len(grads_in) == 2:
        summands = {
            0: [summand_of(sizes, grads_in)],
            1: [grad_down.reshape(tuple(sizes) + grad_down.shape[1:])],
        }
    else:
        summands = {0: [grads_in[0], grad_down]}
    left, got = {}, {}

    grads = {0: grad_attn_two}
    both = {0: stats}
    grad_kv, grad_q, grad_rows, returned = {}, {}, {}, {}
    for r in range(PLANES):
        jobs = []
        if r + 1 < PLANES:
            jobs.append(("line", -(r + 1), grad_attn_two))
            jobs.append(("line", -(r + 1), stats))
        if r >= 1:
            jobs.append(("return", 0, cut(grad_rows[r - 1])))
        if r >= 2:
            jobs.append(("line", r - 1, grad_q[r - 1]))
        (grad_kv[r], grad_q[r], grad_rows[r]), moved = cross_backward(
            Courier(sizes, jobs),
            5 + r,
            r,
            queries[r],
            grads[r],
            forward["keyvals"],
            forward["probs"],
            forward["tops"],
            both[r],
            cross_key,
            cross_value,
            summands.get(r, []),
        )
        moved = list(moved)
        if r in summands:
            for value in moved[len(moved) - len(summands[r]) :]:
                left[len(left)] = value
        if r + 1 < PLANES:
            grads[r + 1], both[r + 1] = moved.pop(0), moved.pop(0)
        if r >= 1:
            returned[r - 1] = moved.pop(0)
        if r >= 2:
            grad_q[r - 1] = moved.pop(0)
    last = PLANES - 1
    part = width // devices
    if part % 8 == 0:
        decoder_in_grad, sums, norm_sums, moved = ending(
            sizes,
            9,
            [rows[r] for r in range(PLANES)],
            [grad_kv[r] for r in range(PLANES)],
            [grad_q[r] for r in range(PLANES)],
            cut(grad_rows[last]),
            [left[0], left[1]],
            grad_two,
            (decoder_in[0], hidden_one, grad_cross_out, query_one, key_one, value_one, attn_one)
            + (self_query, self_key, self_value, self_out, cross_query),
            lse_one,
            (norm_self, norm_cross, grad_norm_ffn),
        )
        returned[last], got[0], got[1] = moved
        ffn, halves, norm_rows, whole = finish(
            [returned[r] for r in range(PLANES)],
            left[0],
            got[0],
            left[1],
            got[1],
            sums,
            norm_sums,
            decoder_in_grad,
            output,
        )
        memory_grad, decoder_in_grad, output = whole
        norm_self_sum, norm_cross_sum, norm_ffn_sum = (v[0, :part] for v in norm_rows)
        sum_cross_key, sum_cross_value, sum_cross_query, sum_cross_out = halves[:4]
        return (
            output[None],
            decoder_in_grad[None],
            memory_grad,
            norm_self_sum,
            *halves[4:],
            norm_cross_sum,
            sum_cross_query,
            sum_cross_key,
            sum_cross_value,
            sum_cross_out,
            norm_ffn_sum,
            *ffn,
        )

    jobs = [
        ("line", last, grad_q[last]),
        ("return", 0, cut(grad_rows[last])),
        ("scatter", 0, left[0]),
        ("scatter", 0, left[1]),
    ]
    (grad_cross_key, grad_cross_value), (grad_q[last], returned[last], got[0], got[1]) = weight_terms(
        Courier(sizes, jobs),
        9,
        [rows[r] for r in range(PLANES)],
        [grad_kv[r] for r in range(PLANES)],
    )
    memory_grad = place([returned[r] for r in range(PLANES)])

    inputs = decoder_in[0].astype(F32)
    normed_one = norm_apply(inputs, norm_self).astype(BF)
    normed_two = norm_apply(hidden_one, norm_cross).astype(BF)
    grad_q_two = sum(grad_q[r].astype(F32) for r in range(PLANES)).astype(BF)
    grad_cross_query = tmatmul(normed_two, grad_q_two)
    grad_normed_two = matmul_t(grad_q_two, cross_query)
    back_one, grad_norm_cross = norm_back(hidden_one, norm_cross, grad_normed_two)
    grad_one = grad_two + back_one
    branch_one = grad_one.astype(BF)
    grad_self_out = tmatmul(attn_one, branch_one)
    grad_attn_one = matmul_t(branch_one, self_out).astype(BF)
    (grad_q_one, grad_k_one, grad_v_one), (cross_left,) = self_backward(
        Courier(sizes, []),
        10,
        query_one,
        grad_attn_one,
        key_one,
        value_one,
        lse_one,
        summand_of(sizes, (grad_cross_key, grad_cross_value)),
    )
    grad_normed_one = (
        matmul_t(grad_q_one, self_query)
        + matmul_t(grad_k_one, self_key)
        + matmul_t(grad_v_one, self_value)
    )
    back_in, grad_norm_self = norm_back(inputs, norm_self, grad_normed_one)
    decoder_in_grad = (grad_one + back_in)[None]
    share_of_norms = width // devices
    norms = jnp.stack(
        [g.reshape(devices, share_of_norms) for g in (grad_norm_self, grad_norm_cross, grad_norm_ffn[0])],
        axis=1,
    ).reshape(devices, 1, 3 * share_of_norms)
    norms = jnp.pad(norms, ((0, 0), (0, 15), (0, 256 - 3 * share_of_norms)))
    (cross_got,), sums = reduce_all(
        sizes,
        11,
        [
            norms.astype(BF).reshape(tuple(sizes) + norms.shape[1:]),
            summand_of(sizes, (grad_cross_query, grad_cross_out.astype(F32))),
            summand_of(sizes, (tmatmul(normed_one, grad_q_one), tmatmul(normed_one, grad_k_one))),
            summand_of(sizes, (tmatmul(normed_one, grad_v_one), grad_self_out)),
        ],
        [cross_left],
    )
    norm_sums = sums[0][0, : 3 * share_of_norms].reshape(3, share_of_norms)
    gate_up = over_z(left[0], got[0])
    cross_kv = over_z(cross_left, cross_got)
    part = share_of_norms
    return (
        decoder_out,
        decoder_in_grad,
        memory_grad,
        norm_sums[0],
        sums[2][:part],
        sums[2][part:],
        sums[3][:part],
        sums[3][part:],
        norm_sums[1],
        sums[1][:part],
        cross_kv[:part],
        cross_kv[part:],
        sums[1][part:],
        norm_sums[2],
        gate_up[:part],
        gate_up[part:],
        over_z(left[1], got[1]),
    )


def solution(mesh):
    dp, seq = mesh.devices.shape
    cores = 2
    lines = dp // PLANES
    split = Mesh(mesh.devices.reshape(PLANES, lines, seq // cores, cores), ALL)
    sizes = split.devices.shape
    first = P(ALL)
    middle = P(None, ALL)
    whole = P()
    return jax.shard_map(
        functools.partial(on_device, sizes),
        mesh=split,
        in_specs=(first, middle, first, first) + (whole,) * 14,
        out_specs=(first, first, middle) + (first,) * 14,
        check_vma=False,
    )
```
